32 devices in a mesh: section: 4 (over y, x), dp: 8 (over z, core).
Axes of the slice: x: 2, y: 2, z: 4, core: 2. Of those that a mesh axis runs over, the one named last changes fastest.
Arguments:
- node_table: bfloat16 [131072, 128], P('dp'), may hold values from -6 to 6
- owners: int32 [4, 245760, 1], P('section', 'dp'), may hold values from 0 to 7; in each aligned block of 30720 rows (0 to 30719, 30720 to 61439, ..., all dimensions but the last counted through in order) at most 7680 rows name the same one
- local_rows: int32 [4, 245760], P('section', 'dp'), may hold values from 0 to 16383
- inner_neighbours: int32 [4, 22528, 15], P(None, 'dp'), may hold values from 0 to 30719
- inner_counts: int32 [4, 22528], P(None, 'dp'), may hold values from 1 to 15
- outer_neighbours: int32 [4, 2048, 10], P(None, 'dp'), may hold values from 0 to 2815
- outer_counts: int32 [4, 2048], P(None, 'dp'), may hold values from 1 to 10
- labels: int32 [4, 2048], P(None, 'dp'), may hold values from 0 to 171
- label_mask: int32 [4, 2048], P(None, 'dp'), may hold values from 0 to 1, as said below
- weight_inner: float32 [256, 256], P(('section', 'dp')), may hold values from -0.375 to 0.375
- weight_outer: float32 [512, 256], P(('section', 'dp')), may hold values from -0.25 to 0.25
- weight_head: float32 [256, 172], P(('section', 'dp')), may hold values from -1.125 to 1.125
- biases: float32 [684], replicated, may hold values from -1.8 to 1.8
- first_inner: float32 [256, 256], P(('section', 'dp')), may hold values from -6.9211565e-05 to 6.9211565e-05
- first_outer: float32 [512, 256], P(('section', 'dp')), may hold values from -6.9211565e-05 to 6.9211565e-05
- first_head: float32 [256, 172], P(('section', 'dp')), may hold values from -6.9211565e-05 to 6.9211565e-05
- first_biases: float32 [684], replicated, may hold values from -0.00020356342 to 0.00020356342
- second_inner: float32 [256, 256], P(('section', 'dp')), may hold values from 1.0369886e-11 to 4.1479545e-11
- second_outer: float32 [512, 256], P(('section', 'dp')), may hold values from 1.0369886e-11 to 4.1479545e-11
- second_head: float32 [256, 172], P(('section', 'dp')), may hold values from 1.0369886e-11 to 4.1479545e-11
- second_biases: float32 [684], replicated, may hold values from 9.3328976e-11 to 3.733159e-10
- smooth_inner: float32 [256, 256], P(('section', 'dp')), may hold values from -0.375 to 0.375
- smooth_outer: float32 [512, 256], P(('section', 'dp')), may hold values from -0.25 to 0.25
- smooth_head: float32 [256, 172], P(('section', 'dp')), may hold values from -0.375 to 0.375
- smooth_biases: float32 [684], replicated, may hold values from -1.8 to 1.8
Outputs:
- loss_sum: float32 [], replicated
- label_count: float32 [], replicated
- clip_norm: float32 [], replicated
- matrix_norms: float32 [3, 2], replicated
- new_inner: float32 [256, 256], P(('section', 'dp'))
- new_outer: float32 [512, 256], P(('section', 'dp'))
- new_head: float32 [256, 172], P(('section', 'dp'))
- new_biases: float32 [684], replicated
- moment_inner: float32 [256, 256], P(('section', 'dp'))
- moment_outer: float32 [512, 256], P(('section', 'dp'))
- moment_head: float32 [256, 172], P(('section', 'dp'))
- moment_biases: float32 [684], replicated
- square_inner: float32 [256, 256], P(('section', 'dp'))
- square_outer: float32 [512, 256], P(('section', 'dp'))
- square_head: float32 [256, 172], P(('section', 'dp'))
- square_biases: float32 [684], replicated
- average_inner: float32 [256, 256], P(('section', 'dp'))
- average_outer: float32 [512, 256], P(('section', 'dp'))
- average_head: float32 [256, 172], P(('section', 'dp'))
- average_biases: float32 [684], replicated
The draws below stay inside these ranges and needn't reach their ends.
Inputs may be any that keep to these rules, and one draw needn't show every extreme that they name: `owners`: the frontier of one micro-batch on one data index names each owner at most 7680 times, a bound that some block reaches. `label_mask`: the share of labelled seeds rises with the data index.
All inputs are finite; a program needn't handle non-finite values.
Results may differ from the reference program's by a relative error of at most 0.0042.
Values may be sent and summed in bfloat16 or wider, within the bound.
A program may use at most 192 MiB of HBM per device.

```python
import math
import jax
import jax.numpy as jnp
import numpy as np
from jax import lax

D_IN = 128
HID = 256
CLASSES = 172
F1 = 15
F2 = 10
STEP = 5
SEEDS = 256
NODE_DEV = 16384
MICRO = 4
DST1 = 2816
FRONT = 30720
SLOTS = 7680
PARAMS = 241324
N_DP = 8


def draw_label_mask(key, part):
    key = jax.random.fold_in(key, 11)
    column = jnp.arange(N_DP * SEEDS)[None, :] // SEEDS
    limit = 250 + 500 * column // max(N_DP - 1, 1)
    ticket = jax.random.randint(key, (MICRO, N_DP * SEEDS), 0, 1000)
    return (ticket < limit).astype(jnp.int32)


def plant(entries, stream_key, least, high):
    shape = entries.shape
    place = [jax.random.randint(jax.random.fold_in(stream_key, axis), (), 0, shape[axis]) for axis in range(len(shape))]
    entries = entries.at[tuple(place)].set(least)
    longest = shape.index(max(shape))
    place[longest] = (place[longest] + 1) % shape[longest]
    return entries.at[tuple(place)].set(high)


def block_scale(rng, extent, split, smallest, high):
    factor_of = 1.0
    for dim, blocks in split:
        steps = jax.random.uniform(jax.random.fold_in(jax.random.fold_in(rng, 6), dim), (blocks,), jnp.float32, smallest / len(split), high / len(split))
        factor_of = factor_of * jnp.repeat(jnp.exp(steps), extent[dim] // blocks).reshape((-1,) + (1,) * (len(extent) - 1 - dim))
    return factor_of


def shared_out(key, own, number, rows, number_of, top, reach, skew):
    ranking = jax.random.permutation(key, number_of)
    heavy_load, common = load_shares(number_of, rows * top, reach, skew, True), load_shares(number_of, rows * top, reach, skew, False)
    places = jnp.arange(number_of)

    def named(lengths, rotation):
        used = int((lengths > 0).sum())
        fixed = max(1, used // 4)
        shifted = fixed + (places - fixed + rotation * (used - fixed)) % max(1, number_of - fixed)
        return jnp.zeros((number_of,), jnp.int32).at[ranking[jnp.where(places < fixed, places, shifted)]].set(jnp.asarray(lengths, jnp.int32))

    lengths = jnp.where(number % 4 == 0, named(heavy_load, number // 4), named(common, number - number // 4 - 1))
    mixed = jax.random.permutation(jax.random.fold_in(own, 3), number_of)
    giver, sink = mixed[0:number_of // 2 * 2:2], mixed[1:number_of // 2 * 2:2]
    margin = jnp.minimum(lengths[giver] - 1, reach - lengths[sink]) // 2
    margin = jnp.where((giver == ranking[0]) | (sink == ranking[0]) | (lengths[sink] == 0), 0, jnp.maximum(margin, 0))
    shifted = jax.random.randint(jax.random.fold_in(own, 4), (number_of // 2,), 0, 1 << 20) % (margin + 1)
    lengths = lengths.at[giver].add(-shifted).at[sink].add(shifted)
    items = jnp.searchsorted(jnp.cumsum(lengths), jnp.arange(rows * top), side="right").astype(jnp.int32)
    listing = items.reshape(top, rows).T
    listing = listing[jax.random.permutation(jax.random.fold_in(own, 1), rows)]
    rotation = jax.random.randint(jax.random.fold_in(own, 2), (rows, 1), 0, top)
    return jnp.take_along_axis(listing, (jnp.arange(top)[None, :] + rotation) % top, axis=1)


def load_shares(count, total, most, lean, full):
    portions = [(1 << 20) // math.isqrt(grade ** lean) + 1 for grade in range(1, count + 1)]
    largest = most if full else min(most, max(-(-total // count), total * portions[0] // sum(portions)))
    least = 1 if total - largest >= count - 1 else 0
    given, surplus = [largest] + [least] * (count - 1), total - largest - least * (count - 1)
    while surplus > 0:
        free = [i for i in range(1, count) if given[i] < largest] or [i for i in range(1, count) if given[i] < most]
        mass, budget = sum([portions[i] for i in free]), surplus
        for i in free:
            addition = min(most - given[i], max(1, budget * portions[i] // mass), surplus)
            given[i] = given[i] + addition
            surplus = surplus - addition
    return np.array(given)


def gaussian(own_key, extent, deviation, most, cuts=(), kind=jnp.bfloat16):
    array = jax.random.normal(own_key, extent, jnp.float32) * deviation
    if len(cuts) > 0:
        array = block_scale(own_key, extent, cuts, -0.22, 0.18) * array
    return jnp.clip(array, min=-most, max=most).astype(kind)


def setup_inputs(seed: int = 0) -> dict:
    splits = jax.random.split(jax.random.key(seed), 26)
    node_table = gaussian(splits[0], (NODE_DEV * N_DP, D_IN), 1.0, 6.0, ((0, 8),))
    owners_keys = jax.random.split(jax.random.fold_in(splits[1], 1), MICRO * (N_DP * FRONT) // FRONT)
    owners_turns = jax.random.permutation(jax.random.fold_in(splits[1], 3), MICRO * (N_DP * FRONT) // FRONT)
    owners = jax.vmap(lambda own, number: shared_out(jax.random.fold_in(splits[1], 2), own, number, FRONT, N_DP, 1, SLOTS, 1))(owners_keys, owners_turns).reshape((MICRO, N_DP * FRONT, 1))
    local_rows = plant(jax.random.randint(splits[2], (MICRO, N_DP * FRONT), 0, NODE_DEV), jax.random.fold_in(splits[2], 1), 0, NODE_DEV - 1).astype(jnp.int32)
    inner_neighbours = plant(jax.random.randint(splits[3], (MICRO, N_DP * DST1, F1), 0, FRONT), jax.random.fold_in(splits[3], 1), 0, FRONT - 1).astype(jnp.int32)
    inner_counts = plant(jax.random.randint(splits[4], (MICRO, N_DP * DST1), 1, F1 + 1), jax.random.fold_in(splits[4], 1), 1, F1).astype(jnp.int32)
    outer_neighbours = plant(jax.random.randint(splits[5], (MICRO, N_DP * SEEDS, F2), 0, DST1), jax.random.fold_in(splits[5], 1), 0, DST1 - 1).astype(jnp.int32)
    outer_counts = plant(jax.random.randint(splits[6], (MICRO, N_DP * SEEDS), 1, F2 + 1), jax.random.fold_in(splits[6], 1), 1, F2).astype(jnp.int32)
    labels = plant(jax.random.randint(splits[7], (MICRO, N_DP * SEEDS), 0, CLASSES), jax.random.fold_in(splits[7], 1), 0, CLASSES - 1).astype(jnp.int32)
    label_mask = draw_label_mask(jax.random.fold_in(splits[25], 71), 0)
    weight_inner = gaussian(splits[9], (2 * D_IN, HID), (2 * D_IN) ** -0.5, 0.375, ((0, 32),), jnp.float32)
    weight_outer = gaussian(splits[10], (2 * HID, HID), (2 * HID) ** -0.5, 0.25, ((0, 32),), jnp.float32)
    weight_head = gaussian(splits[11], (HID, CLASSES), (3.0 / HID ** 0.5), 1.125, ((0, 32),), jnp.float32)
    biases = gaussian(splits[12], (2 * HID + CLASSES,), 0.3, 1.8, (), jnp.float32)
    first_inner = gaussian(splits[13], (2 * D_IN, HID), (0.0056 / PARAMS ** 0.5), 6.921156455064192e-05, ((0, 32),), jnp.float32)
    first_outer = gaussian(splits[14], (2 * HID, HID), (0.0056 / PARAMS ** 0.5), 6.921156455064192e-05, ((0, 32),), jnp.float32)
    first_head = gaussian(splits[15], (HID, CLASSES), (0.0056 / PARAMS ** 0.5), 6.921156455064192e-05, ((0, 32),), jnp.float32)
    first_biases = gaussian(splits[16], (2 * HID + CLASSES,), (0.017 / PARAMS ** 0.5), 0.00020356342, (), jnp.float32)
    second_inner = jnp.clip(jnp.exp(math.log(4.147954549282851e-11) - 1.3862944 * jax.random.uniform(splits[17], (2 * D_IN, HID), jnp.float32) ** block_scale(splits[17], (2 * D_IN, HID), ((0, 32),), -0.2, 0.2)), 1.0369886373207127e-11, 4.147954549282851e-11)
    second_outer = jnp.clip(jnp.exp(math.log(4.147954549282851e-11) - 1.3862944 * jax.random.uniform(splits[18], (2 * HID, HID), jnp.float32) ** block_scale(splits[18], (2 * HID, HID), ((0, 32),), -0.2, 0.2)), 1.0369886373207127e-11, 4.147954549282851e-11)
    second_head = jnp.clip(jnp.exp(math.log(4.147954549282851e-11) - 1.3862944 * jax.random.uniform(splits[19], (HID, CLASSES), jnp.float32) ** block_scale(splits[19], (HID, CLASSES), ((0, 32),), -0.2, 0.2)), 1.0369886373207127e-11, 4.147954549282851e-11)
    second_biases = jnp.clip(jnp.exp(jax.random.uniform(splits[20], (2 * HID + CLASSES,), jnp.float32, math.log(9.33289764915024e-11), math.log(3.733159059660096e-10))), 9.33289764915024e-11, 3.733159059660096e-10)
    smooth_inner = gaussian(splits[21], (2 * D_IN, HID), (2 * D_IN) ** -0.5, 0.375, ((0, 32),), jnp.float32)
    smooth_outer = gaussian(splits[22], (2 * HID, HID), (2 * HID) ** -0.5, 0.25, ((0, 32),), jnp.float32)
    smooth_head = gaussian(splits[23], (HID, CLASSES), HID ** -0.5, 0.375, ((0, 32),), jnp.float32)
    smooth_biases = gaussian(splits[24], (2 * HID + CLASSES,), 0.3, 1.8, (), jnp.float32)
    return dict(node_table=node_table, owners=owners, local_rows=local_rows, inner_neighbours=inner_neighbours, inner_counts=inner_counts, outer_neighbours=outer_neighbours, outer_counts=outer_counts, labels=labels, label_mask=label_mask, weight_inner=weight_inner, weight_outer=weight_outer, weight_head=weight_head, biases=biases, first_inner=first_inner, first_outer=first_outer, first_head=first_head, first_biases=first_biases, second_inner=second_inner, second_outer=second_outer, second_head=second_head, second_biases=second_biases, smooth_inner=smooth_inner, smooth_outer=smooth_outer, smooth_head=smooth_head, smooth_biases=smooth_biases)


BETA_ONE = 0.9
BETA_TWO = 0.999
EPSILON = 1e-06
DECAY = 0.01
RATE = 0.25
CLIP = 0.05
AVERAGE = 0.9

@jax.custom_vjp
def low(v):
    return lax.optimization_barrier(v.astype(jnp.bfloat16)).astype(jnp.float32)

@jax.custom_vjp
def low_back(v):
    return v

def low_keep(v):
    return (low(v), None)

def low_pass(kept, grad):
    return (grad,)

def back_keep(v):
    return (v, None)

def back_low(kept, grad):
    return (low(grad),)
low.defvjp(low_keep, low_pass)
low_back.defvjp(back_keep, back_low)

def dense(left, right):
    return jnp.dot(left, right, precision=lax.Precision.HIGHEST)

def sage_layer(source, neighbours, counts, weight, bias):
    dest_rows = neighbours.shape[0]
    fanout = neighbours.shape[1]
    taken = source[neighbours]
    keep_mask = jnp.arange(fanout)[None, :] < counts[:, None]
    summed = lax.optimization_barrier(jnp.sum(jnp.where(keep_mask[:, :, None], taken, 0.0), axis=1))
    average_in = low(summed / counts[:, None].astype(jnp.float32))
    joined = jnp.concatenate([source[:dest_rows], average_in], axis=1)
    before = low_back(dense(joined, weight) + bias)
    return low_back(low(jax.nn.silu(before)))

def total_loss(params, table, groups, label_count):
    weight_inner = low(params[0])
    weight_outer = low(params[1])
    weight_head = low(params[2])
    biases = params[3]

    def one_group(carry, group):
        owner_ids, row_ids, nbr_inner, cnt_inner, nbr_outer, cnt_outer, group_labels, group_mask = group
        features = table[owner_ids * NODE_DEV + row_ids]
        hidden_one = sage_layer(features, nbr_inner, cnt_inner, weight_inner, biases[:HID])
        hidden_two = sage_layer(hidden_one, nbr_outer, cnt_outer, weight_outer, biases[HID:2 * HID])
        logits = low_back(dense(hidden_two, weight_head) + biases[2 * HID:])
        highest = lax.optimization_barrier(jnp.max(logits, axis=1, keepdims=True))
        log_total = highest[:, 0] + jnp.log(lax.optimization_barrier(jnp.sum(jnp.exp(logits - highest), axis=1)))
        picked = jnp.take_along_axis(logits, group_labels[:, None], axis=1)[:, 0]
        return (carry + jnp.sum((log_total - picked) * group_mask.astype(jnp.float32)), None)
    total, unused = lax.scan(jax.checkpoint(one_group), jnp.zeros((), jnp.float32), groups)
    return (total / label_count, total)

def moments(weight, gradient, first, second):
    first = BETA_ONE * first + (1.0 - BETA_ONE) * gradient
    second = BETA_TWO * second + (1.0 - BETA_TWO) * gradient * gradient
    update = first / (1.0 - BETA_ONE ** STEP) / (jnp.sqrt(second / (1.0 - BETA_TWO ** STEP)) + EPSILON) + DECAY * weight
    return (first, second, update)

def bias_ratio(weight, update, hidden):
    bounds = ((0, hidden), (hidden, 2 * hidden), (2 * hidden, weight.shape[0]))
    pieces = []
    for start_at, stop_at in bounds:
        weight_norm = jnp.sqrt(jnp.sum(weight[start_at:stop_at] ** 2))
        update_norm = jnp.sqrt(jnp.sum(update[start_at:stop_at] ** 2))
        pieces.append(jnp.zeros((stop_at - start_at,), weight.dtype) + weight_norm / update_norm)
    return jnp.concatenate(pieces)

def reference(node_table, owners, local_rows, inner_neighbours, inner_counts, outer_neighbours, outer_counts, labels, label_mask, weight_inner, weight_outer, weight_head, biases, first_inner, first_outer, first_head, first_biases, second_inner, second_outer, second_head, second_biases, smooth_inner, smooth_outer, smooth_head, smooth_biases):
    batches = MICRO * N_DP
    groups = (owners.reshape(batches, FRONT), local_rows.reshape(batches, FRONT), inner_neighbours.reshape(batches, DST1, F1), inner_counts.reshape(batches, DST1), outer_neighbours.reshape(batches, SEEDS, F2), outer_counts.reshape(batches, SEEDS), labels.reshape(batches, SEEDS), label_mask.reshape(batches, SEEDS))
    label_count = jnp.maximum(jnp.sum(label_mask.astype(jnp.float32)), 1.0)
    table = node_table.astype(jnp.float32)

    def scaled(params):
        return total_loss(params, table, groups, label_count)
    params = (weight_inner, weight_outer, weight_head, biases)
    scaled_loss, pullback, loss_sum = jax.vjp(scaled, params, has_aux=True)
    gradients = pullback(jnp.ones_like(scaled_loss))[0]
    square_total = sum((jnp.sum(gradient * gradient) for gradient in gradients))
    clip_norm = jnp.sqrt(square_total)
    factor = jnp.minimum(1.0, CLIP / clip_norm)
    weights = (weight_inner, weight_outer, weight_head)
    firsts = (first_inner, first_outer, first_head)
    seconds = (second_inner, second_outer, second_head)
    smooths = (smooth_inner, smooth_outer, smooth_head)
    news, moment_list, square_list, average_list, norm_rows = ([], [], [], [], [])
    for slot_at in range(3):
        first, second, update = moments(weights[slot_at], gradients[slot_at] * factor, firsts[slot_at], seconds[slot_at])
        weight_norm = jnp.sqrt(jnp.sum(weights[slot_at] ** 2))
        update_norm = jnp.sqrt(jnp.sum(update ** 2))
        fresh = weights[slot_at] - RATE * (weight_norm / update_norm) * update
        news.append(fresh)
        moment_list.append(first)
        square_list.append(second)
        average_list.append(AVERAGE * smooths[slot_at] + (1.0 - AVERAGE) * fresh)
        norm_rows.append(jnp.stack([weight_norm, update_norm]))
    bias_first, bias_second, bias_update = moments(biases, gradients[3] * factor, first_biases, second_biases)
    bias_new = biases - RATE * bias_ratio(biases, bias_update, HID) * bias_update
    bias_average = AVERAGE * smooth_biases + (1.0 - AVERAGE) * bias_new
    return (loss_sum, label_count, clip_norm, jnp.stack(norm_rows), news[0], news[1], news[2], bias_new, moment_list[0], moment_list[1], moment_list[2], bias_first, square_list[0], square_list[1], square_list[2], bias_second, average_list[0], average_list[1], average_list[2], bias_average)
```

```python
import jax
import jax.numpy as jnp
from jax import lax
from jax.sharding import PartitionSpec as P

STEP = 5


BETA_ONE = 0.9
BETA_TWO = 0.999
EPSILON = 1e-06
DECAY = 0.01
RATE = 0.25
CLIP = 0.05
AVERAGE = 0.9

WHOLE_TABLE_LIMIT = 64 * 2**20


def outer_product(left, right):
    return lax.dot_general(
        left, right, (((0,), (0,)), ((), ())), preferred_element_type=jnp.float32
    )


def against(left, right):
    return lax.dot_general(
        left, right, (((1,), (1,)), ((), ())), preferred_element_type=jnp.float32
    )


def silu_slope(before, grad_out):
    sigmoid = jax.nn.sigmoid(before)
    return (grad_out * sigmoid * (1.0 + before * (1.0 - sigmoid))).astype(jnp.bfloat16)


def moments(weight, gradient, first, second):
    first = BETA_ONE * first + (1.0 - BETA_ONE) * gradient
    second = BETA_TWO * second + (1.0 - BETA_TWO) * gradient * gradient
    update = (
        first / (1.0 - BETA_ONE**STEP) / (jnp.sqrt(second / (1.0 - BETA_TWO**STEP)) + EPSILON)
        + DECAY * weight
    )
    return (first, second, update)


def bias_ratio(weight, update, hidden):
    bounds = ((0, hidden), (hidden, 2 * hidden), (2 * hidden, weight.shape[0]))
    pieces = []
    for start_at, stop_at in bounds:
        weight_norm = jnp.sqrt(jnp.sum(weight[start_at:stop_at] ** 2))
        update_norm = jnp.sqrt(jnp.sum(update[start_at:stop_at] ** 2))
        pieces.append(jnp.zeros((stop_at - start_at,), jnp.float32) + weight_norm / update_norm)
    return jnp.concatenate(pieces)


def gathered_rows(node_table, owner_ids, row_ids):
    peer_count = lax.axis_size("dp")
    parts = lax.axis_size("section")
    table_rows = node_table.shape[0]
    if peer_count * node_table.size * 2 <= WHOLE_TABLE_LIMIT and table_rows % parts == 0:
        part_rows = table_rows // parts
        quarter = lax.dynamic_slice_in_dim(
            node_table, lax.axis_index("section") * part_rows, part_rows, 0
        )
        source = lax.all_gather(quarter, ("section", "dp"), axis=0, tiled=True)
        place = (row_ids // part_rows * peer_count + owner_ids) * part_rows + row_ids % part_rows
        return source, place
    frontier_rows = owner_ids.shape[0]
    slot_count = max(2, 2 * frontier_rows // peer_count)
    owner_hot = (owner_ids[:, None] == jnp.arange(peer_count)[None, :]).astype(jnp.int32)
    ranking = jnp.sum((jnp.cumsum(owner_hot, axis=0) - 1) * owner_hot, axis=1)
    placed = owner_ids * slot_count + ranking
    request = (
        jnp.zeros((peer_count * slot_count,), jnp.int32)
        .at[placed]
        .set(row_ids)
        .reshape(peer_count, slot_count)
    )
    returned = lax.all_to_all(
        node_table[lax.all_to_all(request, "dp", split_axis=0, concat_axis=0, tiled=True)],
        "dp",
        split_axis=0,
        concat_axis=0,
        tiled=True,
    )
    return returned.reshape(peer_count * slot_count, -1), placed


def on_device(
    node_table,
    owners,
    local_rows,
    inner_neighbours,
    inner_counts,
    outer_neighbours,
    outer_counts,
    labels,
    label_mask,
    weight_inner,
    weight_outer,
    weight_head,
    biases,
    first_inner,
    first_outer,
    first_head,
    first_biases,
    second_inner,
    second_outer,
    second_head,
    second_biases,
    smooth_inner,
    smooth_outer,
    smooth_head,
    smooth_biases,
):
    at = lax.axis_index("section")
    every = ("section", "dp")
    hidden = weight_inner.shape[1]
    dest_count, fan_inner = inner_neighbours.shape[1:]
    seed_count, fan_outer = outer_neighbours.shape[1:]
    classes = weight_head.shape[1]
    label_count = jnp.maximum(lax.psum(jnp.sum(label_mask.astype(jnp.float32)), "dp"), 1.0)

    def mine(array):
        return lax.dynamic_index_in_dim(array, at, 0, keepdims=False)

    inner_neighbours, inner_counts = mine(inner_neighbours), mine(inner_counts)
    outer_neighbours, outer_counts = mine(outer_neighbours), mine(outer_counts)
    labels, label_mask = mine(labels), mine(label_mask)
    sizes = [weight.shape[0] for weight in (weight_inner, weight_outer, weight_head)]
    full_inner, full_outer, full_head = (
        lax.all_gather(weight.astype(jnp.bfloat16), every, axis=0, tiled=True)
        for weight in (weight_inner, weight_outer, weight_head)
    )
    bias_inner = biases[:hidden]
    bias_outer = biases[hidden : 2 * hidden]
    bias_head = biases[2 * hidden :]

    source, place = gathered_rows(node_table, owners.reshape(-1), local_rows.reshape(-1))
    keep = jnp.arange(fan_inner)[None, :] < inner_counts[:, None]
    rows = source[place[inner_neighbours]]
    summed = jnp.sum(
        jnp.where(keep[:, :, None], rows, jnp.zeros((), rows.dtype)), axis=1, dtype=jnp.float32
    )
    mean_one = (summed / inner_counts[:, None].astype(jnp.float32)).astype(jnp.bfloat16)
    joined_one = jnp.concatenate([source[place[:dest_count]], mean_one], axis=1)
    pre_one = jnp.dot(joined_one, full_inner, preferred_element_type=jnp.float32) + bias_inner
    hidden_one = jax.nn.silu(pre_one).astype(jnp.bfloat16)

    keep_outer = jnp.arange(fan_outer)[None, :] < outer_counts[:, None]
    pick = jnp.sum(
        (
            jnp.where(keep_outer, outer_neighbours, -1)[:, :, None]
            == jnp.arange(dest_count)[None, None, :]
        ).astype(jnp.float32),
        axis=1,
    ).astype(jnp.bfloat16)
    count_two = outer_counts[:, None].astype(jnp.float32)
    mean_two = (jnp.dot(pick, hidden_one, preferred_element_type=jnp.float32) / count_two).astype(
        jnp.bfloat16
    )
    joined_two = jnp.concatenate([hidden_one[:seed_count], mean_two], axis=1)
    pre_two = jnp.dot(joined_two, full_outer, preferred_element_type=jnp.float32) + bias_outer
    hidden_two = jax.nn.silu(pre_two).astype(jnp.bfloat16)

    logits = jnp.dot(hidden_two, full_head, preferred_element_type=jnp.float32) + bias_head
    shifted = logits - jnp.max(logits, axis=1, keepdims=True)
    log_total = jnp.log(jnp.sum(jnp.exp(shifted), axis=1, keepdims=True))
    chosen = (jnp.arange(classes)[None, :] == labels[:, None]).astype(jnp.float32)
    row_weight = label_mask.astype(jnp.float32)
    loss_part = jnp.sum((log_total[:, 0] - jnp.sum(shifted * chosen, axis=1)) * row_weight)
    grad_logits = (
        (jnp.exp(shifted - log_total) - chosen) * (row_weight / label_count)[:, None]
    ).astype(jnp.bfloat16)
    grad_head = outer_product(hidden_two, grad_logits)
    grad_two = against(grad_logits, full_head).astype(jnp.bfloat16).astype(jnp.float32)
    grad_pre_two = silu_slope(pre_two, grad_two)
    grad_outer = outer_product(joined_two, grad_pre_two)
    grad_joined = against(grad_pre_two, full_outer)
    share = grad_joined[:, hidden:] / count_two
    share_high = share.astype(jnp.bfloat16)
    share_low = (share - share_high.astype(jnp.float32)).astype(jnp.bfloat16)
    grad_one = outer_product(pick, share_high) + outer_product(pick, share_low)
    grad_one = jnp.concatenate(
        [grad_one[:seed_count] + grad_joined[:, :hidden], grad_one[seed_count:]], axis=0
    )
    grad_one = grad_one.astype(jnp.bfloat16).astype(jnp.float32)
    grad_pre_one = silu_slope(pre_one, grad_one)
    grad_inner = outer_product(joined_one, grad_pre_one)
    bias_part = jnp.concatenate(
        [
            jnp.sum(part.astype(jnp.float32), axis=0)
            for part in (grad_pre_one, grad_pre_two, grad_logits)
        ]
    )

    devices = lax.axis_size(every)
    grads = jnp.concatenate(
        [grad.reshape(devices, -1) for grad in (grad_inner, grad_outer, grad_head)], axis=1
    )
    shard = lax.psum_scatter(grads, every, scatter_dimension=0, tiled=True).reshape(-1)
    weights = (weight_inner, weight_outer, weight_head)
    shards = []
    for weight in weights:
        shards.append(shard[: weight.size].reshape(weight.shape))
        shard = shard[weight.size :]
    packed = lax.psum(jnp.concatenate([bias_part, loss_part[None]]), every)
    bias_grad, loss_sum = packed[:-1], packed[-1]
    grad_partial = sum((jnp.sum(part * part) for part in shards))
    weight_partial = [jnp.sum(weight * weight) for weight in weights]
    squares = lax.psum(jnp.stack([grad_partial] + weight_partial), every)
    clip_norm = jnp.sqrt(squares[0] + jnp.sum(bias_grad * bias_grad))
    factor = jnp.minimum(1.0, CLIP / clip_norm)
    firsts = (first_inner, first_outer, first_head)
    seconds = (second_inner, second_outer, second_head)
    smooths = (smooth_inner, smooth_outer, smooth_head)
    states = [
        moments(weights[slot_at], shards[slot_at] * factor, firsts[slot_at], seconds[slot_at])
        for slot_at in range(3)
    ]
    update_square = lax.psum(jnp.stack([jnp.sum(state[2] * state[2]) for state in states]), every)
    weight_norms = jnp.sqrt(squares[1:])
    update_norms = jnp.sqrt(update_square)
    news = [
        weights[slot_at]
        - RATE * (weight_norms[slot_at] / update_norms[slot_at]) * states[slot_at][2]
        for slot_at in range(3)
    ]
    averages = [
        AVERAGE * smooths[slot_at] + (1.0 - AVERAGE) * news[slot_at] for slot_at in range(3)
    ]
    bias_first, bias_second, bias_update = moments(
        biases, bias_grad * factor, first_biases, second_biases
    )
    bias_new = biases - RATE * bias_ratio(biases, bias_update, hidden) * bias_update
    bias_average = AVERAGE * smooth_biases + (1.0 - AVERAGE) * bias_new
    return (
        loss_sum,
        label_count,
        clip_norm,
        jnp.stack([weight_norms, update_norms], axis=1),
        news[0],
        news[1],
        news[2],
        bias_new,
        states[0][0],
        states[1][0],
        states[2][0],
        bias_first,
        states[0][1],
        states[1][1],
        states[2][1],
        bias_second,
        averages[0],
        averages[1],
        averages[2],
        bias_average,
    )


def solution(mesh):
    in_specs = (
        P("dp", None),
        P("section", "dp", None),
        P("section", "dp"),
        P(None, "dp", None),
        P(None, "dp"),
        P(None, "dp", None),
        P(None, "dp"),
        P(None, "dp"),
        P(None, "dp"),
        P(("section", "dp"), None),
        P(("section", "dp"), None),
        P(("section", "dp"), None),
        P(),
        P(("section", "dp"), None),
        P(("section", "dp"), None),
        P(("section", "dp"), None),
        P(),
        P(("section", "dp"), None),
        P(("section", "dp"), None),
        P(("section", "dp"), None),
        P(),
        P(("section", "dp"), None),
        P(("section", "dp"), None),
        P(("section", "dp"), None),
        P(),
    )
    out_specs = (
        P(),
        P(),
        P(),
        P(),
        P(("section", "dp"), None),
        P(("section", "dp"), None),
        P(("section", "dp"), None),
        P(),
        P(("section", "dp"), None),
        P(("section", "dp"), None),
        P(("section", "dp"), None),
        P(),
        P(("section", "dp"), None),
        P(("section", "dp"), None),
        P(("section", "dp"), None),
        P(),
        P(("section", "dp"), None),
        P(("section", "dp"), None),
        P(("section", "dp"), None),
        P(),
    )
    return jax.shard_map(
        on_device, mesh=mesh, in_specs=in_specs, out_specs=out_specs, check_vma=False
    )
```

```python
import jax
import jax.numpy as jnp
from jax import lax
from jax.experimental import pallas as pl
from jax.experimental.pallas import tpu as pltpu
from jax.sharding import PartitionSpec as P

STEP = 5


BETA_ONE = 0.9
BETA_TWO = 0.999
EPSILON = 1e-06
DECAY = 0.01
RATE = 0.25
CLIP = 0.05
AVERAGE = 0.9


VMEM_TABLE_LIMIT = 36 * 2**20
WHOLE_TABLE_LIMIT = 64 * 2**20
MESH = pl.DeviceIdType.MESH
SLOT = 16
BLOCK = 16
CHUNKS = 4
GROUP = 4
SETS = 4


def spread_kernel(
    table_ref,
    weight_ref,
    place_ref,
    near_ref,
    live_ref,
    full_ref,
    weights_ref,
    idx_ref,
    mix_ref,
    parts,
    own_sem,
    z_sem,
    x_sem,
    y_sem,
    far_sem,
    twin_sem,
    twin_own_sem,
    double_sem,
    send_sem,
    double_send_sem,
):
    section, at = lax.axis_index("section"), lax.axis_index("dp")
    z, core = at // 2, at % 2
    flipped = z // 2
    height = z + flipped * (3 - 2 * z)
    pairs = table_ref.shape[0]
    quarter = pairs // 4
    chunk = quarter // CHUNKS

    def level(value):
        return value + flipped * (3 - 2 * value)

    here = (section, at)
    twin = (section, z * 2 + 1 - core)
    beside_x = (section + 1 - 2 * (section % 2), at)
    beside_y = (section + 2 - 4 * (section // 2), at)
    inner_z = (section, level(1 - height) * 2 + core)
    across_z = (section, level(2) * 2 + core)
    outer_z = (section, level(0) * 2 + core)
    skip_z = (section, ((z + 2) % 4) * 2 + core)
    sources = [level(1 - height), level(2), level(3)]
    crosses = height == 1

    barrier = pltpu.get_barrier_semaphore()
    for partner in (twin, beside_x, beside_y, inner_z, skip_z):
        pl.semaphore_signal(barrier, inc=1, device_id=partner, device_id_type=MESH)

    @pl.when(crosses)
    def greet_across():
        pl.semaphore_signal(barrier, inc=1, device_id=across_z, device_id_type=MESH)

    pl.semaphore_wait(barrier, 5 + height)

    sent = []

    def region(shard, part, piece):
        start_at = shard * pairs + part * quarter + piece * chunk
        return full_ref.at[pl.ds(pl.multiple_of(start_at, chunk), chunk)]

    def send(source, target, recv, device, when=None):
        number = len(sent)
        copy = pltpu.make_async_remote_copy(
            src_ref=source,
            dst_ref=target,
            send_sem=send_sem.at[number],
            recv_sem=recv,
            device_id=device,
            device_id_type=MESH,
        )
        sent.append((copy, when))
        if when is None:
            copy.start()
        else:
            pl.when(when)(copy.start)
        return copy

    def arrived(target, recv):
        pltpu.make_async_copy(target, target, recv).wait()

    mine = section * (lax.axis_size("dp")) + at
    pltpu.sync_copy(weight_ref, weights_ref.at[mine])
    doubling = [(twin, 1), (inner_z, 2), (skip_z, 4), (beside_x, 8), (beside_y, 16)]
    doubled = []

    def double_start(number):
        device, size = doubling[number]
        start_at = (mine // size) * size
        block = weights_ref.at[pl.ds(start_at, size)]
        copy = pltpu.make_async_remote_copy(
            src_ref=block,
            dst_ref=block,
            send_sem=double_send_sem.at[number],
            recv_sem=double_sem.at[number],
            device_id=device,
            device_id_type=MESH,
        )
        copy.start()
        doubled.append(copy)

    double_start(0)
    for piece in range(CHUNKS):
        start_at = section * quarter + piece * chunk
        block = table_ref.at[pl.ds(pl.multiple_of(start_at, chunk), chunk)]
        goal = region(at, section, piece)
        send(block, goal, z_sem.at[piece], inner_z)
        send(block, goal, z_sem.at[CHUNKS + piece], across_z, crosses)
    whole = full_ref.at[pl.ds(pl.multiple_of(at * pairs, pairs), pairs)]
    own = pltpu.make_async_copy(table_ref, whole, own_sem)
    own.start()
    send(table_ref, whole, twin_own_sem, twin)

    placed = place_ref[...]
    pair_at = placed // 2
    high = place_ref.shape[1]
    parts[0:128, :] = (pair_at % 256).astype(jnp.float32).astype(jnp.bfloat16)
    parts[128:256, :] = (pair_at // 256).astype(jnp.float32).astype(jnp.bfloat16)
    parts[256:384, :] = (placed % 2).astype(jnp.float32).astype(jnp.bfloat16)
    looked_rows = near_ref.shape[0]
    steps = 3 * CHUNKS + 2
    per_step = -(-looked_rows // (8 * steps)) * 8

    def look_up(first, last):
        def rows_of(block, carry):
            start_at = pl.multiple_of(block * 8, 8)
            sub = lax.broadcasted_iota(jnp.int32, (high, 256), 0)
            low_at = lax.broadcasted_iota(jnp.int32, (128, 256), 0)
            row = lax.broadcasted_iota(jnp.int32, (256, 512), 0)
            column = lax.broadcasted_iota(jnp.int32, (256, 512), 1)
            for k in range(8):
                node = near_ref[pl.ds(start_at + k, 1), :]
                hot = (sub == node // 128).astype(jnp.float32).astype(jnp.bfloat16)
                got = jnp.dot(parts[...], hot, preferred_element_type=jnp.float32)
                chosen = low_at == node % 128
                found = jnp.where(chosen, got[0:128] + 256.0 * got[128:256], 0.0)
                odd = jnp.where(chosen, got[256:384], 0.0)
                idx_ref[pl.ds(start_at + k, 1), :] = jnp.sum(found, axis=0, keepdims=True).astype(
                    jnp.int32
                )
                mix_ref[pl.ds(start_at + k, 1), 0:256] = jnp.sum(odd, axis=0, keepdims=True)
            odd = mix_ref[pl.ds(start_at, 8), 0:256]
            live = live_ref[pl.ds(start_at, 8), :]
            mix_ref[pl.ds(start_at, 8), :] = jnp.dot(
                (live * (1.0 - odd)).astype(jnp.bfloat16),
                (column == 2 * row).astype(jnp.float32).astype(jnp.bfloat16),
                preferred_element_type=jnp.float32,
            ) + jnp.dot(
                (live * odd).astype(jnp.bfloat16),
                (column == 2 * row + 1).astype(jnp.float32).astype(jnp.bfloat16),
                preferred_element_type=jnp.float32,
            )
            return carry

        lax.fori_loop(first // 8, last // 8, rows_of, 0)

    total = 3 * CHUNKS
    twins = []

    def to_twin(block, number):
        send(block, block, twin_sem.at[number], twin)
        twins.append(number)

    for step in range(steps):
        if step < total:
            turn, piece = divmod(step, CHUNKS)
            shard = sources[turn] * 2 + core
            block = region(shard, section, piece)
            arrived(block, z_sem.at[step])
            if turn == 0:
                send(block, block, z_sem.at[2 * CHUNKS + piece], across_z, crosses)
            else:
                send(block, block, z_sem.at[step], outer_z, crosses)
            send(block, block, x_sem.at[step], beside_x)
            send(block, block, y_sem.at[step], beside_y)
            to_twin(block, step)
        late = step - 1
        if 0 <= late < total:
            turn, piece = divmod(late, CHUNKS)
            shard = sources[turn] * 2 + core
            block = region(shard, beside_x[0], piece)
            arrived(block, x_sem.at[late])
            if piece % 2 == 0:
                send(block, block, far_sem.at[late], beside_y)
            to_twin(block, total + late)
            block = region(shard, beside_y[0], piece)
            arrived(block, y_sem.at[late])
            if piece % 2 == 1:
                send(block, block, far_sem.at[late], beside_x)
            to_twin(block, 2 * total + late)
        later = step - 2
        if 0 <= later < total:
            turn, piece = divmod(later, CHUNKS)
            shard = sources[turn] * 2 + core
            block = region(shard, 3 - section, piece)
            arrived(block, far_sem.at[later])
            to_twin(block, 3 * total + later)
        if step % 2 == 0 and step // 2 < len(doubling):
            doubled[step // 2].wait()
            if step // 2 + 1 < len(doubling):
                double_start(step // 2 + 1)
        first = min(step * per_step, looked_rows)
        last = min(first + per_step, looked_rows)
        if last > first:
            look_up(first, last)

    for number in range(len(twins)):
        kind, step = divmod(number, total)
        turn, piece = divmod(step, CHUNKS)
        part = (section, beside_x[0], beside_y[0], 3 - section)[kind]
        arrived(region(sources[turn] * 2 + 1 - core, part, piece), twin_sem.at[number])
    other = full_ref.at[pl.ds(pl.multiple_of((z * 2 + 1 - core) * pairs, pairs), pairs)]
    arrived(other, twin_own_sem)
    own.wait()
    for copy, when in sent:
        if when is None:
            copy.wait_send()
        else:
            pl.when(when)(copy.wait_send)


def spread(node_table, packed, place, near, live):
    devices = lax.axis_size(("section", "dp"))
    table_rows = node_table.shape[0]
    frontier_high = place.shape[1]
    looked = near.shape[0]
    total = 3 * CHUNKS
    sends = 2 * CHUNKS + 1 + 3 * total + total + 4 * total
    vmem = pl.BlockSpec(memory_space=pltpu.VMEM)
    return pl.pallas_call(
        spread_kernel,
        out_shape=(
            pltpu.VMEM((lax.axis_size("dp") * table_rows // 2, 2, node_table.shape[1]), jnp.bfloat16),
            jax.ShapeDtypeStruct((devices,) + packed.shape, packed.dtype),
            jax.ShapeDtypeStruct((looked, 256), jnp.int32),
            jax.ShapeDtypeStruct((looked, 512), jnp.float32),
        ),
        in_specs=[pl.BlockSpec(memory_space=pl.ANY), vmem, vmem, vmem, vmem],
        out_specs=(vmem, vmem, vmem, vmem),
        scratch_shapes=[
            pltpu.VMEM((384, frontier_high), jnp.bfloat16),
            pltpu.SemaphoreType.DMA(()),
            pltpu.SemaphoreType.DMA((total,)),
            pltpu.SemaphoreType.DMA((total,)),
            pltpu.SemaphoreType.DMA((total,)),
            pltpu.SemaphoreType.DMA((total,)),
            pltpu.SemaphoreType.DMA((4 * total,)),
            pltpu.SemaphoreType.DMA(()),
            pltpu.SemaphoreType.DMA((5,)),
            pltpu.SemaphoreType.DMA((sends,)),
            pltpu.SemaphoreType.DMA((5,)),
        ],
        compiler_params=pltpu.CompilerParams(
            collective_id=0, has_side_effects=True, vmem_limit_bytes=12 * 2**20
        ),
    )(node_table.reshape(table_rows // 2, 2, -1), packed, place, near, live)


def pick_kernel(idx_ref, mix_ref, table_ref, sum_ref, self_ref, *scratch):
    blocks = mix_ref.shape[0]
    stages = (scratch[:GROUP], scratch[GROUP : 2 * GROUP])
    lists = scratch[2 * GROUP : 2 * GROUP + SETS]
    sems = scratch[2 * GROUP + SETS]
    words = GROUP * BLOCK * SLOT
    lane = lax.broadcasted_iota(jnp.int32, (BLOCK, 2 * BLOCK * SLOT), 1)
    same = lane // (2 * SLOT) == lax.broadcasted_iota(jnp.int32, lane.shape, 0)
    near_part = jnp.logical_and(same, lane % (2 * SLOT) < 2 * SLOT - 2).astype(jnp.float32)
    self_part = jnp.logical_and(same, lane % (2 * SLOT) >= 2 * SLOT - 2).astype(jnp.float32)
    last = blocks // GROUP - 1

    def fetch(turn, slot):
        start_at = pl.multiple_of(jnp.minimum(turn, last) * words, words)
        return pltpu.make_async_copy(idx_ref.at[pl.ds(start_at, words)], lists[slot], sems.at[slot])

    def pick(member, slot, stage):
        for unit in range(BLOCK * SLOT):
            entry = table_ref[lists[slot][member * BLOCK * SLOT + unit]]
            stage[pl.ds(2 * unit, 2), :] = entry.astype(jnp.float32)

    def reduce(block, stage):
        mix = mix_ref[pl.ds(block, 1), :]
        left = jnp.concatenate([mix * near_part, mix * self_part], axis=0).astype(jnp.bfloat16)
        out = jnp.dot(left, stage[...].astype(jnp.bfloat16), preferred_element_type=jnp.float32)
        start_at = pl.multiple_of(block * BLOCK, BLOCK)
        sum_ref[pl.ds(start_at, BLOCK), :] = out[:BLOCK]
        self_ref[pl.ds(start_at, BLOCK), :] = out[BLOCK:].astype(jnp.bfloat16)

    for slot in range(SETS):
        fetch(slot, slot).start()
    for member in range(GROUP):
        stages[1][member][...] = jnp.zeros(stages[1][member].shape, jnp.float32)

    def round_of(number, carry):
        for slot in range(SETS):
            turn = number * SETS + slot
            fetch(turn, slot).wait()
            for member in range(GROUP):
                pick(member, slot, stages[slot % 2][member])
                reduce(
                    jnp.maximum((turn - 1) * GROUP + member, 0), stages[1 - slot % 2][member]
                )
            fetch(turn + SETS, slot).start()
        return carry

    lax.fori_loop(0, blocks // (GROUP * SETS), round_of, 0)
    for slot in range(SETS):
        fetch(0, slot).wait()
    for member in range(GROUP):
        reduce(blocks - GROUP + member, stages[(SETS - 1) % 2][member])


def picked(idx, mix, table):
    rows = mix.shape[0] * BLOCK
    width = table.shape[2]
    vmem = pl.BlockSpec(memory_space=pltpu.VMEM)
    return pl.pallas_call(
        pick_kernel,
        out_shape=(
            jax.ShapeDtypeStruct((rows, width), jnp.float32),
            jax.ShapeDtypeStruct((rows, width), jnp.bfloat16),
        ),
        in_specs=[pl.BlockSpec(memory_space=pl.ANY), vmem, vmem],
        out_specs=(vmem, vmem),
        scratch_shapes=[pltpu.VMEM((2 * BLOCK * SLOT, width), jnp.float32)] * (2 * GROUP)
        + [pltpu.SMEM((GROUP * BLOCK * SLOT,), jnp.int32)] * SETS
        + [pltpu.SemaphoreType.DMA((SETS,))],
        compiler_params=pltpu.CompilerParams(vmem_limit_bytes=16 * 2**20),
    )(idx.reshape(-1), mix, table)


def on_slice_kernels(node_table, owner_ids, dest_count, fan_inner):
    parts, peers = lax.axis_size("section"), lax.axis_size("dp")
    return (
        parts == 4
        and peers == 8
        and peers * node_table.size * 2 <= VMEM_TABLE_LIMIT
        and node_table.shape[1] == 128
        and node_table.shape[0] % (64 * CHUNKS) == 0
        and peers * node_table.shape[0] <= 131072
        and owner_ids.shape[0] % 1024 == 0
        and owner_ids.shape[0] <= 32768
        and fan_inner == SLOT - 1
        and dest_count % (BLOCK * GROUP * SETS) == 0
    )


def outer_product(left, right):
    return lax.dot_general(
        left, right, (((0,), (0,)), ((), ())), preferred_element_type=jnp.float32
    )


def against(left, right):
    return lax.dot_general(
        left, right, (((1,), (1,)), ((), ())), preferred_element_type=jnp.float32
    )


def silu_slope(before, grad_out):
    sigmoid = jax.nn.sigmoid(before)
    return (grad_out * sigmoid * (1.0 + before * (1.0 - sigmoid))).astype(jnp.bfloat16)


def moments(weight, gradient, first, second):
    first = BETA_ONE * first + (1.0 - BETA_ONE) * gradient
    second = BETA_TWO * second + (1.0 - BETA_TWO) * gradient * gradient
    update = (
        first / (1.0 - BETA_ONE**STEP) / (jnp.sqrt(second / (1.0 - BETA_TWO**STEP)) + EPSILON)
        + DECAY * weight
    )
    return (first, second, update)


def bias_ratio(weight, update, hidden):
    bounds = ((0, hidden), (hidden, 2 * hidden), (2 * hidden, weight.shape[0]))
    pieces = []
    for start_at, stop_at in bounds:
        weight_norm = jnp.sqrt(jnp.sum(weight[start_at:stop_at] ** 2))
        update_norm = jnp.sqrt(jnp.sum(update[start_at:stop_at] ** 2))
        pieces.append(jnp.zeros((stop_at - start_at,), jnp.float32) + weight_norm / update_norm)
    return jnp.concatenate(pieces)


def gathered_rows(node_table, owner_ids, row_ids):
    peer_count = lax.axis_size("dp")
    parts = lax.axis_size("section")
    table_rows = node_table.shape[0]
    if peer_count * node_table.size * 2 <= WHOLE_TABLE_LIMIT and table_rows % parts == 0:
        part_rows = table_rows // parts
        quarter = lax.dynamic_slice_in_dim(
            node_table, lax.axis_index("section") * part_rows, part_rows, 0
        )
        source = lax.all_gather(quarter, ("section", "dp"), axis=0, tiled=True)
        place = (row_ids // part_rows * peer_count + owner_ids) * part_rows + row_ids % part_rows
        return source, place
    frontier_rows = owner_ids.shape[0]
    slot_count = max(2, 2 * frontier_rows // peer_count)
    owner_hot = (owner_ids[:, None] == jnp.arange(peer_count)[None, :]).astype(jnp.int32)
    ranking = jnp.sum((jnp.cumsum(owner_hot, axis=0) - 1) * owner_hot, axis=1)
    placed = owner_ids * slot_count + ranking
    request = (
        jnp.zeros((peer_count * slot_count,), jnp.int32)
        .at[placed]
        .set(row_ids)
        .reshape(peer_count, slot_count)
    )
    returned = lax.all_to_all(
        node_table[lax.all_to_all(request, "dp", split_axis=0, concat_axis=0, tiled=True)],
        "dp",
        split_axis=0,
        concat_axis=0,
        tiled=True,
    )
    return returned.reshape(peer_count * slot_count, -1), placed


def on_device(
    node_table,
    owners,
    local_rows,
    inner_neighbours,
    inner_counts,
    outer_neighbours,
    outer_counts,
    labels,
    label_mask,
    weight_inner,
    weight_outer,
    weight_head,
    biases,
    first_inner,
    first_outer,
    first_head,
    first_biases,
    second_inner,
    second_outer,
    second_head,
    second_biases,
    smooth_inner,
    smooth_outer,
    smooth_head,
    smooth_biases,
):
    at = lax.axis_index("section")
    every = ("section", "dp")
    hidden = weight_inner.shape[1]
    dest_count, fan_inner = inner_neighbours.shape[1:]
    seed_count, fan_outer = outer_neighbours.shape[1:]
    classes = weight_head.shape[1]
    label_part = jnp.sum(label_mask.astype(jnp.float32))

    def mine(array):
        return lax.dynamic_index_in_dim(array, at, 0, keepdims=False)

    inner_neighbours, inner_counts = mine(inner_neighbours), mine(inner_counts)
    outer_neighbours, outer_counts = mine(outer_neighbours), mine(outer_counts)
    labels, label_mask = mine(labels), mine(label_mask)
    bias_inner = biases[:hidden]
    bias_outer = biases[hidden : 2 * hidden]
    bias_head = biases[2 * hidden :]

    owner_ids, row_ids = owners.reshape(-1), local_rows.reshape(-1)
    weights = (weight_inner, weight_outer, weight_head)
    keep = jnp.arange(fan_inner)[None, :] < inner_counts[:, None]
    if on_slice_kernels(node_table, owner_ids, dest_count, fan_inner):
        devices, peers = lax.axis_size(every), lax.axis_size("dp")
        place = (owner_ids * node_table.shape[0] + row_ids).reshape(-1, 128).T
        own = jnp.arange(dest_count, dtype=jnp.int32)[:, None]
        near = jnp.concatenate([inner_neighbours, own], axis=1).reshape(-1, BLOCK * SLOT)
        live = jnp.concatenate([keep.astype(jnp.float32), jnp.ones(own.shape, jnp.float32)], axis=1)
        live = live.reshape(near.shape)
        tail = jnp.stack([label_part // 256, label_part % 256])
        tail = jnp.pad(tail[None], ((0, weight_head.shape[0] - 1), (0, hidden - classes - 2)))
        packed = jnp.concatenate(
            [weight_inner, weight_outer, jnp.concatenate([weight_head, tail], axis=1)], axis=0
        ).astype(jnp.bfloat16)
        table, everyone, idx, mix = spread(node_table, packed, place, near, live)
        row_inner, row_outer = weight_inner.shape[0], weight_outer.shape[0]
        full_inner = everyone[:, :row_inner].reshape(-1, hidden)
        full_outer = everyone[:, row_inner : row_inner + row_outer].reshape(-1, hidden)
        full_head = everyone[:, row_inner + row_outer :].reshape(-1, hidden)[:, :classes]
        counts = everyone[:peers, row_inner + row_outer, classes : classes + 2].astype(jnp.float32)
        label_count = jnp.maximum(jnp.sum(counts[:, 0] * 256 + counts[:, 1]), 1.0)
        summed, self_rows = picked(idx, mix, table)
    else:
        label_count = jnp.maximum(lax.psum(label_part, "dp"), 1.0)
        full_inner, full_outer, full_head = (
            lax.all_gather(weight.astype(jnp.bfloat16), every, axis=0, tiled=True)
            for weight in weights
        )
        source, place = gathered_rows(node_table, owner_ids, row_ids)
        rows = source[place[inner_neighbours]]
        summed = jnp.sum(
            jnp.where(keep[:, :, None], rows, jnp.zeros((), rows.dtype)), axis=1, dtype=jnp.float32
        )
        self_rows = source[place[:dest_count]]
    mean_one = (summed / inner_counts[:, None].astype(jnp.float32)).astype(jnp.bfloat16)
    joined_one = jnp.concatenate([self_rows, mean_one], axis=1)
    pre_one = jnp.dot(joined_one, full_inner, preferred_element_type=jnp.float32) + bias_inner
    hidden_one = jax.nn.silu(pre_one).astype(jnp.bfloat16)

    keep_outer = jnp.arange(fan_outer)[None, :] < outer_counts[:, None]
    pick = jnp.sum(
        (
            jnp.where(keep_outer, outer_neighbours, -1)[:, :, None]
            == jnp.arange(dest_count)[None, None, :]
        ).astype(jnp.float32),
        axis=1,
    ).astype(jnp.bfloat16)
    count_two = outer_counts[:, None].astype(jnp.float32)
    mean_two = (jnp.dot(pick, hidden_one, preferred_element_type=jnp.float32) / count_two).astype(
        jnp.bfloat16
    )
    joined_two = jnp.concatenate([hidden_one[:seed_count], mean_two], axis=1)
    pre_two = jnp.dot(joined_two, full_outer, preferred_element_type=jnp.float32) + bias_outer
    hidden_two = jax.nn.silu(pre_two).astype(jnp.bfloat16)

    logits = jnp.dot(hidden_two, full_head, preferred_element_type=jnp.float32) + bias_head
    shifted = logits - jnp.max(logits, axis=1, keepdims=True)
    log_total = jnp.log(jnp.sum(jnp.exp(shifted), axis=1, keepdims=True))
    chosen = (jnp.arange(classes)[None, :] == labels[:, None]).astype(jnp.float32)
    row_weight = label_mask.astype(jnp.float32)
    loss_part = jnp.sum((log_total[:, 0] - jnp.sum(shifted * chosen, axis=1)) * row_weight)
    grad_logits = (
        (jnp.exp(shifted - log_total) - chosen) * (row_weight / label_count)[:, None]
    ).astype(jnp.bfloat16)
    grad_head = outer_product(hidden_two, grad_logits)
    grad_two = against(grad_logits, full_head).astype(jnp.bfloat16).astype(jnp.float32)
    grad_pre_two = silu_slope(pre_two, grad_two)
    grad_outer = outer_product(joined_two, grad_pre_two)
    grad_joined = against(grad_pre_two, full_outer)
    share = grad_joined[:, hidden:] / count_two
    share_high = share.astype(jnp.bfloat16)
    share_low = (share - share_high.astype(jnp.float32)).astype(jnp.bfloat16)
    grad_one = outer_product(pick, share_high) + outer_product(pick, share_low)
    grad_one = jnp.concatenate(
        [grad_one[:seed_count] + grad_joined[:, :hidden], grad_one[seed_count:]], axis=0
    )
    grad_one = grad_one.astype(jnp.bfloat16).astype(jnp.float32)
    grad_pre_one = silu_slope(pre_one, grad_one)
    grad_inner = outer_product(joined_one, grad_pre_one)
    bias_part = jnp.concatenate(
        [
            jnp.sum(part.astype(jnp.float32), axis=0)
            for part in (grad_pre_one, grad_pre_two, grad_logits)
        ]
    )

    devices = lax.axis_size(every)
    grads = jnp.concatenate(
        [grad.reshape(devices, -1) for grad in (grad_inner, grad_outer, grad_head)], axis=1
    )
    shard = lax.psum_scatter(grads, every, scatter_dimension=0, tiled=True).reshape(-1)
    shards = []
    for weight in weights:
        shards.append(shard[: weight.size].reshape(weight.shape))
        shard = shard[weight.size :]
    packed = lax.psum(jnp.concatenate([bias_part, loss_part[None]]), every)
    bias_grad, loss_sum = packed[:-1], packed[-1]
    grad_partial = sum((jnp.sum(part * part) for part in shards))
    weight_partial = [jnp.sum(weight * weight) for weight in weights]
    squares = lax.psum(jnp.stack([grad_partial] + weight_partial), every)
    clip_norm = jnp.sqrt(squares[0] + jnp.sum(bias_grad * bias_grad))
    factor = jnp.minimum(1.0, CLIP / clip_norm)
    firsts = (first_inner, first_outer, first_head)
    seconds = (second_inner, second_outer, second_head)
    smooths = (smooth_inner, smooth_outer, smooth_head)
    states = [
        moments(weights[slot_at], shards[slot_at] * factor, firsts[slot_at], seconds[slot_at])
        for slot_at in range(3)
    ]
    update_square = lax.psum(jnp.stack([jnp.sum(state[2] * state[2]) for state in states]), every)
    weight_norms = jnp.sqrt(squares[1:])
    update_norms = jnp.sqrt(update_square)
    news = [
        weights[slot_at]
        - RATE * (weight_norms[slot_at] / update_norms[slot_at]) * states[slot_at][2]
        for slot_at in range(3)
    ]
    averages = [
        AVERAGE * smooths[slot_at] + (1.0 - AVERAGE) * news[slot_at] for slot_at in range(3)
    ]
    bias_first, bias_second, bias_update = moments(
        biases, bias_grad * factor, first_biases, second_biases
    )
    bias_new = biases - RATE * bias_ratio(biases, bias_update, hidden) * bias_update
    bias_average = AVERAGE * smooth_biases + (1.0 - AVERAGE) * bias_new
    return (
        loss_sum,
        label_count,
        clip_norm,
        jnp.stack([weight_norms, update_norms], axis=1),
        news[0],
        news[1],
        news[2],
        bias_new,
        states[0][0],
        states[1][0],
        states[2][0],
        bias_first,
        states[0][1],
        states[1][1],
        states[2][1],
        bias_second,
        averages[0],
        averages[1],
        averages[2],
        bias_average,
    )


def solution(mesh):
    in_specs = (
        P("dp", None),
        P("section", "dp", None),
        P("section", "dp"),
        P(None, "dp", None),
        P(None, "dp"),
        P(None, "dp", None),
        P(None, "dp"),
        P(None, "dp"),
        P(None, "dp"),
        P(("section", "dp"), None),
        P(("section", "dp"), None),
        P(("section", "dp"), None),
        P(),
        P(("section", "dp"), None),
        P(("section", "dp"), None),
        P(("section", "dp"), None),
        P(),
        P(("section", "dp"), None),
        P(("section", "dp"), None),
        P(("section", "dp"), None),
        P(),
        P(("section", "dp"), None),
        P(("section", "dp"), None),
        P(("section", "dp"), None),
        P(),
    )
    out_specs = (
        P(),
        P(),
        P(),
        P(),
        P(("section", "dp"), None),
        P(("section", "dp"), None),
        P(("section", "dp"), None),
        P(),
        P(("section", "dp"), None),
        P(("section", "dp"), None),
        P(("section", "dp"), None),
        P(),
        P(("section", "dp"), None),
        P(("section", "dp"), None),
        P(("section", "dp"), None),
        P(),
        P(("section", "dp"), None),
        P(("section", "dp"), None),
        P(("section", "dp"), None),
        P(),
    )
    return jax.shard_map(
        on_device, mesh=mesh, in_specs=in_specs, out_specs=out_specs, check_vma=False
    )
```

```python
import functools

import jax
import jax.numpy as jnp
from jax import lax
from jax.experimental import pallas as pl
from jax.experimental.pallas import tpu as pltpu
from jax.sharding import PartitionSpec as P

STEP = 5


BETA_ONE = 0.9
BETA_TWO = 0.999
EPSILON = 1e-06
DECAY = 0.01
RATE = 0.25
CLIP = 0.05
AVERAGE = 0.9


VMEM_TABLE_LIMIT = 36 * 2**20
WHOLE_TABLE_LIMIT = 64 * 2**20
MESH = pl.DeviceIdType.MESH
SLOT = 16
BLOCK = 16
CHUNKS = 4
GROUP = 4
SETS = 4


def spread_kernel(
    table_ref,
    weight_ref,
    place_ref,
    near_ref,
    live_ref,
    full_ref,
    weights_ref,
    idx_ref,
    mix_ref,
    parts,
    own_sem,
    z_sem,
    x_sem,
    y_sem,
    far_sem,
    twin_sem,
    twin_own_sem,
    double_sem,
    send_sem,
    double_send_sem,
):
    section, at = lax.axis_index("section"), lax.axis_index("dp")
    z, core = at // 2, at % 2
    flipped = z // 2
    height = z + flipped * (3 - 2 * z)
    pairs = table_ref.shape[0]
    quarter = pairs // 4
    chunk = quarter // CHUNKS

    def level(value):
        return value + flipped * (3 - 2 * value)

    here = (section, at)
    twin = (section, z * 2 + 1 - core)
    beside_x = (section + 1 - 2 * (section % 2), at)
    beside_y = (section + 2 - 4 * (section // 2), at)
    inner_z = (section, level(1 - height) * 2 + core)
    across_z = (section, level(2) * 2 + core)
    outer_z = (section, level(0) * 2 + core)
    skip_z = (section, ((z + 2) % 4) * 2 + core)
    sources = [level(1 - height), level(2), level(3)]
    crosses = height == 1

    barrier = pltpu.get_barrier_semaphore()
    for partner in (twin, beside_x, beside_y, inner_z, skip_z):
        pl.semaphore_signal(barrier, inc=1, device_id=partner, device_id_type=MESH)

    @pl.when(crosses)
    def greet_across():
        pl.semaphore_signal(barrier, inc=1, device_id=across_z, device_id_type=MESH)

    pl.semaphore_wait(barrier, 5 + height)

    sent = []

    def region(shard, part, piece):
        start_at = shard * pairs + part * quarter + piece * chunk
        return full_ref.at[pl.ds(pl.multiple_of(start_at, chunk), chunk)]

    def send(source, target, recv, device, when=None):
        number = len(sent)
        copy = pltpu.make_async_remote_copy(
            src_ref=source,
            dst_ref=target,
            send_sem=send_sem.at[number],
            recv_sem=recv,
            device_id=device,
            device_id_type=MESH,
        )
        sent.append((copy, when))
        if when is None:
            copy.start()
        else:
            pl.when(when)(copy.start)
        return copy

    def arrived(target, recv):
        pltpu.make_async_copy(target, target, recv).wait()

    mine = (core * 4 + section) * 4 + z
    pltpu.sync_copy(weight_ref, weights_ref.at[mine])
    doubling = [(inner_z, 1), (skip_z, 2), (beside_x, 4), (beside_y, 8), (twin, 16)]
    doubled = []

    def double_start(number):
        device, size = doubling[number]
        start_at = (mine // size) * size
        block = weights_ref.at[pl.ds(start_at, size)]
        copy = pltpu.make_async_remote_copy(
            src_ref=block,
            dst_ref=block,
            send_sem=double_send_sem.at[number],
            recv_sem=double_sem.at[number],
            device_id=device,
            device_id_type=MESH,
        )
        copy.start()
        doubled.append(copy)

    double_start(0)
    for piece in range(CHUNKS):
        start_at = section * quarter + piece * chunk
        block = table_ref.at[pl.ds(pl.multiple_of(start_at, chunk), chunk)]
        goal = region(at, section, piece)
        send(block, goal, z_sem.at[piece], inner_z)
        send(block, goal, z_sem.at[CHUNKS + piece], across_z, crosses)
    whole = full_ref.at[pl.ds(pl.multiple_of(at * pairs, pairs), pairs)]
    own = pltpu.make_async_copy(table_ref, whole, own_sem)
    own.start()
    send(table_ref, whole, twin_own_sem, twin)

    placed = place_ref[...]
    pair_at = placed // 2
    high = place_ref.shape[1]
    parts[0:128, :] = (pair_at % 256).astype(jnp.float32).astype(jnp.bfloat16)
    parts[128:256, :] = (pair_at // 256).astype(jnp.float32).astype(jnp.bfloat16)
    parts[256:384, :] = (placed % 2).astype(jnp.float32).astype(jnp.bfloat16)
    looked_rows = near_ref.shape[0]
    steps = 3 * CHUNKS + 2
    per_step = -(-looked_rows // (8 * steps)) * 8

    def look_up(first, last):
        def rows_of(block, carry):
            start_at = pl.multiple_of(block * 8, 8)
            sub = lax.broadcasted_iota(jnp.int32, (high, 256), 0)
            low_at = lax.broadcasted_iota(jnp.int32, (128, 256), 0)
            row = lax.broadcasted_iota(jnp.int32, (256, 512), 0)
            column = lax.broadcasted_iota(jnp.int32, (256, 512), 1)
            for k in range(8):
                node = near_ref[pl.ds(start_at + k, 1), :]
                hot = (sub == node // 128).astype(jnp.float32).astype(jnp.bfloat16)
                got = jnp.dot(parts[...], hot, preferred_element_type=jnp.float32)
                chosen = low_at == node % 128
                found = jnp.where(chosen, got[0:128] + 256.0 * got[128:256], 0.0)
                odd = jnp.where(chosen, got[256:384], 0.0)
                idx_ref[pl.ds(start_at + k, 1), :] = jnp.sum(found, axis=0, keepdims=True).astype(
                    jnp.int32
                )
                mix_ref[pl.ds(start_at + k, 1), 0:256] = jnp.sum(odd, axis=0, keepdims=True)
            odd = mix_ref[pl.ds(start_at, 8), 0:256]
            live = live_ref[pl.ds(start_at, 8), :]
            mix_ref[pl.ds(start_at, 8), :] = jnp.dot(
                (live * (1.0 - odd)).astype(jnp.bfloat16),
                (column == 2 * row).astype(jnp.float32).astype(jnp.bfloat16),
                preferred_element_type=jnp.float32,
            ) + jnp.dot(
                (live * odd).astype(jnp.bfloat16),
                (column == 2 * row + 1).astype(jnp.float32).astype(jnp.bfloat16),
                preferred_element_type=jnp.float32,
            )
            return carry

        lax.fori_loop(first // 8, last // 8, rows_of, 0)

    total = 3 * CHUNKS
    twins = []

    def to_twin(block, number):
        send(block, block, twin_sem.at[number], twin)
        twins.append(number)

    for step in range(steps):
        if step < total:
            turn, piece = divmod(step, CHUNKS)
            shard = sources[turn] * 2 + core
            block = region(shard, section, piece)
            arrived(block, z_sem.at[step])
            if turn == 0:
                send(block, block, z_sem.at[2 * CHUNKS + piece], across_z, crosses)
            else:
                send(block, block, z_sem.at[step], outer_z, crosses)
            send(block, block, x_sem.at[step], beside_x)
            send(block, block, y_sem.at[step], beside_y)
            to_twin(block, step)
        late = step - 1
        if 0 <= late < total:
            turn, piece = divmod(late, CHUNKS)
            shard = sources[turn] * 2 + core
            block = region(shard, beside_x[0], piece)
            arrived(block, x_sem.at[late])
            if piece % 2 == 0:
                send(block, block, far_sem.at[late], beside_y)
            to_twin(block, total + late)
            block = region(shard, beside_y[0], piece)
            arrived(block, y_sem.at[late])
            if piece % 2 == 1:
                send(block, block, far_sem.at[late], beside_x)
            to_twin(block, 2 * total + late)
        later = step - 2
        if 0 <= later < total:
            turn, piece = divmod(later, CHUNKS)
            shard = sources[turn] * 2 + core
            block = region(shard, 3 - section, piece)
            arrived(block, far_sem.at[later])
            to_twin(block, 3 * total + later)
        if step % 2 == 0 and step // 2 < len(doubling):
            doubled[step // 2].wait()
            if step // 2 + 1 < len(doubling):
                double_start(step // 2 + 1)
        first = min(step * per_step, looked_rows)
        last = min(first + per_step, looked_rows)
        if last > first:
            look_up(first, last)

    for number in range(len(twins)):
        kind, step = divmod(number, total)
        turn, piece = divmod(step, CHUNKS)
        part = (section, beside_x[0], beside_y[0], 3 - section)[kind]
        arrived(region(sources[turn] * 2 + 1 - core, part, piece), twin_sem.at[number])
    other = full_ref.at[pl.ds(pl.multiple_of((z * 2 + 1 - core) * pairs, pairs), pairs)]
    arrived(other, twin_own_sem)
    own.wait()
    for copy, when in sent:
        if when is None:
            copy.wait_send()
        else:
            pl.when(when)(copy.wait_send)


def spread(node_table, packed, place, near, live):
    devices = lax.axis_size(("section", "dp"))
    table_rows = node_table.shape[0]
    frontier_high = place.shape[1]
    looked = near.shape[0]
    total = 3 * CHUNKS
    sends = 2 * CHUNKS + 1 + 3 * total + total + 4 * total
    vmem = pl.BlockSpec(memory_space=pltpu.VMEM)
    return pl.pallas_call(
        spread_kernel,
        out_shape=(
            pltpu.VMEM((lax.axis_size("dp") * table_rows // 2, 2, node_table.shape[1]), jnp.bfloat16),
            jax.ShapeDtypeStruct((devices,) + packed.shape, packed.dtype),
            jax.ShapeDtypeStruct((looked, 256), jnp.int32),
            jax.ShapeDtypeStruct((looked, 512), jnp.float32),
        ),
        in_specs=[pl.BlockSpec(memory_space=pl.ANY), vmem, vmem, vmem, vmem],
        out_specs=(vmem, vmem, vmem, vmem),
        scratch_shapes=[
            pltpu.VMEM((384, frontier_high), jnp.bfloat16),
            pltpu.SemaphoreType.DMA(()),
            pltpu.SemaphoreType.DMA((total,)),
            pltpu.SemaphoreType.DMA((total,)),
            pltpu.SemaphoreType.DMA((total,)),
            pltpu.SemaphoreType.DMA((total,)),
            pltpu.SemaphoreType.DMA((4 * total,)),
            pltpu.SemaphoreType.DMA(()),
            pltpu.SemaphoreType.DMA((5,)),
            pltpu.SemaphoreType.DMA((sends,)),
            pltpu.SemaphoreType.DMA((5,)),
        ],
        compiler_params=pltpu.CompilerParams(
            collective_id=0, has_side_effects=True, vmem_limit_bytes=12 * 2**20
        ),
    )(node_table.reshape(table_rows // 2, 2, -1), packed, place, near, live)


def pick_kernel(idx_ref, mix_ref, table_ref, joined_ref, *scratch):
    blocks = mix_ref.shape[0]
    stages = (scratch[:GROUP], scratch[GROUP : 2 * GROUP])
    lists = scratch[2 * GROUP : 2 * GROUP + SETS]
    sems = scratch[2 * GROUP + SETS]
    words = GROUP * BLOCK * SLOT
    lane = lax.broadcasted_iota(jnp.int32, (BLOCK, 2 * BLOCK * SLOT), 1)
    same = lane // (2 * SLOT) == lax.broadcasted_iota(jnp.int32, lane.shape, 0)
    near_part = jnp.logical_and(same, lane % (2 * SLOT) < 2 * SLOT - 2).astype(jnp.float32)
    self_part = jnp.logical_and(same, lane % (2 * SLOT) >= 2 * SLOT - 2).astype(jnp.float32)
    last = blocks // GROUP - 1

    def fetch(turn, slot):
        start_at = pl.multiple_of(jnp.minimum(turn, last) * words, words)
        return pltpu.make_async_copy(idx_ref.at[pl.ds(start_at, words)], lists[slot], sems.at[slot])

    def pick(member, slot, stage):
        for unit in range(BLOCK * SLOT):
            entry = table_ref[lists[slot][member * BLOCK * SLOT + unit]]
            stage[pl.ds(2 * unit, 2), :] = entry.astype(jnp.float32)

    def reduce(block, stage):
        mix = mix_ref[pl.ds(block, 1), :]
        near = mix * near_part
        left = jnp.concatenate([near, mix * self_part], axis=0).astype(jnp.bfloat16)
        out = jnp.dot(left, stage[...].astype(jnp.bfloat16), preferred_element_type=jnp.float32)
        count = jnp.maximum(jnp.sum(near, axis=1, keepdims=True), 1.0)
        both = jnp.concatenate([out[BLOCK:], out[:BLOCK] / count], axis=1)
        start_at = pl.multiple_of(block * BLOCK, BLOCK)
        joined_ref[pl.ds(start_at, BLOCK), :] = both.astype(jnp.bfloat16)

    for slot in range(SETS):
        fetch(slot, slot).start()
    for member in range(GROUP):
        stages[1][member][...] = jnp.zeros(stages[1][member].shape, jnp.float32)

    def round_of(number, carry):
        for slot in range(SETS):
            turn = number * SETS + slot
            fetch(turn, slot).wait()
            for member in range(GROUP):
                pick(member, slot, stages[slot % 2][member])
                reduce(
                    jnp.maximum((turn - 1) * GROUP + member, 0), stages[1 - slot % 2][member]
                )
            fetch(turn + SETS, slot).start()
        return carry

    lax.fori_loop(0, blocks // (GROUP * SETS), round_of, 0)
    for slot in range(SETS):
        fetch(0, slot).wait()
    for member in range(GROUP):
        reduce(blocks - GROUP + member, stages[(SETS - 1) % 2][member])


def picked(idx, mix, table):
    rows = mix.shape[0] * BLOCK
    width = table.shape[2]
    vmem = pl.BlockSpec(memory_space=pltpu.VMEM)
    return pl.pallas_call(
        pick_kernel,
        out_shape=jax.ShapeDtypeStruct((rows, 2 * width), jnp.bfloat16),
        in_specs=[pl.BlockSpec(memory_space=pl.ANY), vmem, vmem],
        out_specs=vmem,
        scratch_shapes=[pltpu.VMEM((2 * BLOCK * SLOT, width), jnp.float32)] * (2 * GROUP)
        + [pltpu.SMEM((GROUP * BLOCK * SLOT,), jnp.int32)] * SETS
        + [pltpu.SemaphoreType.DMA((SETS,))],
        compiler_params=pltpu.CompilerParams(vmem_limit_bytes=16 * 2**20),
    )(idx.reshape(-1), mix, table)


TILE = 256


def block_order():
    return [(e % 2) * 16 + (e // 8) * 4 + (e % 8) // 2 for e in range(32)]


def dense_kernel(
    sizes,
    joined_ref,
    everyone_ref,
    bias_ref,
    seed_ref,
    seed_across_ref,
    grads_ref,
    extra_ref,
    first_pre,
    first_hidden,
    wide,
    mean_sum,
    pick_back,
    inner_sum,
):
    classes, fan_outer, row_inner, row_outer, row_head = sizes
    dest_count, hidden = joined_ref.shape
    tiles = dest_count // TILE
    order = block_order()
    weights = everyone_ref[...].astype(jnp.float32)
    split = (0, row_inner, row_inner + row_outer, row_inner + row_outer + row_head)
    full_inner, full_outer, full_head = (
        jnp.concatenate([weights[place, split[k] : split[k + 1]] for place in order], axis=0)
        for k in range(3)
    )
    lane = lax.broadcasted_iota(jnp.int32, (1, hidden), 1)
    tails = weights[0:4, split[2] : split[2] + 1] + weights[16:20, split[2] : split[2] + 1]
    tails = jnp.sum(tails.reshape(4, hidden), axis=0, keepdims=True)
    scale = jnp.where(lane == classes, 256.0, jnp.where(lane == classes + 1, 1.0, 0.0))
    label_count = jnp.maximum(jnp.sum(tails * scale), 1.0)
    full_inner = full_inner.astype(jnp.bfloat16)
    full_outer = full_outer.astype(jnp.bfloat16)
    full_head = jnp.where(lane < classes, full_head, 0.0).astype(jnp.bfloat16)
    bias_inner, bias_outer, bias_head = (bias_ref[k : k + 1, :] for k in range(3))
    seeds = seed_ref.shape[0]
    kept = seed_ref[:, 0:fan_outer]
    count_two = jnp.sum((kept >= 0).astype(jnp.float32), axis=1, keepdims=True)
    for j in range(fan_outer):
        wide[j] = jnp.broadcast_to(seed_ref[:, j : j + 1], (seeds, TILE))
    mean_sum[...] = jnp.zeros(mean_sum.shape, jnp.float32)

    def forward(tile, carry):
        start_at = pl.multiple_of(tile * TILE, TILE)
        rows = pl.ds(start_at, TILE)
        before = (
            jnp.dot(joined_ref[rows, :], full_inner, preferred_element_type=jnp.float32) + bias_inner
        )
        first_pre[rows, :] = before
        out = (before * lax.logistic(before)).astype(jnp.bfloat16)
        first_hidden[rows, :] = out
        dest = lax.broadcasted_iota(jnp.int32, (seeds, TILE), 1) + start_at
        hits = jnp.zeros((seeds, TILE), jnp.float32)
        for j in range(fan_outer):
            hits = hits + (wide[j] == dest).astype(jnp.float32)
        mean_sum[...] += jnp.dot(
            hits.astype(jnp.bfloat16), out, preferred_element_type=jnp.float32
        )
        return carry

    lax.fori_loop(0, tiles, forward, 0)
    mean_two = (mean_sum[...] / count_two).astype(jnp.bfloat16)
    joined_two = jnp.concatenate([first_hidden[0:seeds, :], mean_two], axis=1)
    pre_two = jnp.dot(joined_two, full_outer, preferred_element_type=jnp.float32) + bias_outer
    gate_two = lax.logistic(pre_two)
    hidden_two = (pre_two * gate_two).astype(jnp.bfloat16)
    logits = jnp.dot(hidden_two, full_head, preferred_element_type=jnp.float32) + bias_head
    inside = lane < classes
    highest = jnp.max(jnp.where(inside, logits, -jnp.inf), axis=1, keepdims=True)
    shifted = jnp.where(inside, logits - highest, 0.0)
    total = jnp.sum(jnp.where(inside, jnp.exp(shifted), 0.0), axis=1, keepdims=True)
    log_total = jnp.log(total)
    chosen = (lane == seed_ref[:, fan_outer : fan_outer + 1]).astype(jnp.float32)
    row_weight = seed_ref[:, fan_outer + 1 : fan_outer + 2].astype(jnp.float32)
    loss = jnp.sum((log_total - jnp.sum(shifted * chosen, axis=1, keepdims=True)) * row_weight)
    grad_logits = (jnp.exp(shifted - log_total) - chosen) * (row_weight / label_count)
    grad_logits = jnp.where(inside, grad_logits, 0.0).astype(jnp.bfloat16)
    grad_head = outer_product(hidden_two, grad_logits)
    grad_two = against(grad_logits, full_head).astype(jnp.bfloat16).astype(jnp.float32)
    grad_pre_two = (grad_two * gate_two * (1.0 + pre_two * (1.0 - gate_two))).astype(jnp.bfloat16)
    grad_outer = outer_product(joined_two, grad_pre_two)
    grad_joined = against(grad_pre_two, full_outer)
    share = grad_joined[:, hidden:] / count_two
    share_high = share.astype(jnp.bfloat16)
    share_low = (share - share_high.astype(jnp.float32)).astype(jnp.bfloat16)
    for number, place in enumerate(order):
        grads_ref[place, split[1] : split[2], :] = grad_outer[
            number * row_outer : (number + 1) * row_outer
        ]
        grads_ref[place, split[2] : split[3], :] = grad_head[
            number * row_head : (number + 1) * row_head
        ]
    inner_sum[...] = jnp.zeros(inner_sum.shape, jnp.float32)
    share_parts = jnp.concatenate([share_high, share_low], axis=0)

    def backward(tile, bias_sum, own=None):
        start_at = pl.multiple_of(jnp.int32(tile) * TILE, TILE)
        rows = pl.ds(start_at, TILE)
        dest = lax.broadcasted_iota(jnp.int32, (TILE, seeds), 0) + start_at
        hits = jnp.zeros((TILE, seeds), jnp.float32)
        for j in range(fan_outer):
            hits = hits + (seed_across_ref[j : j + 1, :] == dest).astype(jnp.float32)
        hits = hits.astype(jnp.bfloat16)
        both_hits = jnp.concatenate([hits, hits], axis=1)
        grad_one = jnp.dot(both_hits, share_parts, preferred_element_type=jnp.float32)
        if own is not None:
            grad_one = grad_one + own
        grad_one = grad_one.astype(jnp.bfloat16).astype(jnp.float32)
        before = first_pre[rows, :]
        gate = lax.logistic(before)
        grad_pre = (grad_one * gate * (1.0 + before * (1.0 - gate))).astype(jnp.bfloat16)
        inner_sum[...] += outer_product(joined_ref[rows, :], grad_pre)
        return bias_sum + jnp.sum(grad_pre.astype(jnp.float32), axis=0, keepdims=True)

    pick_back[...] = jnp.zeros(pick_back.shape, jnp.float32)
    pick_back[0:seeds, :] = grad_joined[:, 0:hidden]
    bias_sum = backward(0, jnp.zeros((1, hidden), jnp.float32), pick_back[...])
    bias_sum = lax.fori_loop(1, tiles, backward, bias_sum)
    grad_inner = inner_sum[...]
    for number, place in enumerate(order):
        grads_ref[place, split[0] : split[1], :] = grad_inner[
            number * row_inner : (number + 1) * row_inner
        ]
    extra_ref[0:1, :] = bias_sum
    extra_ref[1:2, :] = jnp.sum(grad_pre_two.astype(jnp.float32), axis=0, keepdims=True)
    extra_ref[2:3, :] = jnp.sum(grad_logits.astype(jnp.float32), axis=0, keepdims=True)
    extra_ref[3:4, :] = jnp.where(lane == 0, loss, jnp.where(lane == 1, label_count, 0.0))
    extra_ref[4:8, :] = jnp.zeros((4, hidden), jnp.float32)


def dense(sizes, joined, everyone, bias_rows, seed_table):
    dest_count, hidden = joined.shape
    seeds = seed_table.shape[0]
    vmem = pl.BlockSpec(memory_space=pltpu.VMEM)
    return pl.pallas_call(
        functools.partial(dense_kernel, sizes),
        out_shape=(
            jax.ShapeDtypeStruct(everyone.shape, jnp.float32),
            jax.ShapeDtypeStruct((8, hidden), jnp.float32),
        ),
        in_specs=[vmem] * 5,
        out_specs=(vmem, vmem),
        scratch_shapes=[
            pltpu.VMEM((dest_count, hidden), jnp.float32),
            pltpu.VMEM((dest_count, hidden), jnp.bfloat16),
            pltpu.VMEM((sizes[1], seeds, TILE), jnp.int32),
            pltpu.VMEM((seeds, hidden), jnp.float32),
            pltpu.VMEM((TILE, hidden), jnp.float32),
            pltpu.VMEM((hidden, hidden), jnp.float32),
        ],
        compiler_params=pltpu.CompilerParams(vmem_limit_bytes=32 * 2**20),
    )(joined, everyone, bias_rows, seed_table, seed_table.T)


def reduce_kernel(
    sizes,
    grads_ref,
    extra_ref,
    weight_refs,
    first_refs,
    second_refs,
    out_ref,
    half,
    half_in,
    fourth,
    plane_in,
    line_in,
    extra_twin,
    extra_plane,
    extra_line,
    sums_twin,
    sums_plane,
    sums_line,
    recv_sem,
    send_sem,
):
    section, at = lax.axis_index("section"), lax.axis_index("dp")
    z, core = at // 2, at % 2
    rows, hidden = grads_ref.shape[1], grads_ref.shape[2]
    twin = (section, z * 2 + 1 - core)
    plane = [((section + k) % 4, at) for k in range(1, 4)]
    line = [(section, ((z + k) % 4) * 2 + core) for k in range(1, 4)]
    barrier = pltpu.get_barrier_semaphore()
    for partner in [twin] + plane + line:
        pl.semaphore_signal(barrier, inc=1, device_id=partner, device_id_type=MESH)
    pl.semaphore_wait(barrier, 7)
    copies = []

    def send(source, target, number, device):
        copy = pltpu.make_async_remote_copy(
            src_ref=source,
            dst_ref=target,
            send_sem=send_sem.at[len(copies)],
            recv_sem=recv_sem.at[number],
            device_id=device,
            device_id_type=MESH,
        )
        copies.append(copy)
        copy.start()

    def arrived(target, number):
        pltpu.make_async_copy(target, target, recv_sem.at[number]).wait()

    def over_twin(value, slots, base):
        slots[core] = value
        send(slots.at[core], slots.at[core], base, twin)
        arrived(slots.at[1 - core], base)
        return slots[0] + slots[1]

    def over_four(value, slots, base, me, partners):
        slots[me] = value
        for partner in partners:
            send(slots.at[me], slots.at[me], base + me, partner)
        for k in range(1, 4):
            other = (me + k) % 4
            arrived(slots.at[other], base + other)
        return (slots[0] + slots[1]) + (slots[2] + slots[3])

    send(grads_ref.at[pl.ds((1 - core) * 16, 16)], half_in, 0, twin)
    extra = over_twin(extra_ref[...], extra_twin, 1)
    arrived(half_in, 0)
    half[...] = grads_ref[pl.ds(core * 16, 16)] + half_in[...]
    for k, partner in enumerate(plane):
        send(half.at[pl.ds(partner[0] * 4, 4)], plane_in.at[section], 2 + section, partner)
    extra = over_four(extra, extra_plane, 6, section, plane)
    plane_in[section] = half[pl.ds(section * 4, 4)]
    for k in range(1, 4):
        other = (section + k) % 4
        arrived(plane_in.at[other], 2 + other)
    quarter = (plane_in[0] + plane_in[1]) + (plane_in[2] + plane_in[3])
    fourth[...] = quarter
    for k, partner in enumerate(line):
        send(fourth.at[pl.ds((z + k + 1) % 4, 1)], line_in.at[pl.ds(z, 1)], 10 + z, partner)
    extra = over_four(extra, extra_line, 14, z, line)
    line_in[z] = fourth[z]
    for k in range(1, 4):
        other = (z + k) % 4
        arrived(line_in.at[pl.ds(other, 1)], 10 + other)
    shard = (line_in[0] + line_in[1]) + (line_in[2] + line_in[3])

    lane = lax.broadcasted_iota(jnp.int32, (8, 128), 1)

    def packed(values):
        found = jnp.zeros((8, 128), jnp.float32)
        for k, value in enumerate(values):
            found = jnp.where(lane == k, value, found)
        return found

    def unpacked(found, k):
        return jnp.sum(jnp.where(lane[0:1] == k, found[0:1], 0.0))

    classes, row_inner, row_outer, row_head = sizes
    split = (0, row_inner, row_inner + row_outer, rows)
    widths = (hidden, hidden, classes)
    pieces = [shard[split[k] : split[k + 1], : widths[k]] for k in range(3)]
    weights = [ref[...] for ref in weight_refs]
    values = packed(
        [jnp.sum(shard * shard)] + [jnp.sum(weight * weight) for weight in weights]
    )
    values = over_twin(values, sums_twin.at[0], 18)
    values = over_four(values, sums_plane.at[0], 19, section, plane)
    values = over_four(values, sums_line.at[0], 23, z, line)
    bias_square = jnp.sum(extra[0:3] * extra[0:3])
    clip_norm = jnp.sqrt(jnp.full((1, 1), unpacked(values, 0) + bias_square, jnp.float32))
    factor = jnp.minimum(1.0, CLIP / clip_norm)
    parts = []
    for k in range(3):
        update = moments(weights[k], pieces[k] * factor, first_refs[k][...], second_refs[k][...])[2]
        parts.append(jnp.sum(update * update))
    updates = packed(parts)
    updates = over_twin(updates, sums_twin.at[1], 27)
    updates = over_four(updates, sums_plane.at[1], 28, section, plane)
    updates = over_four(updates, sums_line.at[1], 32, z, line)
    out_ref[0:rows, :] = shard
    out_ref[rows : rows + 8, :] = extra
    out_ref[rows + 8 : rows + 16, 0:128] = values
    out_ref[rows + 8 : rows + 16, 128:256] = updates
    for copy in copies:
        copy.wait_send()


def reduced(sizes, grads, extra, weights, firsts, seconds):
    blocks, rows, hidden = grads.shape
    vmem = pl.BlockSpec(memory_space=pltpu.VMEM)
    return pl.pallas_call(
        functools.partial(reduce_kernel, sizes),
        out_shape=jax.ShapeDtypeStruct((rows + 16, hidden), jnp.float32),
        in_specs=[vmem, vmem, (vmem,) * 3, (vmem,) * 3, (vmem,) * 3],
        out_specs=vmem,
        scratch_shapes=[
            pltpu.VMEM((16, rows, hidden), jnp.float32),
            pltpu.VMEM((16, rows, hidden), jnp.float32),
            pltpu.VMEM((4, rows, hidden), jnp.float32),
            pltpu.VMEM((4, 4, rows, hidden), jnp.float32),
            pltpu.VMEM((4, rows, hidden), jnp.float32),
            pltpu.VMEM((2, 8, hidden), jnp.float32),
            pltpu.VMEM((4, 8, hidden), jnp.float32),
            pltpu.VMEM((4, 8, hidden), jnp.float32),
            pltpu.VMEM((2, 2, 8, 128), jnp.float32),
            pltpu.VMEM((2, 4, 8, 128), jnp.float32),
            pltpu.VMEM((2, 4, 8, 128), jnp.float32),
            pltpu.SemaphoreType.DMA((36,)),
            pltpu.SemaphoreType.DMA((28,)),
        ],
        compiler_params=pltpu.CompilerParams(
            collective_id=1, has_side_effects=True, vmem_limit_bytes=16 * 2**20
        ),
    )(grads, extra, weights, firsts, seconds)


def final_kernel(
    sizes,
    sums_ref,
    weight_refs,
    first_refs,
    second_refs,
    smooth_refs,
    bias_ref,
    scalar_ref,
    norms_ref,
    new_refs,
    moment_refs,
    square_refs,
    average_refs,
    bias_out_ref,
):
    classes, row_inner, row_outer, row_head = sizes
    hidden = sums_ref.shape[1]
    rows = row_inner + row_outer + row_head
    split = (0, row_inner, row_inner + row_outer, rows)
    widths = (hidden, hidden, classes)
    lane = lax.broadcasted_iota(jnp.int32, (1, 128), 1)

    def number(k, start_at):
        found = sums_ref[rows + 8 : rows + 9, start_at : start_at + 128]
        return jnp.sum(jnp.where(lane == k, found, 0.0), keepdims=True)

    bias_grad = sums_ref[rows : rows + 3, :]
    bias_square = jnp.sum(jnp.sum(bias_grad * bias_grad, axis=1, keepdims=True), axis=0, keepdims=True)
    clip_norm = jnp.sqrt(number(0, 0) + bias_square)
    factor = jnp.minimum(1.0, CLIP / clip_norm)
    wide = lax.broadcasted_iota(jnp.int32, (8, 128), 1)
    deep = lax.broadcasted_iota(jnp.int32, (8, 128), 0)
    norms = jnp.zeros((8, 128), jnp.float32)
    for k in range(3):
        weight = weight_refs[k][...]
        gradient = sums_ref[split[k] : split[k + 1], 0 : widths[k]] * factor
        first, second, update = moments(weight, gradient, first_refs[k][...], second_refs[k][...])
        weight_norm, update_norm = jnp.sqrt(number(1 + k, 0)), jnp.sqrt(number(k, 128))
        fresh = weight - RATE * (weight_norm / update_norm) * update
        new_refs[k][...] = fresh
        moment_refs[k][...] = first
        square_refs[k][...] = second
        average_refs[k][...] = AVERAGE * smooth_refs[k][...] + (1.0 - AVERAGE) * fresh
        norms = jnp.where(jnp.logical_and(deep == k, wide == 0), weight_norm, norms)
        norms = jnp.where(jnp.logical_and(deep == k, wide == 1), update_norm, norms)
    norms_ref[...] = norms[0:3, 0:2]
    weight = bias_ref[0:3, :]
    first, second, update = moments(
        weight, bias_grad * factor, bias_ref[3:6, :], bias_ref[6:9, :]
    )
    column = lax.broadcasted_iota(jnp.int32, weight.shape, 1)
    row = lax.broadcasted_iota(jnp.int32, weight.shape, 0)
    update = jnp.where(jnp.logical_or(row < 2, column < classes), update, 0.0)
    ratio = jnp.sqrt(jnp.sum(weight * weight, axis=1, keepdims=True)) / jnp.sqrt(
        jnp.sum(update * update, axis=1, keepdims=True)
    )
    fresh = weight - RATE * ratio * update
    average = AVERAGE * bias_ref[9:12, :] + (1.0 - AVERAGE) * fresh
    for k, value in enumerate((fresh, first, second, average)):
        bias_out_ref[4 * k : 4 * k + 3, :] = value
    tail = sums_ref[rows + 3 : rows + 4, 0:128]
    scalar_ref[...] = jnp.where(wide == 0, tail, jnp.where(wide == 1, clip_norm, 0.0))


def finished(sizes, sums, weights, firsts, seconds, smooths, bias_rows):
    hidden = sums.shape[1]
    vmem = pl.BlockSpec(memory_space=pltpu.VMEM)
    like = [jax.ShapeDtypeStruct(weight.shape, jnp.float32) for weight in weights]
    return pl.pallas_call(
        functools.partial(final_kernel, sizes),
        out_shape=(
            jax.ShapeDtypeStruct((8, 128), jnp.float32),
            jax.ShapeDtypeStruct((3, 2), jnp.float32),
            like,
            like,
            like,
            like,
            jax.ShapeDtypeStruct((16, hidden), jnp.float32),
        ),
        in_specs=[vmem] + [(vmem,) * 3] * 4 + [vmem],
        out_specs=(vmem, vmem, [vmem] * 3, [vmem] * 3, [vmem] * 3, [vmem] * 3, vmem),
    )(sums, weights, firsts, seconds, smooths, bias_rows)


def on_slice_kernels(
    node_table, owner_ids, dest_count, fan_inner, hidden, classes, seed_count, fan_outer, mask_sizes, weight_rows
):
    parts, peers = lax.axis_size("section"), lax.axis_size("dp")
    return (
        parts == 4
        and peers == 8
        and peers * node_table.size * 2 <= VMEM_TABLE_LIMIT
        and node_table.shape[1] == 128
        and node_table.shape[0] % (64 * CHUNKS) == 0
        and peers * node_table.shape[0] <= 131072
        and owner_ids.shape[0] % 1024 == 0
        and owner_ids.shape[0] <= 32768
        and fan_inner == SLOT - 1
        and dest_count % (BLOCK * GROUP * SETS) == 0
        and dest_count % TILE == 0
        and hidden == 256
        and classes + 2 <= hidden
        and seed_count <= TILE
        and seed_count % 16 == 0
        and fan_outer + 2 <= SLOT
        and len(mask_sizes) == 2
        and mask_sizes[0] * mask_sizes[1] <= 65536
        and all(rows % 8 == 0 for rows in weight_rows)
        and sum(weight_rows) % 32 == 0
    )


def outer_product(left, right):
    return lax.dot_general(
        left, right, (((0,), (0,)), ((), ())), preferred_element_type=jnp.float32
    )


def against(left, right):
    return lax.dot_general(
        left, right, (((1,), (1,)), ((), ())), preferred_element_type=jnp.float32
    )


def silu_slope(before, grad_out):
    sigmoid = jax.nn.sigmoid(before)
    return (grad_out * sigmoid * (1.0 + before * (1.0 - sigmoid))).astype(jnp.bfloat16)


def moments(weight, gradient, first, second):
    first = BETA_ONE * first + (1.0 - BETA_ONE) * gradient
    second = BETA_TWO * second + (1.0 - BETA_TWO) * gradient * gradient
    update = (
        first / (1.0 - BETA_ONE**STEP) / (jnp.sqrt(second / (1.0 - BETA_TWO**STEP)) + EPSILON)
        + DECAY * weight
    )
    return (first, second, update)


def bias_ratio(weight, update, hidden):
    bounds = ((0, hidden), (hidden, 2 * hidden), (2 * hidden, weight.shape[0]))
    pieces = []
    for start_at, stop_at in bounds:
        weight_norm = jnp.sqrt(jnp.sum(weight[start_at:stop_at] ** 2))
        update_norm = jnp.sqrt(jnp.sum(update[start_at:stop_at] ** 2))
        pieces.append(jnp.zeros((stop_at - start_at,), jnp.float32) + weight_norm / update_norm)
    return jnp.concatenate(pieces)


def gathered_rows(node_table, owner_ids, row_ids):
    peer_count = lax.axis_size("dp")
    parts = lax.axis_size("section")
    table_rows = node_table.shape[0]
    if peer_count * node_table.size * 2 <= WHOLE_TABLE_LIMIT and table_rows % parts == 0:
        part_rows = table_rows // parts
        quarter = lax.dynamic_slice_in_dim(
            node_table, lax.axis_index("section") * part_rows, part_rows, 0
        )
        source = lax.all_gather(quarter, ("section", "dp"), axis=0, tiled=True)
        place = (row_ids // part_rows * peer_count + owner_ids) * part_rows + row_ids % part_rows
        return source, place
    frontier_rows = owner_ids.shape[0]
    slot_count = max(2, 2 * frontier_rows // peer_count)
    owner_hot = (owner_ids[:, None] == jnp.arange(peer_count)[None, :]).astype(jnp.int32)
    ranking = jnp.sum((jnp.cumsum(owner_hot, axis=0) - 1) * owner_hot, axis=1)
    placed = owner_ids * slot_count + ranking
    request = (
        jnp.zeros((peer_count * slot_count,), jnp.int32)
        .at[placed]
        .set(row_ids)
        .reshape(peer_count, slot_count)
    )
    returned = lax.all_to_all(
        node_table[lax.all_to_all(request, "dp", split_axis=0, concat_axis=0, tiled=True)],
        "dp",
        split_axis=0,
        concat_axis=0,
        tiled=True,
    )
    return returned.reshape(peer_count * slot_count, -1), placed


def on_device(
    node_table,
    owners,
    local_rows,
    inner_neighbours,
    inner_counts,
    outer_neighbours,
    outer_counts,
    labels,
    label_mask,
    weight_inner,
    weight_outer,
    weight_head,
    biases,
    first_inner,
    first_outer,
    first_head,
    first_biases,
    second_inner,
    second_outer,
    second_head,
    second_biases,
    smooth_inner,
    smooth_outer,
    smooth_head,
    smooth_biases,
):
    at = lax.axis_index("section")
    every = ("section", "dp")
    hidden = weight_inner.shape[1]
    dest_count, fan_inner = inner_neighbours.shape[1:]
    seed_count, fan_outer = outer_neighbours.shape[1:]
    classes = weight_head.shape[1]
    mask_sizes = label_mask.shape
    label_part = jnp.sum(label_mask.astype(jnp.float32))

    def mine(array):
        return lax.dynamic_index_in_dim(array, at, 0, keepdims=False)

    inner_neighbours, inner_counts = mine(inner_neighbours), mine(inner_counts)
    outer_neighbours, outer_counts = mine(outer_neighbours), mine(outer_counts)
    labels, label_mask = mine(labels), mine(label_mask)
    bias_inner = biases[:hidden]
    bias_outer = biases[hidden : 2 * hidden]
    bias_head = biases[2 * hidden :]

    owner_ids, row_ids = owners.reshape(-1), local_rows.reshape(-1)
    weights = (weight_inner, weight_outer, weight_head)
    keep = jnp.arange(fan_inner)[None, :] < inner_counts[:, None]
    if on_slice_kernels(
        node_table,
        owner_ids,
        dest_count,
        fan_inner,
        hidden,
        classes,
        seed_count,
        fan_outer,
        mask_sizes,
        [weight.shape[0] for weight in weights],
    ):
        devices, peers = lax.axis_size(every), lax.axis_size("dp")
        place = (owner_ids * node_table.shape[0] + row_ids).reshape(-1, 128).T
        own = jnp.arange(dest_count, dtype=jnp.int32)[:, None]
        near = jnp.concatenate([inner_neighbours, own], axis=1).reshape(-1, BLOCK * SLOT)
        live = jnp.concatenate([keep.astype(jnp.float32), jnp.ones(own.shape, jnp.float32)], axis=1)
        live = live.reshape(near.shape)
        tail = jnp.stack([label_part // 256, label_part % 256])
        tail = jnp.pad(tail[None], ((0, weight_head.shape[0] - 1), (0, hidden - classes - 2)))
        packed = jnp.concatenate(
            [weight_inner, weight_outer, jnp.concatenate([weight_head, tail], axis=1)], axis=0
        ).astype(jnp.bfloat16)
        table, everyone, idx, mix = spread(node_table, packed, place, near, live)
        firsts = (first_inner, first_outer, first_head)
        seconds = (second_inner, second_outer, second_head)
        smooths = (smooth_inner, smooth_outer, smooth_head)
        rows = [weight.shape[0] for weight in weights]

        def in_rows(*arrays):
            return jnp.concatenate(
                [jnp.pad(a, (0, 3 * hidden - a.shape[0])).reshape(3, hidden) for a in arrays]
            )

        bias_rows = in_rows(biases, first_biases, second_biases, smooth_biases)
        keep_outer = jnp.arange(fan_outer)[None, :] < outer_counts[:, None]
        seed_table = jnp.concatenate(
            [
                jnp.where(keep_outer, outer_neighbours, -1),
                labels[:, None],
                label_mask[:, None],
                jnp.zeros((seed_count, SLOT - fan_outer - 2), jnp.int32),
            ],
            axis=1,
        )
        joined_one = picked(idx, mix, table)
        grads, extra = dense(
            (classes, fan_outer, *rows), joined_one, everyone, bias_rows, seed_table
        )
        sums = reduced((classes, *rows), grads, extra, weights, firsts, seconds)
        scalars, norms, news, moment, square, average, bias_out = finished(
            (classes, *rows), sums, weights, firsts, seconds, smooths, bias_rows
        )
        bias_outs = [
            bias_out[4 * k : 4 * k + 3].reshape(-1)[: biases.shape[0]] for k in range(4)
        ]
        return (
            scalars[0, 0],
            extra[3, 1],
            scalars[1, 1],
            norms,
            *news,
            bias_outs[0],
            *moment,
            bias_outs[1],
            *square,
            bias_outs[2],
            *average,
            bias_outs[3],
        )

    label_count = jnp.maximum(lax.psum(label_part, "dp"), 1.0)
    full_inner, full_outer, full_head = (
        lax.all_gather(weight.astype(jnp.bfloat16), every, axis=0, tiled=True)
        for weight in weights
    )
    source, place = gathered_rows(node_table, owner_ids, row_ids)
    rows = source[place[inner_neighbours]]
    summed = jnp.sum(
        jnp.where(keep[:, :, None], rows, jnp.zeros((), rows.dtype)), axis=1, dtype=jnp.float32
    )
    self_rows = source[place[:dest_count]]
    mean_one = (summed / inner_counts[:, None].astype(jnp.float32)).astype(jnp.bfloat16)
    joined_one = jnp.concatenate([self_rows, mean_one], axis=1)
    pre_one = jnp.dot(joined_one, full_inner, preferred_element_type=jnp.float32) + bias_inner
    hidden_one = jax.nn.silu(pre_one).astype(jnp.bfloat16)

    keep_outer = jnp.arange(fan_outer)[None, :] < outer_counts[:, None]
    pick = jnp.sum(
        (
            jnp.where(keep_outer, outer_neighbours, -1)[:, :, None]
            == jnp.arange(dest_count)[None, None, :]
        ).astype(jnp.float32),
        axis=1,
    ).astype(jnp.bfloat16)
    count_two = outer_counts[:, None].astype(jnp.float32)
    mean_two = (jnp.dot(pick, hidden_one, preferred_element_type=jnp.float32) / count_two).astype(
        jnp.bfloat16
    )
    joined_two = jnp.concatenate([hidden_one[:seed_count], mean_two], axis=1)
    pre_two = jnp.dot(joined_two, full_outer, preferred_element_type=jnp.float32) + bias_outer
    hidden_two = jax.nn.silu(pre_two).astype(jnp.bfloat16)

    logits = jnp.dot(hidden_two, full_head, preferred_element_type=jnp.float32) + bias_head
    shifted = logits - jnp.max(logits, axis=1, keepdims=True)
    log_total = jnp.log(jnp.sum(jnp.exp(shifted), axis=1, keepdims=True))
    chosen = (jnp.arange(classes)[None, :] == labels[:, None]).astype(jnp.float32)
    row_weight = label_mask.astype(jnp.float32)
    loss_part = jnp.sum((log_total[:, 0] - jnp.sum(shifted * chosen, axis=1)) * row_weight)
    grad_logits = (
        (jnp.exp(shifted - log_total) - chosen) * (row_weight / label_count)[:, None]
    ).astype(jnp.bfloat16)
    grad_head = outer_product(hidden_two, grad_logits)
    grad_two = against(grad_logits, full_head).astype(jnp.bfloat16).astype(jnp.float32)
    grad_pre_two = silu_slope(pre_two, grad_two)
    grad_outer = outer_product(joined_two, grad_pre_two)
    grad_joined = against(grad_pre_two, full_outer)
    share = grad_joined[:, hidden:] / count_two
    share_high = share.astype(jnp.bfloat16)
    share_low = (share - share_high.astype(jnp.float32)).astype(jnp.bfloat16)
    grad_one = outer_product(pick, share_high) + outer_product(pick, share_low)
    grad_one = jnp.concatenate(
        [grad_one[:seed_count] + grad_joined[:, :hidden], grad_one[seed_count:]], axis=0
    )
    grad_one = grad_one.astype(jnp.bfloat16).astype(jnp.float32)
    grad_pre_one = silu_slope(pre_one, grad_one)
    grad_inner = outer_product(joined_one, grad_pre_one)
    bias_part = jnp.concatenate(
        [
            jnp.sum(part.astype(jnp.float32), axis=0)
            for part in (grad_pre_one, grad_pre_two, grad_logits)
        ]
    )

    devices = lax.axis_size(every)
    grads = jnp.concatenate(
        [grad.reshape(devices, -1) for grad in (grad_inner, grad_outer, grad_head)], axis=1
    )
    shard = lax.psum_scatter(grads, every, scatter_dimension=0, tiled=True).reshape(-1)
    shards = []
    for weight in weights:
        shards.append(shard[: weight.size].reshape(weight.shape))
        shard = shard[weight.size :]
    packed = lax.psum(jnp.concatenate([bias_part, loss_part[None]]), every)
    bias_grad, loss_sum = packed[:-1], packed[-1]
    grad_partial = sum((jnp.sum(part * part) for part in shards))
    weight_partial = [jnp.sum(weight * weight) for weight in weights]
    squares = lax.psum(jnp.stack([grad_partial] + weight_partial), every)
    clip_norm = jnp.sqrt(squares[0] + jnp.sum(bias_grad * bias_grad))
    factor = jnp.minimum(1.0, CLIP / clip_norm)
    firsts = (first_inner, first_outer, first_head)
    seconds = (second_inner, second_outer, second_head)
    smooths = (smooth_inner, smooth_outer, smooth_head)
    states = [
        moments(weights[slot_at], shards[slot_at] * factor, firsts[slot_at], seconds[slot_at])
        for slot_at in range(3)
    ]
    update_square = lax.psum(jnp.stack([jnp.sum(state[2] * state[2]) for state in states]), every)
    weight_norms = jnp.sqrt(squares[1:])
    update_norms = jnp.sqrt(update_square)
    news = [
        weights[slot_at]
        - RATE * (weight_norms[slot_at] / update_norms[slot_at]) * states[slot_at][2]
        for slot_at in range(3)
    ]
    averages = [
        AVERAGE * smooths[slot_at] + (1.0 - AVERAGE) * news[slot_at] for slot_at in range(3)
    ]
    bias_first, bias_second, bias_update = moments(
        biases, bias_grad * factor, first_biases, second_biases
    )
    bias_new = biases - RATE * bias_ratio(biases, bias_update, hidden) * bias_update
    bias_average = AVERAGE * smooth_biases + (1.0 - AVERAGE) * bias_new
    return (
        loss_sum,
        label_count,
        clip_norm,
        jnp.stack([weight_norms, update_norms], axis=1),
        news[0],
        news[1],
        news[2],
        bias_new,
        states[0][0],
        states[1][0],
        states[2][0],
        bias_first,
        states[0][1],
        states[1][1],
        states[2][1],
        bias_second,
        averages[0],
        averages[1],
        averages[2],
        bias_average,
    )


def solution(mesh):
    in_specs = (
        P("dp", None),
        P("section", "dp", None),
        P("section", "dp"),
        P(None, "dp", None),
        P(None, "dp"),
        P(None, "dp", None),
        P(None, "dp"),
        P(None, "dp"),
        P(None, "dp"),
        P(("section", "dp"), None),
        P(("section", "dp"), None),
        P(("section", "dp"), None),
        P(),
        P(("section", "dp"), None),
        P(("section", "dp"), None),
        P(("section", "dp"), None),
        P(),
        P(("section", "dp"), None),
        P(("section", "dp"), None),
        P(("section", "dp"), None),
        P(),
        P(("section", "dp"), None),
        P(("section", "dp"), None),
        P(("section", "dp"), None),
        P(),
    )
    out_specs = (
        P(),
        P(),
        P(),
        P(),
        P(("section", "dp"), None),
        P(("section", "dp"), None),
        P(("section", "dp"), None),
        P(),
        P(("section", "dp"), None),
        P(("section", "dp"), None),
        P(("section", "dp"), None),
        P(),
        P(("section", "dp"), None),
        P(("section", "dp"), None),
        P(("section", "dp"), None),
        P(),
        P(("section", "dp"), None),
        P(("section", "dp"), None),
        P(("section", "dp"), None),
        P(),
    )
    return jax.shard_map(
        on_device, mesh=mesh, in_specs=in_specs, out_specs=out_specs, check_vma=False
    )
```

```python
import functools

import jax
import jax.numpy as jnp
from jax import lax
from jax.experimental import pallas as pl
from jax.experimental.pallas import tpu as pltpu
from jax.sharding import PartitionSpec as P

STEP = 5


BETA_ONE = 0.9
BETA_TWO = 0.999
EPSILON = 1e-06
DECAY = 0.01
RATE = 0.25
CLIP = 0.05
AVERAGE = 0.9


VMEM_TABLE_LIMIT = 36 * 2**20
WHOLE_TABLE_LIMIT = 64 * 2**20
MESH = pl.DeviceIdType.MESH
SLOT = 16
BLOCK = 16
CHUNKS = 4
GROUP = 4
SETS = 4
SPARE = 8
SPARE_EARLY = False
TILE = 256


def gather_kernel(
    classes,
    fan_outer,
    table_ref,
    weight_refs,
    mask_ref,
    place_ref,
    near_ref,
    seed_ref,
    seed_across_ref,
    joined_ref,
    weights_ref,
    hits_ref,
    hits_back_ref,
    full_ref,
    packed,
    parts,
    idx_ref,
    mix_ref,
    wide,
    stages,
    lists,
    own_sem,
    z_sem,
    spare_sem,
    x_sem,
    y_sem,
    far_sem,
    twin_sem,
    twin_own_sem,
    double_sem,
    send_sem,
    double_send_sem,
    list_sem,
):
    section, at = lax.axis_index("section"), lax.axis_index("dp")
    z, core = at // 2, at % 2
    flipped = z // 2
    height = z + flipped * (3 - 2 * z)
    pairs = table_ref.shape[0]
    spare = pairs // SPARE
    quarter = (pairs - spare) // 4
    chunk = quarter // CHUNKS
    spare_chunk = spare // CHUNKS

    def level(value):
        return value + flipped * (3 - 2 * value)

    twin = (section, z * 2 + 1 - core)
    beside_x = (section + 1 - 2 * (section % 2), at)
    beside_y = (section + 2 - 4 * (section // 2), at)
    inner_z = (section, level(1 - height) * 2 + core)
    across_z = (section, level(2) * 2 + core)
    outer_z = (section, level(0) * 2 + core)
    skip_z = (section, ((z + 2) % 4) * 2 + core)
    sources = [level(1 - height), level(2), level(3)]
    crosses = height == 1

    barrier = pltpu.get_barrier_semaphore()
    for partner in (twin, beside_x, beside_y, inner_z, skip_z):
        pl.semaphore_signal(barrier, inc=1, device_id=partner, device_id_type=MESH)

    @pl.when(crosses)
    def greet_across():
        pl.semaphore_signal(barrier, inc=1, device_id=across_z, device_id_type=MESH)

    pl.semaphore_wait(barrier, 5 + height)

    sent = []

    def region(shard, part, piece):
        return full_ref.at[pl.ds(shard * pairs + part * quarter + piece * chunk, chunk)]

    def spare_region(shard, piece):
        return full_ref.at[pl.ds(shard * pairs + 4 * quarter + piece * spare_chunk, spare_chunk)]

    def send(source, target, recv, device, when=None):
        number = len(sent)
        copy = pltpu.make_async_remote_copy(
            src_ref=source,
            dst_ref=target,
            send_sem=send_sem.at[number],
            recv_sem=recv,
            device_id=device,
            device_id_type=MESH,
        )
        sent.append((copy, when))
        if when is None:
            copy.start()
        else:
            pl.when(when)(copy.start)
        return copy

    def arrived(target, recv):
        pltpu.make_async_copy(target, target, recv).wait()

    for piece in range(CHUNKS):
        block = table_ref.at[pl.ds(section * quarter + piece * chunk, chunk)]
        goal = region(at, section, piece)
        send(block, goal, z_sem.at[piece], inner_z)
        send(block, goal, z_sem.at[CHUNKS + piece], across_z, crosses)
        if SPARE_EARLY:
            block = table_ref.at[pl.ds(4 * quarter + piece * spare_chunk, spare_chunk)]
            goal = spare_region(at, piece)
            send(block, goal, spare_sem.at[piece], inner_z)
            send(block, goal, spare_sem.at[CHUNKS + piece], across_z, crosses)
    whole = full_ref.at[pl.ds(at * pairs, pairs)]
    own = pltpu.make_async_copy(table_ref, whole, own_sem)
    own.start()
    send(table_ref, whole, twin_own_sem, twin)

    inner_ref, outer_ref, head_ref = weight_refs
    row_inner, row_outer, row_head = (ref.shape[0] for ref in weight_refs)
    hidden = inner_ref.shape[1]
    head_at = row_inner + row_outer
    packed[0:row_inner, :] = inner_ref[...]
    packed[row_inner:head_at, :] = outer_ref[...]
    packed[head_at:, :] = jnp.zeros((row_head, hidden), jnp.float32)
    packed[head_at:, 0:classes] = head_ref[...]
    labelled = jnp.sum(mask_ref[...].astype(jnp.float32)).astype(jnp.int32)
    lane = lax.broadcasted_iota(jnp.int32, (1, hidden), 1)
    high_part = (labelled // 256).astype(jnp.float32)
    low_part = (labelled % 256).astype(jnp.float32)
    tail = jnp.where(lane == classes, high_part, jnp.where(lane == classes + 1, low_part, 0.0))
    packed[head_at : head_at + 1, :] += tail
    mine = (core * 4 + section) * 4 + z
    weights_ref[mine] = packed[...].astype(jnp.bfloat16)
    doubling = [(inner_z, 1), (skip_z, 2), (beside_x, 4), (beside_y, 8), (twin, 16)]
    doubled = []

    def double_start(number):
        device, size = doubling[number]
        block = weights_ref.at[pl.ds((mine // size) * size, size)]
        copy = pltpu.make_async_remote_copy(
            src_ref=block,
            dst_ref=block,
            send_sem=double_send_sem.at[number],
            recv_sem=double_sem.at[number],
            device_id=device,
            device_id_type=MESH,
        )
        copy.start()
        doubled.append(copy)

    double_start(0)

    placed = place_ref[...]
    pair_at = placed // 2
    high = place_ref.shape[1]
    parts[0:128, :] = (pair_at % 256).astype(jnp.float32).astype(jnp.bfloat16)
    parts[128:256, :] = (pair_at // 256).astype(jnp.float32).astype(jnp.bfloat16)
    parts[256:384, :] = (placed % 2).astype(jnp.float32).astype(jnp.bfloat16)
    looked_rows = near_ref.shape[0]
    seeds = seed_ref.shape[0]
    tiles = hits_ref.shape[1] // TILE
    total = 3 * CHUNKS
    steps = total + 2
    per_step = -(-looked_rows // (8 * steps)) * 8
    for j in range(fan_outer):
        wide[j] = jnp.broadcast_to(seed_ref[:, j : j + 1], (seeds, TILE))

    def look_up(first, last):
        def rows_of(block, carry):
            start_at = pl.multiple_of(block * 8, 8)
            sub = lax.broadcasted_iota(jnp.int32, (high, 256), 0)
            low_at = lax.broadcasted_iota(jnp.int32, (128, 256), 0)
            row = lax.broadcasted_iota(jnp.int32, (256, 512), 0)
            column = lax.broadcasted_iota(jnp.int32, (256, 512), 1)
            for k in range(8):
                node = near_ref[pl.ds(start_at + k, 1), :]
                hot = (sub == node // 128).astype(jnp.float32).astype(jnp.bfloat16)
                got = jnp.dot(parts[...], hot, preferred_element_type=jnp.float32)
                chosen = low_at == node % 128
                found = jnp.where(chosen, got[0:128] + 256.0 * got[128:256], 0.0)
                odd = jnp.where(chosen, got[256:384], 0.0)
                entry_at = jnp.sum(found, axis=0, keepdims=True).astype(jnp.int32)
                idx_ref[block * 2 + k // 4, k % 4 : k % 4 + 1, :] = jnp.clip(
                    entry_at, 0, full_ref.shape[0] - 1
                )
                mix_ref[pl.ds(start_at + k, 1), 0:256] = jnp.sum(odd, axis=0, keepdims=True)
            odd = mix_ref[pl.ds(start_at, 8), 0:256]
            live = (near_ref[pl.ds(start_at, 8), :] >= 0).astype(jnp.float32)
            mix_ref[pl.ds(start_at, 8), :] = jnp.dot(
                (live * (1.0 - odd)).astype(jnp.bfloat16),
                (column == 2 * row).astype(jnp.float32).astype(jnp.bfloat16),
                preferred_element_type=jnp.float32,
            ) + jnp.dot(
                (live * odd).astype(jnp.bfloat16),
                (column == 2 * row + 1).astype(jnp.float32).astype(jnp.bfloat16),
                preferred_element_type=jnp.float32,
            )
            return carry

        lax.fori_loop(first // 8, last // 8, rows_of, 0)

    def mark(tile):
        start_at = tile * TILE
        dest = lax.broadcasted_iota(jnp.int32, (seeds, TILE), 1) + start_at
        hits = jnp.zeros((seeds, TILE), jnp.float32)
        for j in range(fan_outer):
            hits = hits + (wide[j] == dest).astype(jnp.float32)
        hits_ref[:, start_at : start_at + TILE] = hits.astype(jnp.bfloat16)
        dest = lax.broadcasted_iota(jnp.int32, (TILE, seeds), 0) + start_at
        hits = jnp.zeros((TILE, seeds), jnp.float32)
        for j in range(fan_outer):
            hits = hits + (seed_across_ref[j : j + 1, :] == dest).astype(jnp.float32)
        hits_back_ref[start_at : start_at + TILE, :] = hits.astype(jnp.bfloat16)

    twins = []

    def to_twin(block, number):
        send(block, block, twin_sem.at[number], twin)
        twins.append(number)

    for step in range(steps):
        if step < total:
            turn, piece = divmod(step, CHUNKS)
            shard = sources[turn] * 2 + core
            goes, number = (across_z, 2 * CHUNKS + piece) if turn == 0 else (outer_z, step)
            block = region(shard, section, piece)
            arrived(block, z_sem.at[step])
            send(block, block, z_sem.at[number], goes, crosses)
            send(block, block, x_sem.at[step], beside_x)
            send(block, block, y_sem.at[step], beside_y)
            to_twin(block, step)
            if not SPARE_EARLY and turn == 0:
                block = table_ref.at[pl.ds(4 * quarter + piece * spare_chunk, spare_chunk)]
                goal = spare_region(at, piece)
                send(block, goal, spare_sem.at[piece], inner_z)
                send(block, goal, spare_sem.at[CHUNKS + piece], across_z, crosses)
        late = step - 1
        if 0 <= late < total:
            turn, piece = divmod(late, CHUNKS)
            shard = sources[turn] * 2 + core
            goes, number = (across_z, 2 * CHUNKS + piece) if turn == 0 else (outer_z, late)
            block = spare_region(shard, piece)
            arrived(block, spare_sem.at[late])
            send(block, block, spare_sem.at[number], goes, crosses)
            to_twin(block, 4 * total + late)
            block = region(shard, beside_x[0], piece)
            arrived(block, x_sem.at[late])
            if piece % 2 == 0:
                send(block, block, far_sem.at[late], beside_y)
            to_twin(block, total + late)
            block = region(shard, beside_y[0], piece)
            arrived(block, y_sem.at[late])
            if piece % 2 == 1:
                send(block, block, far_sem.at[late], beside_x)
            to_twin(block, 2 * total + late)
        later = step - 2
        if 0 <= later < total:
            turn, piece = divmod(later, CHUNKS)
            shard = sources[turn] * 2 + core
            block = region(shard, 3 - section, piece)
            arrived(block, far_sem.at[later])
            to_twin(block, 3 * total + later)
        if step % 2 == 0 and step // 2 < len(doubling):
            doubled[step // 2].wait()
            if step // 2 + 1 < len(doubling):
                double_start(step // 2 + 1)
        first = min(step * per_step, looked_rows)
        last = min(first + per_step, looked_rows)
        if last > first:
            look_up(first, last)
        for tile in range(step * tiles // steps, (step + 1) * tiles // steps):
            mark(tile)

    for number in sorted(twins):
        kind, step = divmod(number, total)
        turn, piece = divmod(step, CHUNKS)
        shard = sources[turn] * 2 + 1 - core
        if kind == 4:
            block = spare_region(shard, piece)
        else:
            block = region(shard, (section, beside_x[0], beside_y[0], 3 - section)[kind], piece)
        arrived(block, twin_sem.at[number])
    arrived(full_ref.at[pl.ds((z * 2 + 1 - core) * pairs, pairs)], twin_own_sem)
    own.wait()

    blocks = looked_rows
    lane = lax.broadcasted_iota(jnp.int32, (BLOCK, 2 * BLOCK * SLOT), 1)
    same = lane // (2 * SLOT) == lax.broadcasted_iota(jnp.int32, lane.shape, 0)
    near_part = jnp.logical_and(same, lane % (2 * SLOT) < 2 * SLOT - 2).astype(jnp.float32)
    self_part = jnp.logical_and(same, lane % (2 * SLOT) >= 2 * SLOT - 2).astype(jnp.float32)
    turns = blocks // GROUP

    def fetch(turn, slot):
        return pltpu.make_async_copy(
            idx_ref.at[jnp.minimum(turn, turns - 1)], lists[slot], list_sem.at[slot]
        )

    def pick(member, slot, stage):
        def unit(number, carry):
            entry = full_ref[lists[slot][member, number]]
            stage[pl.ds(2 * number, 2), :] = entry.astype(jnp.float32)
            return carry

        lax.fori_loop(0, BLOCK * SLOT, unit, 0, unroll=BLOCK * SLOT)

    def reduce(block, stage):
        mix = mix_ref[pl.ds(block, 1), :]
        near = mix * near_part
        left = jnp.concatenate([near, mix * self_part], axis=0).astype(jnp.bfloat16)
        out = jnp.dot(left, stage[...].astype(jnp.bfloat16), preferred_element_type=jnp.float32)
        count = jnp.maximum(jnp.sum(near, axis=1, keepdims=True), 1.0)
        both = jnp.concatenate([out[BLOCK:], out[:BLOCK] / count], axis=1)
        start_at = pl.multiple_of(block * BLOCK, BLOCK)
        joined_ref[pl.ds(start_at, BLOCK), :] = both.astype(jnp.bfloat16)

    near_stages, far_stages = stages
    for slot in range(SETS):
        fetch(slot, slot).start()
    for member in range(GROUP):
        far_stages[member][...] = jnp.zeros(far_stages[member].shape, jnp.float32)

    def round_of(number, carry):
        for slot in range(SETS):
            turn = number * SETS + slot
            fetch(turn, slot).wait()
            for member in range(GROUP):
                pick(member, slot, stages[slot % 2][member])
                reduce(
                    jnp.maximum((turn - 1) * GROUP + member, 0), stages[1 - slot % 2][member]
                )
            fetch(turn + SETS, slot).start()
        return carry

    lax.fori_loop(0, blocks // (GROUP * SETS), round_of, 0)
    for slot in range(SETS):
        fetch(0, slot).wait()
    for member in range(GROUP):
        reduce(blocks - GROUP + member, stages[(SETS - 1) % 2][member])
    for copy, when in sent:
        if when is None:
            copy.wait_send()
        else:
            pl.when(when)(copy.wait_send)


def gathered(classes, fan_outer, node_table, weights, label_mask, place, near, seed_table):
    devices = lax.axis_size(("section", "dp"))
    table_rows, width = node_table.shape
    frontier_high = place.shape[1]
    looked = near.shape[0]
    dest_count = looked * BLOCK
    seeds = seed_table.shape[0]
    hidden = weights[0].shape[1]
    rows = sum(weight.shape[0] for weight in weights)
    total = 3 * CHUNKS
    sends = 4 * CHUNKS + 1 + 3 * total + total + total + 5 * total
    vmem = pl.BlockSpec(memory_space=pltpu.VMEM)
    stage = (pltpu.VMEM((2 * BLOCK * SLOT, width), jnp.float32),) * GROUP
    return pl.pallas_call(
        functools.partial(gather_kernel, classes, fan_outer),
        out_shape=(
            jax.ShapeDtypeStruct((dest_count, 2 * width), jnp.bfloat16),
            jax.ShapeDtypeStruct((devices, rows, hidden), jnp.bfloat16),
            jax.ShapeDtypeStruct((seeds, dest_count), jnp.bfloat16),
            jax.ShapeDtypeStruct((dest_count, seeds), jnp.bfloat16),
        ),
        in_specs=[pl.BlockSpec(memory_space=pl.ANY), (vmem,) * 3] + [vmem] * 5,
        out_specs=(vmem,) * 4,
        scratch_shapes=[
            pltpu.VMEM((lax.axis_size("dp") * table_rows // 2, 2, width), jnp.bfloat16),
            pltpu.VMEM((rows, hidden), jnp.float32),
            pltpu.VMEM((384, frontier_high), jnp.bfloat16),
            pltpu.VMEM((looked // GROUP, GROUP, 256), jnp.int32),
            pltpu.VMEM((looked, 512), jnp.float32),
            pltpu.VMEM((fan_outer, seeds, TILE), jnp.int32),
            (stage, stage),
            (pltpu.SMEM((GROUP, BLOCK * SLOT), jnp.int32),) * SETS,
            pltpu.SemaphoreType.DMA(()),
            pltpu.SemaphoreType.DMA((total,)),
            pltpu.SemaphoreType.DMA((total,)),
            pltpu.SemaphoreType.DMA((total,)),
            pltpu.SemaphoreType.DMA((total,)),
            pltpu.SemaphoreType.DMA((total,)),
            pltpu.SemaphoreType.DMA((5 * total,)),
            pltpu.SemaphoreType.DMA(()),
            pltpu.SemaphoreType.DMA((5,)),
            pltpu.SemaphoreType.DMA((sends,)),
            pltpu.SemaphoreType.DMA((5,)),
            pltpu.SemaphoreType.DMA((SETS,)),
        ],
        compiler_params=pltpu.CompilerParams(
            collective_id=0, has_side_effects=True, vmem_limit_bytes=52 * 2**20
        ),
    )(
        pltpu.with_memory_space_constraint(
            node_table.reshape(table_rows // 2, 2, width), pltpu.HBM
        ),
        weights,
        label_mask,
        place,
        near,
        seed_table,
        seed_table.T,
    )


def block_order():
    return [(e % 2) * 16 + (e // 8) * 4 + (e % 8) // 2 for e in range(32)]


def dense_kernel(
    sizes,
    joined_ref,
    everyone_ref,
    hits_ref,
    hits_back_ref,
    bias_ref,
    seed_ref,
    grads_ref,
    extra_ref,
    first_pre,
    first_hidden,
    own_part,
    inner_sum,
):
    classes, fan_outer, row_inner, row_outer, row_head = sizes
    dest_count, hidden = joined_ref.shape
    tiles = dest_count // TILE
    order = block_order()
    weights = everyone_ref[...].astype(jnp.float32)
    split = (0, row_inner, row_inner + row_outer, row_inner + row_outer + row_head)
    full_inner, full_outer, full_head = (
        jnp.concatenate([weights[place, split[k] : split[k + 1]] for place in order], axis=0)
        for k in range(3)
    )
    lane = lax.broadcasted_iota(jnp.int32, (1, hidden), 1)
    tails = weights[0:4, split[2] : split[2] + 1] + weights[16:20, split[2] : split[2] + 1]
    tails = jnp.sum(tails.reshape(4, hidden), axis=0, keepdims=True)
    scale = jnp.where(lane == classes, 256.0, jnp.where(lane == classes + 1, 1.0, 0.0))
    label_count = jnp.maximum(jnp.sum(tails * scale), 1.0)
    full_inner = full_inner.astype(jnp.bfloat16)
    full_outer = full_outer.astype(jnp.bfloat16)
    full_head = jnp.where(lane < classes, full_head, 0.0).astype(jnp.bfloat16)
    bias_inner, bias_outer, bias_head = bias_rows_of(bias_ref, hidden)
    seeds = seed_ref.shape[0]
    kept = seed_ref[:, 0:fan_outer]
    count_two = jnp.sum((kept >= 0).astype(jnp.float32), axis=1, keepdims=True)

    def forward(tile, carry):
        start_at = pl.multiple_of(tile * TILE, TILE)
        rows = pl.ds(start_at, TILE)
        before = (
            jnp.dot(joined_ref[rows, :], full_inner, preferred_element_type=jnp.float32) + bias_inner
        )
        first_pre[rows, :] = before
        out = (before * lax.logistic(before)).astype(jnp.bfloat16)
        first_hidden[rows, :] = out
        return carry

    lax.fori_loop(0, tiles, forward, 0)
    mean_sum = jnp.dot(hits_ref[...], first_hidden[...], preferred_element_type=jnp.float32)
    mean_two = (mean_sum / count_two).astype(jnp.bfloat16)
    joined_two = jnp.concatenate([first_hidden[0:seeds, :], mean_two], axis=1)
    pre_two = jnp.dot(joined_two, full_outer, preferred_element_type=jnp.float32) + bias_outer
    gate_two = lax.logistic(pre_two)
    hidden_two = (pre_two * gate_two).astype(jnp.bfloat16)
    logits = jnp.dot(hidden_two, full_head, preferred_element_type=jnp.float32) + bias_head
    inside = lane < classes
    highest = jnp.max(jnp.where(inside, logits, -jnp.inf), axis=1, keepdims=True)
    shifted = jnp.where(inside, logits - highest, 0.0)
    total = jnp.sum(jnp.where(inside, jnp.exp(shifted), 0.0), axis=1, keepdims=True)
    log_total = jnp.log(total)
    chosen = (lane == seed_ref[:, fan_outer : fan_outer + 1]).astype(jnp.float32)
    row_weight = seed_ref[:, fan_outer + 1 : fan_outer + 2].astype(jnp.float32)
    loss = jnp.sum((log_total - jnp.sum(shifted * chosen, axis=1, keepdims=True)) * row_weight)
    grad_logits = (jnp.exp(shifted - log_total) - chosen) * (row_weight / label_count)
    grad_logits = jnp.where(inside, grad_logits, 0.0).astype(jnp.bfloat16)
    grad_head = outer_product(hidden_two, grad_logits)
    grad_two = against(grad_logits, full_head).astype(jnp.bfloat16).astype(jnp.float32)
    grad_pre_two = (grad_two * gate_two * (1.0 + pre_two * (1.0 - gate_two))).astype(jnp.bfloat16)
    grad_outer = outer_product(joined_two, grad_pre_two)
    grad_joined = against(grad_pre_two, full_outer)
    share = grad_joined[:, hidden:] / count_two
    share_high = share.astype(jnp.bfloat16)
    share_low = (share - share_high.astype(jnp.float32)).astype(jnp.bfloat16)
    for number, place in enumerate(order):
        grads_ref[place, split[1] : split[2], :] = grad_outer[
            number * row_outer : (number + 1) * row_outer
        ]
        grads_ref[place, split[2] : split[3], :] = grad_head[
            number * row_head : (number + 1) * row_head
        ]
    inner_sum[...] = jnp.zeros(inner_sum.shape, jnp.float32)
    share_parts = jnp.concatenate([share_high, share_low], axis=0)

    def backward(tile, bias_sum, own=None):
        start_at = pl.multiple_of(jnp.int32(tile) * TILE, TILE)
        rows = pl.ds(start_at, TILE)
        hits = hits_back_ref[rows, :]
        both_hits = jnp.concatenate([hits, hits], axis=1)
        grad_one = jnp.dot(both_hits, share_parts, preferred_element_type=jnp.float32)
        if own is not None:
            grad_one = grad_one + own
        grad_one = grad_one.astype(jnp.bfloat16).astype(jnp.float32)
        before = first_pre[rows, :]
        gate = lax.logistic(before)
        grad_pre = (grad_one * gate * (1.0 + before * (1.0 - gate))).astype(jnp.bfloat16)
        inner_sum[...] += outer_product(joined_ref[rows, :], grad_pre)
        return bias_sum + jnp.sum(grad_pre.astype(jnp.float32), axis=0, keepdims=True)

    own_part[...] = jnp.zeros(own_part.shape, jnp.float32)
    own_part[0:seeds, :] = grad_joined[:, 0:hidden]
    bias_sum = backward(0, jnp.zeros((1, hidden), jnp.float32), own_part[...])
    bias_sum = lax.fori_loop(1, tiles, backward, bias_sum)
    grad_inner = inner_sum[...]
    for number, place in enumerate(order):
        grads_ref[place, split[0] : split[1], :] = grad_inner[
            number * row_inner : (number + 1) * row_inner
        ]
    extra_ref[0:1, :] = bias_sum
    extra_ref[1:2, :] = jnp.sum(grad_pre_two.astype(jnp.float32), axis=0, keepdims=True)
    extra_ref[2:3, :] = jnp.sum(grad_logits.astype(jnp.float32), axis=0, keepdims=True)
    extra_ref[3:4, :] = jnp.where(lane == 0, loss, jnp.where(lane == 1, label_count, 0.0))
    extra_ref[4:8, :] = jnp.zeros((4, hidden), jnp.float32)


def bias_rows_of(ref, hidden):
    width = ref.shape[0] - 2 * hidden
    last = ref[pl.ds(2 * hidden, width)].reshape(1, width)
    return (
        ref[pl.ds(0, hidden)].reshape(1, hidden),
        ref[pl.ds(hidden, hidden)].reshape(1, hidden),
        jnp.concatenate([last, jnp.zeros((1, hidden - width), jnp.float32)], axis=1),
    )


def dense(sizes, joined, everyone, hits, hits_back, biases, seed_table):
    dest_count, hidden = joined.shape
    vmem = pl.BlockSpec(memory_space=pltpu.VMEM)
    return pl.pallas_call(
        functools.partial(dense_kernel, sizes),
        out_shape=(
            jax.ShapeDtypeStruct(everyone.shape, jnp.float32),
            jax.ShapeDtypeStruct((8, hidden), jnp.float32),
        ),
        in_specs=[vmem] * 6,
        out_specs=(vmem, vmem),
        scratch_shapes=[
            pltpu.VMEM((dest_count, hidden), jnp.float32),
            pltpu.VMEM((dest_count, hidden), jnp.bfloat16),
            pltpu.VMEM((TILE, hidden), jnp.float32),
            pltpu.VMEM((hidden, hidden), jnp.float32),
        ],
        compiler_params=pltpu.CompilerParams(vmem_limit_bytes=32 * 2**20),
    )(joined, everyone, hits, hits_back, biases, seed_table)


def reduce_kernel(
    sizes,
    grads_ref,
    extra_ref,
    weight_refs,
    first_refs,
    second_refs,
    out_ref,
    half,
    half_in,
    fourth,
    plane_in,
    line_in,
    extra_plane,
    extra_line,
    sums_plane,
    sums_line,
    recv_sem,
    send_sem,
):
    section, at = lax.axis_index("section"), lax.axis_index("dp")
    z, core = at // 2, at % 2
    rows, hidden = grads_ref.shape[1], grads_ref.shape[2]
    twin = (section, z * 2 + 1 - core)
    plane = [((section + k) % 4, at) for k in range(1, 4)]
    beyond = [((section + k) % 4, z * 2 + 1 - core) for k in range(1, 4)]
    line = [(section, ((z + k) % 4) * 2 + core) for k in range(1, 4)]
    barrier = pltpu.get_barrier_semaphore()
    for partner in [twin] + plane + beyond + line:
        pl.semaphore_signal(barrier, inc=1, device_id=partner, device_id_type=MESH)
    pl.semaphore_wait(barrier, 10)
    copies = []

    def send(source, target, number, device):
        copy = pltpu.make_async_remote_copy(
            src_ref=source,
            dst_ref=target,
            send_sem=send_sem.at[len(copies)],
            recv_sem=recv_sem.at[number],
            device_id=device,
            device_id_type=MESH,
        )
        copies.append(copy)
        copy.start()

    def arrived(target, number):
        pltpu.make_async_copy(target, target, recv_sem.at[number]).wait()

    def share(value, slots, base, me, partners):
        slots[me] = value
        for partner in partners:
            send(slots.at[me], slots.at[me], base + me, partner)

    def collect(slots, base, me):
        count = slots.shape[0]
        for k in range(1, count):
            other = (me + k) % count
            arrived(slots.at[other], base + other)
        values = [slots[k] for k in range(count)]
        while len(values) > 1:
            values = [values[k] + values[k + 1] for k in range(0, len(values), 2)]
        return values[0]

    place = section * 2 + core
    neighbours = [twin] + plane + beyond

    send(grads_ref.at[pl.ds((1 - core) * 16, 16)], half_in, 0, twin)
    share(extra_ref[...], extra_plane, 9, place, neighbours)
    arrived(half_in, 0)
    half[...] = grads_ref[pl.ds(core * 16, 16)] + half_in[...]
    for partner in plane:
        send(half.at[pl.ds(partner[0] * 4, 4)], plane_in.at[section], 1 + section, partner)
    share(collect(extra_plane, 9, place), extra_line, 17, z, line)
    plane_in[section] = half[pl.ds(section * 4, 4)]
    for k in range(1, 4):
        other = (section + k) % 4
        arrived(plane_in.at[other], 1 + other)
    fourth[...] = (plane_in[0] + plane_in[1]) + (plane_in[2] + plane_in[3])
    for k, partner in enumerate(line):
        send(fourth.at[pl.ds((z + k + 1) % 4, 1)], line_in.at[pl.ds(z, 1)], 5 + z, partner)
    line_in[z] = fourth[z]
    extra = collect(extra_line, 17, z)
    for k in range(1, 4):
        other = (z + k) % 4
        arrived(line_in.at[pl.ds(other, 1)], 5 + other)
    shard = (line_in[0] + line_in[1]) + (line_in[2] + line_in[3])

    lane = lax.broadcasted_iota(jnp.int32, (8, 128), 1)

    def packed(values):
        found = jnp.zeros((8, 128), jnp.float32)
        for k, value in enumerate(values):
            found = jnp.where(lane == k, value, found)
        return found

    def unpacked(found, k):
        return jnp.sum(jnp.where(lane[0:1] == k, found[0:1], 0.0))

    classes, row_inner, row_outer, row_head = sizes
    split = (0, row_inner, row_inner + row_outer, rows)
    widths = (hidden, hidden, classes)
    pieces = [shard[split[k] : split[k + 1], : widths[k]] for k in range(3)]
    weights = [ref[...] for ref in weight_refs]
    values = packed(
        [jnp.sum(shard * shard)] + [jnp.sum(weight * weight) for weight in weights]
    )
    share(values, sums_plane.at[0], 21, place, neighbours)
    share(collect(sums_plane.at[0], 21, place), sums_line.at[0], 29, z, line)
    values = collect(sums_line.at[0], 29, z)
    bias_square = jnp.sum(extra[0:3] * extra[0:3])
    clip_norm = jnp.sqrt(jnp.full((1, 1), unpacked(values, 0) + bias_square, jnp.float32))
    factor = jnp.minimum(1.0, CLIP / clip_norm)
    parts = []
    for k in range(3):
        update = moments(weights[k], pieces[k] * factor, first_refs[k][...], second_refs[k][...])[2]
        parts.append(jnp.sum(update * update))
    updates = packed(parts)
    share(updates, sums_plane.at[1], 33, place, neighbours)
    share(collect(sums_plane.at[1], 33, place), sums_line.at[1], 41, z, line)
    updates = collect(sums_line.at[1], 41, z)
    out_ref[0:rows, :] = shard
    out_ref[rows : rows + 8, :] = extra
    out_ref[rows + 8 : rows + 16, 0:128] = values
    out_ref[rows + 8 : rows + 16, 128:256] = updates
    for copy in copies:
        copy.wait_send()


def reduced(sizes, grads, extra, weights, firsts, seconds):
    blocks, rows, hidden = grads.shape
    vmem = pl.BlockSpec(memory_space=pltpu.VMEM)
    return pl.pallas_call(
        functools.partial(reduce_kernel, sizes),
        out_shape=jax.ShapeDtypeStruct((rows + 16, hidden), jnp.float32),
        in_specs=[vmem, vmem, (vmem,) * 3, (vmem,) * 3, (vmem,) * 3],
        out_specs=vmem,
        scratch_shapes=[
            pltpu.VMEM((16, rows, hidden), jnp.float32),
            pltpu.VMEM((16, rows, hidden), jnp.float32),
            pltpu.VMEM((4, rows, hidden), jnp.float32),
            pltpu.VMEM((4, 4, rows, hidden), jnp.float32),
            pltpu.VMEM((4, rows, hidden), jnp.float32),
            pltpu.VMEM((8, 8, hidden), jnp.float32),
            pltpu.VMEM((4, 8, hidden), jnp.float32),
            pltpu.VMEM((2, 8, 8, 128), jnp.float32),
            pltpu.VMEM((2, 4, 8, 128), jnp.float32),
            pltpu.SemaphoreType.DMA((45,)),
            pltpu.SemaphoreType.DMA((37,)),
        ],
        compiler_params=pltpu.CompilerParams(
            collective_id=1, has_side_effects=True, vmem_limit_bytes=16 * 2**20
        ),
    )(grads, extra, weights, firsts, seconds)


def final_kernel(
    sizes,
    devices,
    sums_ref,
    weight_refs,
    first_refs,
    second_refs,
    smooth_refs,
    bias_refs,
    loss_ref,
    count_ref,
    clip_ref,
    norms_ref,
    new_refs,
    moment_refs,
    square_refs,
    average_refs,
    bias_out_refs,
):
    classes, row_inner, row_outer, row_head = sizes
    hidden = sums_ref.shape[1]
    rows = row_inner + row_outer + row_head
    split = (0, row_inner, row_inner + row_outer, rows)
    widths = (hidden, hidden, classes)
    lane = lax.broadcasted_iota(jnp.int32, (1, 128), 1)

    def number(k, start_at):
        found = sums_ref[rows + 8 : rows + 9, start_at : start_at + 128]
        return jnp.sum(jnp.where(lane == k, found, 0.0), axis=1, keepdims=True)

    bias_grad = sums_ref[rows : rows + 3, :]
    bias_square = jnp.sum(jnp.sum(bias_grad * bias_grad, axis=1, keepdims=True), axis=0, keepdims=True)
    clip_norm = jnp.sqrt(number(0, 0) + bias_square)
    factor = jnp.minimum(1.0, CLIP / clip_norm)
    wide = lax.broadcasted_iota(jnp.int32, (8, 128), 1)
    deep = lax.broadcasted_iota(jnp.int32, (8, 128), 0)
    norms = jnp.zeros((8, 128), jnp.float32)
    for k in range(3):
        weight = weight_refs[k][...]
        gradient = sums_ref[split[k] : split[k + 1], 0 : widths[k]] * factor
        first, second, update = moments(weight, gradient, first_refs[k][...], second_refs[k][...])
        weight_norm, update_norm = jnp.sqrt(number(1 + k, 0)), jnp.sqrt(number(k, 128))
        fresh = weight - RATE * (weight_norm / update_norm) * update
        new_refs[k][...] = fresh
        moment_refs[k][...] = first
        square_refs[k][...] = second
        average_refs[k][...] = AVERAGE * smooth_refs[k][...] + (1.0 - AVERAGE) * fresh
        norms = jnp.where(jnp.logical_and(deep == k, wide == 0), weight_norm, norms)
        norms = jnp.where(jnp.logical_and(deep == k, wide == 1), update_norm, norms)
    norms_ref[...] = norms[0:3, 0:2]
    weight, first, second, smooth = (
        jnp.concatenate(bias_rows_of(ref, hidden), axis=0) for ref in bias_refs
    )
    first, second, update = moments(weight, bias_grad * factor, first, second)
    column = lax.broadcasted_iota(jnp.int32, weight.shape, 1)
    row = lax.broadcasted_iota(jnp.int32, weight.shape, 0)
    update = jnp.where(jnp.logical_or(row < 2, column < classes), update, 0.0)
    ratio = jnp.sqrt(jnp.sum(weight * weight, axis=1, keepdims=True)) / jnp.sqrt(
        jnp.sum(update * update, axis=1, keepdims=True)
    )
    fresh = weight - RATE * ratio * update
    average = AVERAGE * smooth + (1.0 - AVERAGE) * fresh
    for ref, value in zip(bias_out_refs, (fresh, first, second, average)):
        ref[pl.ds(0, hidden)] = value[0:1].reshape(hidden)
        ref[pl.ds(hidden, hidden)] = value[1:2].reshape(hidden)
        ref[pl.ds(2 * hidden, classes)] = value[2:3, 0:classes].reshape(classes)
    tail = sums_ref[rows + 3 : rows + 4, 0:128]
    loss_ref[...] = jnp.sum(jnp.where(lane == 0, tail, 0.0), axis=1, keepdims=True)
    count = jnp.sum(jnp.where(lane == 1, tail, 0.0), axis=1, keepdims=True)
    count_ref[...] = count / devices
    clip_ref[...] = clip_norm


def finished(sizes, sums, weights, firsts, seconds, smooths, biases):
    vmem = pl.BlockSpec(memory_space=pltpu.VMEM)
    like = [jax.ShapeDtypeStruct(weight.shape, jnp.float32) for weight in weights]
    scalar = jax.ShapeDtypeStruct((1, 1), jnp.float32)
    return pl.pallas_call(
        functools.partial(final_kernel, sizes, float(lax.axis_size(("section", "dp")))),
        out_shape=(
            scalar,
            scalar,
            scalar,
            jax.ShapeDtypeStruct((3, 2), jnp.float32),
            like,
            like,
            like,
            like,
            [jax.ShapeDtypeStruct(biases[0].shape, jnp.float32)] * 4,
        ),
        in_specs=[vmem] + [(vmem,) * 3] * 4 + [(vmem,) * 4],
        out_specs=(vmem,) * 4 + ([vmem] * 3,) * 4 + ([vmem] * 4,),
    )(sums, weights, firsts, seconds, smooths, biases)


def on_slice_kernels(
    node_table, owner_ids, dest_count, fan_inner, hidden, classes, seed_count, fan_outer, mask_sizes, weight_rows
):
    parts, peers = lax.axis_size("section"), lax.axis_size("dp")
    return (
        parts == 4
        and peers == 8
        and peers * node_table.size * 2 <= VMEM_TABLE_LIMIT
        and node_table.shape[1] == 128
        and node_table.shape[0] % (2 * SPARE * CHUNKS) == 0
        and (node_table.shape[0] // 2 - node_table.shape[0] // 2 // SPARE) % (4 * CHUNKS) == 0
        and peers * node_table.shape[0] <= 131072
        and owner_ids.shape[0] % 1024 == 0
        and owner_ids.shape[0] <= 32768
        and fan_inner == SLOT - 1
        and dest_count % (BLOCK * GROUP * SETS) == 0
        and dest_count % TILE == 0
        and hidden == 256
        and classes + 2 <= hidden
        and seed_count <= TILE
        and seed_count % 16 == 0
        and fan_outer + 2 <= SLOT
        and len(mask_sizes) == 2
        and mask_sizes[0] * mask_sizes[1] <= 65536
        and all(rows % 8 == 0 for rows in weight_rows)
        and sum(weight_rows) % 32 == 0
    )


def outer_product(left, right):
    return lax.dot_general(
        left, right, (((0,), (0,)), ((), ())), preferred_element_type=jnp.float32
    )


def against(left, right):
    return lax.dot_general(
        left, right, (((1,), (1,)), ((), ())), preferred_element_type=jnp.float32
    )


def silu_slope(before, grad_out):
    sigmoid = jax.nn.sigmoid(before)
    return (grad_out * sigmoid * (1.0 + before * (1.0 - sigmoid))).astype(jnp.bfloat16)


def moments(weight, gradient, first, second):
    first = BETA_ONE * first + (1.0 - BETA_ONE) * gradient
    second = BETA_TWO * second + (1.0 - BETA_TWO) * gradient * gradient
    update = (
        first / (1.0 - BETA_ONE**STEP) / (jnp.sqrt(second / (1.0 - BETA_TWO**STEP)) + EPSILON)
        + DECAY * weight
    )
    return (first, second, update)


def bias_ratio(weight, update, hidden):
    bounds = ((0, hidden), (hidden, 2 * hidden), (2 * hidden, weight.shape[0]))
    pieces = []
    for start_at, stop_at in bounds:
        weight_norm = jnp.sqrt(jnp.sum(weight[start_at:stop_at] ** 2))
        update_norm = jnp.sqrt(jnp.sum(update[start_at:stop_at] ** 2))
        pieces.append(jnp.zeros((stop_at - start_at,), jnp.float32) + weight_norm / update_norm)
    return jnp.concatenate(pieces)


def gathered_rows(node_table, owner_ids, row_ids):
    peer_count = lax.axis_size("dp")
    parts = lax.axis_size("section")
    table_rows = node_table.shape[0]
    if peer_count * node_table.size * 2 <= WHOLE_TABLE_LIMIT and table_rows % parts == 0:
        part_rows = table_rows // parts
        quarter = lax.dynamic_slice_in_dim(
            node_table, lax.axis_index("section") * part_rows, part_rows, 0
        )
        source = lax.all_gather(quarter, ("section", "dp"), axis=0, tiled=True)
        place = (row_ids // part_rows * peer_count + owner_ids) * part_rows + row_ids % part_rows
        return source, place
    frontier_rows = owner_ids.shape[0]
    slot_count = max(2, 2 * frontier_rows // peer_count)
    owner_hot = (owner_ids[:, None] == jnp.arange(peer_count)[None, :]).astype(jnp.int32)
    ranking = jnp.sum((jnp.cumsum(owner_hot, axis=0) - 1) * owner_hot, axis=1)
    placed = owner_ids * slot_count + ranking
    request = (
        jnp.zeros((peer_count * slot_count,), jnp.int32)
        .at[placed]
        .set(row_ids)
        .reshape(peer_count, slot_count)
    )
    returned = lax.all_to_all(
        node_table[lax.all_to_all(request, "dp", split_axis=0, concat_axis=0, tiled=True)],
        "dp",
        split_axis=0,
        concat_axis=0,
        tiled=True,
    )
    return returned.reshape(peer_count * slot_count, -1), placed


def on_device(
    node_table,
    owners,
    local_rows,
    inner_neighbours,
    inner_counts,
    outer_neighbours,
    outer_counts,
    labels,
    label_mask,
    weight_inner,
    weight_outer,
    weight_head,
    biases,
    first_inner,
    first_outer,
    first_head,
    first_biases,
    second_inner,
    second_outer,
    second_head,
    second_biases,
    smooth_inner,
    smooth_outer,
    smooth_head,
    smooth_biases,
):
    at = lax.axis_index("section")
    every = ("section", "dp")
    hidden = weight_inner.shape[1]
    dest_count, fan_inner = inner_neighbours.shape[1:]
    seed_count, fan_outer = outer_neighbours.shape[1:]
    classes = weight_head.shape[1]
    whole_mask = label_mask
    mask_sizes = label_mask.shape

    def mine(array):
        return lax.dynamic_index_in_dim(array, at, 0, keepdims=False)

    inner_neighbours, inner_counts = mine(inner_neighbours), mine(inner_counts)
    outer_neighbours, outer_counts = mine(outer_neighbours), mine(outer_counts)
    labels, label_mask = mine(labels), mine(label_mask)
    bias_inner = biases[:hidden]
    bias_outer = biases[hidden : 2 * hidden]
    bias_head = biases[2 * hidden :]

    owner_ids, row_ids = owners.reshape(-1), local_rows.reshape(-1)
    weights = (weight_inner, weight_outer, weight_head)
    keep = jnp.arange(fan_inner)[None, :] < inner_counts[:, None]
    if on_slice_kernels(
        node_table,
        owner_ids,
        dest_count,
        fan_inner,
        hidden,
        classes,
        seed_count,
        fan_outer,
        mask_sizes,
        [weight.shape[0] for weight in weights],
    ):
        place = (owner_ids * node_table.shape[0] + row_ids).reshape(-1, 128).T
        own = jnp.arange(dest_count, dtype=jnp.int32)[:, None]
        near = jnp.concatenate([jnp.where(keep, inner_neighbours, -1), own], axis=1)
        near = near.reshape(-1, BLOCK * SLOT)
        firsts = (first_inner, first_outer, first_head)
        seconds = (second_inner, second_outer, second_head)
        smooths = (smooth_inner, smooth_outer, smooth_head)
        rows = [weight.shape[0] for weight in weights]
        keep_outer = jnp.arange(fan_outer)[None, :] < outer_counts[:, None]
        seed_table = jnp.concatenate(
            [
                jnp.where(keep_outer, outer_neighbours, -1),
                labels[:, None],
                label_mask[:, None],
                jnp.zeros((seed_count, SLOT - fan_outer - 2), jnp.int32),
            ],
            axis=1,
        )
        joined_one, everyone, hits, hits_back = gathered(
            classes, fan_outer, node_table, weights, whole_mask, place, near, seed_table
        )
        grads, extra = dense(
            (classes, fan_outer, *rows), joined_one, everyone, hits, hits_back, biases, seed_table
        )
        sums = reduced((classes, *rows), grads, extra, weights, firsts, seconds)
        loss, count, clip, norms, news, moment, square, average, bias_outs = finished(
            (classes, *rows),
            sums,
            weights,
            firsts,
            seconds,
            smooths,
            (biases, first_biases, second_biases, smooth_biases),
        )
        return (
            loss.reshape(()),
            count.reshape(()),
            clip.reshape(()),
            norms,
            *news,
            bias_outs[0],
            *moment,
            bias_outs[1],
            *square,
            bias_outs[2],
            *average,
            bias_outs[3],
        )

    label_part = jnp.sum(whole_mask.astype(jnp.float32))
    label_count = jnp.maximum(lax.psum(label_part, "dp"), 1.0)
    full_inner, full_outer, full_head = (
        lax.all_gather(weight.astype(jnp.bfloat16), every, axis=0, tiled=True)
        for weight in weights
    )
    source, place = gathered_rows(node_table, owner_ids, row_ids)
    rows = source[place[inner_neighbours]]
    summed = jnp.sum(
        jnp.where(keep[:, :, None], rows, jnp.zeros((), rows.dtype)), axis=1, dtype=jnp.float32
    )
    self_rows = source[place[:dest_count]]
    mean_one = (summed / inner_counts[:, None].astype(jnp.float32)).astype(jnp.bfloat16)
    joined_one = jnp.concatenate([self_rows, mean_one], axis=1)
    pre_one = jnp.dot(joined_one, full_inner, preferred_element_type=jnp.float32) + bias_inner
    hidden_one = jax.nn.silu(pre_one).astype(jnp.bfloat16)

    keep_outer = jnp.arange(fan_outer)[None, :] < outer_counts[:, None]
    pick = jnp.sum(
        (
            jnp.where(keep_outer, outer_neighbours, -1)[:, :, None]
            == jnp.arange(dest_count)[None, None, :]
        ).astype(jnp.float32),
        axis=1,
    ).astype(jnp.bfloat16)
    count_two = outer_counts[:, None].astype(jnp.float32)
    mean_two = (jnp.dot(pick, hidden_one, preferred_element_type=jnp.float32) / count_two).astype(
        jnp.bfloat16
    )
    joined_two = jnp.concatenate([hidden_one[:seed_count], mean_two], axis=1)
    pre_two = jnp.dot(joined_two, full_outer, preferred_element_type=jnp.float32) + bias_outer
    hidden_two = jax.nn.silu(pre_two).astype(jnp.bfloat16)

    logits = jnp.dot(hidden_two, full_head, preferred_element_type=jnp.float32) + bias_head
    shifted = logits - jnp.max(logits, axis=1, keepdims=True)
    log_total = jnp.log(jnp.sum(jnp.exp(shifted), axis=1, keepdims=True))
    chosen = (jnp.arange(classes)[None, :] == labels[:, None]).astype(jnp.float32)
    row_weight = label_mask.astype(jnp.float32)
    loss_part = jnp.sum((log_total[:, 0] - jnp.sum(shifted * chosen, axis=1)) * row_weight)
    grad_logits = (
        (jnp.exp(shifted - log_total) - chosen) * (row_weight / label_count)[:, None]
    ).astype(jnp.bfloat16)
    grad_head = outer_product(hidden_two, grad_logits)
    grad_two = against(grad_logits, full_head).astype(jnp.bfloat16).astype(jnp.float32)
    grad_pre_two = silu_slope(pre_two, grad_two)
    grad_outer = outer_product(joined_two, grad_pre_two)
    grad_joined = against(grad_pre_two, full_outer)
    share = grad_joined[:, hidden:] / count_two
    share_high = share.astype(jnp.bfloat16)
    share_low = (share - share_high.astype(jnp.float32)).astype(jnp.bfloat16)
    grad_one = outer_product(pick, share_high) + outer_product(pick, share_low)
    grad_one = jnp.concatenate(
        [grad_one[:seed_count] + grad_joined[:, :hidden], grad_one[seed_count:]], axis=0
    )
    grad_one = grad_one.astype(jnp.bfloat16).astype(jnp.float32)
    grad_pre_one = silu_slope(pre_one, grad_one)
    grad_inner = outer_product(joined_one, grad_pre_one)
    bias_part = jnp.concatenate(
        [
            jnp.sum(part.astype(jnp.float32), axis=0)
            for part in (grad_pre_one, grad_pre_two, grad_logits)
        ]
    )

    devices = lax.axis_size(every)
    grads = jnp.concatenate(
        [grad.reshape(devices, -1) for grad in (grad_inner, grad_outer, grad_head)], axis=1
    )
    shard = lax.psum_scatter(grads, every, scatter_dimension=0, tiled=True).reshape(-1)
    shards = []
    for weight in weights:
        shards.append(shard[: weight.size].reshape(weight.shape))
        shard = shard[weight.size :]
    packed = lax.psum(jnp.concatenate([bias_part, loss_part[None]]), every)
    bias_grad, loss_sum = packed[:-1], packed[-1]
    grad_partial = sum((jnp.sum(part * part) for part in shards))
    weight_partial = [jnp.sum(weight * weight) for weight in weights]
    squares = lax.psum(jnp.stack([grad_partial] + weight_partial), every)
    clip_norm = jnp.sqrt(squares[0] + jnp.sum(bias_grad * bias_grad))
    factor = jnp.minimum(1.0, CLIP / clip_norm)
    firsts = (first_inner, first_outer, first_head)
    seconds = (second_inner, second_outer, second_head)
    smooths = (smooth_inner, smooth_outer, smooth_head)
    states = [
        moments(weights[slot_at], shards[slot_at] * factor, firsts[slot_at], seconds[slot_at])
        for slot_at in range(3)
    ]
    update_square = lax.psum(jnp.stack([jnp.sum(state[2] * state[2]) for state in states]), every)
    weight_norms = jnp.sqrt(squares[1:])
    update_norms = jnp.sqrt(update_square)
    news = [
        weights[slot_at]
        - RATE * (weight_norms[slot_at] / update_norms[slot_at]) * states[slot_at][2]
        for slot_at in range(3)
    ]
    averages = [
        AVERAGE * smooths[slot_at] + (1.0 - AVERAGE) * news[slot_at] for slot_at in range(3)
    ]
    bias_first, bias_second, bias_update = moments(
        biases, bias_grad * factor, first_biases, second_biases
    )
    bias_new = biases - RATE * bias_ratio(biases, bias_update, hidden) * bias_update
    bias_average = AVERAGE * smooth_biases + (1.0 - AVERAGE) * bias_new
    return (
        loss_sum,
        label_count,
        clip_norm,
        jnp.stack([weight_norms, update_norms], axis=1),
        news[0],
        news[1],
        news[2],
        bias_new,
        states[0][0],
        states[1][0],
        states[2][0],
        bias_first,
        states[0][1],
        states[1][1],
        states[2][1],
        bias_second,
        averages[0],
        averages[1],
        averages[2],
        bias_average,
    )


def solution(mesh):
    in_specs = (
        P("dp", None),
        P("section", "dp", None),
        P("section", "dp"),
        P(None, "dp", None),
        P(None, "dp"),
        P(None, "dp", None),
        P(None, "dp"),
        P(None, "dp"),
        P(None, "dp"),
        P(("section", "dp"), None),
        P(("section", "dp"), None),
        P(("section", "dp"), None),
        P(),
        P(("section", "dp"), None),
        P(("section", "dp"), None),
        P(("section", "dp"), None),
        P(),
        P(("section", "dp"), None),
        P(("section", "dp"), None),
        P(("section", "dp"), None),
        P(),
        P(("section", "dp"), None),
        P(("section", "dp"), None),
        P(("section", "dp"), None),
        P(),
    )
    out_specs = (
        P(),
        P(),
        P(),
        P(),
        P(("section", "dp"), None),
        P(("section", "dp"), None),
        P(("section", "dp"), None),
        P(),
        P(("section", "dp"), None),
        P(("section", "dp"), None),
        P(("section", "dp"), None),
        P(),
        P(("section", "dp"), None),
        P(("section", "dp"), None),
        P(("section", "dp"), None),
        P(),
        P(("section", "dp"), None),
        P(("section", "dp"), None),
        P(("section", "dp"), None),
        P(),
    )
    return jax.shard_map(
        on_device, mesh=mesh, in_specs=in_specs, out_specs=out_specs, check_vma=False
    )
```

```python
import functools

import jax
import jax.numpy as jnp
from jax import lax
from jax.experimental import pallas as pl
from jax.experimental.pallas import tpu as pltpu
from jax.sharding import PartitionSpec as P

STEP = 5


BETA_ONE = 0.9
BETA_TWO = 0.999
EPSILON = 1e-06
DECAY = 0.01
RATE = 0.25
CLIP = 0.05
AVERAGE = 0.9


VMEM_TABLE_LIMIT = 36 * 2**20
WHOLE_TABLE_LIMIT = 64 * 2**20
MESH = pl.DeviceIdType.MESH
SLOT = 16
BLOCK = 16
CHUNKS = 4
GROUP = 4
SETS = 4
SPARE = 8
AHEAD = 2
AHEAD_ACROSS = 1
LAG = 1
FAR_LAG = 2
SPARE_AFTER = 2
SPARE_LAG = 3
TILE = 256
PAUSE = 6


class Parts:
    def __init__(self, refs, base):
        self.grads, self.half_in, self.half, self.plane_in, self.fourth, self.line_in = refs
        self.base = base


def step_kernel(
    fan_outer,
    table_ref,
    weight_refs,
    first_refs,
    second_refs,
    bias_ref,
    mask_ref,
    place_ref,
    near_ref,
    seed_ref,
    seed_across_ref,
    out_ref,
    joined_ref,
    weights_ref,
    hits_ref,
    hits_back_ref,
    full_ref,
    packed,
    parts,
    idx_ref,
    mix_ref,
    wide,
    stages,
    lists,
    first_pre,
    first_hidden,
    own_part,
    inner_sum,
    early_refs,
    late_refs,
    extra_ref,
    extra_plane,
    extra_line,
    sums_plane,
    sums_line,
    own_sem,
    z_sem,
    spare_sem,
    x_sem,
    y_sem,
    far_sem,
    twin_sem,
    twin_own_sem,
    double_sem,
    send_sem,
    double_send_sem,
    list_sem,
    sum_sem,
    sum_send_sem,
):
    section, at = lax.axis_index("section"), lax.axis_index("dp")
    z, core = at // 2, at % 2
    flipped = z // 2
    height = z + flipped * (3 - 2 * z)
    pairs = table_ref.shape[0]
    spare = pairs // SPARE
    quarter = (pairs - spare) // 4
    chunk = quarter // CHUNKS
    spare_chunk = spare // CHUNKS

    def level(value):
        return value + flipped * (3 - 2 * value)

    twin = (section, z * 2 + 1 - core)
    beside_x = (section + 1 - 2 * (section % 2), at)
    beside_y = (section + 2 - 4 * (section // 2), at)
    inner_z = (section, level(1 - height) * 2 + core)
    across_z = (section, level(2) * 2 + core)
    outer_z = (section, level(0) * 2 + core)
    skip_z = (section, ((z + 2) % 4) * 2 + core)
    sources = [level(1 - height), level(2), level(3)]
    crosses = height == 1
    plane = [((section + k) % 4, at) for k in range(1, 4)]
    beyond = [((section + k) % 4, z * 2 + 1 - core) for k in range(1, 4)]
    line = [(section, ((z + k) % 4) * 2 + core) for k in range(1, 4)]
    neighbours = [twin] + plane + beyond

    barrier = pltpu.get_barrier_semaphore()
    for partner in neighbours + line:
        pl.semaphore_signal(barrier, inc=1, device_id=partner, device_id_type=MESH)
    pl.semaphore_wait(barrier, 10)

    sent = []

    def region(shard, part, piece):
        return full_ref.at[pl.ds(shard * pairs + part * quarter + piece * chunk, chunk)]

    def spare_region(shard, piece):
        return full_ref.at[pl.ds(shard * pairs + 4 * quarter + piece * spare_chunk, spare_chunk)]

    def send(source, target, recv, device, when=None):
        number = len(sent)
        copy = pltpu.make_async_remote_copy(
            src_ref=source,
            dst_ref=target,
            send_sem=send_sem.at[number],
            recv_sem=recv,
            device_id=device,
            device_id_type=MESH,
        )
        sent.append((copy, when))
        if when is None:
            copy.start()
        else:
            pl.when(when)(copy.start)
        return copy

    def arrived(target, recv):
        pltpu.make_async_copy(target, target, recv).wait()

    def own_piece(piece, device, number, when=None):
        block = table_ref.at[pl.ds(section * quarter + piece * chunk, chunk)]
        send(block, region(at, section, piece), z_sem.at[number], device, when)

    for piece in range(min(AHEAD, CHUNKS)):
        own_piece(piece, inner_z, piece)
    for piece in range(min(AHEAD_ACROSS, CHUNKS)):
        own_piece(piece, across_z, CHUNKS + piece, crosses)
    whole = full_ref.at[pl.ds(at * pairs, pairs)]
    own = pltpu.make_async_copy(table_ref, whole, own_sem)
    own.start()
    send(table_ref, whole, twin_own_sem, twin)

    inner_ref, outer_ref, head_ref = weight_refs
    row_inner, row_outer, row_head = (ref.shape[0] for ref in weight_refs)
    hidden, classes = inner_ref.shape[1], head_ref.shape[1]
    head_at = row_inner + row_outer
    packed[0:row_inner, :] = inner_ref[...]
    packed[row_inner:head_at, :] = outer_ref[...]
    packed[head_at:, :] = jnp.zeros((row_head, hidden), jnp.float32)
    packed[head_at:, 0:classes] = head_ref[...]
    labelled = jnp.sum(mask_ref[...].astype(jnp.float32)).astype(jnp.int32)
    lane = lax.broadcasted_iota(jnp.int32, (1, hidden), 1)
    high_part = (labelled // 256).astype(jnp.float32)
    low_part = (labelled % 256).astype(jnp.float32)
    tail = jnp.where(lane == classes, high_part, jnp.where(lane == classes + 1, low_part, 0.0))
    packed[head_at : head_at + 1, :] += tail
    mine = (core * 4 + section) * 4 + z
    weights_ref[mine] = packed[...].astype(jnp.bfloat16)
    doubling = [(inner_z, 1), (skip_z, 2), (beside_x, 4), (beside_y, 8), (twin, 16)]
    doubled = []

    def double_start(number):
        device, size = doubling[number]
        block = weights_ref.at[pl.ds((mine // size) * size, size)]
        copy = pltpu.make_async_remote_copy(
            src_ref=block,
            dst_ref=block,
            send_sem=double_send_sem.at[number],
            recv_sem=double_sem.at[number],
            device_id=device,
            device_id_type=MESH,
        )
        copy.start()
        doubled.append(copy)

    double_start(0)

    placed = place_ref[...]
    pair_at = placed // 2
    high = place_ref.shape[1]
    parts[0:128, :] = (pair_at % 256).astype(jnp.float32).astype(jnp.bfloat16)
    parts[128:256, :] = (pair_at // 256).astype(jnp.float32).astype(jnp.bfloat16)
    parts[256:384, :] = (placed % 2).astype(jnp.float32).astype(jnp.bfloat16)
    looked_rows = near_ref.shape[0]
    seeds = seed_ref.shape[0]
    tiles = hits_ref.shape[1] // TILE
    total = 3 * CHUNKS
    steps = total + max(FAR_LAG, SPARE_LAG)
    per_step = -(-looked_rows // (8 * steps)) * 8
    for j in range(fan_outer):
        wide[j] = jnp.broadcast_to(seed_ref[:, j : j + 1], (seeds, TILE))

    def look_up(first, last):
        def rows_of(block, carry):
            start_at = pl.multiple_of(block * 8, 8)
            sub = lax.broadcasted_iota(jnp.int32, (high, 256), 0)
            low_at = lax.broadcasted_iota(jnp.int32, (128, 256), 0)
            row = lax.broadcasted_iota(jnp.int32, (256, 512), 0)
            column = lax.broadcasted_iota(jnp.int32, (256, 512), 1)
            for k in range(8):
                node = near_ref[pl.ds(start_at + k, 1), :]
                hot = (sub == node // 128).astype(jnp.float32).astype(jnp.bfloat16)
                got = jnp.dot(parts[...], hot, preferred_element_type=jnp.float32)
                chosen = low_at == node % 128
                found = jnp.where(chosen, got[0:128] + 256.0 * got[128:256], 0.0)
                odd = jnp.where(chosen, got[256:384], 0.0)
                entry_at = jnp.sum(found, axis=0, keepdims=True).astype(jnp.int32)
                idx_ref[block * 2 + k // 4, k % 4 : k % 4 + 1, :] = jnp.clip(
                    entry_at, 0, full_ref.shape[0] - 1
                )
                mix_ref[pl.ds(start_at + k, 1), 0:256] = jnp.sum(odd, axis=0, keepdims=True)
            odd = mix_ref[pl.ds(start_at, 8), 0:256]
            live = (near_ref[pl.ds(start_at, 8), :] >= 0).astype(jnp.float32)
            mix_ref[pl.ds(start_at, 8), :] = jnp.dot(
                (live * (1.0 - odd)).astype(jnp.bfloat16),
                (column == 2 * row).astype(jnp.float32).astype(jnp.bfloat16),
                preferred_element_type=jnp.float32,
            ) + jnp.dot(
                (live * odd).astype(jnp.bfloat16),
                (column == 2 * row + 1).astype(jnp.float32).astype(jnp.bfloat16),
                preferred_element_type=jnp.float32,
            )
            return carry

        lax.fori_loop(first // 8, last // 8, rows_of, 0)

    def mark(tile):
        start_at = tile * TILE
        dest = lax.broadcasted_iota(jnp.int32, (seeds, TILE), 1) + start_at
        hits = jnp.zeros((seeds, TILE), jnp.float32)
        for j in range(fan_outer):
            hits = hits + (wide[j] == dest).astype(jnp.float32)
        hits_ref[:, start_at : start_at + TILE] = hits.astype(jnp.bfloat16)
        dest = lax.broadcasted_iota(jnp.int32, (TILE, seeds), 0) + start_at
        hits = jnp.zeros((TILE, seeds), jnp.float32)
        for j in range(fan_outer):
            hits = hits + (seed_across_ref[j : j + 1, :] == dest).astype(jnp.float32)
        hits_back_ref[start_at : start_at + TILE, :] = hits.astype(jnp.bfloat16)

    twins = []

    def to_twin(block, number):
        send(block, block, twin_sem.at[number], twin)
        twins.append(number)

    for step in range(steps):
        if step < total:
            turn, piece = divmod(step, CHUNKS)
            shard = sources[turn] * 2 + core
            goes, number = (across_z, 2 * CHUNKS + piece) if turn == 0 else (outer_z, step)
            block = region(shard, section, piece)
            arrived(block, z_sem.at[step])
            send(block, block, z_sem.at[number], goes, crosses)
            send(block, block, x_sem.at[step], beside_x)
            send(block, block, y_sem.at[step], beside_y)
            to_twin(block, step)
            if step + AHEAD < CHUNKS:
                own_piece(step + AHEAD, inner_z, step + AHEAD)
            if step + AHEAD_ACROSS < CHUNKS:
                piece = step + AHEAD_ACROSS
                own_piece(piece, across_z, CHUNKS + piece, crosses)
            piece = step - SPARE_AFTER
            if 0 <= piece < CHUNKS:
                block = table_ref.at[pl.ds(4 * quarter + piece * spare_chunk, spare_chunk)]
                goal = spare_region(at, piece)
                send(block, goal, spare_sem.at[piece], inner_z)
                send(block, goal, spare_sem.at[CHUNKS + piece], across_z, crosses)
        late = step - SPARE_LAG
        if 0 <= late < total:
            turn, piece = divmod(late, CHUNKS)
            shard = sources[turn] * 2 + core
            goes, number = (across_z, 2 * CHUNKS + piece) if turn == 0 else (outer_z, late)
            block = spare_region(shard, piece)
            arrived(block, spare_sem.at[late])
            send(block, block, spare_sem.at[number], goes, crosses)
            to_twin(block, 4 * total + late)
        late = step - LAG
        if 0 <= late < total:
            turn, piece = divmod(late, CHUNKS)
            shard = sources[turn] * 2 + core
            block = region(shard, beside_x[0], piece)
            arrived(block, x_sem.at[late])
            send(block, block, far_sem.at[late], beside_y, core == piece % 2)
            to_twin(block, total + late)
            block = region(shard, beside_y[0], piece)
            arrived(block, y_sem.at[late])
            send(block, block, far_sem.at[late], beside_x, core != piece % 2)
            to_twin(block, 2 * total + late)
        later = step - FAR_LAG
        if 0 <= later < total:
            turn, piece = divmod(later, CHUNKS)
            shard = sources[turn] * 2 + core
            block = region(shard, 3 - section, piece)
            arrived(block, far_sem.at[later])
            to_twin(block, 3 * total + later)
        if step % 2 == 0 and step // 2 < len(doubling):
            doubled[step // 2].wait()
            if step // 2 + 1 < len(doubling):
                double_start(step // 2 + 1)
        first = min(step * per_step, looked_rows)
        last = min(first + per_step, looked_rows)
        if last > first:
            look_up(first, last)
        for tile in range(step * tiles // steps, (step + 1) * tiles // steps):
            mark(tile)

    for number in sorted(twins):
        kind, step = divmod(number, total)
        turn, piece = divmod(step, CHUNKS)
        shard = sources[turn] * 2 + 1 - core
        if kind == 4:
            block = spare_region(shard, piece)
        else:
            block = region(shard, (section, beside_x[0], beside_y[0], 3 - section)[kind], piece)
        arrived(block, twin_sem.at[number])
    arrived(full_ref.at[pl.ds((z * 2 + 1 - core) * pairs, pairs)], twin_own_sem)
    own.wait()

    blocks = looked_rows
    lane = lax.broadcasted_iota(jnp.int32, (BLOCK, 2 * BLOCK * SLOT), 1)
    same = lane // (2 * SLOT) == lax.broadcasted_iota(jnp.int32, lane.shape, 0)
    near_part = jnp.logical_and(same, lane % (2 * SLOT) < 2 * SLOT - 2).astype(jnp.float32)
    self_part = jnp.logical_and(same, lane % (2 * SLOT) >= 2 * SLOT - 2).astype(jnp.float32)
    turns = blocks // GROUP

    def fetch(turn, slot):
        return pltpu.make_async_copy(
            idx_ref.at[jnp.minimum(turn, turns - 1)], lists[slot], list_sem.at[slot]
        )

    def pick(member, slot, stage):
        def unit(number, carry):
            entry = full_ref[lists[slot][member, number]]
            stage[pl.ds(2 * number, 2), :] = entry.astype(jnp.float32)
            return carry

        lax.fori_loop(0, BLOCK * SLOT, unit, 0, unroll=BLOCK * SLOT)

    def reduce(block, stage):
        mix = mix_ref[pl.ds(block, 1), :]
        near = mix * near_part
        left = jnp.concatenate([near, mix * self_part], axis=0).astype(jnp.bfloat16)
        out = jnp.dot(left, stage[...].astype(jnp.bfloat16), preferred_element_type=jnp.float32)
        count = jnp.maximum(jnp.sum(near, axis=1, keepdims=True), 1.0)
        both = jnp.concatenate([out[BLOCK:], out[:BLOCK] / count], axis=1)
        start_at = pl.multiple_of(block * BLOCK, BLOCK)
        joined_ref[pl.ds(start_at, BLOCK), :] = both.astype(jnp.bfloat16)

    near_stages, far_stages = stages
    for slot in range(SETS):
        fetch(slot, slot).start()
    for member in range(GROUP):
        far_stages[member][...] = jnp.zeros(far_stages[member].shape, jnp.float32)

    def round_of(number, carry):
        for slot in range(SETS):
            turn = number * SETS + slot
            fetch(turn, slot).wait()
            for member in range(GROUP):
                pick(member, slot, stages[slot % 2][member])
                reduce(
                    jnp.maximum((turn - 1) * GROUP + member, 0), stages[1 - slot % 2][member]
                )
            fetch(turn + SETS, slot).start()
        return carry

    lax.fori_loop(0, blocks // (GROUP * SETS), round_of, 0)
    for slot in range(SETS):
        fetch(0, slot).wait()
    for member in range(GROUP):
        reduce(blocks - GROUP + member, stages[(SETS - 1) % 2][member])
    for copy, when in sent:
        if when is None:
            copy.wait_send()
        else:
            pl.when(when)(copy.wait_send)

    summing = []

    def pass_on(source, target, number, device):
        copy = pltpu.make_async_remote_copy(
            src_ref=source,
            dst_ref=target,
            send_sem=sum_send_sem.at[len(summing)],
            recv_sem=sum_sem.at[number],
            device_id=device,
            device_id_type=MESH,
        )
        summing.append(copy)
        copy.start()

    def passed(target, number):
        arrived(target, sum_sem.at[number])

    def to_other_core(part):
        pass_on(part.grads.at[pl.ds((1 - core) * 16, 16)], part.half_in, part.base, twin)

    def to_plane(part):
        passed(part.half_in, part.base)
        part.half[...] = part.grads[pl.ds(core * 16, 16)] + part.half_in[...]
        for partner in plane:
            block = part.half.at[pl.ds(partner[0] * 4, 4)]
            pass_on(block, part.plane_in.at[section], part.base + 1 + section, partner)
        part.plane_in[section] = part.half[pl.ds(section * 4, 4)]

    def to_line(part):
        for k in range(1, 4):
            other = (section + k) % 4
            passed(part.plane_in.at[other], part.base + 1 + other)
        part.fourth[...] = (part.plane_in[0] + part.plane_in[1]) + (
            part.plane_in[2] + part.plane_in[3]
        )
        for k, partner in enumerate(line):
            block = part.fourth.at[pl.ds((z + k + 1) % 4, 1)]
            pass_on(block, part.line_in.at[pl.ds(z, 1)], part.base + 5 + z, partner)
        part.line_in[z] = part.fourth[z]

    def whole_sum(part):
        for k in range(1, 4):
            other = (z + k) % 4
            passed(part.line_in.at[pl.ds(other, 1)], part.base + 5 + other)
        return (part.line_in[0] + part.line_in[1]) + (part.line_in[2] + part.line_in[3])

    def share(value, slots, base, me, partners):
        slots[me] = value
        for partner in partners:
            pass_on(slots.at[me], slots.at[me], base + me, partner)

    def collect(slots, base, me):
        count = slots.shape[0]
        for k in range(1, count):
            other = (me + k) % count
            passed(slots.at[other], base + other)
        values = [slots[k] for k in range(count)]
        while len(values) > 1:
            values = [values[k] + values[k + 1] for k in range(0, len(values), 2)]
        return values[0]

    early, late_part = Parts(early_refs, 0), Parts(late_refs, 9)
    dest_count = joined_ref.shape[0]
    order = block_order()
    weights = weights_ref[...].astype(jnp.float32)
    split = (0, row_inner, head_at, head_at + row_head)
    full_inner, full_outer, full_head = (
        jnp.concatenate([weights[spot, split[k] : split[k + 1]] for spot in order], axis=0)
        for k in range(3)
    )
    lane = lax.broadcasted_iota(jnp.int32, (1, hidden), 1)
    tails = weights[0:4, head_at : head_at + 1] + weights[16:20, head_at : head_at + 1]
    tails = jnp.sum(tails.reshape(4, hidden), axis=0, keepdims=True)
    scale = jnp.where(lane == classes, 256.0, jnp.where(lane == classes + 1, 1.0, 0.0))
    label_count = jnp.maximum(jnp.sum(tails * scale), 1.0)
    full_inner = full_inner.astype(jnp.bfloat16)
    full_outer = full_outer.astype(jnp.bfloat16)
    full_head = jnp.where(lane < classes, full_head, 0.0).astype(jnp.bfloat16)
    bias_inner, bias_outer, bias_head = bias_rows_of(bias_ref, hidden)
    kept = seed_ref[:, 0:fan_outer]
    count_two = jnp.sum((kept >= 0).astype(jnp.float32), axis=1, keepdims=True)

    def forward(tile, carry):
        tile_rows = pl.ds(pl.multiple_of(tile * TILE, TILE), TILE)
        before = (
            jnp.dot(joined_ref[tile_rows, :], full_inner, preferred_element_type=jnp.float32)
            + bias_inner
        )
        first_pre[tile_rows, :] = before
        first_hidden[tile_rows, :] = (before * lax.logistic(before)).astype(jnp.bfloat16)
        return carry

    lax.fori_loop(0, tiles, forward, 0)
    mean_sum = jnp.dot(hits_ref[...], first_hidden[...], preferred_element_type=jnp.float32)
    mean_two = (mean_sum / count_two).astype(jnp.bfloat16)
    joined_two = jnp.concatenate([first_hidden[0:seeds, :], mean_two], axis=1)
    pre_two = jnp.dot(joined_two, full_outer, preferred_element_type=jnp.float32) + bias_outer
    gate_two = lax.logistic(pre_two)
    hidden_two = (pre_two * gate_two).astype(jnp.bfloat16)
    logits = jnp.dot(hidden_two, full_head, preferred_element_type=jnp.float32) + bias_head
    inside = lane < classes
    highest = jnp.max(jnp.where(inside, logits, -jnp.inf), axis=1, keepdims=True)
    shifted = jnp.where(inside, logits - highest, 0.0)
    total_exp = jnp.sum(jnp.where(inside, jnp.exp(shifted), 0.0), axis=1, keepdims=True)
    log_total = jnp.log(total_exp)
    chosen = (lane == seed_ref[:, fan_outer : fan_outer + 1]).astype(jnp.float32)
    row_weight = seed_ref[:, fan_outer + 1 : fan_outer + 2].astype(jnp.float32)
    loss = jnp.sum((log_total - jnp.sum(shifted * chosen, axis=1, keepdims=True)) * row_weight)
    grad_logits = (jnp.exp(shifted - log_total) - chosen) * (row_weight / label_count)
    grad_logits = jnp.where(inside, grad_logits, 0.0).astype(jnp.bfloat16)
    grad_head = outer_product(hidden_two, grad_logits)
    grad_two = against(grad_logits, full_head).astype(jnp.bfloat16).astype(jnp.float32)
    grad_pre_two = (grad_two * gate_two * (1.0 + pre_two * (1.0 - gate_two))).astype(jnp.bfloat16)
    grad_outer = outer_product(joined_two, grad_pre_two)
    for number, spot in enumerate(order):
        early.grads[spot, 0:row_outer, :] = grad_outer[
            number * row_outer : (number + 1) * row_outer
        ]
        early.grads[spot, row_outer : row_outer + row_head, :] = grad_head[
            number * row_head : (number + 1) * row_head
        ]
    to_other_core(early)
    extra_ref[1:2, :] = jnp.sum(grad_pre_two.astype(jnp.float32), axis=0, keepdims=True)
    extra_ref[2:3, :] = jnp.sum(grad_logits.astype(jnp.float32), axis=0, keepdims=True)
    extra_ref[3:4, :] = jnp.where(lane == 0, loss, jnp.where(lane == 1, label_count, 0.0))
    extra_ref[4:8, :] = jnp.zeros((4, hidden), jnp.float32)
    grad_joined = against(grad_pre_two, full_outer)
    share_part = grad_joined[:, hidden:] / count_two
    share_high = share_part.astype(jnp.bfloat16)
    share_low = (share_part - share_high.astype(jnp.float32)).astype(jnp.bfloat16)
    inner_sum[...] = jnp.zeros(inner_sum.shape, jnp.float32)
    share_both = jnp.concatenate([share_high, share_low], axis=0)
    own_part[...] = jnp.zeros(own_part.shape, jnp.float32)
    own_part[0:seeds, :] = grad_joined[:, 0:hidden]

    def backward(tile, bias_sum, own=None):
        tile_rows = pl.ds(pl.multiple_of(jnp.int32(tile) * TILE, TILE), TILE)
        hits = hits_back_ref[tile_rows, :]
        both_hits = jnp.concatenate([hits, hits], axis=1)
        grad_one = jnp.dot(both_hits, share_both, preferred_element_type=jnp.float32)
        if own is not None:
            grad_one = grad_one + own
        grad_one = grad_one.astype(jnp.bfloat16).astype(jnp.float32)
        before = first_pre[tile_rows, :]
        gate = lax.logistic(before)
        grad_pre = (grad_one * gate * (1.0 + before * (1.0 - gate))).astype(jnp.bfloat16)
        inner_sum[...] += outer_product(joined_ref[tile_rows, :], grad_pre)
        return bias_sum + jnp.sum(grad_pre.astype(jnp.float32), axis=0, keepdims=True)

    bias_sum = backward(0, jnp.zeros((1, hidden), jnp.float32), own_part[...])
    bias_sum = lax.fori_loop(1, PAUSE, backward, bias_sum)
    to_plane(early)
    bias_sum = lax.fori_loop(PAUSE, tiles, backward, bias_sum)
    extra_ref[0:1, :] = bias_sum
    grad_inner = inner_sum[...]
    for number, spot in enumerate(order):
        late_part.grads[spot] = grad_inner[number * row_inner : (number + 1) * row_inner]
    to_other_core(late_part)
    share(extra_ref[...], extra_plane, 18, section * 2 + core, neighbours)
    to_plane(late_part)
    to_line(early)
    share(collect(extra_plane, 18, section * 2 + core), extra_line, 26, z, line)
    to_line(late_part)

    deep_lane = lax.broadcasted_iota(jnp.int32, (8, 128), 1)

    def packed_up(values):
        found = jnp.zeros((8, 128), jnp.float32)
        for k, value in enumerate(values):
            found = jnp.where(deep_lane == k, value, found)
        return found

    def everywhere(values, number):
        base = 30 + 12 * number
        place_in = section * 2 + core
        share(packed_up(values), sums_plane.at[number], base, place_in, neighbours)
        plane_sum = collect(sums_plane.at[number], base, place_in)
        share(plane_sum, sums_line.at[number], base + 8, z, line)
        return collect(sums_line.at[number], base + 8, z)

    held = [ref[...] for ref in weight_refs]
    weight_squares = [jnp.sum(weight * weight) for weight in held]
    rest = whole_sum(early)
    shard = whole_sum(late_part)
    extra = collect(extra_line, 26, z)
    pieces = [shard, rest[0:row_outer], rest[row_outer:, 0:classes]]
    values = everywhere([jnp.sum(shard * shard) + jnp.sum(rest * rest)] + weight_squares, 0)
    grad_square = jnp.sum(jnp.where(deep_lane[0:1] == 0, values[0:1], 0.0))
    bias_square = jnp.sum(extra[0:3] * extra[0:3])
    clip_norm = jnp.sqrt(jnp.full((1, 1), grad_square + bias_square, jnp.float32))
    factor = jnp.minimum(1.0, CLIP / clip_norm)
    update_squares = []
    for k in range(3):
        update = moments(held[k], pieces[k] * factor, first_refs[k][...], second_refs[k][...])[2]
        update_squares.append(jnp.sum(update * update))
    updates = everywhere(update_squares, 1)
    rows = row_inner + row_outer + row_head
    out_ref[0:row_inner, :] = shard
    out_ref[row_inner:rows, :] = rest
    out_ref[rows : rows + 8, :] = extra
    out_ref[rows + 8 : rows + 16, 0:128] = values
    out_ref[rows + 8 : rows + 16, 128:256] = updates
    for copy in summing:
        copy.wait_send()


def block_order():
    return [(e % 2) * 16 + (e // 8) * 4 + (e % 8) // 2 for e in range(32)]


def bias_rows_of(ref, hidden):
    width = ref.shape[0] - 2 * hidden
    last = ref[pl.ds(2 * hidden, width)].reshape(1, width)
    return (
        ref[pl.ds(0, hidden)].reshape(1, hidden),
        ref[pl.ds(hidden, hidden)].reshape(1, hidden),
        jnp.concatenate([last, jnp.zeros((1, hidden - width), jnp.float32)], axis=1),
    )


def summed_step(fan_outer, node_table, weights, firsts, seconds, biases, label_mask, place, near, seed_table):
    devices = lax.axis_size(("section", "dp"))
    table_rows, width = node_table.shape
    frontier_high = place.shape[1]
    looked = near.shape[0]
    dest_count = looked * BLOCK
    seeds = seed_table.shape[0]
    hidden = weights[0].shape[1]
    row_inner = weights[0].shape[0]
    rows = sum(weight.shape[0] for weight in weights)
    total = 3 * CHUNKS
    sends = 4 * CHUNKS + 1 + 3 * total + total + 2 * total + 5 * total
    vmem = pl.BlockSpec(memory_space=pltpu.VMEM)
    stage = (pltpu.VMEM((2 * BLOCK * SLOT, width), jnp.float32),) * GROUP

    def on_the_way(depth):
        return (
            pltpu.VMEM((devices, depth, hidden), jnp.float32),
            pltpu.VMEM((16, depth, hidden), jnp.float32),
            pltpu.VMEM((16, depth, hidden), jnp.float32),
            pltpu.VMEM((4, 4, depth, hidden), jnp.float32),
            pltpu.VMEM((4, depth, hidden), jnp.float32),
            pltpu.VMEM((4, depth, hidden), jnp.float32),
        )

    return pl.pallas_call(
        functools.partial(step_kernel, fan_outer),
        out_shape=jax.ShapeDtypeStruct((rows + 16, hidden), jnp.float32),
        in_specs=[pl.BlockSpec(memory_space=pl.ANY)] + [(vmem,) * 3] * 3 + [vmem] * 6,
        out_specs=vmem,
        scratch_shapes=[
            pltpu.VMEM((dest_count, 2 * width), jnp.bfloat16),
            pltpu.VMEM((devices, rows, hidden), jnp.bfloat16),
            pltpu.VMEM((seeds, dest_count), jnp.bfloat16),
            pltpu.VMEM((dest_count, seeds), jnp.bfloat16),
            pltpu.VMEM((lax.axis_size("dp") * table_rows // 2, 2, width), jnp.bfloat16),
            pltpu.VMEM((rows, hidden), jnp.float32),
            pltpu.VMEM((384, frontier_high), jnp.bfloat16),
            pltpu.VMEM((looked // GROUP, GROUP, 256), jnp.int32),
            pltpu.VMEM((looked, 512), jnp.float32),
            pltpu.VMEM((fan_outer, seeds, TILE), jnp.int32),
            (stage, stage),
            (pltpu.SMEM((GROUP, BLOCK * SLOT), jnp.int32),) * SETS,
            pltpu.VMEM((dest_count, hidden), jnp.float32),
            pltpu.VMEM((dest_count, hidden), jnp.bfloat16),
            pltpu.VMEM((TILE, hidden), jnp.float32),
            pltpu.VMEM((hidden, hidden), jnp.float32),
            on_the_way(rows - row_inner),
            on_the_way(row_inner),
            pltpu.VMEM((8, hidden), jnp.float32),
            pltpu.VMEM((8, 8, hidden), jnp.float32),
            pltpu.VMEM((4, 8, hidden), jnp.float32),
            pltpu.VMEM((2, 8, 8, 128), jnp.float32),
            pltpu.VMEM((2, 4, 8, 128), jnp.float32),
            pltpu.SemaphoreType.DMA(()),
            pltpu.SemaphoreType.DMA((total,)),
            pltpu.SemaphoreType.DMA((total,)),
            pltpu.SemaphoreType.DMA((total,)),
            pltpu.SemaphoreType.DMA((total,)),
            pltpu.SemaphoreType.DMA((total,)),
            pltpu.SemaphoreType.DMA((5 * total,)),
            pltpu.SemaphoreType.DMA(()),
            pltpu.SemaphoreType.DMA((5,)),
            pltpu.SemaphoreType.DMA((sends,)),
            pltpu.SemaphoreType.DMA((5,)),
            pltpu.SemaphoreType.DMA((SETS,)),
            pltpu.SemaphoreType.DMA((54,)),
            pltpu.SemaphoreType.DMA((44,)),
        ],
        compiler_params=pltpu.CompilerParams(
            collective_id=0, has_side_effects=True, vmem_limit_bytes=56 * 2**20
        ),
    )(
        pltpu.with_memory_space_constraint(
            node_table.reshape(table_rows // 2, 2, width), pltpu.HBM
        ),
        weights,
        firsts,
        seconds,
        biases,
        label_mask,
        place,
        near,
        seed_table,
        seed_table.T,
    )


def final_kernel(
    sizes,
    devices,
    sums_ref,
    weight_refs,
    first_refs,
    second_refs,
    smooth_refs,
    bias_refs,
    loss_ref,
    count_ref,
    clip_ref,
    norms_ref,
    new_refs,
    moment_refs,
    square_refs,
    average_refs,
    bias_out_refs,
):
    classes, row_inner, row_outer, row_head = sizes
    hidden = sums_ref.shape[1]
    rows = row_inner + row_outer + row_head
    split = (0, row_inner, row_inner + row_outer, rows)
    widths = (hidden, hidden, classes)
    lane = lax.broadcasted_iota(jnp.int32, (1, 128), 1)

    def number(k, start_at):
        found = sums_ref[rows + 8 : rows + 9, start_at : start_at + 128]
        return jnp.sum(jnp.where(lane == k, found, 0.0), axis=1, keepdims=True)

    bias_grad = sums_ref[rows : rows + 3, :]
    bias_square = jnp.sum(jnp.sum(bias_grad * bias_grad, axis=1, keepdims=True), axis=0, keepdims=True)
    clip_norm = jnp.sqrt(number(0, 0) + bias_square)
    factor = jnp.minimum(1.0, CLIP / clip_norm)
    wide = lax.broadcasted_iota(jnp.int32, (8, 128), 1)
    deep = lax.broadcasted_iota(jnp.int32, (8, 128), 0)
    norms = jnp.zeros((8, 128), jnp.float32)
    for k in range(3):
        weight = weight_refs[k][...]
        gradient = sums_ref[split[k] : split[k + 1], 0 : widths[k]] * factor
        first, second, update = moments(weight, gradient, first_refs[k][...], second_refs[k][...])
        weight_norm, update_norm = jnp.sqrt(number(1 + k, 0)), jnp.sqrt(number(k, 128))
        fresh = weight - RATE * (weight_norm / update_norm) * update
        new_refs[k][...] = fresh
        moment_refs[k][...] = first
        square_refs[k][...] = second
        average_refs[k][...] = AVERAGE * smooth_refs[k][...] + (1.0 - AVERAGE) * fresh
        norms = jnp.where(jnp.logical_and(deep == k, wide == 0), weight_norm, norms)
        norms = jnp.where(jnp.logical_and(deep == k, wide == 1), update_norm, norms)
    norms_ref[...] = norms[0:3, 0:2]
    weight, first, second, smooth = (
        jnp.concatenate(bias_rows_of(ref, hidden), axis=0) for ref in bias_refs
    )
    first, second, update = moments(weight, bias_grad * factor, first, second)
    column = lax.broadcasted_iota(jnp.int32, weight.shape, 1)
    row = lax.broadcasted_iota(jnp.int32, weight.shape, 0)
    update = jnp.where(jnp.logical_or(row < 2, column < classes), update, 0.0)
    ratio = jnp.sqrt(jnp.sum(weight * weight, axis=1, keepdims=True)) / jnp.sqrt(
        jnp.sum(update * update, axis=1, keepdims=True)
    )
    fresh = weight - RATE * ratio * update
    average = AVERAGE * smooth + (1.0 - AVERAGE) * fresh
    for ref, value in zip(bias_out_refs, (fresh, first, second, average)):
        ref[pl.ds(0, hidden)] = value[0:1].reshape(hidden)
        ref[pl.ds(hidden, hidden)] = value[1:2].reshape(hidden)
        ref[pl.ds(2 * hidden, classes)] = value[2:3, 0:classes].reshape(classes)
    tail = sums_ref[rows + 3 : rows + 4, 0:128]
    loss_ref[...] = jnp.sum(jnp.where(lane == 0, tail, 0.0), axis=1, keepdims=True)
    count = jnp.sum(jnp.where(lane == 1, tail, 0.0), axis=1, keepdims=True)
    count_ref[...] = count / devices
    clip_ref[...] = clip_norm


def finished(sizes, sums, weights, firsts, seconds, smooths, biases):
    vmem = pl.BlockSpec(memory_space=pltpu.VMEM)
    like = [jax.ShapeDtypeStruct(weight.shape, jnp.float32) for weight in weights]
    scalar = jax.ShapeDtypeStruct((1, 1), jnp.float32)
    return pl.pallas_call(
        functools.partial(final_kernel, sizes, float(lax.axis_size(("section", "dp")))),
        out_shape=(
            scalar,
            scalar,
            scalar,
            jax.ShapeDtypeStruct((3, 2), jnp.float32),
            like,
            like,
            like,
            like,
            [jax.ShapeDtypeStruct(biases[0].shape, jnp.float32)] * 4,
        ),
        in_specs=[vmem] + [(vmem,) * 3] * 4 + [(vmem,) * 4],
        out_specs=(vmem,) * 4 + ([vmem] * 3,) * 4 + ([vmem] * 4,),
    )(sums, weights, firsts, seconds, smooths, biases)


def on_slice_kernels(
    node_table, owner_ids, dest_count, fan_inner, hidden, classes, seed_count, fan_outer, mask_sizes, weight_rows
):
    parts, peers = lax.axis_size("section"), lax.axis_size("dp")
    return (
        parts == 4
        and peers == 8
        and peers * node_table.size * 2 <= VMEM_TABLE_LIMIT
        and node_table.shape[1] == 128
        and node_table.shape[0] % (2 * SPARE * CHUNKS) == 0
        and (node_table.shape[0] // 2 - node_table.shape[0] // 2 // SPARE) % (4 * CHUNKS) == 0
        and peers * node_table.shape[0] <= 131072
        and owner_ids.shape[0] % 1024 == 0
        and owner_ids.shape[0] <= 32768
        and fan_inner == SLOT - 1
        and dest_count % (BLOCK * GROUP * SETS) == 0
        and dest_count % TILE == 0
        and hidden == 256
        and classes + 2 <= hidden
        and seed_count <= TILE
        and seed_count % 16 == 0
        and fan_outer + 2 <= SLOT
        and len(mask_sizes) == 2
        and mask_sizes[0] * mask_sizes[1] <= 65536
        and all(rows % 8 == 0 for rows in weight_rows)
        and sum(weight_rows) % 16 == 0
        and dest_count // TILE > PAUSE
    )


def outer_product(left, right):
    return lax.dot_general(
        left, right, (((0,), (0,)), ((), ())), preferred_element_type=jnp.float32
    )


def against(left, right):
    return lax.dot_general(
        left, right, (((1,), (1,)), ((), ())), preferred_element_type=jnp.float32
    )


def silu_slope(before, grad_out):
    sigmoid = jax.nn.sigmoid(before)
    return (grad_out * sigmoid * (1.0 + before * (1.0 - sigmoid))).astype(jnp.bfloat16)


def moments(weight, gradient, first, second):
    first = BETA_ONE * first + (1.0 - BETA_ONE) * gradient
    second = BETA_TWO * second + (1.0 - BETA_TWO) * gradient * gradient
    update = (
        first / (1.0 - BETA_ONE**STEP) / (jnp.sqrt(second / (1.0 - BETA_TWO**STEP)) + EPSILON)
        + DECAY * weight
    )
    return (first, second, update)


def bias_ratio(weight, update, hidden):
    bounds = ((0, hidden), (hidden, 2 * hidden), (2 * hidden, weight.shape[0]))
    pieces = []
    for start_at, stop_at in bounds:
        weight_norm = jnp.sqrt(jnp.sum(weight[start_at:stop_at] ** 2))
        update_norm = jnp.sqrt(jnp.sum(update[start_at:stop_at] ** 2))
        pieces.append(jnp.zeros((stop_at - start_at,), jnp.float32) + weight_norm / update_norm)
    return jnp.concatenate(pieces)


def gathered_rows(node_table, owner_ids, row_ids):
    peer_count = lax.axis_size("dp")
    parts = lax.axis_size("section")
    table_rows = node_table.shape[0]
    if peer_count * node_table.size * 2 <= WHOLE_TABLE_LIMIT and table_rows % parts == 0:
        part_rows = table_rows // parts
        quarter = lax.dynamic_slice_in_dim(
            node_table, lax.axis_index("section") * part_rows, part_rows, 0
        )
        source = lax.all_gather(quarter, ("section", "dp"), axis=0, tiled=True)
        place = (row_ids // part_rows * peer_count + owner_ids) * part_rows + row_ids % part_rows
        return source, place
    frontier_rows = owner_ids.shape[0]
    slot_count = max(2, 2 * frontier_rows // peer_count)
    owner_hot = (owner_ids[:, None] == jnp.arange(peer_count)[None, :]).astype(jnp.int32)
    ranking = jnp.sum((jnp.cumsum(owner_hot, axis=0) - 1) * owner_hot, axis=1)
    placed = owner_ids * slot_count + ranking
    request = (
        jnp.zeros((peer_count * slot_count,), jnp.int32)
        .at[placed]
        .set(row_ids)
        .reshape(peer_count, slot_count)
    )
    returned = lax.all_to_all(
        node_table[lax.all_to_all(request, "dp", split_axis=0, concat_axis=0, tiled=True)],
        "dp",
        split_axis=0,
        concat_axis=0,
        tiled=True,
    )
    return returned.reshape(peer_count * slot_count, -1), placed


def on_device(
    node_table,
    owners,
    local_rows,
    inner_neighbours,
    inner_counts,
    outer_neighbours,
    outer_counts,
    labels,
    label_mask,
    weight_inner,
    weight_outer,
    weight_head,
    biases,
    first_inner,
    first_outer,
    first_head,
    first_biases,
    second_inner,
    second_outer,
    second_head,
    second_biases,
    smooth_inner,
    smooth_outer,
    smooth_head,
    smooth_biases,
):
    at = lax.axis_index("section")
    every = ("section", "dp")
    hidden = weight_inner.shape[1]
    dest_count, fan_inner = inner_neighbours.shape[1:]
    seed_count, fan_outer = outer_neighbours.shape[1:]
    classes = weight_head.shape[1]
    whole_mask = label_mask
    mask_sizes = label_mask.shape

    def mine(array):
        return lax.dynamic_index_in_dim(array, at, 0, keepdims=False)

    inner_neighbours, inner_counts = mine(inner_neighbours), mine(inner_counts)
    outer_neighbours, outer_counts = mine(outer_neighbours), mine(outer_counts)
    labels, label_mask = mine(labels), mine(label_mask)
    bias_inner = biases[:hidden]
    bias_outer = biases[hidden : 2 * hidden]
    bias_head = biases[2 * hidden :]

    owner_ids, row_ids = owners.reshape(-1), local_rows.reshape(-1)
    weights = (weight_inner, weight_outer, weight_head)
    keep = jnp.arange(fan_inner)[None, :] < inner_counts[:, None]
    if on_slice_kernels(
        node_table,
        owner_ids,
        dest_count,
        fan_inner,
        hidden,
        classes,
        seed_count,
        fan_outer,
        mask_sizes,
        [weight.shape[0] for weight in weights],
    ):
        place = (owner_ids * node_table.shape[0] + row_ids).reshape(-1, 128).T
        own = jnp.arange(dest_count, dtype=jnp.int32)[:, None]
        near = jnp.concatenate([jnp.where(keep, inner_neighbours, -1), own], axis=1)
        near = near.reshape(-1, BLOCK * SLOT)
        firsts = (first_inner, first_outer, first_head)
        seconds = (second_inner, second_outer, second_head)
        smooths = (smooth_inner, smooth_outer, smooth_head)
        rows = [weight.shape[0] for weight in weights]
        keep_outer = jnp.arange(fan_outer)[None, :] < outer_counts[:, None]
        seed_table = jnp.concatenate(
            [
                jnp.where(keep_outer, outer_neighbours, -1),
                labels[:, None],
                label_mask[:, None],
                jnp.zeros((seed_count, SLOT - fan_outer - 2), jnp.int32),
            ],
            axis=1,
        )
        sums = summed_step(
            fan_outer,
            node_table,
            weights,
            firsts,
            seconds,
            biases,
            whole_mask,
            place,
            near,
            seed_table,
        )
        loss, count, clip, norms, news, moment, square, average, bias_outs = finished(
            (classes, *rows),
            sums,
            weights,
            firsts,
            seconds,
            smooths,
            (biases, first_biases, second_biases, smooth_biases),
        )
        return (
            loss.reshape(()),
            count.reshape(()),
            clip.reshape(()),
            norms,
            *news,
            bias_outs[0],
            *moment,
            bias_outs[1],
            *square,
            bias_outs[2],
            *average,
            bias_outs[3],
        )

    label_part = jnp.sum(whole_mask.astype(jnp.float32))
    label_count = jnp.maximum(lax.psum(label_part, "dp"), 1.0)
    full_inner, full_outer, full_head = (
        lax.all_gather(weight.astype(jnp.bfloat16), every, axis=0, tiled=True)
        for weight in weights
    )
    source, place = gathered_rows(node_table, owner_ids, row_ids)
    rows = source[place[inner_neighbours]]
    summed = jnp.sum(
        jnp.where(keep[:, :, None], rows, jnp.zeros((), rows.dtype)), axis=1, dtype=jnp.float32
    )
    self_rows = source[place[:dest_count]]
    mean_one = (summed / inner_counts[:, None].astype(jnp.float32)).astype(jnp.bfloat16)
    joined_one = jnp.concatenate([self_rows, mean_one], axis=1)
    pre_one = jnp.dot(joined_one, full_inner, preferred_element_type=jnp.float32) + bias_inner
    hidden_one = jax.nn.silu(pre_one).astype(jnp.bfloat16)

    keep_outer = jnp.arange(fan_outer)[None, :] < outer_counts[:, None]
    pick = jnp.sum(
        (
            jnp.where(keep_outer, outer_neighbours, -1)[:, :, None]
            == jnp.arange(dest_count)[None, None, :]
        ).astype(jnp.float32),
        axis=1,
    ).astype(jnp.bfloat16)
    count_two = outer_counts[:, None].astype(jnp.float32)
    mean_two = (jnp.dot(pick, hidden_one, preferred_element_type=jnp.float32) / count_two).astype(
        jnp.bfloat16
    )
    joined_two = jnp.concatenate([hidden_one[:seed_count], mean_two], axis=1)
    pre_two = jnp.dot(joined_two, full_outer, preferred_element_type=jnp.float32) + bias_outer
    hidden_two = jax.nn.silu(pre_two).astype(jnp.bfloat16)

    logits = jnp.dot(hidden_two, full_head, preferred_element_type=jnp.float32) + bias_head
    shifted = logits - jnp.max(logits, axis=1, keepdims=True)
    log_total = jnp.log(jnp.sum(jnp.exp(shifted), axis=1, keepdims=True))
    chosen = (jnp.arange(classes)[None, :] == labels[:, None]).astype(jnp.float32)
    row_weight = label_mask.astype(jnp.float32)
    loss_part = jnp.sum((log_total[:, 0] - jnp.sum(shifted * chosen, axis=1)) * row_weight)
    grad_logits = (
        (jnp.exp(shifted - log_total) - chosen) * (row_weight / label_count)[:, None]
    ).astype(jnp.bfloat16)
    grad_head = outer_product(hidden_two, grad_logits)
    grad_two = against(grad_logits, full_head).astype(jnp.bfloat16).astype(jnp.float32)
    grad_pre_two = silu_slope(pre_two, grad_two)
    grad_outer = outer_product(joined_two, grad_pre_two)
    grad_joined = against(grad_pre_two, full_outer)
    share = grad_joined[:, hidden:] / count_two
    share_high = share.astype(jnp.bfloat16)
    share_low = (share - share_high.astype(jnp.float32)).astype(jnp.bfloat16)
    grad_one = outer_product(pick, share_high) + outer_product(pick, share_low)
    grad_one = jnp.concatenate(
        [grad_one[:seed_count] + grad_joined[:, :hidden], grad_one[seed_count:]], axis=0
    )
    grad_one = grad_one.astype(jnp.bfloat16).astype(jnp.float32)
    grad_pre_one = silu_slope(pre_one, grad_one)
    grad_inner = outer_product(joined_one, grad_pre_one)
    bias_part = jnp.concatenate(
        [
            jnp.sum(part.astype(jnp.float32), axis=0)
            for part in (grad_pre_one, grad_pre_two, grad_logits)
        ]
    )

    devices = lax.axis_size(every)
    grads = jnp.concatenate(
        [grad.reshape(devices, -1) for grad in (grad_inner, grad_outer, grad_head)], axis=1
    )
    shard = lax.psum_scatter(grads, every, scatter_dimension=0, tiled=True).reshape(-1)
    shards = []
    for weight in weights:
        shards.append(shard[: weight.size].reshape(weight.shape))
        shard = shard[weight.size :]
    packed = lax.psum(jnp.concatenate([bias_part, loss_part[None]]), every)
    bias_grad, loss_sum = packed[:-1], packed[-1]
    grad_partial = sum((jnp.sum(part * part) for part in shards))
    weight_partial = [jnp.sum(weight * weight) for weight in weights]
    squares = lax.psum(jnp.stack([grad_partial] + weight_partial), every)
    clip_norm = jnp.sqrt(squares[0] + jnp.sum(bias_grad * bias_grad))
    factor = jnp.minimum(1.0, CLIP / clip_norm)
    firsts = (first_inner, first_outer, first_head)
    seconds = (second_inner, second_outer, second_head)
    smooths = (smooth_inner, smooth_outer, smooth_head)
    states = [
        moments(weights[slot_at], shards[slot_at] * factor, firsts[slot_at], seconds[slot_at])
        for slot_at in range(3)
    ]
    update_square = lax.psum(jnp.stack([jnp.sum(state[2] * state[2]) for state in states]), every)
    weight_norms = jnp.sqrt(squares[1:])
    update_norms = jnp.sqrt(update_square)
    news = [
        weights[slot_at]
        - RATE * (weight_norms[slot_at] / update_norms[slot_at]) * states[slot_at][2]
        for slot_at in range(3)
    ]
    averages = [
        AVERAGE * smooths[slot_at] + (1.0 - AVERAGE) * news[slot_at] for slot_at in range(3)
    ]
    bias_first, bias_second, bias_update = moments(
        biases, bias_grad * factor, first_biases, second_biases
    )
    bias_new = biases - RATE * bias_ratio(biases, bias_update, hidden) * bias_update
    bias_average = AVERAGE * smooth_biases + (1.0 - AVERAGE) * bias_new
    return (
        loss_sum,
        label_count,
        clip_norm,
        jnp.stack([weight_norms, update_norms], axis=1),
        news[0],
        news[1],
        news[2],
        bias_new,
        states[0][0],
        states[1][0],
        states[2][0],
        bias_first,
        states[0][1],
        states[1][1],
        states[2][1],
        bias_second,
        averages[0],
        averages[1],
        averages[2],
        bias_average,
    )


def solution(mesh):
    in_specs = (
        P("dp", None),
        P("section", "dp", None),
        P("section", "dp"),
        P(None, "dp", None),
        P(None, "dp"),
        P(None, "dp", None),
        P(None, "dp"),
        P(None, "dp"),
        P(None, "dp"),
        P(("section", "dp"), None),
        P(("section", "dp"), None),
        P(("section", "dp"), None),
        P(),
        P(("section", "dp"), None),
        P(("section", "dp"), None),
        P(("section", "dp"), None),
        P(),
        P(("section", "dp"), None),
        P(("section", "dp"), None),
        P(("section", "dp"), None),
        P(),
        P(("section", "dp"), None),
        P(("section", "dp"), None),
        P(("section", "dp"), None),
        P(),
    )
    out_specs = (
        P(),
        P(),
        P(),
        P(),
        P(("section", "dp"), None),
        P(("section", "dp"), None),
        P(("section", "dp"), None),
        P(),
        P(("section", "dp"), None),
        P(("section", "dp"), None),
        P(("section", "dp"), None),
        P(),
        P(("section", "dp"), None),
        P(("section", "dp"), None),
        P(("section", "dp"), None),
        P(),
        P(("section", "dp"), None),
        P(("section", "dp"), None),
        P(("section", "dp"), None),
        P(),
    )
    return jax.shard_map(
        on_device, mesh=mesh, in_specs=in_specs, out_specs=out_specs, check_vma=False
    )
```

```python
import functools

import jax
import jax.numpy as jnp
from jax import lax
from jax.experimental import pallas as pl
from jax.experimental.pallas import tpu as pltpu
from jax.sharding import PartitionSpec as P

STEP = 5


BETA_ONE = 0.9
BETA_TWO = 0.999
EPSILON = 1e-06
DECAY = 0.01
RATE = 0.25
CLIP = 0.05
AVERAGE = 0.9


VMEM_TABLE_LIMIT = 36 * 2**20
WHOLE_TABLE_LIMIT = 64 * 2**20
MESH = pl.DeviceIdType.MESH
SLOT = 16
BLOCK = 16
CHUNKS = 4
GROUP = 4
SETS = 4
SPARE = 8
AHEAD = 1
AHEAD_ACROSS = 1
LAG = 2
FAR_LAG = 5
SPARE_AFTER = 2
SPARE_LAG = 4
TILE = 256
PAUSE = 6
FORWARD_SLOT = 2


class Parts:
    def __init__(self, refs, base):
        self.grads, self.half_in, self.half, self.plane_in, self.fourth, self.line_in = refs
        self.base = base


def step_kernel(
    fan_outer,
    table_ref,
    weight_refs,
    first_refs,
    second_refs,
    bias_ref,
    mask_ref,
    owner_ref,
    local_ref,
    near_ref,
    seed_near_ref,
    seed_count_ref,
    label_ref,
    out_ref,
    joined_ref,
    weights_ref,
    hits_ref,
    hits_back_ref,
    full_ref,
    packed,
    parts,
    idx_ref,
    mix_ref,
    wide,
    seed_ref,
    seed_across_ref,
    stages,
    lists,
    full_inner_ref,
    full_outer_ref,
    full_head_ref,
    count_ref,
    first_pre,
    first_hidden,
    own_part,
    inner_sum,
    early_refs,
    late_refs,
    extra_ref,
    extra_plane,
    extra_line,
    sums,
    own_sem,
    z_sem,
    spare_sem,
    x_sem,
    y_sem,
    far_sem,
    twin_sem,
    twin_own_sem,
    double_sem,
    send_sem,
    double_send_sem,
    list_sem,
    sum_sem,
    sum_send_sem,
):
    section, at = lax.axis_index("section"), lax.axis_index("dp")
    z, core = at // 2, at % 2
    flipped = z // 2
    height = z + flipped * (3 - 2 * z)
    pairs = table_ref.shape[0]
    spare = pairs // SPARE
    quarter = (pairs - spare) // 4
    chunk = quarter // CHUNKS
    spare_chunk = spare // CHUNKS

    def level(value):
        return value + flipped * (3 - 2 * value)

    twin = (section, z * 2 + 1 - core)
    beside_x = (section + 1 - 2 * (section % 2), at)
    beside_y = (section + 2 - 4 * (section // 2), at)
    inner_z = (section, level(1 - height) * 2 + core)
    across_z = (section, level(2) * 2 + core)
    outer_z = (section, level(0) * 2 + core)
    skip_z = (section, ((z + 2) % 4) * 2 + core)
    sources = [level(1 - height), level(2), level(3)]
    crosses = height == 1
    plane = [((section + k) % 4, at) for k in range(1, 4)]
    beyond = [((section + k) % 4, z * 2 + 1 - core) for k in range(1, 4)]
    line = [(section, ((z + k) % 4) * 2 + core) for k in range(1, 4)]
    neighbours = [twin] + plane + beyond

    barrier = pltpu.get_barrier_semaphore()
    others = [((section + k // 8) % 4, (at + k % 8) % 8) for k in range(1, 32)]
    for partner in others:
        pl.semaphore_signal(barrier, inc=1, device_id=partner, device_id_type=MESH)
    pl.semaphore_wait(barrier, 31)

    sent = []

    def region(shard, part, piece):
        return full_ref.at[pl.ds(shard * pairs + part * quarter + piece * chunk, chunk)]

    def spare_region(shard, piece):
        return full_ref.at[pl.ds(shard * pairs + 4 * quarter + piece * spare_chunk, spare_chunk)]

    def send(source, target, recv, device, when=None):
        number = len(sent)
        copy = pltpu.make_async_remote_copy(
            src_ref=source,
            dst_ref=target,
            send_sem=send_sem.at[number],
            recv_sem=recv,
            device_id=device,
            device_id_type=MESH,
        )
        sent.append((copy, when))
        if when is None:
            copy.start()
        else:
            pl.when(when)(copy.start)
        return copy

    def arrived(target, recv):
        pltpu.make_async_copy(target, target, recv).wait()

    def own_piece(piece, device, number, when=None):
        block = table_ref.at[pl.ds(section * quarter + piece * chunk, chunk)]
        send(block, region(at, section, piece), z_sem.at[number], device, when)

    for piece in range(min(AHEAD, CHUNKS)):
        own_piece(piece, inner_z, piece)
    for piece in range(min(AHEAD_ACROSS, CHUNKS)):
        own_piece(piece, across_z, CHUNKS + piece, crosses)
    whole = full_ref.at[pl.ds(at * pairs, pairs)]
    own = pltpu.make_async_copy(table_ref, whole, own_sem)
    own.start()
    send(table_ref, whole, twin_own_sem, twin)

    inner_ref, outer_ref, head_ref = weight_refs
    row_inner, row_outer, row_head = (ref.shape[0] for ref in weight_refs)
    hidden, classes = inner_ref.shape[1], head_ref.shape[1]
    head_at = row_inner + row_outer
    packed[0:row_inner, :] = inner_ref[...]
    packed[row_inner:head_at, :] = outer_ref[...]
    packed[head_at:, :] = jnp.zeros((row_head, hidden), jnp.float32)
    packed[head_at:, 0:classes] = head_ref[...]
    labelled = jnp.sum(mask_ref[...].astype(jnp.float32)).astype(jnp.int32)
    lane = lax.broadcasted_iota(jnp.int32, (1, hidden), 1)
    high_part = (labelled // 256).astype(jnp.float32)
    low_part = (labelled % 256).astype(jnp.float32)
    tail = jnp.where(lane == classes, high_part, jnp.where(lane == classes + 1, low_part, 0.0))
    packed[head_at : head_at + 1, :] += tail
    mine = (core * 4 + section) * 4 + z
    weights_ref[mine] = packed[...].astype(jnp.bfloat16)
    doubling = [(inner_z, 1), (skip_z, 2), (beside_x, 4), (beside_y, 8), (twin, 16)]
    doubled = []

    def double_start(number):
        device, size = doubling[number]
        block = weights_ref.at[pl.ds((mine // size) * size, size)]
        copy = pltpu.make_async_remote_copy(
            src_ref=block,
            dst_ref=block,
            send_sem=double_send_sem.at[number],
            recv_sem=double_sem.at[number],
            device_id=device,
            device_id_type=MESH,
        )
        copy.start()
        doubled.append(copy)

    double_start(0)

    def eye(size):
        same_place = lax.broadcasted_iota(jnp.int32, (size, size), 0) == lax.broadcasted_iota(
            jnp.int32, (size, size), 1
        )
        return same_place.astype(jnp.float32).astype(jnp.bfloat16)

    def as_low(values):
        return values.astype(jnp.float32).astype(jnp.bfloat16)

    placed = owner_ref[...] * (2 * pairs) + local_ref[...]
    pair_at = placed // 2
    high = owner_ref.shape[0]
    for k, values in enumerate((pair_at % 256, pair_at // 256, placed % 2)):
        parts[128 * k : 128 * (k + 1), :] = against(eye(128), as_low(values)).astype(jnp.bfloat16)
    looked_rows = near_ref.shape[0]
    seeds = seed_ref.shape[0]
    tiles = hits_ref.shape[1] // TILE
    seed_row = pl.ds(section, 1)
    live_seeds = seed_count_ref[seed_row, :]
    for j in range(fan_outer):
        near_seeds = seed_near_ref[j, seed_row, :]
        seed_across_ref[j : j + 1, :] = jnp.where(live_seeds > j, near_seeds, -1)
    seed_across_ref[fan_outer : fan_outer + 1, :] = label_ref[seed_row, :]
    seed_across_ref[fan_outer + 1 : fan_outer + 2, :] = mask_ref[seed_row, :]
    seed_across_ref[fan_outer + 2 :, :] = jnp.zeros((SLOT - fan_outer - 2, seeds), jnp.int32)
    shifted_up = seed_across_ref[...] + 1
    seed_ref[...] = (
        64.0 * against(eye(seeds), as_low(shifted_up // 64))
        + against(eye(seeds), as_low(shifted_up % 64))
    ).astype(jnp.int32) - 1
    total = 3 * CHUNKS
    steps = total + max(FAR_LAG, SPARE_LAG)
    per_step = -(-looked_rows // (8 * steps)) * 8
    for j in range(fan_outer):
        wide[j] = jnp.broadcast_to(seed_ref[:, j : j + 1], (seeds, TILE))

    def look_up(first, last):
        def rows_of(block, carry):
            start_at = pl.multiple_of(block * 8, 8)
            sub = lax.broadcasted_iota(jnp.int32, (high, 256), 0)
            low_at = lax.broadcasted_iota(jnp.int32, (128, 256), 0)
            row = lax.broadcasted_iota(jnp.int32, (256, 512), 0)
            column = lax.broadcasted_iota(jnp.int32, (256, 512), 1)
            for k in range(8):
                node = near_ref[pl.ds(start_at + k, 1), :]
                hot = (sub == node // 128).astype(jnp.float32).astype(jnp.bfloat16)
                got = jnp.dot(parts[...], hot, preferred_element_type=jnp.float32)
                chosen = low_at == node % 128
                found = jnp.where(chosen, got[0:128] + 256.0 * got[128:256], 0.0)
                odd = jnp.where(chosen, got[256:384], 0.0)
                entry_at = jnp.sum(found, axis=0, keepdims=True).astype(jnp.int32)
                idx_ref[block * 2 + k // 4, k % 4 : k % 4 + 1, :] = jnp.clip(
                    entry_at, 0, full_ref.shape[0] - 1
                )
                mix_ref[pl.ds(start_at + k, 1), 0:256] = jnp.sum(odd, axis=0, keepdims=True)
            odd = mix_ref[pl.ds(start_at, 8), 0:256]
            live = (near_ref[pl.ds(start_at, 8), :] >= 0).astype(jnp.float32)
            mix_ref[pl.ds(start_at, 8), :] = jnp.dot(
                (live * (1.0 - odd)).astype(jnp.bfloat16),
                (column == 2 * row).astype(jnp.float32).astype(jnp.bfloat16),
                preferred_element_type=jnp.float32,
            ) + jnp.dot(
                (live * odd).astype(jnp.bfloat16),
                (column == 2 * row + 1).astype(jnp.float32).astype(jnp.bfloat16),
                preferred_element_type=jnp.float32,
            )
            return carry

        lax.fori_loop(first // 8, last // 8, rows_of, 0)

    def mark(tile):
        start_at = tile * TILE
        dest = lax.broadcasted_iota(jnp.int32, (seeds, TILE), 1) + start_at
        hits = jnp.zeros((seeds, TILE), jnp.float32)
        for j in range(fan_outer):
            hits = hits + (wide[j] == dest).astype(jnp.float32)
        hits_ref[:, start_at : start_at + TILE] = hits.astype(jnp.bfloat16)
        dest = lax.broadcasted_iota(jnp.int32, (TILE, seeds), 0) + start_at
        hits = jnp.zeros((TILE, seeds), jnp.float32)
        for j in range(fan_outer):
            hits = hits + (seed_across_ref[j : j + 1, :] == dest).astype(jnp.float32)
        hits_back_ref[start_at : start_at + TILE, :] = hits.astype(jnp.bfloat16)

    def sort_weights():
        everyone = weights_ref[...].astype(jnp.float32)
        order = block_order()
        inner, outer, head = (
            jnp.concatenate([everyone[spot, lower:upper] for spot in order], axis=0)
            for lower, upper in ((0, row_inner), (row_inner, head_at), (head_at, head_at + row_head))
        )
        full_inner_ref[...] = inner.astype(jnp.bfloat16)
        full_outer_ref[...] = outer.astype(jnp.bfloat16)
        full_head_ref[...] = jnp.where(lane < classes, head, 0.0).astype(jnp.bfloat16)
        tails = everyone[0:4, head_at : head_at + 1] + everyone[16:20, head_at : head_at + 1]
        tails = jnp.sum(tails.reshape(4, hidden), axis=0, keepdims=True)
        scale = jnp.where(lane == classes, 256.0, jnp.where(lane == classes + 1, 1.0, 0.0))
        count = jnp.sum(tails * scale, axis=1, keepdims=True)
        count_ref[...] = jnp.broadcast_to(jnp.maximum(count, 1.0), count_ref.shape)

    twins = []

    def to_twin(block, number):
        send(block, block, twin_sem.at[number], twin)
        twins.append(number)

    for step in range(steps):
        if step < total:
            turn, piece = divmod(step, CHUNKS)
            shard = sources[turn] * 2 + core
            goes, number = (across_z, 2 * CHUNKS + piece) if turn == 0 else (outer_z, step)
            block = region(shard, section, piece)
            arrived(block, z_sem.at[step])
            send(block, block, z_sem.at[number], goes, crosses)
            send(block, block, x_sem.at[step], beside_x)
            send(block, block, y_sem.at[step], beside_y)
            to_twin(block, step)
            if step + AHEAD < CHUNKS:
                own_piece(step + AHEAD, inner_z, step + AHEAD)
            if step + AHEAD_ACROSS < CHUNKS:
                piece = step + AHEAD_ACROSS
                own_piece(piece, across_z, CHUNKS + piece, crosses)
            piece = step - SPARE_AFTER
            if 0 <= piece < CHUNKS:
                block = table_ref.at[pl.ds(4 * quarter + piece * spare_chunk, spare_chunk)]
                goal = spare_region(at, piece)
                send(block, goal, spare_sem.at[piece], inner_z)
                send(block, goal, spare_sem.at[CHUNKS + piece], across_z, crosses)
        late = step - SPARE_LAG
        if 0 <= late < total:
            turn, piece = divmod(late, CHUNKS)
            shard = sources[turn] * 2 + core
            goes, number = (across_z, 2 * CHUNKS + piece) if turn == 0 else (outer_z, late)
            block = spare_region(shard, piece)
            arrived(block, spare_sem.at[late])
            send(block, block, spare_sem.at[number], goes, crosses)
            to_twin(block, 4 * total + late)
        late = step - LAG
        if 0 <= late < total:
            turn, piece = divmod(late, CHUNKS)
            shard = sources[turn] * 2 + core
            block = region(shard, beside_x[0], piece)
            arrived(block, x_sem.at[late])
            send(block, block, far_sem.at[late], beside_y, core == piece % 2)
            to_twin(block, total + late)
            block = region(shard, beside_y[0], piece)
            arrived(block, y_sem.at[late])
            send(block, block, far_sem.at[late], beside_x, core != piece % 2)
            to_twin(block, 2 * total + late)
        later = step - FAR_LAG
        if 0 <= later < total:
            turn, piece = divmod(later, CHUNKS)
            shard = sources[turn] * 2 + core
            block = region(shard, 3 - section, piece)
            arrived(block, far_sem.at[later])
            to_twin(block, 3 * total + later)
        if step % 2 == 0 and step // 2 < len(doubling):
            doubled[step // 2].wait()
            if step // 2 + 1 < len(doubling):
                double_start(step // 2 + 1)
        first = min(step * per_step, looked_rows)
        last = min(first + per_step, looked_rows)
        if last > first:
            look_up(first, last)
        for tile in range(step * tiles // steps, (step + 1) * tiles // steps):
            mark(tile)

    sort_weights()
    for number in sorted(twins):
        kind, step = divmod(number, total)
        turn, piece = divmod(step, CHUNKS)
        shard = sources[turn] * 2 + 1 - core
        if kind == 4:
            block = spare_region(shard, piece)
        else:
            block = region(shard, (section, beside_x[0], beside_y[0], 3 - section)[kind], piece)
        arrived(block, twin_sem.at[number])
    arrived(full_ref.at[pl.ds((z * 2 + 1 - core) * pairs, pairs)], twin_own_sem)
    own.wait()

    blocks = looked_rows
    unit_at = lax.broadcasted_iota(jnp.int32, (BLOCK, 2 * BLOCK * SLOT), 1)
    same = unit_at // (2 * SLOT) == lax.broadcasted_iota(jnp.int32, unit_at.shape, 0)
    near_part = jnp.logical_and(same, unit_at % (2 * SLOT) < 2 * SLOT - 2).astype(jnp.float32)
    self_part = jnp.logical_and(same, unit_at % (2 * SLOT) >= 2 * SLOT - 2).astype(jnp.float32)
    turns = blocks // GROUP

    def fetch(turn, slot):
        return pltpu.make_async_copy(
            idx_ref.at[jnp.minimum(turn, turns - 1)], lists[slot], list_sem.at[slot]
        )

    def pick(member, slot, stage):
        def unit(number, carry):
            entry = full_ref[lists[slot][member, number]]
            stage[pl.ds(2 * number, 2), :] = entry.astype(jnp.float32)
            return carry

        lax.fori_loop(0, BLOCK * SLOT, unit, 0, unroll=BLOCK * SLOT)

    def reduce(block, stage):
        mix = mix_ref[pl.ds(block, 1), :]
        near = mix * near_part
        left = jnp.concatenate([near, mix * self_part], axis=0).astype(jnp.bfloat16)
        out = jnp.dot(left, stage[...].astype(jnp.bfloat16), preferred_element_type=jnp.float32)
        count = jnp.maximum(jnp.sum(near, axis=1, keepdims=True), 1.0)
        both = jnp.concatenate([out[BLOCK:], out[:BLOCK] / count], axis=1)
        start_at = pl.multiple_of(block * BLOCK, BLOCK)
        joined_ref[pl.ds(start_at, BLOCK), :] = both.astype(jnp.bfloat16)

    bias_inner, bias_outer, bias_head = bias_rows_of(bias_ref, hidden)

    def forward(tile):
        tile_rows = pl.ds(pl.multiple_of(tile * TILE, TILE), TILE)
        before = (
            jnp.dot(
                joined_ref[tile_rows, :], full_inner_ref[...], preferred_element_type=jnp.float32
            )
            + bias_inner
        )
        first_pre[tile_rows, :] = before
        first_hidden[tile_rows, :] = (before * lax.logistic(before)).astype(jnp.bfloat16)

    near_stages, far_stages = stages
    joined_ref[0:TILE, :] = jnp.zeros((TILE, joined_ref.shape[1]), jnp.bfloat16)
    for slot in range(SETS):
        fetch(slot, slot).start()
    for member in range(GROUP):
        far_stages[member][...] = jnp.zeros(far_stages[member].shape, jnp.float32)

    def round_of(number, carry):
        for slot in range(SETS):
            turn = number * SETS + slot
            fetch(turn, slot).wait()
            for member in range(GROUP):
                pick(member, slot, stages[slot % 2][member])
                reduce(
                    jnp.maximum((turn - 1) * GROUP + member, 0), stages[1 - slot % 2][member]
                )
            fetch(turn + SETS, slot).start()
            if slot == FORWARD_SLOT:
                forward(jnp.maximum(number - 1, 0))
        return carry

    lax.fori_loop(0, blocks // (GROUP * SETS), round_of, 0)
    for slot in range(SETS):
        fetch(0, slot).wait()
    for member in range(GROUP):
        reduce(blocks - GROUP + member, stages[(SETS - 1) % 2][member])
    forward(tiles - 1)
    for copy, when in sent:
        if when is None:
            copy.wait_send()
        else:
            pl.when(when)(copy.wait_send)

    summing = []

    def pass_on(source, target, number, device):
        copy = pltpu.make_async_remote_copy(
            src_ref=source,
            dst_ref=target,
            send_sem=sum_send_sem.at[len(summing)],
            recv_sem=sum_sem.at[number],
            device_id=device,
            device_id_type=MESH,
        )
        summing.append(copy)
        copy.start()

    def passed(target, number):
        arrived(target, sum_sem.at[number])

    def to_other_core(part):
        pass_on(part.grads.at[pl.ds((1 - core) * 16, 16)], part.half_in, part.base, twin)

    def to_plane(part):
        passed(part.half_in, part.base)
        part.half[...] = part.grads[pl.ds(core * 16, 16)] + part.half_in[...]
        for partner in plane:
            block = part.half.at[pl.ds(partner[0] * 4, 4)]
            pass_on(block, part.plane_in.at[section], part.base + 1 + section, partner)
        part.plane_in[section] = part.half[pl.ds(section * 4, 4)]

    def to_line(part):
        for k in range(1, 4):
            other = (section + k) % 4
            passed(part.plane_in.at[other], part.base + 1 + other)
        part.fourth[...] = (part.plane_in[0] + part.plane_in[1]) + (
            part.plane_in[2] + part.plane_in[3]
        )
        for k, partner in enumerate(line):
            block = part.fourth.at[pl.ds((z + k + 1) % 4, 1)]
            pass_on(block, part.line_in.at[pl.ds(z, 1)], part.base + 5 + z, partner)
        part.line_in[z] = part.fourth[z]

    def whole_sum(part):
        for k in range(1, 4):
            other = (z + k) % 4
            passed(part.line_in.at[pl.ds(other, 1)], part.base + 5 + other)
        return (part.line_in[0] + part.line_in[1]) + (part.line_in[2] + part.line_in[3])

    def share(value, slots, base, me, partners):
        slots[me] = value
        for partner in partners:
            pass_on(slots.at[me], slots.at[me], base + me, partner)

    def collect(slots, base, me):
        count = slots.shape[0]
        for k in range(1, count):
            other = (me + k) % count
            passed(slots.at[other], base + other)
        values = [slots[k] for k in range(count)]
        while len(values) > 1:
            values = [values[k] + values[k + 1] for k in range(0, len(values), 2)]
        return values[0]

    early, late_part = Parts(early_refs, 0), Parts(late_refs, 9)
    order = block_order()
    full_outer, full_head = full_outer_ref[...], full_head_ref[...]
    label_count = count_ref[:, 0:1]
    kept = seed_ref[:, 0:fan_outer]
    count_two = jnp.sum((kept >= 0).astype(jnp.float32), axis=1, keepdims=True)
    mean_sum = jnp.dot(hits_ref[...], first_hidden[...], preferred_element_type=jnp.float32)
    mean_two = (mean_sum / count_two).astype(jnp.bfloat16)
    joined_two = jnp.concatenate([first_hidden[0:seeds, :], mean_two], axis=1)
    pre_two = jnp.dot(joined_two, full_outer, preferred_element_type=jnp.float32) + bias_outer
    gate_two = lax.logistic(pre_two)
    hidden_two = (pre_two * gate_two).astype(jnp.bfloat16)
    logits = jnp.dot(hidden_two, full_head, preferred_element_type=jnp.float32) + bias_head
    inside = lane < classes
    highest = jnp.max(jnp.where(inside, logits, -jnp.inf), axis=1, keepdims=True)
    shifted = jnp.where(inside, logits - highest, 0.0)
    total_exp = jnp.sum(jnp.where(inside, jnp.exp(shifted), 0.0), axis=1, keepdims=True)
    log_total = jnp.log(total_exp)
    chosen = (lane == seed_ref[:, fan_outer : fan_outer + 1]).astype(jnp.float32)
    row_weight = seed_ref[:, fan_outer + 1 : fan_outer + 2].astype(jnp.float32)
    loss = jnp.sum((log_total - jnp.sum(shifted * chosen, axis=1, keepdims=True)) * row_weight)
    grad_logits = (jnp.exp(shifted - log_total) - chosen) * (row_weight / label_count)
    grad_logits = jnp.where(inside, grad_logits, 0.0).astype(jnp.bfloat16)
    grad_head = outer_product(hidden_two, grad_logits)
    grad_two = against(grad_logits, full_head).astype(jnp.bfloat16).astype(jnp.float32)
    grad_pre_two = (grad_two * gate_two * (1.0 + pre_two * (1.0 - gate_two))).astype(jnp.bfloat16)
    grad_outer = outer_product(joined_two, grad_pre_two)
    for number, spot in enumerate(order):
        early.grads[spot, 0:row_outer, :] = grad_outer[
            number * row_outer : (number + 1) * row_outer
        ]
        early.grads[spot, row_outer : row_outer + row_head, :] = grad_head[
            number * row_head : (number + 1) * row_head
        ]
    to_other_core(early)
    extra_ref[1:2, :] = jnp.sum(grad_pre_two.astype(jnp.float32), axis=0, keepdims=True)
    extra_ref[2:3, :] = jnp.sum(grad_logits.astype(jnp.float32), axis=0, keepdims=True)
    extra_ref[3:4, :] = jnp.where(lane == 0, loss, jnp.where(lane == 1, label_count, 0.0))
    extra_ref[4:8, :] = jnp.zeros((4, hidden), jnp.float32)
    grad_joined = against(grad_pre_two, full_outer)
    share_part = grad_joined[:, hidden:] / count_two
    share_high = share_part.astype(jnp.bfloat16)
    share_low = (share_part - share_high.astype(jnp.float32)).astype(jnp.bfloat16)
    inner_sum[...] = jnp.zeros(inner_sum.shape, jnp.float32)
    share_both = jnp.concatenate([share_high, share_low], axis=0)
    own_part[...] = jnp.zeros(own_part.shape, jnp.float32)
    own_part[0:seeds, :] = grad_joined[:, 0:hidden]

    def backward(tile, bias_sum, own=None):
        tile_rows = pl.ds(pl.multiple_of(jnp.int32(tile) * TILE, TILE), TILE)
        hits = hits_back_ref[tile_rows, :]
        both_hits = jnp.concatenate([hits, hits], axis=1)
        grad_one = jnp.dot(both_hits, share_both, preferred_element_type=jnp.float32)
        if own is not None:
            grad_one = grad_one + own
        grad_one = grad_one.astype(jnp.bfloat16).astype(jnp.float32)
        before = first_pre[tile_rows, :]
        gate = lax.logistic(before)
        grad_pre = (grad_one * gate * (1.0 + before * (1.0 - gate))).astype(jnp.bfloat16)
        inner_sum[...] += outer_product(joined_ref[tile_rows, :], grad_pre)
        return bias_sum + jnp.sum(grad_pre.astype(jnp.float32), axis=0, keepdims=True)

    bias_sum = backward(0, jnp.zeros((1, hidden), jnp.float32), own_part[...])
    bias_sum = lax.fori_loop(1, PAUSE, backward, bias_sum)
    to_plane(early)
    bias_sum = lax.fori_loop(PAUSE, tiles, backward, bias_sum)
    extra_ref[0:1, :] = bias_sum
    grad_inner = inner_sum[...]
    for number, spot in enumerate(order):
        late_part.grads[spot] = grad_inner[number * row_inner : (number + 1) * row_inner]
    to_other_core(late_part)
    share(extra_ref[...], extra_plane, 18, section * 2 + core, neighbours)
    to_plane(late_part)
    to_line(early)
    share(collect(extra_plane, 18, section * 2 + core), extra_line, 26, z, line)
    to_line(late_part)

    short_lane = lax.broadcasted_iota(jnp.int32, (1, 128), 1)
    my_number = section * 8 + at

    def square_sum(value):
        return jnp.sum(jnp.sum(value * value, axis=0, keepdims=True), axis=1, keepdims=True)

    def everywhere(values, number):
        base = 30 + 32 * number
        found = jnp.zeros((1, 128), jnp.float32)
        for k, value in enumerate(values):
            found = jnp.where(short_lane == k, value, found)
        sums[number, my_number] = found
        for partner in others:
            mine_there = sums.at[number, my_number]
            pass_on(mine_there, mine_there, base + my_number, partner)
        for partner in others:
            other = partner[0] * 8 + partner[1]
            passed(sums.at[number, other], base + other)
        return jnp.sum(sums[number], axis=0)

    held = [ref[...] for ref in weight_refs]
    weight_squares = [square_sum(weight) for weight in held]
    rest = whole_sum(early)
    shard = whole_sum(late_part)
    extra = collect(extra_line, 26, z)
    pieces = [shard, rest[0:row_outer], rest[row_outer:, 0:classes]]
    values = everywhere([square_sum(shard) + square_sum(rest)] + weight_squares, 0)
    grad_square = jnp.sum(jnp.where(short_lane == 0, values, 0.0), axis=1, keepdims=True)
    clip_norm = jnp.sqrt(grad_square + square_sum(extra[0:3]))
    factor = jnp.minimum(1.0, CLIP / clip_norm)
    update_squares = []
    for k in range(3):
        update = moments(held[k], pieces[k] * factor, first_refs[k][...], second_refs[k][...])[2]
        update_squares.append(square_sum(update))
    updates = everywhere(update_squares, 1)
    rows = row_inner + row_outer + row_head
    out_ref[0:row_inner, :] = shard
    out_ref[row_inner:rows, :] = rest
    out_ref[rows : rows + 8, :] = extra
    out_ref[rows + 8 : rows + 9, 0:128] = values
    out_ref[rows + 8 : rows + 9, 128:256] = updates
    out_ref[rows + 9 :, :] = jnp.zeros((7, hidden), jnp.float32)
    for copy in summing:
        copy.wait_send()


def block_order():
    return [(e % 2) * 16 + (e // 8) * 4 + (e % 8) // 2 for e in range(32)]


def bias_rows_of(ref, hidden):
    width = ref.shape[0] - 2 * hidden
    last = ref[pl.ds(2 * hidden, width)].reshape(1, width)
    return (
        ref[pl.ds(0, hidden)].reshape(1, hidden),
        ref[pl.ds(hidden, hidden)].reshape(1, hidden),
        jnp.concatenate([last, jnp.zeros((1, hidden - width), jnp.float32)], axis=1),
    )


def summed_step(
    node_table,
    weights,
    firsts,
    seconds,
    biases,
    label_mask,
    owner_ids,
    row_ids,
    near,
    outer_neighbours,
    outer_counts,
    labels,
):
    devices = lax.axis_size(("section", "dp"))
    table_rows, width = node_table.shape
    frontier_high = owner_ids.size // 128
    fan_outer = outer_neighbours.shape[2]
    looked = near.shape[0]
    dest_count = looked * BLOCK
    seeds = outer_neighbours.shape[1]
    hidden = weights[0].shape[1]
    row_inner = weights[0].shape[0]
    rows = sum(weight.shape[0] for weight in weights)
    total = 3 * CHUNKS
    sends = 4 * CHUNKS + 1 + 3 * total + total + 2 * total + 5 * total
    vmem = pl.BlockSpec(memory_space=pltpu.VMEM)
    stage = (pltpu.VMEM((2 * BLOCK * SLOT, width), jnp.float32),) * GROUP

    def on_the_way(depth):
        return (
            pltpu.VMEM((devices, depth, hidden), jnp.float32),
            pltpu.VMEM((16, depth, hidden), jnp.float32),
            pltpu.VMEM((16, depth, hidden), jnp.float32),
            pltpu.VMEM((4, 4, depth, hidden), jnp.float32),
            pltpu.VMEM((4, depth, hidden), jnp.float32),
            pltpu.VMEM((4, depth, hidden), jnp.float32),
        )

    return pl.pallas_call(
        functools.partial(step_kernel, fan_outer),
        out_shape=jax.ShapeDtypeStruct((rows + 16, hidden), jnp.float32),
        in_specs=[pl.BlockSpec(memory_space=pl.ANY)] + [(vmem,) * 3] * 3 + [vmem] * 8,
        out_specs=vmem,
        scratch_shapes=[
            pltpu.VMEM((dest_count, 2 * width), jnp.bfloat16),
            pltpu.VMEM((devices, rows, hidden), jnp.bfloat16),
            pltpu.VMEM((seeds, dest_count), jnp.bfloat16),
            pltpu.VMEM((dest_count, seeds), jnp.bfloat16),
            pltpu.VMEM((lax.axis_size("dp") * table_rows // 2, 2, width), jnp.bfloat16),
            pltpu.VMEM((rows, hidden), jnp.float32),
            pltpu.VMEM((384, frontier_high), jnp.bfloat16),
            pltpu.VMEM((looked // GROUP, GROUP, 256), jnp.int32),
            pltpu.VMEM((looked, 512), jnp.float32),
            pltpu.VMEM((fan_outer, seeds, TILE), jnp.int32),
            pltpu.VMEM((seeds, SLOT), jnp.int32),
            pltpu.VMEM((SLOT, seeds), jnp.int32),
            (stage, stage),
            (pltpu.SMEM((GROUP, BLOCK * SLOT), jnp.int32),) * SETS,
            pltpu.VMEM((hidden, hidden), jnp.bfloat16),
            pltpu.VMEM((2 * hidden, hidden), jnp.bfloat16),
            pltpu.VMEM((hidden, hidden), jnp.bfloat16),
            pltpu.VMEM((1, hidden), jnp.float32),
            pltpu.VMEM((dest_count, hidden), jnp.float32),
            pltpu.VMEM((dest_count, hidden), jnp.bfloat16),
            pltpu.VMEM((TILE, hidden), jnp.float32),
            pltpu.VMEM((hidden, hidden), jnp.float32),
            on_the_way(rows - row_inner),
            on_the_way(row_inner),
            pltpu.VMEM((8, hidden), jnp.float32),
            pltpu.VMEM((8, 8, hidden), jnp.float32),
            pltpu.VMEM((4, 8, hidden), jnp.float32),
            pltpu.VMEM((2, devices, 1, 128), jnp.float32),
            pltpu.SemaphoreType.DMA(()),
            pltpu.SemaphoreType.DMA((total,)),
            pltpu.SemaphoreType.DMA((total,)),
            pltpu.SemaphoreType.DMA((total,)),
            pltpu.SemaphoreType.DMA((total,)),
            pltpu.SemaphoreType.DMA((total,)),
            pltpu.SemaphoreType.DMA((5 * total,)),
            pltpu.SemaphoreType.DMA(()),
            pltpu.SemaphoreType.DMA((5,)),
            pltpu.SemaphoreType.DMA((sends,)),
            pltpu.SemaphoreType.DMA((5,)),
            pltpu.SemaphoreType.DMA((SETS,)),
            pltpu.SemaphoreType.DMA((30 + 2 * devices,)),
            pltpu.SemaphoreType.DMA((24 + 2 * (devices - 1),)),
        ],
        compiler_params=pltpu.CompilerParams(
            collective_id=0, has_side_effects=True, vmem_limit_bytes=56 * 2**20
        ),
    )(
        pltpu.with_memory_space_constraint(
            node_table.reshape(table_rows // 2, 2, width), pltpu.HBM
        ),
        weights,
        firsts,
        seconds,
        biases,
        label_mask,
        owner_ids.reshape(-1, 128),
        row_ids.reshape(-1, 128),
        near,
        outer_neighbours.transpose(2, 0, 1),
        outer_counts,
        labels,
    )


def final_kernel(
    sizes,
    devices,
    sums_ref,
    weight_refs,
    first_refs,
    second_refs,
    smooth_refs,
    bias_refs,
    loss_ref,
    count_ref,
    clip_ref,
    norms_ref,
    new_refs,
    moment_refs,
    square_refs,
    average_refs,
    bias_out_refs,
):
    classes, row_inner, row_outer, row_head = sizes
    hidden = sums_ref.shape[1]
    rows = row_inner + row_outer + row_head
    split = (0, row_inner, row_inner + row_outer, rows)
    widths = (hidden, hidden, classes)
    lane = lax.broadcasted_iota(jnp.int32, (1, 128), 1)

    def number(k, start_at):
        found = sums_ref[rows + 8 : rows + 9, start_at : start_at + 128]
        return jnp.sum(jnp.where(lane == k, found, 0.0), axis=1, keepdims=True)

    bias_grad = sums_ref[rows : rows + 3, :]
    bias_square = jnp.sum(jnp.sum(bias_grad * bias_grad, axis=0, keepdims=True), axis=1, keepdims=True)
    clip_norm = jnp.sqrt(number(0, 0) + bias_square)
    factor = jnp.minimum(1.0, CLIP / clip_norm)
    wide = lax.broadcasted_iota(jnp.int32, (8, 128), 1)
    deep = lax.broadcasted_iota(jnp.int32, (8, 128), 0)
    norms = jnp.zeros((8, 128), jnp.float32)
    for k in range(3):
        weight = weight_refs[k][...]
        gradient = sums_ref[split[k] : split[k + 1], 0 : widths[k]] * factor
        first, second, update = moments(weight, gradient, first_refs[k][...], second_refs[k][...])
        weight_norm, update_norm = jnp.sqrt(number(1 + k, 0)), jnp.sqrt(number(k, 128))
        fresh = weight - RATE * (weight_norm / update_norm) * update
        new_refs[k][...] = fresh
        moment_refs[k][...] = first
        square_refs[k][...] = second
        average_refs[k][...] = AVERAGE * smooth_refs[k][...] + (1.0 - AVERAGE) * fresh
        norms = jnp.where(jnp.logical_and(deep == 0, wide == k), weight_norm, norms)
        norms = jnp.where(jnp.logical_and(deep == 1, wide == k), update_norm, norms)
    norms_ref[...] = norms[0:2, 0:3]
    weight, first, second, smooth = (
        jnp.concatenate(bias_rows_of(ref, hidden), axis=0) for ref in bias_refs
    )
    first, second, update = moments(weight, bias_grad * factor, first, second)
    column = lax.broadcasted_iota(jnp.int32, weight.shape, 1)
    row = lax.broadcasted_iota(jnp.int32, weight.shape, 0)
    update = jnp.where(jnp.logical_or(row < 2, column < classes), update, 0.0)
    ratio = jnp.sqrt(jnp.sum(weight * weight, axis=1, keepdims=True)) / jnp.sqrt(
        jnp.sum(update * update, axis=1, keepdims=True)
    )
    fresh = weight - RATE * ratio * update
    average = AVERAGE * smooth + (1.0 - AVERAGE) * fresh
    for ref, value in zip(bias_out_refs, (fresh, first, second, average)):
        ref[pl.ds(0, hidden)] = value[0:1].reshape(hidden)
        ref[pl.ds(hidden, hidden)] = value[1:2].reshape(hidden)
        ref[pl.ds(2 * hidden, classes)] = value[2:3, 0:classes].reshape(classes)
    tail = sums_ref[rows + 3 : rows + 4, 0:128]
    loss_ref[...] = jnp.sum(jnp.where(lane == 0, tail, 0.0), axis=1, keepdims=True)
    count = jnp.sum(jnp.where(lane == 1, tail, 0.0), axis=1, keepdims=True)
    count_ref[...] = count / devices
    clip_ref[...] = clip_norm


def finished(sizes, sums, weights, firsts, seconds, smooths, biases):
    vmem = pl.BlockSpec(memory_space=pltpu.VMEM)
    like = [jax.ShapeDtypeStruct(weight.shape, jnp.float32) for weight in weights]
    scalar = jax.ShapeDtypeStruct((1, 1), jnp.float32)
    return pl.pallas_call(
        functools.partial(final_kernel, sizes, float(lax.axis_size(("section", "dp")))),
        out_shape=(
            scalar,
            scalar,
            scalar,
            jax.ShapeDtypeStruct((2, 3), jnp.float32),
            like,
            like,
            like,
            like,
            [jax.ShapeDtypeStruct(biases[0].shape, jnp.float32)] * 4,
        ),
        in_specs=[vmem] + [(vmem,) * 3] * 4 + [(vmem,) * 4],
        out_specs=(vmem,) * 4 + ([vmem] * 3,) * 4 + ([vmem] * 4,),
    )(sums, weights, firsts, seconds, smooths, biases)


def on_slice_kernels(
    node_table, owner_ids, dest_count, fan_inner, hidden, classes, seed_count, fan_outer, mask_sizes, weight_rows
):
    parts, peers = lax.axis_size("section"), lax.axis_size("dp")
    return (
        parts == 4
        and peers == 8
        and peers * node_table.size * 2 <= VMEM_TABLE_LIMIT
        and node_table.shape[1] == 128
        and node_table.shape[0] % (2 * SPARE * CHUNKS) == 0
        and (node_table.shape[0] // 2 - node_table.shape[0] // 2 // SPARE) % (4 * CHUNKS) == 0
        and peers * node_table.shape[0] <= 131072
        and owner_ids.shape[0] % 1024 == 0
        and owner_ids.shape[0] <= 32768
        and fan_inner == SLOT - 1
        and dest_count % (BLOCK * GROUP * SETS) == 0
        and dest_count % TILE == 0
        and hidden == 256
        and classes + 2 <= hidden
        and seed_count <= TILE
        and seed_count % 128 == 0
        and dest_count < 16384
        and BLOCK * GROUP * SETS == TILE
        and fan_outer + 2 <= SLOT
        and len(mask_sizes) == 2
        and mask_sizes[0] * mask_sizes[1] <= 65536
        and all(rows % 8 == 0 for rows in weight_rows)
        and sum(weight_rows) % 16 == 0
        and dest_count // TILE > PAUSE
    )


def outer_product(left, right):
    return lax.dot_general(
        left, right, (((0,), (0,)), ((), ())), preferred_element_type=jnp.float32
    )


def against(left, right):
    return lax.dot_general(
        left, right, (((1,), (1,)), ((), ())), preferred_element_type=jnp.float32
    )


def silu_slope(before, grad_out):
    sigmoid = jax.nn.sigmoid(before)
    return (grad_out * sigmoid * (1.0 + before * (1.0 - sigmoid))).astype(jnp.bfloat16)


def moments(weight, gradient, first, second):
    first = BETA_ONE * first + (1.0 - BETA_ONE) * gradient
    second = BETA_TWO * second + (1.0 - BETA_TWO) * gradient * gradient
    update = (
        first / (1.0 - BETA_ONE**STEP) / (jnp.sqrt(second / (1.0 - BETA_TWO**STEP)) + EPSILON)
        + DECAY * weight
    )
    return (first, second, update)


def bias_ratio(weight, update, hidden):
    bounds = ((0, hidden), (hidden, 2 * hidden), (2 * hidden, weight.shape[0]))
    pieces = []
    for start_at, stop_at in bounds:
        weight_norm = jnp.sqrt(jnp.sum(weight[start_at:stop_at] ** 2))
        update_norm = jnp.sqrt(jnp.sum(update[start_at:stop_at] ** 2))
        pieces.append(jnp.zeros((stop_at - start_at,), jnp.float32) + weight_norm / update_norm)
    return jnp.concatenate(pieces)


def gathered_rows(node_table, owner_ids, row_ids):
    peer_count = lax.axis_size("dp")
    parts = lax.axis_size("section")
    table_rows = node_table.shape[0]
    if peer_count * node_table.size * 2 <= WHOLE_TABLE_LIMIT and table_rows % parts == 0:
        part_rows = table_rows // parts
        quarter = lax.dynamic_slice_in_dim(
            node_table, lax.axis_index("section") * part_rows, part_rows, 0
        )
        source = lax.all_gather(quarter, ("section", "dp"), axis=0, tiled=True)
        place = (row_ids // part_rows * peer_count + owner_ids) * part_rows + row_ids % part_rows
        return source, place
    frontier_rows = owner_ids.shape[0]
    slot_count = max(2, 2 * frontier_rows // peer_count)
    owner_hot = (owner_ids[:, None] == jnp.arange(peer_count)[None, :]).astype(jnp.int32)
    ranking = jnp.sum((jnp.cumsum(owner_hot, axis=0) - 1) * owner_hot, axis=1)
    placed = owner_ids * slot_count + ranking
    request = (
        jnp.zeros((peer_count * slot_count,), jnp.int32)
        .at[placed]
        .set(row_ids)
        .reshape(peer_count, slot_count)
    )
    returned = lax.all_to_all(
        node_table[lax.all_to_all(request, "dp", split_axis=0, concat_axis=0, tiled=True)],
        "dp",
        split_axis=0,
        concat_axis=0,
        tiled=True,
    )
    return returned.reshape(peer_count * slot_count, -1), placed


def on_device(
    node_table,
    owners,
    local_rows,
    inner_neighbours,
    inner_counts,
    outer_neighbours,
    outer_counts,
    labels,
    label_mask,
    weight_inner,
    weight_outer,
    weight_head,
    biases,
    first_inner,
    first_outer,
    first_head,
    first_biases,
    second_inner,
    second_outer,
    second_head,
    second_biases,
    smooth_inner,
    smooth_outer,
    smooth_head,
    smooth_biases,
):
    at = lax.axis_index("section")
    every = ("section", "dp")
    hidden = weight_inner.shape[1]
    dest_count, fan_inner = inner_neighbours.shape[1:]
    seed_count, fan_outer = outer_neighbours.shape[1:]
    classes = weight_head.shape[1]
    whole_mask, whole_labels = label_mask, labels
    whole_outer, whole_outer_counts = outer_neighbours, outer_counts
    mask_sizes = label_mask.shape

    def mine(array):
        return lax.dynamic_index_in_dim(array, at, 0, keepdims=False)

    inner_neighbours, inner_counts = mine(inner_neighbours), mine(inner_counts)
    outer_neighbours, outer_counts = mine(outer_neighbours), mine(outer_counts)
    labels, label_mask = mine(labels), mine(label_mask)
    bias_inner = biases[:hidden]
    bias_outer = biases[hidden : 2 * hidden]
    bias_head = biases[2 * hidden :]

    owner_ids, row_ids = owners.reshape(-1), local_rows.reshape(-1)
    weights = (weight_inner, weight_outer, weight_head)
    keep = jnp.arange(fan_inner)[None, :] < inner_counts[:, None]
    if on_slice_kernels(
        node_table,
        owner_ids,
        dest_count,
        fan_inner,
        hidden,
        classes,
        seed_count,
        fan_outer,
        mask_sizes,
        [weight.shape[0] for weight in weights],
    ):
        own = jnp.arange(dest_count, dtype=jnp.int32)[:, None]
        near = jnp.concatenate([jnp.where(keep, inner_neighbours, -1), own], axis=1)
        near = near.reshape(-1, BLOCK * SLOT)
        firsts = (first_inner, first_outer, first_head)
        seconds = (second_inner, second_outer, second_head)
        smooths = (smooth_inner, smooth_outer, smooth_head)
        rows = [weight.shape[0] for weight in weights]
        sums = summed_step(
            node_table,
            weights,
            firsts,
            seconds,
            biases,
            whole_mask,
            owner_ids,
            row_ids,
            near,
            whole_outer,
            whole_outer_counts,
            whole_labels,
        )
        loss, count, clip, norms, news, moment, square, average, bias_outs = finished(
            (classes, *rows),
            sums,
            weights,
            firsts,
            seconds,
            smooths,
            (biases, first_biases, second_biases, smooth_biases),
        )
        return (
            loss.reshape(()),
            count.reshape(()),
            clip.reshape(()),
            norms.T,
            *news,
            bias_outs[0],
            *moment,
            bias_outs[1],
            *square,
            bias_outs[2],
            *average,
            bias_outs[3],
        )

    label_part = jnp.sum(whole_mask.astype(jnp.float32))
    label_count = jnp.maximum(lax.psum(label_part, "dp"), 1.0)
    full_inner, full_outer, full_head = (
        lax.all_gather(weight.astype(jnp.bfloat16), every, axis=0, tiled=True)
        for weight in weights
    )
    source, place = gathered_rows(node_table, owner_ids, row_ids)
    rows = source[place[inner_neighbours]]
    summed = jnp.sum(
        jnp.where(keep[:, :, None], rows, jnp.zeros((), rows.dtype)), axis=1, dtype=jnp.float32
    )
    self_rows = source[place[:dest_count]]
    mean_one = (summed / inner_counts[:, None].astype(jnp.float32)).astype(jnp.bfloat16)
    joined_one = jnp.concatenate([self_rows, mean_one], axis=1)
    pre_one = jnp.dot(joined_one, full_inner, preferred_element_type=jnp.float32) + bias_inner
    hidden_one = jax.nn.silu(pre_one).astype(jnp.bfloat16)

    keep_outer = jnp.arange(fan_outer)[None, :] < outer_counts[:, None]
    pick = jnp.sum(
        (
            jnp.where(keep_outer, outer_neighbours, -1)[:, :, None]
            == jnp.arange(dest_count)[None, None, :]
        ).astype(jnp.float32),
        axis=1,
    ).astype(jnp.bfloat16)
    count_two = outer_counts[:, None].astype(jnp.float32)
    mean_two = (jnp.dot(pick, hidden_one, preferred_element_type=jnp.float32) / count_two).astype(
        jnp.bfloat16
    )
    joined_two = jnp.concatenate([hidden_one[:seed_count], mean_two], axis=1)
    pre_two = jnp.dot(joined_two, full_outer, preferred_element_type=jnp.float32) + bias_outer
    hidden_two = jax.nn.silu(pre_two).astype(jnp.bfloat16)

    logits = jnp.dot(hidden_two, full_head, preferred_element_type=jnp.float32) + bias_head
    shifted = logits - jnp.max(logits, axis=1, keepdims=True)
    log_total = jnp.log(jnp.sum(jnp.exp(shifted), axis=1, keepdims=True))
    chosen = (jnp.arange(classes)[None, :] == labels[:, None]).astype(jnp.float32)
    row_weight = label_mask.astype(jnp.float32)
    loss_part = jnp.sum((log_total[:, 0] - jnp.sum(shifted * chosen, axis=1)) * row_weight)
    grad_logits = (
        (jnp.exp(shifted - log_total) - chosen) * (row_weight / label_count)[:, None]
    ).astype(jnp.bfloat16)
    grad_head = outer_product(hidden_two, grad_logits)
    grad_two = against(grad_logits, full_head).astype(jnp.bfloat16).astype(jnp.float32)
    grad_pre_two = silu_slope(pre_two, grad_two)
    grad_outer = outer_product(joined_two, grad_pre_two)
    grad_joined = against(grad_pre_two, full_outer)
    share = grad_joined[:, hidden:] / count_two
    share_high = share.astype(jnp.bfloat16)
    share_low = (share - share_high.astype(jnp.float32)).astype(jnp.bfloat16)
    grad_one = outer_product(pick, share_high) + outer_product(pick, share_low)
    grad_one = jnp.concatenate(
        [grad_one[:seed_count] + grad_joined[:, :hidden], grad_one[seed_count:]], axis=0
    )
    grad_one = grad_one.astype(jnp.bfloat16).astype(jnp.float32)
    grad_pre_one = silu_slope(pre_one, grad_one)
    grad_inner = outer_product(joined_one, grad_pre_one)
    bias_part = jnp.concatenate(
        [
            jnp.sum(part.astype(jnp.float32), axis=0)
            for part in (grad_pre_one, grad_pre_two, grad_logits)
        ]
    )

    devices = lax.axis_size(every)
    grads = jnp.concatenate(
        [grad.reshape(devices, -1) for grad in (grad_inner, grad_outer, grad_head)], axis=1
    )
    shard = lax.psum_scatter(grads, every, scatter_dimension=0, tiled=True).reshape(-1)
    shards = []
    for weight in weights:
        shards.append(shard[: weight.size].reshape(weight.shape))
        shard = shard[weight.size :]
    packed = lax.psum(jnp.concatenate([bias_part, loss_part[None]]), every)
    bias_grad, loss_sum = packed[:-1], packed[-1]
    grad_partial = sum((jnp.sum(part * part) for part in shards))
    weight_partial = [jnp.sum(weight * weight) for weight in weights]
    squares = lax.psum(jnp.stack([grad_partial] + weight_partial), every)
    clip_norm = jnp.sqrt(squares[0] + jnp.sum(bias_grad * bias_grad))
    factor = jnp.minimum(1.0, CLIP / clip_norm)
    firsts = (first_inner, first_outer, first_head)
    seconds = (second_inner, second_outer, second_head)
    smooths = (smooth_inner, smooth_outer, smooth_head)
    states = [
        moments(weights[slot_at], shards[slot_at] * factor, firsts[slot_at], seconds[slot_at])
        for slot_at in range(3)
    ]
    update_square = lax.psum(jnp.stack([jnp.sum(state[2] * state[2]) for state in states]), every)
    weight_norms = jnp.sqrt(squares[1:])
    update_norms = jnp.sqrt(update_square)
    news = [
        weights[slot_at]
        - RATE * (weight_norms[slot_at] / update_norms[slot_at]) * states[slot_at][2]
        for slot_at in range(3)
    ]
    averages = [
        AVERAGE * smooths[slot_at] + (1.0 - AVERAGE) * news[slot_at] for slot_at in range(3)
    ]
    bias_first, bias_second, bias_update = moments(
        biases, bias_grad * factor, first_biases, second_biases
    )
    bias_new = biases - RATE * bias_ratio(biases, bias_update, hidden) * bias_update
    bias_average = AVERAGE * smooth_biases + (1.0 - AVERAGE) * bias_new
    return (
        loss_sum,
        label_count,
        clip_norm,
        jnp.stack([weight_norms, update_norms], axis=1),
        news[0],
        news[1],
        news[2],
        bias_new,
        states[0][0],
        states[1][0],
        states[2][0],
        bias_first,
        states[0][1],
        states[1][1],
        states[2][1],
        bias_second,
        averages[0],
        averages[1],
        averages[2],
        bias_average,
    )


def solution(mesh):
    in_specs = (
        P("dp", None),
        P("section", "dp", None),
        P("section", "dp"),
        P(None, "dp", None),
        P(None, "dp"),
        P(None, "dp", None),
        P(None, "dp"),
        P(None, "dp"),
        P(None, "dp"),
        P(("section", "dp"), None),
        P(("section", "dp"), None),
        P(("section", "dp"), None),
        P(),
        P(("section", "dp"), None),
        P(("section", "dp"), None),
        P(("section", "dp"), None),
        P(),
        P(("section", "dp"), None),
        P(("section", "dp"), None),
        P(("section", "dp"), None),
        P(),
        P(("section", "dp"), None),
        P(("section", "dp"), None),
        P(("section", "dp"), None),
        P(),
    )
    out_specs = (
        P(),
        P(),
        P(),
        P(),
        P(("section", "dp"), None),
        P(("section", "dp"), None),
        P(("section", "dp"), None),
        P(),
        P(("section", "dp"), None),
        P(("section", "dp"), None),
        P(("section", "dp"), None),
        P(),
        P(("section", "dp"), None),
        P(("section", "dp"), None),
        P(("section", "dp"), None),
        P(),
        P(("section", "dp"), None),
        P(("section", "dp"), None),
        P(("section", "dp"), None),
        P(),
    )
    return jax.shard_map(
        on_device, mesh=mesh, in_specs=in_specs, out_specs=out_specs, check_vma=False
    )
```

```python
import functools

import jax
import jax.numpy as jnp
from jax import lax
from jax.experimental import pallas as pl
from jax.experimental.pallas import tpu as pltpu
from jax.sharding import PartitionSpec as P

STEP = 5


BETA_ONE = 0.9
BETA_TWO = 0.999
EPSILON = 1e-06
DECAY = 0.01
RATE = 0.25
CLIP = 0.05
AVERAGE = 0.9


VMEM_TABLE_LIMIT = 36 * 2**20
WHOLE_TABLE_LIMIT = 64 * 2**20
MESH = pl.DeviceIdType.MESH
SLOT = 16
BLOCK = 16
CHUNKS = 4
GROUP = 4
SETS = 4
SPARE = 9
SETTLE = 3
AHEAD = 1
AHEAD_ACROSS = 1
LAG = 2
FAR_LAG = 5
SPARE_AFTER = 2
SPARE_LAG = 4
TILE = 256
PAUSE = 6
FORWARD_SLOT = 1
MEAN_SLOT = 3


class Parts:
    def __init__(self, refs, base):
        self.grads, self.half_in, self.half, self.plane_in, self.fourth, self.line_in = refs
        self.base = base


def step_kernel(
    fan_outer,
    table_ref,
    weight_refs,
    first_refs,
    second_refs,
    bias_ref,
    mask_ref,
    owner_ref,
    local_ref,
    near_ref,
    seed_near_ref,
    seed_count_ref,
    label_ref,
    out_ref,
    joined_ref,
    weights_ref,
    hits_ref,
    hits_back_ref,
    full_ref,
    packed,
    parts,
    idx_ref,
    mix_ref,
    wide,
    seed_ref,
    seed_across_ref,
    stages,
    lists,
    full_inner_ref,
    full_outer_ref,
    full_head_ref,
    count_ref,
    first_pre,
    first_hidden,
    mean_ref,
    own_part,
    inner_sum,
    early_refs,
    late_refs,
    extra_ref,
    extra_plane,
    extra_line,
    sums,
    own_sem,
    z_sem,
    spare_sem,
    x_sem,
    y_sem,
    far_sem,
    twin_sem,
    twin_own_sem,
    double_sem,
    send_sem,
    double_send_sem,
    list_sem,
    sum_sem,
    sum_send_sem,
    norm_sem,
    norm_send_sem,
    late_sem,
    late_send_sem,
):
    section, at = lax.axis_index("section"), lax.axis_index("dp")
    z, core = at // 2, at % 2
    flipped = z // 2
    height = z + flipped * (3 - 2 * z)
    pairs = table_ref.shape[0]
    spare = pairs * SPARE // 64
    quarter = (pairs - spare) // 4
    chunk = quarter // CHUNKS
    spare_chunk = spare // CHUNKS

    def level(value):
        return value + flipped * (3 - 2 * value)

    twin = (section, z * 2 + 1 - core)
    beside_x = (section + 1 - 2 * (section % 2), at)
    beside_y = (section + 2 - 4 * (section // 2), at)
    inner_z = (section, level(1 - height) * 2 + core)
    across_z = (section, level(2) * 2 + core)
    outer_z = (section, level(0) * 2 + core)
    skip_z = (section, ((z + 2) % 4) * 2 + core)
    sources = [level(1 - height), level(2), level(3)]
    crosses = height == 1
    plane = [((section + k) % 4, at) for k in range(1, 4)]
    beyond = [((section + k) % 4, z * 2 + 1 - core) for k in range(1, 4)]
    line = [(section, ((z + k) % 4) * 2 + core) for k in range(1, 4)]
    neighbours = [twin] + plane + beyond

    barrier = pltpu.get_barrier_semaphore()
    others = [((section + k // 8) % 4, (at + k % 8) % 8) for k in range(1, 32)]
    for partner in others:
        pl.semaphore_signal(barrier, inc=1, device_id=partner, device_id_type=MESH)
    pl.semaphore_wait(barrier, 31)

    sent, now, count = [], [0], [0]

    def region(shard, part, piece):
        return full_ref.at[pl.ds(shard * pairs + part * quarter + piece * chunk, chunk)]

    def spare_region(shard, piece):
        return full_ref.at[pl.ds(shard * pairs + 4 * quarter + piece * spare_chunk, spare_chunk)]

    def send(source, target, recv, device, when=None):
        number = count[0]
        count[0] += 1
        copy = pltpu.make_async_remote_copy(
            src_ref=source,
            dst_ref=target,
            send_sem=send_sem.at[number],
            recv_sem=recv,
            device_id=device,
            device_id_type=MESH,
        )
        sent.append((copy, when, now[0]))
        if when is None:
            copy.start()
        else:
            pl.when(when)(copy.start)
        return copy

    def arrived(target, recv):
        pltpu.make_async_copy(target, target, recv).wait()

    def own_piece(piece, device, number, when=None):
        block = table_ref.at[pl.ds(section * quarter + piece * chunk, chunk)]
        send(block, region(at, section, piece), z_sem.at[number], device, when)

    for piece in range(min(AHEAD, CHUNKS)):
        own_piece(piece, inner_z, piece)
    for piece in range(min(AHEAD_ACROSS, CHUNKS)):
        own_piece(piece, across_z, CHUNKS + piece, crosses)
    whole = full_ref.at[pl.ds(at * pairs, pairs)]
    own = pltpu.make_async_copy(table_ref, whole, own_sem)
    own.start()
    send(table_ref, whole, twin_own_sem, twin)

    inner_ref, outer_ref, head_ref = weight_refs
    row_inner, row_outer, row_head = (ref.shape[0] for ref in weight_refs)
    hidden, classes = inner_ref.shape[1], head_ref.shape[1]
    head_at = row_inner + row_outer
    packed[0:row_inner, :] = inner_ref[...]
    packed[row_inner:head_at, :] = outer_ref[...]
    packed[head_at:, :] = jnp.zeros((row_head, hidden), jnp.float32)
    packed[head_at:, 0:classes] = head_ref[...]
    labelled = jnp.sum(mask_ref[...].astype(jnp.float32)).astype(jnp.int32)
    lane = lax.broadcasted_iota(jnp.int32, (1, hidden), 1)
    high_part = (labelled // 256).astype(jnp.float32)
    low_part = (labelled % 256).astype(jnp.float32)
    tail = jnp.where(lane == classes, high_part, jnp.where(lane == classes + 1, low_part, 0.0))
    packed[head_at : head_at + 1, :] += tail
    mine = (core * 4 + section) * 4 + z
    weights_ref[mine] = packed[...].astype(jnp.bfloat16)
    doubling = [(inner_z, 1), (skip_z, 2), (beside_x, 4), (beside_y, 8), (twin, 16)]
    doubled = []

    def double_start(number):
        device, size = doubling[number]
        block = weights_ref.at[pl.ds((mine // size) * size, size)]
        copy = pltpu.make_async_remote_copy(
            src_ref=block,
            dst_ref=block,
            send_sem=double_send_sem.at[number],
            recv_sem=double_sem.at[number],
            device_id=device,
            device_id_type=MESH,
        )
        copy.start()
        doubled.append(copy)

    double_start(0)

    def eye(size):
        same_place = lax.broadcasted_iota(jnp.int32, (size, size), 0) == lax.broadcasted_iota(
            jnp.int32, (size, size), 1
        )
        return same_place.astype(jnp.float32).astype(jnp.bfloat16)

    def as_low(values):
        return values.astype(jnp.float32).astype(jnp.bfloat16)

    placed = owner_ref[...] * (2 * pairs) + local_ref[...]
    pair_at = placed // 2
    high = owner_ref.shape[0]
    for k, values in enumerate((pair_at % 256, pair_at // 256, placed % 2)):
        parts[128 * k : 128 * (k + 1), :] = against(eye(128), as_low(values)).astype(jnp.bfloat16)
    looked_rows = near_ref.shape[0]
    seeds = seed_ref.shape[0]
    tiles = hits_ref.shape[1] // TILE
    seed_row = pl.ds(section, 1)
    live_seeds = seed_count_ref[seed_row, :]
    for j in range(fan_outer):
        near_seeds = seed_near_ref[j, seed_row, :]
        seed_across_ref[j : j + 1, :] = jnp.where(live_seeds > j, near_seeds, -1)
    seed_across_ref[fan_outer : fan_outer + 1, :] = label_ref[seed_row, :]
    seed_across_ref[fan_outer + 1 : fan_outer + 2, :] = mask_ref[seed_row, :]
    seed_across_ref[fan_outer + 2 :, :] = jnp.zeros((SLOT - fan_outer - 2, seeds), jnp.int32)
    shifted_up = seed_across_ref[...] + 1
    seed_ref[...] = (
        64.0 * against(eye(seeds), as_low(shifted_up // 64))
        + against(eye(seeds), as_low(shifted_up % 64))
    ).astype(jnp.int32) - 1
    total = 3 * CHUNKS
    steps = total + max(FAR_LAG, SPARE_LAG)
    per_step = -(-looked_rows // (8 * steps)) * 8
    for j in range(fan_outer):
        wide[j] = jnp.broadcast_to(seed_ref[:, j : j + 1], (seeds, TILE))

    def look_up(first, last):
        def rows_of(block, carry):
            start_at = pl.multiple_of(block * 8, 8)
            sub = lax.broadcasted_iota(jnp.int32, (high, 256), 0)
            low_at = lax.broadcasted_iota(jnp.int32, (128, 256), 0)
            row = lax.broadcasted_iota(jnp.int32, (256, 512), 0)
            column = lax.broadcasted_iota(jnp.int32, (256, 512), 1)
            for k in range(8):
                node = near_ref[pl.ds(start_at + k, 1), :]
                hot = (sub == node // 128).astype(jnp.float32).astype(jnp.bfloat16)
                got = jnp.dot(parts[...], hot, preferred_element_type=jnp.float32)
                chosen = low_at == node % 128
                found = jnp.where(chosen, got[0:128] + 256.0 * got[128:256], 0.0)
                odd = jnp.where(chosen, got[256:384], 0.0)
                entry_at = jnp.sum(found, axis=0, keepdims=True).astype(jnp.int32)
                idx_ref[block * 2 + k // 4, k % 4 : k % 4 + 1, :] = jnp.clip(
                    entry_at, 0, full_ref.shape[0] - 1
                )
                mix_ref[pl.ds(start_at + k, 1), 0:256] = jnp.sum(odd, axis=0, keepdims=True)
            odd = mix_ref[pl.ds(start_at, 8), 0:256]
            live = (near_ref[pl.ds(start_at, 8), :] >= 0).astype(jnp.float32)
            mix_ref[pl.ds(start_at, 8), :] = jnp.dot(
                (live * (1.0 - odd)).astype(jnp.bfloat16),
                (column == 2 * row).astype(jnp.float32).astype(jnp.bfloat16),
                preferred_element_type=jnp.float32,
            ) + jnp.dot(
                (live * odd).astype(jnp.bfloat16),
                (column == 2 * row + 1).astype(jnp.float32).astype(jnp.bfloat16),
                preferred_element_type=jnp.float32,
            )
            return carry

        lax.fori_loop(first // 8, last // 8, rows_of, 0)

    def mark(tile):
        start_at = tile * TILE
        dest = lax.broadcasted_iota(jnp.int32, (seeds, TILE), 1) + start_at
        hits = jnp.zeros((seeds, TILE), jnp.float32)
        for j in range(fan_outer):
            hits = hits + (wide[j] == dest).astype(jnp.float32)
        hits_ref[:, start_at : start_at + TILE] = hits.astype(jnp.bfloat16)
        dest = lax.broadcasted_iota(jnp.int32, (TILE, seeds), 0) + start_at
        hits = jnp.zeros((TILE, seeds), jnp.float32)
        for j in range(fan_outer):
            hits = hits + (seed_across_ref[j : j + 1, :] == dest).astype(jnp.float32)
        hits_back_ref[start_at : start_at + TILE, :] = hits.astype(jnp.bfloat16)

    def sort_weights():
        everyone = weights_ref[...].astype(jnp.float32)
        order = block_order()
        inner, outer, head = (
            jnp.concatenate([everyone[spot, lower:upper] for spot in order], axis=0)
            for lower, upper in ((0, row_inner), (row_inner, head_at), (head_at, head_at + row_head))
        )
        full_inner_ref[...] = inner.astype(jnp.bfloat16)
        full_outer_ref[...] = outer.astype(jnp.bfloat16)
        full_head_ref[...] = jnp.where(lane < classes, head, 0.0).astype(jnp.bfloat16)
        tails = everyone[0:4, head_at : head_at + 1] + everyone[16:20, head_at : head_at + 1]
        tails = jnp.sum(tails.reshape(4, hidden), axis=0, keepdims=True)
        scale = jnp.where(lane == classes, 256.0, jnp.where(lane == classes + 1, 1.0, 0.0))
        labels_in_all = jnp.sum(tails * scale, axis=1, keepdims=True)
        count_ref[...] = jnp.broadcast_to(jnp.maximum(labels_in_all, 1.0), count_ref.shape)

    twins = []

    def to_twin(block, number):
        send(block, block, twin_sem.at[number], twin)
        twins.append((number, now[0]))

    def from_twin(number):
        kind, step = divmod(number, total)
        turn, piece = divmod(step, CHUNKS)
        shard = sources[turn] * 2 + 1 - core
        if kind == 4:
            block = spare_region(shard, piece)
        else:
            block = region(shard, (section, beside_x[0], beside_y[0], 3 - section)[kind], piece)
        arrived(block, twin_sem.at[number])

    def settle(until):
        while twins and twins[0][1] <= until:
            from_twin(twins.pop(0)[0])
        while sent and sent[0][2] <= until - SETTLE:
            copy, when, _ = sent.pop(0)
            if when is None:
                copy.wait_send()
            else:
                pl.when(when)(copy.wait_send)

    for step in range(steps):
        now[0] = step
        if step < total:
            turn, piece = divmod(step, CHUNKS)
            shard = sources[turn] * 2 + core
            goes, number = (across_z, 2 * CHUNKS + piece) if turn == 0 else (outer_z, step)
            block = region(shard, section, piece)
            arrived(block, z_sem.at[step])
            send(block, block, z_sem.at[number], goes, crosses)
            send(block, block, x_sem.at[step], beside_x)
            send(block, block, y_sem.at[step], beside_y)
            to_twin(block, step)
            if step + AHEAD < CHUNKS:
                own_piece(step + AHEAD, inner_z, step + AHEAD)
            if step + AHEAD_ACROSS < CHUNKS:
                piece = step + AHEAD_ACROSS
                own_piece(piece, across_z, CHUNKS + piece, crosses)
            piece = step - SPARE_AFTER
            if 0 <= piece < CHUNKS:
                block = table_ref.at[pl.ds(4 * quarter + piece * spare_chunk, spare_chunk)]
                goal = spare_region(at, piece)
                send(block, goal, spare_sem.at[piece], inner_z)
                send(block, goal, spare_sem.at[CHUNKS + piece], across_z, crosses)
        late = step - SPARE_LAG
        if 0 <= late < total:
            turn, piece = divmod(late, CHUNKS)
            shard = sources[turn] * 2 + core
            goes, number = (across_z, 2 * CHUNKS + piece) if turn == 0 else (outer_z, late)
            block = spare_region(shard, piece)
            arrived(block, spare_sem.at[late])
            send(block, block, spare_sem.at[number], goes, crosses)
            to_twin(block, 4 * total + late)
        late = step - LAG
        if 0 <= late < total:
            turn, piece = divmod(late, CHUNKS)
            shard = sources[turn] * 2 + core
            block = region(shard, beside_x[0], piece)
            arrived(block, x_sem.at[late])
            send(block, block, far_sem.at[late], beside_y, core == piece % 2)
            to_twin(block, total + late)
            block = region(shard, beside_y[0], piece)
            arrived(block, y_sem.at[late])
            send(block, block, far_sem.at[late], beside_x, core != piece % 2)
            to_twin(block, 2 * total + late)
        later = step - FAR_LAG
        if 0 <= later < total:
            turn, piece = divmod(later, CHUNKS)
            shard = sources[turn] * 2 + core
            block = region(shard, 3 - section, piece)
            arrived(block, far_sem.at[later])
            to_twin(block, 3 * total + later)
        if step % 2 == 0 and step // 2 < len(doubling):
            doubled[step // 2].wait()
            if step // 2 + 1 < len(doubling):
                double_start(step // 2 + 1)
        first = min(step * per_step, looked_rows)
        last = min(first + per_step, looked_rows)
        if last > first:
            look_up(first, last)
        for tile in range(step * tiles // steps, (step + 1) * tiles // steps):
            mark(tile)
        settle(step - 3)

    sort_weights()
    settle(steps)
    arrived(full_ref.at[pl.ds((z * 2 + 1 - core) * pairs, pairs)], twin_own_sem)
    own.wait()

    blocks = looked_rows
    unit_at = lax.broadcasted_iota(jnp.int32, (BLOCK, 2 * BLOCK * SLOT), 1)
    same = unit_at // (2 * SLOT) == lax.broadcasted_iota(jnp.int32, unit_at.shape, 0)
    near_part = jnp.logical_and(same, unit_at % (2 * SLOT) < 2 * SLOT - 2).astype(jnp.float32)
    self_part = jnp.logical_and(same, unit_at % (2 * SLOT) >= 2 * SLOT - 2).astype(jnp.float32)
    turns = blocks // GROUP

    def fetch(turn, slot):
        return pltpu.make_async_copy(
            idx_ref.at[jnp.minimum(turn, turns - 1)], lists[slot], list_sem.at[slot]
        )

    def pick(member, slot, stage):
        def unit(number, carry):
            entry = full_ref[lists[slot][member, number]]
            stage[pl.ds(2 * number, 2), :] = entry.astype(jnp.float32)
            return carry

        lax.fori_loop(0, BLOCK * SLOT, unit, 0, unroll=BLOCK * SLOT)

    def reduce(block, stage):
        mix = mix_ref[pl.ds(block, 1), :]
        near = mix * near_part
        left = jnp.concatenate([near, mix * self_part], axis=0).astype(jnp.bfloat16)
        out = jnp.dot(left, stage[...].astype(jnp.bfloat16), preferred_element_type=jnp.float32)
        count = jnp.maximum(jnp.sum(near, axis=1, keepdims=True), 1.0)
        both = jnp.concatenate([out[BLOCK:], out[:BLOCK] / count], axis=1)
        start_at = pl.multiple_of(block * BLOCK, BLOCK)
        joined_ref[pl.ds(start_at, BLOCK), :] = both.astype(jnp.bfloat16)

    bias_inner, bias_outer, bias_head = bias_rows_of(bias_ref, hidden)

    def forward(tile):
        tile_rows = pl.ds(pl.multiple_of(tile * TILE, TILE), TILE)
        before = (
            jnp.dot(
                joined_ref[tile_rows, :], full_inner_ref[...], preferred_element_type=jnp.float32
            )
            + bias_inner
        )
        first_pre[tile_rows, :] = before
        first_hidden[tile_rows, :] = (before * lax.logistic(before)).astype(jnp.bfloat16)

    def add_mean(tile, carried):
        tile_rows = pl.ds(pl.multiple_of(tile * TILE, TILE), TILE)
        found = jnp.dot(
            hits_ref[:, tile_rows], first_hidden[tile_rows, :], preferred_element_type=jnp.float32
        )
        mean_ref[...] = mean_ref[...] * carried + found

    near_stages, far_stages = stages
    mean_ref[...] = jnp.zeros(mean_ref.shape, jnp.float32)
    joined_ref[0:TILE, :] = jnp.zeros((TILE, joined_ref.shape[1]), jnp.bfloat16)
    for slot in range(SETS):
        fetch(slot, slot).start()
    for member in range(GROUP):
        far_stages[member][...] = jnp.zeros(far_stages[member].shape, jnp.float32)

    def round_of(number, carry):
        for slot in range(SETS):
            turn = number * SETS + slot
            fetch(turn, slot).wait()
            for member in range(GROUP):
                pick(member, slot, stages[slot % 2][member])
                reduce(
                    jnp.maximum((turn - 1) * GROUP + member, 0), stages[1 - slot % 2][member]
                )
            if slot == FORWARD_SLOT:
                forward(jnp.maximum(number - 1, 0))
            if slot == MEAN_SLOT:
                add_mean(jnp.maximum(number - 1, 0), (number > 1).astype(jnp.float32))
            fetch(turn + SETS, slot).start()
        return carry

    lax.fori_loop(0, blocks // (GROUP * SETS), round_of, 0)
    for slot in range(SETS):
        fetch(0, slot).wait()
    for member in range(GROUP):
        reduce(blocks - GROUP + member, stages[(SETS - 1) % 2][member])
    forward(tiles - 1)
    add_mean(tiles - 1, 1.0)
    settle(steps + SETTLE)

    summing = []

    def pass_on(source, target, number, device):
        copy = pltpu.make_async_remote_copy(
            src_ref=source,
            dst_ref=target,
            send_sem=sum_send_sem.at[len(summing)],
            recv_sem=sum_sem.at[number],
            device_id=device,
            device_id_type=MESH,
        )
        summing.append(copy)
        copy.start()

    def passed(target, number):
        arrived(target, sum_sem.at[number])

    def to_other_core(part):
        pass_on(part.grads.at[pl.ds((1 - core) * 16, 16)], part.half_in, part.base, twin)

    def to_plane(part):
        passed(part.half_in, part.base)
        part.half[...] = part.grads[pl.ds(core * 16, 16)] + part.half_in[...]
        for partner in plane:
            block = part.half.at[pl.ds(partner[0] * 4, 4)]
            pass_on(block, part.plane_in.at[section], part.base + 1 + section, partner)
        part.plane_in[section] = part.half[pl.ds(section * 4, 4)]

    def to_line(part):
        for k in range(1, 4):
            other = (section + k) % 4
            passed(part.plane_in.at[other], part.base + 1 + other)
        part.fourth[...] = (part.plane_in[0] + part.plane_in[1]) + (
            part.plane_in[2] + part.plane_in[3]
        )
        for k, partner in enumerate(line):
            block = part.fourth.at[pl.ds((z + k + 1) % 4, 1)]
            pass_on(block, part.line_in.at[pl.ds(z, 1)], part.base + 5 + z, partner)
        part.line_in[z] = part.fourth[z]

    def whole_sum(part):
        for k in range(1, 4):
            other = (z + k) % 4
            passed(part.line_in.at[pl.ds(other, 1)], part.base + 5 + other)
        return (part.line_in[0] + part.line_in[1]) + (part.line_in[2] + part.line_in[3])

    def share(value, slots, base, me, partners):
        slots[me] = value
        for partner in partners:
            pass_on(slots.at[me], slots.at[me], base + me, partner)

    def collect(slots, base, me):
        count = slots.shape[0]
        for k in range(1, count):
            other = (me + k) % count
            passed(slots.at[other], base + other)
        values = [slots[k] for k in range(count)]
        while len(values) > 1:
            values = [values[k] + values[k + 1] for k in range(0, len(values), 2)]
        return values[0]

    early = Parts(early_refs, 0)
    late_grads, late_half_in, late_half, late_in = late_refs
    order = block_order()
    full_outer, full_head = full_outer_ref[...], full_head_ref[...]
    label_count = count_ref[:, 0:1]
    kept = seed_ref[:, 0:fan_outer]
    count_two = jnp.sum((kept >= 0).astype(jnp.float32), axis=1, keepdims=True)
    mean_two = (mean_ref[...] / count_two).astype(jnp.bfloat16)
    joined_two = jnp.concatenate([first_hidden[0:seeds, :], mean_two], axis=1)
    pre_two = jnp.dot(joined_two, full_outer, preferred_element_type=jnp.float32) + bias_outer
    gate_two = lax.logistic(pre_two)
    hidden_two = (pre_two * gate_two).astype(jnp.bfloat16)
    logits = jnp.dot(hidden_two, full_head, preferred_element_type=jnp.float32) + bias_head
    inside = lane < classes
    highest = jnp.max(jnp.where(inside, logits, -jnp.inf), axis=1, keepdims=True)
    shifted = jnp.where(inside, logits - highest, 0.0)
    total_exp = jnp.sum(jnp.where(inside, jnp.exp(shifted), 0.0), axis=1, keepdims=True)
    log_total = jnp.log(total_exp)
    chosen = (lane == seed_ref[:, fan_outer : fan_outer + 1]).astype(jnp.float32)
    row_weight = seed_ref[:, fan_outer + 1 : fan_outer + 2].astype(jnp.float32)
    loss = jnp.sum((log_total - jnp.sum(shifted * chosen, axis=1, keepdims=True)) * row_weight)
    grad_logits = (jnp.exp(shifted - log_total) - chosen) * (row_weight / label_count)
    grad_logits = jnp.where(inside, grad_logits, 0.0).astype(jnp.bfloat16)
    grad_head = outer_product(hidden_two, grad_logits)
    grad_two = against(grad_logits, full_head).astype(jnp.bfloat16).astype(jnp.float32)
    grad_pre_two = (grad_two * gate_two * (1.0 + pre_two * (1.0 - gate_two))).astype(jnp.bfloat16)
    grad_outer = outer_product(joined_two, grad_pre_two)
    for number, spot in enumerate(order):
        early.grads[spot, 0:row_outer, :] = grad_outer[
            number * row_outer : (number + 1) * row_outer
        ]
        early.grads[spot, row_outer : row_outer + row_head, :] = grad_head[
            number * row_head : (number + 1) * row_head
        ]
    to_other_core(early)
    extra_ref[1:2, :] = jnp.sum(grad_pre_two.astype(jnp.float32), axis=0, keepdims=True)
    extra_ref[2:3, :] = jnp.sum(grad_logits.astype(jnp.float32), axis=0, keepdims=True)
    extra_ref[3:4, :] = jnp.where(lane == 0, loss, jnp.where(lane == 1, label_count, 0.0))
    extra_ref[4:8, :] = jnp.zeros((4, hidden), jnp.float32)
    grad_joined = against(grad_pre_two, full_outer)
    share_part = grad_joined[:, hidden:] / count_two
    share_high = share_part.astype(jnp.bfloat16)
    share_low = (share_part - share_high.astype(jnp.float32)).astype(jnp.bfloat16)
    inner_sum[...] = jnp.zeros(inner_sum.shape, jnp.float32)
    share_both = jnp.concatenate([share_high, share_low], axis=0)
    own_part[...] = jnp.zeros(own_part.shape, jnp.float32)
    own_part[0:seeds, :] = grad_joined[:, 0:hidden]

    def backward(tile, bias_sum, own=None):
        tile_rows = pl.ds(pl.multiple_of(jnp.int32(tile) * TILE, TILE), TILE)
        hits = hits_back_ref[tile_rows, :]
        both_hits = jnp.concatenate([hits, hits], axis=1)
        grad_one = jnp.dot(both_hits, share_both, preferred_element_type=jnp.float32)
        if own is not None:
            grad_one = grad_one + own
        grad_one = grad_one.astype(jnp.bfloat16).astype(jnp.float32)
        before = first_pre[tile_rows, :]
        gate = lax.logistic(before)
        grad_pre = (grad_one * gate * (1.0 + before * (1.0 - gate))).astype(jnp.bfloat16)
        inner_sum[...] += outer_product(joined_ref[tile_rows, :], grad_pre)
        return bias_sum + jnp.sum(grad_pre.astype(jnp.float32), axis=0, keepdims=True)

    bias_sum = backward(0, jnp.zeros((1, hidden), jnp.float32), own_part[...])
    bias_sum = lax.fori_loop(1, PAUSE, backward, bias_sum)
    to_plane(early)
    bias_sum = lax.fori_loop(PAUSE, tiles, backward, bias_sum)
    extra_ref[0:1, :] = bias_sum
    grad_inner = inner_sum[...]
    for number, spot in enumerate(order):
        late_grads[spot] = grad_inner[number * row_inner : (number + 1) * row_inner]
    pass_on(late_grads.at[pl.ds((1 - core) * 16, 16)], late_half_in, 9, twin)
    share(extra_ref[...], extra_plane, 18, section * 2 + core, neighbours)
    passed(late_half_in, 9)
    late_half[...] = late_grads[pl.ds(core * 16, 16)] + late_half_in[...]
    same_core = [((section + k // 4) % 4, (z + k % 4) % 4) for k in range(1, 16)]
    my_place = section * 4 + z
    for to_section, to_z in same_core:
        pltpu.make_async_remote_copy(
            src_ref=late_half.at[to_section * 4 + to_z],
            dst_ref=late_in.at[my_place],
            send_sem=late_send_sem,
            recv_sem=late_sem,
            device_id=(to_section, to_z * 2 + core),
            device_id_type=MESH,
        ).start()
    late_in[my_place] = late_half[my_place]
    to_line(early)
    share(collect(extra_plane, 18, section * 2 + core), extra_line, 26, z, line)

    short_lane = lax.broadcasted_iota(jnp.int32, (1, 128), 1)
    my_number = section * 8 + at

    def square_sum(value):
        return jnp.sum(jnp.sum(value * value, axis=0, keepdims=True), axis=1, keepdims=True)

    def everywhere(values, number):
        found = jnp.zeros((1, 128), jnp.float32)
        for k, value in enumerate(values):
            found = jnp.where(short_lane == k, value, found)
        sums[number, my_number] = found
        mine_there = sums.at[number, my_number]
        for partner in others:
            pltpu.make_async_remote_copy(
                src_ref=mine_there,
                dst_ref=mine_there,
                send_sem=norm_send_sem.at[number],
                recv_sem=norm_sem.at[number],
                device_id=partner,
                device_id_type=MESH,
            ).start()
        all_others = sums.at[number, pl.ds(0, 31)]
        arrived(all_others, norm_sem.at[number])
        return jnp.sum(sums[number], axis=0)

    held = [ref[...] for ref in weight_refs]
    weight_squares = [square_sum(weight) for weight in held]
    rest = whole_sum(early)
    arrived(late_in.at[pl.ds(0, 15)], late_sem)
    shard = jnp.sum(late_in[...], axis=0)
    extra = collect(extra_line, 26, z)
    pieces = [shard, rest[0:row_outer], rest[row_outer:, 0:classes]]
    values = everywhere([square_sum(shard) + square_sum(rest)] + weight_squares, 0)
    grad_square = jnp.sum(jnp.where(short_lane == 0, values, 0.0), axis=1, keepdims=True)
    clip_norm = jnp.sqrt(grad_square + square_sum(extra[0:3]))
    factor = jnp.minimum(1.0, CLIP / clip_norm)
    update_squares = []
    for k in range(3):
        update = moments(held[k], pieces[k] * factor, first_refs[k][...], second_refs[k][...])[2]
        update_squares.append(square_sum(update))
    updates = everywhere(update_squares, 1)
    rows = row_inner + row_outer + row_head
    out_ref[0:row_inner, :] = shard
    out_ref[row_inner:rows, :] = rest
    out_ref[rows : rows + 8, :] = extra
    out_ref[rows + 8 : rows + 9, 0:128] = values
    out_ref[rows + 8 : rows + 9, 128:256] = updates
    out_ref[rows + 9 :, :] = jnp.zeros((7, hidden), jnp.float32)
    for copy in summing:
        copy.wait_send()
    for number in range(2):
        arrived(sums.at[number, pl.ds(0, 31)], norm_send_sem.at[number])
    arrived(late_in.at[pl.ds(0, 15)], late_send_sem)


def block_order():
    return [(e % 2) * 16 + (e // 8) * 4 + (e % 8) // 2 for e in range(32)]


def bias_rows_of(ref, hidden):
    width = ref.shape[0] - 2 * hidden
    last = ref[pl.ds(2 * hidden, width)].reshape(1, width)
    return (
        ref[pl.ds(0, hidden)].reshape(1, hidden),
        ref[pl.ds(hidden, hidden)].reshape(1, hidden),
        jnp.concatenate([last, jnp.zeros((1, hidden - width), jnp.float32)], axis=1),
    )


def summed_step(
    node_table,
    weights,
    firsts,
    seconds,
    biases,
    label_mask,
    owner_ids,
    row_ids,
    near,
    outer_neighbours,
    outer_counts,
    labels,
):
    devices = lax.axis_size(("section", "dp"))
    table_rows, width = node_table.shape
    frontier_high = owner_ids.size // 128
    fan_outer = outer_neighbours.shape[2]
    looked = near.shape[0]
    dest_count = looked * BLOCK
    seeds = outer_neighbours.shape[1]
    hidden = weights[0].shape[1]
    row_inner = weights[0].shape[0]
    rows = sum(weight.shape[0] for weight in weights)
    total = 3 * CHUNKS
    sends = 4 * CHUNKS + 1 + 3 * total + total + 2 * total + 5 * total
    vmem = pl.BlockSpec(memory_space=pltpu.VMEM)
    stage = (pltpu.VMEM((2 * BLOCK * SLOT, width), jnp.float32),) * GROUP

    def on_the_way(depth):
        return (
            pltpu.VMEM((devices, depth, hidden), jnp.float32),
            pltpu.VMEM((16, depth, hidden), jnp.float32),
            pltpu.VMEM((16, depth, hidden), jnp.float32),
            pltpu.VMEM((4, 4, depth, hidden), jnp.float32),
            pltpu.VMEM((4, depth, hidden), jnp.float32),
            pltpu.VMEM((4, depth, hidden), jnp.float32),
        )

    return pl.pallas_call(
        functools.partial(step_kernel, fan_outer),
        out_shape=jax.ShapeDtypeStruct((rows + 16, hidden), jnp.float32),
        in_specs=[pl.BlockSpec(memory_space=pl.ANY)] + [(vmem,) * 3] * 3 + [vmem] * 8,
        out_specs=vmem,
        scratch_shapes=[
            pltpu.VMEM((dest_count, 2 * width), jnp.bfloat16),
            pltpu.VMEM((devices, rows, hidden), jnp.bfloat16),
            pltpu.VMEM((seeds, dest_count), jnp.bfloat16),
            pltpu.VMEM((dest_count, seeds), jnp.bfloat16),
            pltpu.VMEM((lax.axis_size("dp") * table_rows // 2, 2, width), jnp.bfloat16),
            pltpu.VMEM((rows, hidden), jnp.float32),
            pltpu.VMEM((384, frontier_high), jnp.bfloat16),
            pltpu.VMEM((looked // GROUP, GROUP, 256), jnp.int32),
            pltpu.VMEM((looked, 512), jnp.float32),
            pltpu.VMEM((fan_outer, seeds, TILE), jnp.int32),
            pltpu.VMEM((seeds, SLOT), jnp.int32),
            pltpu.VMEM((SLOT, seeds), jnp.int32),
            (stage, stage),
            (pltpu.SMEM((GROUP, BLOCK * SLOT), jnp.int32),) * SETS,
            pltpu.VMEM((hidden, hidden), jnp.bfloat16),
            pltpu.VMEM((2 * hidden, hidden), jnp.bfloat16),
            pltpu.VMEM((hidden, hidden), jnp.bfloat16),
            pltpu.VMEM((1, hidden), jnp.float32),
            pltpu.VMEM((dest_count, hidden), jnp.float32),
            pltpu.VMEM((dest_count, hidden), jnp.bfloat16),
            pltpu.VMEM((seeds, hidden), jnp.float32),
            pltpu.VMEM((TILE, hidden), jnp.float32),
            pltpu.VMEM((hidden, hidden), jnp.float32),
            on_the_way(rows - row_inner),
            (
                pltpu.VMEM((devices, row_inner, hidden), jnp.float32),
                pltpu.VMEM((16, row_inner, hidden), jnp.float32),
                pltpu.VMEM((16, row_inner, hidden), jnp.float32),
                pltpu.VMEM((16, row_inner, hidden), jnp.float32),
            ),
            pltpu.VMEM((8, hidden), jnp.float32),
            pltpu.VMEM((8, 8, hidden), jnp.float32),
            pltpu.VMEM((4, 8, hidden), jnp.float32),
            pltpu.VMEM((2, devices, 1, 128), jnp.float32),
            pltpu.SemaphoreType.DMA(()),
            pltpu.SemaphoreType.DMA((total,)),
            pltpu.SemaphoreType.DMA((total,)),
            pltpu.SemaphoreType.DMA((total,)),
            pltpu.SemaphoreType.DMA((total,)),
            pltpu.SemaphoreType.DMA((total,)),
            pltpu.SemaphoreType.DMA((5 * total,)),
            pltpu.SemaphoreType.DMA(()),
            pltpu.SemaphoreType.DMA((5,)),
            pltpu.SemaphoreType.DMA((sends,)),
            pltpu.SemaphoreType.DMA((5,)),
            pltpu.SemaphoreType.DMA((SETS,)),
            pltpu.SemaphoreType.DMA((30,)),
            pltpu.SemaphoreType.DMA((24,)),
            pltpu.SemaphoreType.DMA((2,)),
            pltpu.SemaphoreType.DMA((2,)),
            pltpu.SemaphoreType.DMA(()),
            pltpu.SemaphoreType.DMA(()),
        ],
        compiler_params=pltpu.CompilerParams(
            collective_id=0, has_side_effects=True, vmem_limit_bytes=56 * 2**20
        ),
    )(
        pltpu.with_memory_space_constraint(
            node_table.reshape(table_rows // 2, 2, width), pltpu.HBM
        ),
        weights,
        firsts,
        seconds,
        biases,
        label_mask,
        owner_ids.reshape(-1, 128),
        row_ids.reshape(-1, 128),
        near,
        outer_neighbours.transpose(2, 0, 1),
        outer_counts,
        labels,
    )


def final_kernel(
    sizes,
    devices,
    sums_ref,
    weight_refs,
    first_refs,
    second_refs,
    smooth_refs,
    bias_refs,
    loss_ref,
    count_ref,
    clip_ref,
    norms_ref,
    new_refs,
    moment_refs,
    square_refs,
    average_refs,
    bias_out_refs,
):
    classes, row_inner, row_outer, row_head = sizes
    hidden = sums_ref.shape[1]
    rows = row_inner + row_outer + row_head
    split = (0, row_inner, row_inner + row_outer, rows)
    widths = (hidden, hidden, classes)
    lane = lax.broadcasted_iota(jnp.int32, (1, 128), 1)

    def number(k, start_at):
        found = sums_ref[rows + 8 : rows + 9, start_at : start_at + 128]
        return jnp.sum(jnp.where(lane == k, found, 0.0), axis=1, keepdims=True)

    bias_grad = sums_ref[rows : rows + 3, :]
    bias_square = jnp.sum(jnp.sum(bias_grad * bias_grad, axis=0, keepdims=True), axis=1, keepdims=True)
    clip_norm = jnp.sqrt(number(0, 0) + bias_square)
    factor = jnp.minimum(1.0, CLIP / clip_norm)
    wide = lax.broadcasted_iota(jnp.int32, (8, 128), 1)
    deep = lax.broadcasted_iota(jnp.int32, (8, 128), 0)
    norms = jnp.zeros((8, 128), jnp.float32)
    for k in range(3):
        weight = weight_refs[k][...]
        gradient = sums_ref[split[k] : split[k + 1], 0 : widths[k]] * factor
        first, second, update = moments(weight, gradient, first_refs[k][...], second_refs[k][...])
        weight_norm, update_norm = jnp.sqrt(number(1 + k, 0)), jnp.sqrt(number(k, 128))
        fresh = weight - RATE * (weight_norm / update_norm) * update
        new_refs[k][...] = fresh
        moment_refs[k][...] = first
        square_refs[k][...] = second
        average_refs[k][...] = AVERAGE * smooth_refs[k][...] + (1.0 - AVERAGE) * fresh
        norms = jnp.where(jnp.logical_and(deep == 0, wide == k), weight_norm, norms)
        norms = jnp.where(jnp.logical_and(deep == 1, wide == k), update_norm, norms)
    norms_ref[...] = norms[0:2, 0:3]
    weight, first, second, smooth = (
        jnp.concatenate(bias_rows_of(ref, hidden), axis=0) for ref in bias_refs
    )
    first, second, update = moments(weight, bias_grad * factor, first, second)
    column = lax.broadcasted_iota(jnp.int32, weight.shape, 1)
    row = lax.broadcasted_iota(jnp.int32, weight.shape, 0)
    update = jnp.where(jnp.logical_or(row < 2, column < classes), update, 0.0)
    ratio = jnp.sqrt(jnp.sum(weight * weight, axis=1, keepdims=True)) / jnp.sqrt(
        jnp.sum(update * update, axis=1, keepdims=True)
    )
    fresh = weight - RATE * ratio * update
    average = AVERAGE * smooth + (1.0 - AVERAGE) * fresh
    for ref, value in zip(bias_out_refs, (fresh, first, second, average)):
        ref[pl.ds(0, hidden)] = value[0:1].reshape(hidden)
        ref[pl.ds(hidden, hidden)] = value[1:2].reshape(hidden)
        ref[pl.ds(2 * hidden, classes)] = value[2:3, 0:classes].reshape(classes)
    tail = sums_ref[rows + 3 : rows + 4, 0:128]
    loss_ref[...] = jnp.sum(jnp.where(lane == 0, tail, 0.0), axis=1, keepdims=True)
    count = jnp.sum(jnp.where(lane == 1, tail, 0.0), axis=1, keepdims=True)
    count_ref[...] = count / devices
    clip_ref[...] = clip_norm


def finished(sizes, sums, weights, firsts, seconds, smooths, biases):
    vmem = pl.BlockSpec(memory_space=pltpu.VMEM)
    like = [jax.ShapeDtypeStruct(weight.shape, jnp.float32) for weight in weights]
    scalar = jax.ShapeDtypeStruct((1, 1), jnp.float32)
    return pl.pallas_call(
        functools.partial(final_kernel, sizes, float(lax.axis_size(("section", "dp")))),
        out_shape=(
            scalar,
            scalar,
            scalar,
            jax.ShapeDtypeStruct((2, 3), jnp.float32),
            like,
            like,
            like,
            like,
            [jax.ShapeDtypeStruct(biases[0].shape, jnp.float32)] * 4,
        ),
        in_specs=[vmem] + [(vmem,) * 3] * 4 + [(vmem,) * 4],
        out_specs=(vmem,) * 4 + ([vmem] * 3,) * 4 + ([vmem] * 4,),
    )(sums, weights, firsts, seconds, smooths, biases)


def on_slice_kernels(
    node_table, owner_ids, dest_count, fan_inner, hidden, classes, seed_count, fan_outer, mask_sizes, weight_rows
):
    parts, peers = lax.axis_size("section"), lax.axis_size("dp")
    return (
        parts == 4
        and peers == 8
        and peers * node_table.size * 2 <= VMEM_TABLE_LIMIT
        and node_table.shape[1] == 128
        and node_table.shape[0] % (512 * CHUNKS) == 0
        and peers * node_table.shape[0] <= 131072
        and owner_ids.shape[0] % 1024 == 0
        and owner_ids.shape[0] <= 32768
        and fan_inner == SLOT - 1
        and dest_count % (BLOCK * GROUP * SETS) == 0
        and dest_count % TILE == 0
        and hidden == 256
        and classes + 2 <= hidden
        and seed_count <= TILE
        and seed_count % 128 == 0
        and dest_count < 16384
        and BLOCK * GROUP * SETS == TILE
        and fan_outer + 2 <= SLOT
        and len(mask_sizes) == 2
        and mask_sizes[0] * mask_sizes[1] <= 65536
        and all(rows % 8 == 0 for rows in weight_rows)
        and sum(weight_rows) % 16 == 0
        and dest_count // TILE > PAUSE
    )


def outer_product(left, right):
    return lax.dot_general(
        left, right, (((0,), (0,)), ((), ())), preferred_element_type=jnp.float32
    )


def against(left, right):
    return lax.dot_general(
        left, right, (((1,), (1,)), ((), ())), preferred_element_type=jnp.float32
    )


def silu_slope(before, grad_out):
    sigmoid = jax.nn.sigmoid(before)
    return (grad_out * sigmoid * (1.0 + before * (1.0 - sigmoid))).astype(jnp.bfloat16)


def moments(weight, gradient, first, second):
    first = BETA_ONE * first + (1.0 - BETA_ONE) * gradient
    second = BETA_TWO * second + (1.0 - BETA_TWO) * gradient * gradient
    update = (
        first / (1.0 - BETA_ONE**STEP) / (jnp.sqrt(second / (1.0 - BETA_TWO**STEP)) + EPSILON)
        + DECAY * weight
    )
    return (first, second, update)


def bias_ratio(weight, update, hidden):
    bounds = ((0, hidden), (hidden, 2 * hidden), (2 * hidden, weight.shape[0]))
    pieces = []
    for start_at, stop_at in bounds:
        weight_norm = jnp.sqrt(jnp.sum(weight[start_at:stop_at] ** 2))
        update_norm = jnp.sqrt(jnp.sum(update[start_at:stop_at] ** 2))
        pieces.append(jnp.zeros((stop_at - start_at,), jnp.float32) + weight_norm / update_norm)
    return jnp.concatenate(pieces)


def gathered_rows(node_table, owner_ids, row_ids):
    peer_count = lax.axis_size("dp")
    parts = lax.axis_size("section")
    table_rows = node_table.shape[0]
    if peer_count * node_table.size * 2 <= WHOLE_TABLE_LIMIT and table_rows % parts == 0:
        part_rows = table_rows // parts
        quarter = lax.dynamic_slice_in_dim(
            node_table, lax.axis_index("section") * part_rows, part_rows, 0
        )
        source = lax.all_gather(quarter, ("section", "dp"), axis=0, tiled=True)
        place = (row_ids // part_rows * peer_count + owner_ids) * part_rows + row_ids % part_rows
        return source, place
    frontier_rows = owner_ids.shape[0]
    slot_count = max(2, 2 * frontier_rows // peer_count)
    owner_hot = (owner_ids[:, None] == jnp.arange(peer_count)[None, :]).astype(jnp.int32)
    ranking = jnp.sum((jnp.cumsum(owner_hot, axis=0) - 1) * owner_hot, axis=1)
    placed = owner_ids * slot_count + ranking
    request = (
        jnp.zeros((peer_count * slot_count,), jnp.int32)
        .at[placed]
        .set(row_ids)
        .reshape(peer_count, slot_count)
    )
    returned = lax.all_to_all(
        node_table[lax.all_to_all(request, "dp", split_axis=0, concat_axis=0, tiled=True)],
        "dp",
        split_axis=0,
        concat_axis=0,
        tiled=True,
    )
    return returned.reshape(peer_count * slot_count, -1), placed


def on_device(
    node_table,
    owners,
    local_rows,
    inner_neighbours,
    inner_counts,
    outer_neighbours,
    outer_counts,
    labels,
    label_mask,
    weight_inner,
    weight_outer,
    weight_head,
    biases,
    first_inner,
    first_outer,
    first_head,
    first_biases,
    second_inner,
    second_outer,
    second_head,
    second_biases,
    smooth_inner,
    smooth_outer,
    smooth_head,
    smooth_biases,
):
    at = lax.axis_index("section")
    every = ("section", "dp")
    hidden = weight_inner.shape[1]
    dest_count, fan_inner = inner_neighbours.shape[1:]
    seed_count, fan_outer = outer_neighbours.shape[1:]
    classes = weight_head.shape[1]
    whole_mask, whole_labels = label_mask, labels
    whole_outer, whole_outer_counts = outer_neighbours, outer_counts
    mask_sizes = label_mask.shape

    def mine(array):
        return lax.dynamic_index_in_dim(array, at, 0, keepdims=False)

    inner_neighbours, inner_counts = mine(inner_neighbours), mine(inner_counts)
    outer_neighbours, outer_counts = mine(outer_neighbours), mine(outer_counts)
    labels, label_mask = mine(labels), mine(label_mask)
    bias_inner = biases[:hidden]
    bias_outer = biases[hidden : 2 * hidden]
    bias_head = biases[2 * hidden :]

    owner_ids, row_ids = owners.reshape(-1), local_rows.reshape(-1)
    weights = (weight_inner, weight_outer, weight_head)
    keep = jnp.arange(fan_inner)[None, :] < inner_counts[:, None]
    if on_slice_kernels(
        node_table,
        owner_ids,
        dest_count,
        fan_inner,
        hidden,
        classes,
        seed_count,
        fan_outer,
        mask_sizes,
        [weight.shape[0] for weight in weights],
    ):
        own = jnp.arange(dest_count, dtype=jnp.int32)[:, None]
        near = jnp.concatenate([jnp.where(keep, inner_neighbours, -1), own], axis=1)
        near = near.reshape(-1, BLOCK * SLOT)
        firsts = (first_inner, first_outer, first_head)
        seconds = (second_inner, second_outer, second_head)
        smooths = (smooth_inner, smooth_outer, smooth_head)
        rows = [weight.shape[0] for weight in weights]
        sums = summed_step(
            node_table,
            weights,
            firsts,
            seconds,
            biases,
            whole_mask,
            owner_ids,
            row_ids,
            near,
            whole_outer,
            whole_outer_counts,
            whole_labels,
        )
        loss, count, clip, norms, news, moment, square, average, bias_outs = finished(
            (classes, *rows),
            sums,
            weights,
            firsts,
            seconds,
            smooths,
            (biases, first_biases, second_biases, smooth_biases),
        )
        return (
            loss.reshape(()),
            count.reshape(()),
            clip.reshape(()),
            norms.T,
            *news,
            bias_outs[0],
            *moment,
            bias_outs[1],
            *square,
            bias_outs[2],
            *average,
            bias_outs[3],
        )

    label_part = jnp.sum(whole_mask.astype(jnp.float32))
    label_count = jnp.maximum(lax.psum(label_part, "dp"), 1.0)
    full_inner, full_outer, full_head = (
        lax.all_gather(weight.astype(jnp.bfloat16), every, axis=0, tiled=True)
        for weight in weights
    )
    source, place = gathered_rows(node_table, owner_ids, row_ids)
    rows = source[place[inner_neighbours]]
    summed = jnp.sum(
        jnp.where(keep[:, :, None], rows, jnp.zeros((), rows.dtype)), axis=1, dtype=jnp.float32
    )
    self_rows = source[place[:dest_count]]
    mean_one = (summed / inner_counts[:, None].astype(jnp.float32)).astype(jnp.bfloat16)
    joined_one = jnp.concatenate([self_rows, mean_one], axis=1)
    pre_one = jnp.dot(joined_one, full_inner, preferred_element_type=jnp.float32) + bias_inner
    hidden_one = jax.nn.silu(pre_one).astype(jnp.bfloat16)

    keep_outer = jnp.arange(fan_outer)[None, :] < outer_counts[:, None]
    pick = jnp.sum(
        (
            jnp.where(keep_outer, outer_neighbours, -1)[:, :, None]
            == jnp.arange(dest_count)[None, None, :]
        ).astype(jnp.float32),
        axis=1,
    ).astype(jnp.bfloat16)
    count_two = outer_counts[:, None].astype(jnp.float32)
    mean_two = (jnp.dot(pick, hidden_one, preferred_element_type=jnp.float32) / count_two).astype(
        jnp.bfloat16
    )
    joined_two = jnp.concatenate([hidden_one[:seed_count], mean_two], axis=1)
    pre_two = jnp.dot(joined_two, full_outer, preferred_element_type=jnp.float32) + bias_outer
    hidden_two = jax.nn.silu(pre_two).astype(jnp.bfloat16)

    logits = jnp.dot(hidden_two, full_head, preferred_element_type=jnp.float32) + bias_head
    shifted = logits - jnp.max(logits, axis=1, keepdims=True)
    log_total = jnp.log(jnp.sum(jnp.exp(shifted), axis=1, keepdims=True))
    chosen = (jnp.arange(classes)[None, :] == labels[:, None]).astype(jnp.float32)
    row_weight = label_mask.astype(jnp.float32)
    loss_part = jnp.sum((log_total[:, 0] - jnp.sum(shifted * chosen, axis=1)) * row_weight)
    grad_logits = (
        (jnp.exp(shifted - log_total) - chosen) * (row_weight / label_count)[:, None]
    ).astype(jnp.bfloat16)
    grad_head = outer_product(hidden_two, grad_logits)
    grad_two = against(grad_logits, full_head).astype(jnp.bfloat16).astype(jnp.float32)
    grad_pre_two = silu_slope(pre_two, grad_two)
    grad_outer = outer_product(joined_two, grad_pre_two)
    grad_joined = against(grad_pre_two, full_outer)
    share = grad_joined[:, hidden:] / count_two
    share_high = share.astype(jnp.bfloat16)
    share_low = (share - share_high.astype(jnp.float32)).astype(jnp.bfloat16)
    grad_one = outer_product(pick, share_high) + outer_product(pick, share_low)
    grad_one = jnp.concatenate(
        [grad_one[:seed_count] + grad_joined[:, :hidden], grad_one[seed_count:]], axis=0
    )
    grad_one = grad_one.astype(jnp.bfloat16).astype(jnp.float32)
    grad_pre_one = silu_slope(pre_one, grad_one)
    grad_inner = outer_product(joined_one, grad_pre_one)
    bias_part = jnp.concatenate(
        [
            jnp.sum(part.astype(jnp.float32), axis=0)
            for part in (grad_pre_one, grad_pre_two, grad_logits)
        ]
    )

    devices = lax.axis_size(every)
    grads = jnp.concatenate(
        [grad.reshape(devices, -1) for grad in (grad_inner, grad_outer, grad_head)], axis=1
    )
    shard = lax.psum_scatter(grads, every, scatter_dimension=0, tiled=True).reshape(-1)
    shards = []
    for weight in weights:
        shards.append(shard[: weight.size].reshape(weight.shape))
        shard = shard[weight.size :]
    packed = lax.psum(jnp.concatenate([bias_part, loss_part[None]]), every)
    bias_grad, loss_sum = packed[:-1], packed[-1]
    grad_partial = sum((jnp.sum(part * part) for part in shards))
    weight_partial = [jnp.sum(weight * weight) for weight in weights]
    squares = lax.psum(jnp.stack([grad_partial] + weight_partial), every)
    clip_norm = jnp.sqrt(squares[0] + jnp.sum(bias_grad * bias_grad))
    factor = jnp.minimum(1.0, CLIP / clip_norm)
    firsts = (first_inner, first_outer, first_head)
    seconds = (second_inner, second_outer, second_head)
    smooths = (smooth_inner, smooth_outer, smooth_head)
    states = [
        moments(weights[slot_at], shards[slot_at] * factor, firsts[slot_at], seconds[slot_at])
        for slot_at in range(3)
    ]
    update_square = lax.psum(jnp.stack([jnp.sum(state[2] * state[2]) for state in states]), every)
    weight_norms = jnp.sqrt(squares[1:])
    update_norms = jnp.sqrt(update_square)
    news = [
        weights[slot_at]
        - RATE * (weight_norms[slot_at] / update_norms[slot_at]) * states[slot_at][2]
        for slot_at in range(3)
    ]
    averages = [
        AVERAGE * smooths[slot_at] + (1.0 - AVERAGE) * news[slot_at] for slot_at in range(3)
    ]
    bias_first, bias_second, bias_update = moments(
        biases, bias_grad * factor, first_biases, second_biases
    )
    bias_new = biases - RATE * bias_ratio(biases, bias_update, hidden) * bias_update
    bias_average = AVERAGE * smooth_biases + (1.0 - AVERAGE) * bias_new
    return (
        loss_sum,
        label_count,
        clip_norm,
        jnp.stack([weight_norms, update_norms], axis=1),
        news[0],
        news[1],
        news[2],
        bias_new,
        states[0][0],
        states[1][0],
        states[2][0],
        bias_first,
        states[0][1],
        states[1][1],
        states[2][1],
        bias_second,
        averages[0],
        averages[1],
        averages[2],
        bias_average,
    )


def solution(mesh):
    in_specs = (
        P("dp", None),
        P("section", "dp", None),
        P("section", "dp"),
        P(None, "dp", None),
        P(None, "dp"),
        P(None, "dp", None),
        P(None, "dp"),
        P(None, "dp"),
        P(None, "dp"),
        P(("section", "dp"), None),
        P(("section", "dp"), None),
        P(("section", "dp"), None),
        P(),
        P(("section", "dp"), None),
        P(("section", "dp"), None),
        P(("section", "dp"), None),
        P(),
        P(("section", "dp"), None),
        P(("section", "dp"), None),
        P(("section", "dp"), None),
        P(),
        P(("section", "dp"), None),
        P(("section", "dp"), None),
        P(("section", "dp"), None),
        P(),
    )
    out_specs = (
        P(),
        P(),
        P(),
        P(),
        P(("section", "dp"), None),
        P(("section", "dp"), None),
        P(("section", "dp"), None),
        P(),
        P(("section", "dp"), None),
        P(("section", "dp"), None),
        P(("section", "dp"), None),
        P(),
        P(("section", "dp"), None),
        P(("section", "dp"), None),
        P(("section", "dp"), None),
        P(),
        P(("section", "dp"), None),
        P(("section", "dp"), None),
        P(("section", "dp"), None),
        P(),
    )
    return jax.shard_map(
        on_device, mesh=mesh, in_specs=in_specs, out_specs=out_specs, check_vma=False
    )
```

```python
import functools

import jax
import jax.numpy as jnp
from jax import lax
from jax.experimental import pallas as pl
from jax.experimental.pallas import tpu as pltpu
from jax.sharding import PartitionSpec as P

STEP = 5


BETA_ONE = 0.9
BETA_TWO = 0.999
EPSILON = 1e-06
DECAY = 0.01
RATE = 0.25
CLIP = 0.05
AVERAGE = 0.9


VMEM_TABLE_LIMIT = 36 * 2**20
WHOLE_TABLE_LIMIT = 64 * 2**20
MESH = pl.DeviceIdType.MESH
SLOT = 16
BLOCK = 16
SHARES = (1, 3, 3, 3, 1)
SPARE_SHARES = (1, 2, 2, 2, 2)
CHUNKS = len(SHARES)
GROUP = 4
SETS = 4
SPARE = 9
SETTLE = 3
AHEAD = 1
AHEAD_ACROSS = 1
LAG = 2
FAR_LAG = 5
SPARE_AFTER = 2
SPARE_LAG = 4
TILE = 256
PAUSE = 6
FORWARD_SLOT = 1
MEAN_SLOT = 3


class Parts:
    def __init__(self, refs, base):
        self.grads, self.half_in, self.half, self.plane_in, self.fourth, self.line_in = refs
        self.base = base


def step_kernel(
    fan_outer,
    table_ref,
    weight_refs,
    first_refs,
    second_refs,
    bias_ref,
    mask_ref,
    owner_ref,
    local_ref,
    near_ref,
    seed_near_ref,
    seed_count_ref,
    label_ref,
    out_ref,
    joined_ref,
    weights_ref,
    hits_ref,
    hits_back_ref,
    full_ref,
    packed,
    parts,
    idx_ref,
    mix_ref,
    wide,
    seed_ref,
    seed_across_ref,
    stages,
    lists,
    full_inner_ref,
    full_outer_ref,
    full_head_ref,
    count_ref,
    first_pre,
    first_hidden,
    mean_ref,
    own_part,
    inner_sum,
    early_refs,
    late_refs,
    extra_ref,
    extra_plane,
    extra_line,
    sums,
    own_sem,
    z_sem,
    spare_sem,
    x_sem,
    y_sem,
    far_sem,
    twin_sem,
    twin_own_sem,
    double_sem,
    send_sem,
    double_send_sem,
    list_sem,
    sum_sem,
    sum_send_sem,
    norm_sem,
    norm_send_sem,
    late_sem,
    late_send_sem,
):
    section, at = lax.axis_index("section"), lax.axis_index("dp")
    z, core = at // 2, at % 2
    flipped = z // 2
    height = z + flipped * (3 - 2 * z)
    pairs = table_ref.shape[0]
    spare = pairs * SPARE // 64
    quarter = (pairs - spare) // 4
    part_sizes = [quarter // sum(SHARES) * share for share in SHARES]
    spare_sizes = [spare // sum(SPARE_SHARES) * share for share in SPARE_SHARES]

    def level(value):
        return value + flipped * (3 - 2 * value)

    twin = (section, z * 2 + 1 - core)
    beside_x = (section + 1 - 2 * (section % 2), at)
    beside_y = (section + 2 - 4 * (section // 2), at)
    inner_z = (section, level(1 - height) * 2 + core)
    across_z = (section, level(2) * 2 + core)
    outer_z = (section, level(0) * 2 + core)
    skip_z = (section, ((z + 2) % 4) * 2 + core)
    sources = [level(1 - height), level(2), level(3)]
    crosses = height == 1
    plane = [((section + k) % 4, at) for k in range(1, 4)]
    beyond = [((section + k) % 4, z * 2 + 1 - core) for k in range(1, 4)]
    line = [(section, ((z + k) % 4) * 2 + core) for k in range(1, 4)]
    neighbours = [twin] + plane + beyond

    barrier = pltpu.get_barrier_semaphore()
    others = [((section + k // 8) % 4, (at + k % 8) % 8) for k in range(1, 32)]
    for partner in others:
        pl.semaphore_signal(barrier, inc=1, device_id=partner, device_id_type=MESH)
    pl.semaphore_wait(barrier, 31)

    sent, now, count = [], [0], [0]

    def region(shard, part, piece):
        start_at = shard * pairs + part * quarter + sum(part_sizes[:piece])
        return full_ref.at[pl.ds(start_at, part_sizes[piece])]

    def spare_region(shard, piece):
        start_at = shard * pairs + 4 * quarter + sum(spare_sizes[:piece])
        return full_ref.at[pl.ds(start_at, spare_sizes[piece])]

    def send(source, target, recv, device, when=None):
        number = count[0]
        count[0] += 1
        copy = pltpu.make_async_remote_copy(
            src_ref=source,
            dst_ref=target,
            send_sem=send_sem.at[number],
            recv_sem=recv,
            device_id=device,
            device_id_type=MESH,
        )
        sent.append((copy, when, now[0]))
        if when is None:
            copy.start()
        else:
            pl.when(when)(copy.start)
        return copy

    def arrived(target, recv):
        pltpu.make_async_copy(target, target, recv).wait()

    def own_piece(piece, device, number, when=None):
        start_at = section * quarter + sum(part_sizes[:piece])
        block = table_ref.at[pl.ds(start_at, part_sizes[piece])]
        send(block, region(at, section, piece), z_sem.at[number], device, when)

    for piece in range(min(AHEAD, CHUNKS)):
        own_piece(piece, inner_z, piece)
    for piece in range(min(AHEAD_ACROSS, CHUNKS)):
        own_piece(piece, across_z, CHUNKS + piece, crosses)
    whole = full_ref.at[pl.ds(at * pairs, pairs)]
    own = pltpu.make_async_copy(table_ref, whole, own_sem)
    own.start()
    send(table_ref, whole, twin_own_sem, twin)

    inner_ref, outer_ref, head_ref = weight_refs
    row_inner, row_outer, row_head = (ref.shape[0] for ref in weight_refs)
    hidden, classes = inner_ref.shape[1], head_ref.shape[1]
    head_at = row_inner + row_outer
    packed[0:row_inner, :] = inner_ref[...]
    packed[row_inner:head_at, :] = outer_ref[...]
    packed[head_at:, :] = jnp.zeros((row_head, hidden), jnp.float32)
    packed[head_at:, 0:classes] = head_ref[...]
    labelled = jnp.sum(mask_ref[...].astype(jnp.float32)).astype(jnp.int32)
    lane = lax.broadcasted_iota(jnp.int32, (1, hidden), 1)
    high_part = (labelled // 256).astype(jnp.float32)
    low_part = (labelled % 256).astype(jnp.float32)
    tail = jnp.where(lane == classes, high_part, jnp.where(lane == classes + 1, low_part, 0.0))
    packed[head_at : head_at + 1, :] += tail
    mine = (core * 4 + section) * 4 + z
    weights_ref[mine] = packed[...].astype(jnp.bfloat16)
    doubling = [(inner_z, 1), (skip_z, 2), (beside_x, 4), (beside_y, 8), (twin, 16)]
    doubled = []

    def double_start(number):
        device, size = doubling[number]
        block = weights_ref.at[pl.ds((mine // size) * size, size)]
        copy = pltpu.make_async_remote_copy(
            src_ref=block,
            dst_ref=block,
            send_sem=double_send_sem.at[number],
            recv_sem=double_sem.at[number],
            device_id=device,
            device_id_type=MESH,
        )
        copy.start()
        doubled.append(copy)

    double_start(0)

    def eye(size):
        same_place = lax.broadcasted_iota(jnp.int32, (size, size), 0) == lax.broadcasted_iota(
            jnp.int32, (size, size), 1
        )
        return same_place.astype(jnp.float32).astype(jnp.bfloat16)

    def as_low(values):
        return values.astype(jnp.float32).astype(jnp.bfloat16)

    placed = owner_ref[...] * (2 * pairs) + local_ref[...]
    pair_at = placed // 2
    high = owner_ref.shape[0]
    for k, values in enumerate((pair_at % 256, pair_at // 256, placed % 2)):
        parts[128 * k : 128 * (k + 1), :] = against(eye(128), as_low(values)).astype(jnp.bfloat16)
    looked_rows = near_ref.shape[0]
    seeds = seed_ref.shape[0]
    tiles = hits_ref.shape[1] // TILE
    seed_row = pl.ds(section, 1)
    live_seeds = seed_count_ref[seed_row, :]
    for j in range(fan_outer):
        near_seeds = seed_near_ref[j, seed_row, :]
        seed_across_ref[j : j + 1, :] = jnp.where(live_seeds > j, near_seeds, -1)
    seed_across_ref[fan_outer : fan_outer + 1, :] = label_ref[seed_row, :]
    seed_across_ref[fan_outer + 1 : fan_outer + 2, :] = mask_ref[seed_row, :]
    seed_across_ref[fan_outer + 2 :, :] = jnp.zeros((SLOT - fan_outer - 2, seeds), jnp.int32)
    shifted_up = seed_across_ref[...] + 1
    seed_ref[...] = (
        64.0 * against(eye(seeds), as_low(shifted_up // 64))
        + against(eye(seeds), as_low(shifted_up % 64))
    ).astype(jnp.int32) - 1
    total = 3 * CHUNKS
    steps = total + max(FAR_LAG, SPARE_LAG)
    per_step = -(-looked_rows // (8 * steps)) * 8
    for j in range(fan_outer):
        wide[j] = jnp.broadcast_to(seed_ref[:, j : j + 1], (seeds, TILE))

    def look_up(first, last):
        def rows_of(block, carry):
            start_at = pl.multiple_of(block * 8, 8)
            sub = lax.broadcasted_iota(jnp.int32, (high, 256), 0)
            low_at = lax.broadcasted_iota(jnp.int32, (128, 256), 0)
            row = lax.broadcasted_iota(jnp.int32, (256, 512), 0)
            column = lax.broadcasted_iota(jnp.int32, (256, 512), 1)
            for k in range(8):
                node = near_ref[pl.ds(start_at + k, 1), :]
                hot = (sub == node // 128).astype(jnp.float32).astype(jnp.bfloat16)
                got = jnp.dot(parts[...], hot, preferred_element_type=jnp.float32)
                chosen = low_at == node % 128
                found = jnp.where(chosen, got[0:128] + 256.0 * got[128:256], 0.0)
                odd = jnp.where(chosen, got[256:384], 0.0)
                entry_at = jnp.sum(found, axis=0, keepdims=True).astype(jnp.int32)
                idx_ref[block * 2 + k // 4, k % 4 : k % 4 + 1, :] = jnp.clip(
                    entry_at, 0, full_ref.shape[0] - 1
                )
                mix_ref[pl.ds(start_at + k, 1), 0:256] = jnp.sum(odd, axis=0, keepdims=True)
            odd = mix_ref[pl.ds(start_at, 8), 0:256]
            live = (near_ref[pl.ds(start_at, 8), :] >= 0).astype(jnp.float32)
            mix_ref[pl.ds(start_at, 8), :] = jnp.dot(
                (live * (1.0 - odd)).astype(jnp.bfloat16),
                (column == 2 * row).astype(jnp.float32).astype(jnp.bfloat16),
                preferred_element_type=jnp.float32,
            ) + jnp.dot(
                (live * odd).astype(jnp.bfloat16),
                (column == 2 * row + 1).astype(jnp.float32).astype(jnp.bfloat16),
                preferred_element_type=jnp.float32,
            )
            return carry

        lax.fori_loop(first // 8, last // 8, rows_of, 0)

    def mark(tile):
        start_at = tile * TILE
        dest = lax.broadcasted_iota(jnp.int32, (seeds, TILE), 1) + start_at
        hits = jnp.zeros((seeds, TILE), jnp.float32)
        for j in range(fan_outer):
            hits = hits + (wide[j] == dest).astype(jnp.float32)
        hits_ref[:, start_at : start_at + TILE] = hits.astype(jnp.bfloat16)
        dest = lax.broadcasted_iota(jnp.int32, (TILE, seeds), 0) + start_at
        hits = jnp.zeros((TILE, seeds), jnp.float32)
        for j in range(fan_outer):
            hits = hits + (seed_across_ref[j : j + 1, :] == dest).astype(jnp.float32)
        hits_back_ref[start_at : start_at + TILE, :] = hits.astype(jnp.bfloat16)

    def sort_weights():
        everyone = weights_ref[...].astype(jnp.float32)
        order = block_order()
        inner, outer, head = (
            jnp.concatenate([everyone[spot, lower:upper] for spot in order], axis=0)
            for lower, upper in ((0, row_inner), (row_inner, head_at), (head_at, head_at + row_head))
        )
        full_inner_ref[...] = inner.astype(jnp.bfloat16)
        full_outer_ref[...] = outer.astype(jnp.bfloat16)
        full_head_ref[...] = jnp.where(lane < classes, head, 0.0).astype(jnp.bfloat16)
        tails = everyone[0:4, head_at : head_at + 1] + everyone[16:20, head_at : head_at + 1]
        tails = jnp.sum(tails.reshape(4, hidden), axis=0, keepdims=True)
        scale = jnp.where(lane == classes, 256.0, jnp.where(lane == classes + 1, 1.0, 0.0))
        labels_in_all = jnp.sum(tails * scale, axis=1, keepdims=True)
        count_ref[...] = jnp.broadcast_to(jnp.maximum(labels_in_all, 1.0), count_ref.shape)

    twins = []

    def to_twin(block, number):
        send(block, block, twin_sem.at[number], twin)
        twins.append((number, now[0]))

    def from_twin(number):
        kind, step = divmod(number, total)
        turn, piece = divmod(step, CHUNKS)
        shard = sources[turn] * 2 + 1 - core
        if kind == 4:
            block = spare_region(shard, piece)
        else:
            block = region(shard, (section, beside_x[0], beside_y[0], 3 - section)[kind], piece)
        arrived(block, twin_sem.at[number])

    def settle(until):
        while twins and twins[0][1] <= until:
            from_twin(twins.pop(0)[0])
        while sent and sent[0][2] <= until - SETTLE:
            copy, when, _ = sent.pop(0)
            if when is None:
                copy.wait_send()
            else:
                pl.when(when)(copy.wait_send)

    for step in range(steps):
        now[0] = step
        if step < total:
            turn, piece = divmod(step, CHUNKS)
            shard = sources[turn] * 2 + core
            goes, number = (across_z, 2 * CHUNKS + piece) if turn == 0 else (outer_z, step)
            block = region(shard, section, piece)
            arrived(block, z_sem.at[step])
            send(block, block, z_sem.at[number], goes, crosses)
            send(block, block, x_sem.at[step], beside_x)
            send(block, block, y_sem.at[step], beside_y)
            to_twin(block, step)
            if step + AHEAD < CHUNKS:
                own_piece(step + AHEAD, inner_z, step + AHEAD)
            if step + AHEAD_ACROSS < CHUNKS:
                piece = step + AHEAD_ACROSS
                own_piece(piece, across_z, CHUNKS + piece, crosses)
            piece = step - SPARE_AFTER
            if 0 <= piece < CHUNKS:
                start_at = 4 * quarter + sum(spare_sizes[:piece])
                block = table_ref.at[pl.ds(start_at, spare_sizes[piece])]
                goal = spare_region(at, piece)
                send(block, goal, spare_sem.at[piece], inner_z)
                send(block, goal, spare_sem.at[CHUNKS + piece], across_z, crosses)
        late = step - SPARE_LAG
        if 0 <= late < total:
            turn, piece = divmod(late, CHUNKS)
            shard = sources[turn] * 2 + core
            goes, number = (across_z, 2 * CHUNKS + piece) if turn == 0 else (outer_z, late)
            block = spare_region(shard, piece)
            arrived(block, spare_sem.at[late])
            send(block, block, spare_sem.at[number], goes, crosses)
            to_twin(block, 4 * total + late)
        late = step - LAG
        if 0 <= late < total:
            turn, piece = divmod(late, CHUNKS)
            shard = sources[turn] * 2 + core
            block = region(shard, beside_x[0], piece)
            arrived(block, x_sem.at[late])
            send(block, block, far_sem.at[late], beside_y, core == piece % 2)
            to_twin(block, total + late)
            block = region(shard, beside_y[0], piece)
            arrived(block, y_sem.at[late])
            send(block, block, far_sem.at[late], beside_x, core != piece % 2)
            to_twin(block, 2 * total + late)
        later = step - FAR_LAG
        if 0 <= later < total:
            turn, piece = divmod(later, CHUNKS)
            shard = sources[turn] * 2 + core
            block = region(shard, 3 - section, piece)
            arrived(block, far_sem.at[later])
            to_twin(block, 3 * total + later)
        if step % 2 == 0 and step // 2 < len(doubling):
            doubled[step // 2].wait()
            if step // 2 + 1 < len(doubling):
                double_start(step // 2 + 1)
        first = min(step * per_step, looked_rows)
        last = min(first + per_step, looked_rows)
        if last > first:
            look_up(first, last)
        for tile in range(step * tiles // steps, (step + 1) * tiles // steps):
            mark(tile)
        settle(step - 3)

    sort_weights()
    settle(steps)
    arrived(full_ref.at[pl.ds((z * 2 + 1 - core) * pairs, pairs)], twin_own_sem)
    own.wait()

    blocks = looked_rows
    unit_at = lax.broadcasted_iota(jnp.int32, (BLOCK, 2 * BLOCK * SLOT), 1)
    same = unit_at // (2 * SLOT) == lax.broadcasted_iota(jnp.int32, unit_at.shape, 0)
    near_part = jnp.logical_and(same, unit_at % (2 * SLOT) < 2 * SLOT - 2).astype(jnp.float32)
    self_part = jnp.logical_and(same, unit_at % (2 * SLOT) >= 2 * SLOT - 2).astype(jnp.float32)
    turns = blocks // GROUP

    def fetch(turn, slot):
        return pltpu.make_async_copy(
            idx_ref.at[jnp.minimum(turn, turns - 1)], lists[slot], list_sem.at[slot]
        )

    def pick(member, slot, stage):
        def unit(number, carry):
            entry = full_ref[lists[slot][member, number]]
            stage[pl.ds(2 * number, 2), :] = entry.astype(jnp.float32)
            return carry

        lax.fori_loop(0, BLOCK * SLOT, unit, 0, unroll=BLOCK * SLOT)

    def reduce(block, stage):
        mix = mix_ref[pl.ds(block, 1), :]
        near = mix * near_part
        left = jnp.concatenate([near, mix * self_part], axis=0).astype(jnp.bfloat16)
        out = jnp.dot(left, stage[...].astype(jnp.bfloat16), preferred_element_type=jnp.float32)
        count = jnp.maximum(jnp.sum(near, axis=1, keepdims=True), 1.0)
        both = jnp.concatenate([out[BLOCK:], out[:BLOCK] / count], axis=1)
        start_at = pl.multiple_of(block * BLOCK, BLOCK)
        joined_ref[pl.ds(start_at, BLOCK), :] = both.astype(jnp.bfloat16)

    bias_inner, bias_outer, bias_head = bias_rows_of(bias_ref, hidden)

    def forward(tile):
        tile_rows = pl.ds(pl.multiple_of(tile * TILE, TILE), TILE)
        before = (
            jnp.dot(
                joined_ref[tile_rows, :], full_inner_ref[...], preferred_element_type=jnp.float32
            )
            + bias_inner
        )
        first_pre[tile_rows, :] = before
        first_hidden[tile_rows, :] = (before * lax.logistic(before)).astype(jnp.bfloat16)

    def add_mean(tile, carried):
        tile_rows = pl.ds(pl.multiple_of(tile * TILE, TILE), TILE)
        found = jnp.dot(
            hits_ref[:, tile_rows], first_hidden[tile_rows, :], preferred_element_type=jnp.float32
        )
        mean_ref[...] = mean_ref[...] * carried + found

    near_stages, far_stages = stages
    mean_ref[...] = jnp.zeros(mean_ref.shape, jnp.float32)
    joined_ref[0:TILE, :] = jnp.zeros((TILE, joined_ref.shape[1]), jnp.bfloat16)
    for slot in range(SETS):
        fetch(slot, slot).start()
    for member in range(GROUP):
        far_stages[member][...] = jnp.zeros(far_stages[member].shape, jnp.float32)

    def round_of(number, carry):
        for slot in range(SETS):
            turn = number * SETS + slot
            fetch(turn, slot).wait()
            for member in range(GROUP):
                pick(member, slot, stages[slot % 2][member])
                reduce(
                    jnp.maximum((turn - 1) * GROUP + member, 0), stages[1 - slot % 2][member]
                )
            if slot == FORWARD_SLOT:
                forward(jnp.maximum(number - 1, 0))
            if slot == MEAN_SLOT:
                add_mean(jnp.maximum(number - 1, 0), (number > 1).astype(jnp.float32))
            fetch(turn + SETS, slot).start()
        return carry

    lax.fori_loop(0, blocks // (GROUP * SETS), round_of, 0)
    for slot in range(SETS):
        fetch(0, slot).wait()
    for member in range(GROUP):
        reduce(blocks - GROUP + member, stages[(SETS - 1) % 2][member])
    forward(tiles - 1)
    add_mean(tiles - 1, 1.0)
    summing = []

    def pass_on(source, target, number, device):
        copy = pltpu.make_async_remote_copy(
            src_ref=source,
            dst_ref=target,
            send_sem=sum_send_sem.at[len(summing)],
            recv_sem=sum_sem.at[number],
            device_id=device,
            device_id_type=MESH,
        )
        summing.append(copy)
        copy.start()

    def passed(target, number):
        arrived(target, sum_sem.at[number])

    def to_other_core(part):
        pass_on(part.grads.at[pl.ds((1 - core) * 16, 16)], part.half_in, part.base, twin)

    def to_plane(part):
        passed(part.half_in, part.base)
        part.half[...] = part.grads[pl.ds(core * 16, 16)] + part.half_in[...]
        for partner in plane:
            block = part.half.at[pl.ds(partner[0] * 4, 4)]
            pass_on(block, part.plane_in.at[section], part.base + 1 + section, partner)
        part.plane_in[section] = part.half[pl.ds(section * 4, 4)]

    def to_line(part):
        for k in range(1, 4):
            other = (section + k) % 4
            passed(part.plane_in.at[other], part.base + 1 + other)
        part.fourth[...] = (part.plane_in[0] + part.plane_in[1]) + (
            part.plane_in[2] + part.plane_in[3]
        )
        for k, partner in enumerate(line):
            block = part.fourth.at[pl.ds((z + k + 1) % 4, 1)]
            pass_on(block, part.line_in.at[pl.ds(z, 1)], part.base + 5 + z, partner)
        part.line_in[z] = part.fourth[z]

    def whole_sum(part):
        for k in range(1, 4):
            other = (z + k) % 4
            passed(part.line_in.at[pl.ds(other, 1)], part.base + 5 + other)
        return (part.line_in[0] + part.line_in[1]) + (part.line_in[2] + part.line_in[3])

    def share(value, slots, base, me, partners):
        slots[me] = value
        for partner in partners:
            pass_on(slots.at[me], slots.at[me], base + me, partner)

    def collect(slots, base, me):
        count = slots.shape[0]
        for k in range(1, count):
            other = (me + k) % count
            passed(slots.at[other], base + other)
        values = [slots[k] for k in range(count)]
        while len(values) > 1:
            values = [values[k] + values[k + 1] for k in range(0, len(values), 2)]
        return values[0]

    early = Parts(early_refs, 0)
    late_grads, late_half_in, late_half, late_in = late_refs
    order = block_order()
    full_outer, full_head = full_outer_ref[...], full_head_ref[...]
    label_count = count_ref[:, 0:1]
    kept = seed_ref[:, 0:fan_outer]
    count_two = jnp.sum((kept >= 0).astype(jnp.float32), axis=1, keepdims=True)
    mean_two = (mean_ref[...] / count_two).astype(jnp.bfloat16)
    joined_two = jnp.concatenate([first_hidden[0:seeds, :], mean_two], axis=1)
    pre_two = jnp.dot(joined_two, full_outer, preferred_element_type=jnp.float32) + bias_outer
    gate_two = lax.logistic(pre_two)
    hidden_two = (pre_two * gate_two).astype(jnp.bfloat16)
    logits = jnp.dot(hidden_two, full_head, preferred_element_type=jnp.float32) + bias_head
    inside = lane < classes
    highest = jnp.max(jnp.where(inside, logits, -jnp.inf), axis=1, keepdims=True)
    shifted = jnp.where(inside, logits - highest, 0.0)
    total_exp = jnp.sum(jnp.where(inside, jnp.exp(shifted), 0.0), axis=1, keepdims=True)
    log_total = jnp.log(total_exp)
    chosen = (lane == seed_ref[:, fan_outer : fan_outer + 1]).astype(jnp.float32)
    row_weight = seed_ref[:, fan_outer + 1 : fan_outer + 2].astype(jnp.float32)
    loss = jnp.sum((log_total - jnp.sum(shifted * chosen, axis=1, keepdims=True)) * row_weight)
    grad_logits = (jnp.exp(shifted - log_total) - chosen) * (row_weight / label_count)
    grad_logits = jnp.where(inside, grad_logits, 0.0).astype(jnp.bfloat16)
    grad_head = outer_product(hidden_two, grad_logits)
    grad_two = against(grad_logits, full_head).astype(jnp.bfloat16).astype(jnp.float32)
    grad_pre_two = (grad_two * gate_two * (1.0 + pre_two * (1.0 - gate_two))).astype(jnp.bfloat16)
    grad_outer = outer_product(joined_two, grad_pre_two)
    for number, spot in enumerate(order):
        early.grads[spot, 0:row_outer, :] = grad_outer[
            number * row_outer : (number + 1) * row_outer
        ]
        early.grads[spot, row_outer : row_outer + row_head, :] = grad_head[
            number * row_head : (number + 1) * row_head
        ]
    to_other_core(early)
    extra_ref[1:2, :] = jnp.sum(grad_pre_two.astype(jnp.float32), axis=0, keepdims=True)
    extra_ref[2:3, :] = jnp.sum(grad_logits.astype(jnp.float32), axis=0, keepdims=True)
    extra_ref[3:4, :] = jnp.where(lane == 0, loss, jnp.where(lane == 1, label_count, 0.0))
    extra_ref[4:8, :] = jnp.zeros((4, hidden), jnp.float32)
    grad_joined = against(grad_pre_two, full_outer)
    share_part = grad_joined[:, hidden:] / count_two
    share_high = share_part.astype(jnp.bfloat16)
    share_low = (share_part - share_high.astype(jnp.float32)).astype(jnp.bfloat16)
    inner_sum[...] = jnp.zeros(inner_sum.shape, jnp.float32)
    share_both = jnp.concatenate([share_high, share_low], axis=0)
    own_part[...] = jnp.zeros(own_part.shape, jnp.float32)
    own_part[0:seeds, :] = grad_joined[:, 0:hidden]

    def backward(tile, bias_sum, own=None):
        tile_rows = pl.ds(pl.multiple_of(jnp.int32(tile) * TILE, TILE), TILE)
        hits = hits_back_ref[tile_rows, :]
        both_hits = jnp.concatenate([hits, hits], axis=1)
        grad_one = jnp.dot(both_hits, share_both, preferred_element_type=jnp.float32)
        if own is not None:
            grad_one = grad_one + own
        grad_one = grad_one.astype(jnp.bfloat16).astype(jnp.float32)
        before = first_pre[tile_rows, :]
        gate = lax.logistic(before)
        grad_pre = (grad_one * gate * (1.0 + before * (1.0 - gate))).astype(jnp.bfloat16)
        inner_sum[...] += outer_product(joined_ref[tile_rows, :], grad_pre)
        return bias_sum + jnp.sum(grad_pre.astype(jnp.float32), axis=0, keepdims=True)

    bias_sum = backward(0, jnp.zeros((1, hidden), jnp.float32), own_part[...])
    bias_sum = lax.fori_loop(1, PAUSE, backward, bias_sum, unroll=PAUSE - 1)
    to_plane(early)
    bias_sum = lax.fori_loop(PAUSE, tiles, backward, bias_sum, unroll=tiles - PAUSE)
    extra_ref[0:1, :] = bias_sum
    grad_inner = inner_sum[...]
    for number, spot in enumerate(order):
        late_grads[spot] = grad_inner[number * row_inner : (number + 1) * row_inner]
    pass_on(late_grads.at[pl.ds((1 - core) * 16, 16)], late_half_in, 9, twin)
    share(extra_ref[...], extra_plane, 18, section * 2 + core, neighbours)
    passed(late_half_in, 9)
    late_half[...] = late_grads[pl.ds(core * 16, 16)] + late_half_in[...]
    same_core = [((section + k // 4) % 4, (z + k % 4) % 4) for k in range(1, 16)]
    my_place = section * 4 + z
    for to_section, to_z in same_core:
        pltpu.make_async_remote_copy(
            src_ref=late_half.at[to_section * 4 + to_z],
            dst_ref=late_in.at[my_place],
            send_sem=late_send_sem,
            recv_sem=late_sem,
            device_id=(to_section, to_z * 2 + core),
            device_id_type=MESH,
        ).start()
    late_in[my_place] = late_half[my_place]
    to_line(early)
    share(collect(extra_plane, 18, section * 2 + core), extra_line, 26, z, line)

    short_lane = lax.broadcasted_iota(jnp.int32, (1, 128), 1)
    my_number = section * 8 + at

    def square_sum(value):
        return jnp.sum(jnp.sum(value * value, axis=0, keepdims=True), axis=1, keepdims=True)

    def everywhere(values, number):
        found = jnp.zeros((1, 128), jnp.float32)
        for k, value in enumerate(values):
            found = jnp.where(short_lane == k, value, found)
        sums[number, my_number] = found
        mine_there = sums.at[number, my_number]
        for partner in others:
            pltpu.make_async_remote_copy(
                src_ref=mine_there,
                dst_ref=mine_there,
                send_sem=norm_send_sem.at[number],
                recv_sem=norm_sem.at[number],
                device_id=partner,
                device_id_type=MESH,
            ).start()
        if number == 1:
            for copy in summing:
                copy.wait_send()
        all_others = sums.at[number, pl.ds(0, 31)]
        arrived(all_others, norm_sem.at[number])
        return jnp.sum(sums[number], axis=0)

    held = [ref[...] for ref in weight_refs]
    weight_squares = [square_sum(weight) for weight in held]
    rest = whole_sum(early)
    rest_square = square_sum(rest)
    extra = collect(extra_line, 26, z)
    bias_square = square_sum(extra[0:3])
    settle(steps + SETTLE)
    arrived(late_in.at[pl.ds(0, 15)], late_sem)
    shard = jnp.sum(late_in[...], axis=0)
    pieces = [shard, rest[0:row_outer], rest[row_outer:, 0:classes]]
    values = everywhere([square_sum(shard) + rest_square] + weight_squares, 0)
    grad_square = jnp.sum(jnp.where(short_lane == 0, values, 0.0), axis=1, keepdims=True)
    clip_norm = jnp.sqrt(grad_square + bias_square)
    factor = jnp.minimum(1.0, CLIP / clip_norm)
    update_squares = []
    for k in range(3):
        update = moments(held[k], pieces[k] * factor, first_refs[k][...], second_refs[k][...])[2]
        update_squares.append(square_sum(update))
    updates = everywhere(update_squares, 1)
    rows = row_inner + row_outer + row_head
    out_ref[0:row_inner, :] = shard
    out_ref[row_inner:rows, :] = rest
    out_ref[rows : rows + 8, :] = extra
    out_ref[rows + 8 : rows + 9, 0:128] = values
    out_ref[rows + 8 : rows + 9, 128:256] = updates
    out_ref[rows + 9 :, :] = jnp.zeros((7, hidden), jnp.float32)
    for number in range(2):
        arrived(sums.at[number, pl.ds(0, 31)], norm_send_sem.at[number])
    arrived(late_in.at[pl.ds(0, 15)], late_send_sem)


def block_order():
    return [(e % 2) * 16 + (e // 8) * 4 + (e % 8) // 2 for e in range(32)]


def bias_rows_of(ref, hidden):
    width = ref.shape[0] - 2 * hidden
    last = ref[pl.ds(2 * hidden, width)].reshape(1, width)
    return (
        ref[pl.ds(0, hidden)].reshape(1, hidden),
        ref[pl.ds(hidden, hidden)].reshape(1, hidden),
        jnp.concatenate([last, jnp.zeros((1, hidden - width), jnp.float32)], axis=1),
    )


def summed_step(
    node_table,
    weights,
    firsts,
    seconds,
    biases,
    label_mask,
    owner_ids,
    row_ids,
    near,
    outer_neighbours,
    outer_counts,
    labels,
):
    devices = lax.axis_size(("section", "dp"))
    table_rows, width = node_table.shape
    frontier_high = owner_ids.size // 128
    fan_outer = outer_neighbours.shape[2]
    looked = near.shape[0]
    dest_count = looked * BLOCK
    seeds = outer_neighbours.shape[1]
    hidden = weights[0].shape[1]
    row_inner = weights[0].shape[0]
    rows = sum(weight.shape[0] for weight in weights)
    total = 3 * CHUNKS
    sends = 4 * CHUNKS + 1 + 3 * total + total + 2 * total + 5 * total
    vmem = pl.BlockSpec(memory_space=pltpu.VMEM)
    stage = (pltpu.VMEM((2 * BLOCK * SLOT, width), jnp.float32),) * GROUP

    def on_the_way(depth):
        return (
            pltpu.VMEM((devices, depth, hidden), jnp.float32),
            pltpu.VMEM((16, depth, hidden), jnp.float32),
            pltpu.VMEM((16, depth, hidden), jnp.float32),
            pltpu.VMEM((4, 4, depth, hidden), jnp.float32),
            pltpu.VMEM((4, depth, hidden), jnp.float32),
            pltpu.VMEM((4, depth, hidden), jnp.float32),
        )

    return pl.pallas_call(
        functools.partial(step_kernel, fan_outer),
        out_shape=jax.ShapeDtypeStruct((rows + 16, hidden), jnp.float32),
        in_specs=[pl.BlockSpec(memory_space=pl.ANY)] + [(vmem,) * 3] * 3 + [vmem] * 8,
        out_specs=vmem,
        scratch_shapes=[
            pltpu.VMEM((dest_count, 2 * width), jnp.bfloat16),
            pltpu.VMEM((devices, rows, hidden), jnp.bfloat16),
            pltpu.VMEM((seeds, dest_count), jnp.bfloat16),
            pltpu.VMEM((dest_count, seeds), jnp.bfloat16),
            pltpu.VMEM((lax.axis_size("dp") * table_rows // 2, 2, width), jnp.bfloat16),
            pltpu.VMEM((rows, hidden), jnp.float32),
            pltpu.VMEM((384, frontier_high), jnp.bfloat16),
            pltpu.VMEM((looked // GROUP, GROUP, 256), jnp.int32),
            pltpu.VMEM((looked, 512), jnp.float32),
            pltpu.VMEM((fan_outer, seeds, TILE), jnp.int32),
            pltpu.VMEM((seeds, SLOT), jnp.int32),
            pltpu.VMEM((SLOT, seeds), jnp.int32),
            (stage, stage),
            (pltpu.SMEM((GROUP, BLOCK * SLOT), jnp.int32),) * SETS,
            pltpu.VMEM((hidden, hidden), jnp.bfloat16),
            pltpu.VMEM((2 * hidden, hidden), jnp.bfloat16),
            pltpu.VMEM((hidden, hidden), jnp.bfloat16),
            pltpu.VMEM((1, hidden), jnp.float32),
            pltpu.VMEM((dest_count, hidden), jnp.float32),
            pltpu.VMEM((dest_count, hidden), jnp.bfloat16),
            pltpu.VMEM((seeds, hidden), jnp.float32),
            pltpu.VMEM((TILE, hidden), jnp.float32),
            pltpu.VMEM((hidden, hidden), jnp.float32),
            on_the_way(rows - row_inner),
            (
                pltpu.VMEM((devices, row_inner, hidden), jnp.float32),
                pltpu.VMEM((16, row_inner, hidden), jnp.float32),
                pltpu.VMEM((16, row_inner, hidden), jnp.float32),
                pltpu.VMEM((16, row_inner, hidden), jnp.float32),
            ),
            pltpu.VMEM((8, hidden), jnp.float32),
            pltpu.VMEM((8, 8, hidden), jnp.float32),
            pltpu.VMEM((4, 8, hidden), jnp.float32),
            pltpu.VMEM((2, devices, 1, 128), jnp.float32),
            pltpu.SemaphoreType.DMA(()),
            pltpu.SemaphoreType.DMA((total,)),
            pltpu.SemaphoreType.DMA((total,)),
            pltpu.SemaphoreType.DMA((total,)),
            pltpu.SemaphoreType.DMA((total,)),
            pltpu.SemaphoreType.DMA((total,)),
            pltpu.SemaphoreType.DMA((5 * total,)),
            pltpu.SemaphoreType.DMA(()),
            pltpu.SemaphoreType.DMA((5,)),
            pltpu.SemaphoreType.DMA((sends,)),
            pltpu.SemaphoreType.DMA((5,)),
            pltpu.SemaphoreType.DMA((SETS,)),
            pltpu.SemaphoreType.DMA((30,)),
            pltpu.SemaphoreType.DMA((24,)),
            pltpu.SemaphoreType.DMA((2,)),
            pltpu.SemaphoreType.DMA((2,)),
            pltpu.SemaphoreType.DMA(()),
            pltpu.SemaphoreType.DMA(()),
        ],
        compiler_params=pltpu.CompilerParams(
            collective_id=0, has_side_effects=True, vmem_limit_bytes=56 * 2**20
        ),
    )(
        pltpu.with_memory_space_constraint(
            node_table.reshape(table_rows // 2, 2, width), pltpu.HBM
        ),
        weights,
        firsts,
        seconds,
        biases,
        label_mask,
        owner_ids.reshape(-1, 128),
        row_ids.reshape(-1, 128),
        near,
        outer_neighbours.transpose(2, 0, 1),
        outer_counts,
        labels,
    )


def final_kernel(
    sizes,
    devices,
    sums_ref,
    weight_refs,
    first_refs,
    second_refs,
    smooth_refs,
    bias_refs,
    loss_ref,
    count_ref,
    clip_ref,
    norms_ref,
    new_refs,
    moment_refs,
    square_refs,
    average_refs,
    bias_out_refs,
):
    classes, row_inner, row_outer, row_head = sizes
    hidden = sums_ref.shape[1]
    rows = row_inner + row_outer + row_head
    split = (0, row_inner, row_inner + row_outer, rows)
    widths = (hidden, hidden, classes)
    lane = lax.broadcasted_iota(jnp.int32, (1, 128), 1)

    def number(k, start_at):
        found = sums_ref[rows + 8 : rows + 9, start_at : start_at + 128]
        return jnp.sum(jnp.where(lane == k, found, 0.0), axis=1, keepdims=True)

    bias_grad = sums_ref[rows : rows + 3, :]
    bias_square = jnp.sum(jnp.sum(bias_grad * bias_grad, axis=0, keepdims=True), axis=1, keepdims=True)
    clip_norm = jnp.sqrt(number(0, 0) + bias_square)
    factor = jnp.minimum(1.0, CLIP / clip_norm)
    wide = lax.broadcasted_iota(jnp.int32, (8, 128), 1)
    deep = lax.broadcasted_iota(jnp.int32, (8, 128), 0)
    norms = jnp.zeros((8, 128), jnp.float32)
    for k in range(3):
        weight = weight_refs[k][...]
        gradient = sums_ref[split[k] : split[k + 1], 0 : widths[k]] * factor
        first, second, update = moments(weight, gradient, first_refs[k][...], second_refs[k][...])
        weight_norm, update_norm = jnp.sqrt(number(1 + k, 0)), jnp.sqrt(number(k, 128))
        fresh = weight - RATE * (weight_norm / update_norm) * update
        new_refs[k][...] = fresh
        moment_refs[k][...] = first
        square_refs[k][...] = second
        average_refs[k][...] = AVERAGE * smooth_refs[k][...] + (1.0 - AVERAGE) * fresh
        norms = jnp.where(jnp.logical_and(deep == 0, wide == k), weight_norm, norms)
        norms = jnp.where(jnp.logical_and(deep == 1, wide == k), update_norm, norms)
    norms_ref[...] = norms[0:2, 0:3]
    weight, first, second, smooth = (
        jnp.concatenate(bias_rows_of(ref, hidden), axis=0) for ref in bias_refs
    )
    first, second, update = moments(weight, bias_grad * factor, first, second)
    column = lax.broadcasted_iota(jnp.int32, weight.shape, 1)
    row = lax.broadcasted_iota(jnp.int32, weight.shape, 0)
    update = jnp.where(jnp.logical_or(row < 2, column < classes), update, 0.0)
    ratio = jnp.sqrt(jnp.sum(weight * weight, axis=1, keepdims=True)) / jnp.sqrt(
        jnp.sum(update * update, axis=1, keepdims=True)
    )
    fresh = weight - RATE * ratio * update
    average = AVERAGE * smooth + (1.0 - AVERAGE) * fresh
    for ref, value in zip(bias_out_refs, (fresh, first, second, average)):
        ref[pl.ds(0, hidden)] = value[0:1].reshape(hidden)
        ref[pl.ds(hidden, hidden)] = value[1:2].reshape(hidden)
        ref[pl.ds(2 * hidden, classes)] = value[2:3, 0:classes].reshape(classes)
    tail = sums_ref[rows + 3 : rows + 4, 0:128]
    loss_ref[...] = jnp.sum(jnp.where(lane == 0, tail, 0.0), axis=1, keepdims=True)
    count = jnp.sum(jnp.where(lane == 1, tail, 0.0), axis=1, keepdims=True)
    count_ref[...] = count / devices
    clip_ref[...] = clip_norm


def finished(sizes, sums, weights, firsts, seconds, smooths, biases):
    vmem = pl.BlockSpec(memory_space=pltpu.VMEM)
    like = [jax.ShapeDtypeStruct(weight.shape, jnp.float32) for weight in weights]
    scalar = jax.ShapeDtypeStruct((1, 1), jnp.float32)
    return pl.pallas_call(
        functools.partial(final_kernel, sizes, float(lax.axis_size(("section", "dp")))),
        out_shape=(
            scalar,
            scalar,
            scalar,
            jax.ShapeDtypeStruct((2, 3), jnp.float32),
            like,
            like,
            like,
            like,
            [jax.ShapeDtypeStruct(biases[0].shape, jnp.float32)] * 4,
        ),
        in_specs=[vmem] + [(vmem,) * 3] * 4 + [(vmem,) * 4],
        out_specs=(vmem,) * 4 + ([vmem] * 3,) * 4 + ([vmem] * 4,),
    )(sums, weights, firsts, seconds, smooths, biases)


def on_slice_kernels(
    node_table, owner_ids, dest_count, fan_inner, hidden, classes, seed_count, fan_outer, mask_sizes, weight_rows
):
    parts, peers = lax.axis_size("section"), lax.axis_size("dp")
    return (
        parts == 4
        and peers == 8
        and peers * node_table.size * 2 <= VMEM_TABLE_LIMIT
        and node_table.shape[1] == 128
        and node_table.shape[0] % 512 == 0
        and peers * node_table.shape[0] <= 131072
        and owner_ids.shape[0] % 1024 == 0
        and owner_ids.shape[0] <= 32768
        and fan_inner == SLOT - 1
        and dest_count % (BLOCK * GROUP * SETS) == 0
        and dest_count % TILE == 0
        and hidden == 256
        and classes + 2 <= hidden
        and seed_count <= TILE
        and seed_count % 128 == 0
        and dest_count < 16384
        and BLOCK * GROUP * SETS == TILE
        and fan_outer + 2 <= SLOT
        and len(mask_sizes) == 2
        and mask_sizes[0] * mask_sizes[1] <= 65536
        and all(rows % 8 == 0 for rows in weight_rows)
        and sum(weight_rows) % 16 == 0
        and dest_count // TILE > PAUSE
    )


def outer_product(left, right):
    return lax.dot_general(
        left, right, (((0,), (0,)), ((), ())), preferred_element_type=jnp.float32
    )


def against(left, right):
    return lax.dot_general(
        left, right, (((1,), (1,)), ((), ())), preferred_element_type=jnp.float32
    )


def silu_slope(before, grad_out):
    sigmoid = jax.nn.sigmoid(before)
    return (grad_out * sigmoid * (1.0 + before * (1.0 - sigmoid))).astype(jnp.bfloat16)


def moments(weight, gradient, first, second):
    first = BETA_ONE * first + (1.0 - BETA_ONE) * gradient
    second = BETA_TWO * second + (1.0 - BETA_TWO) * gradient * gradient
    update = (
        first / (1.0 - BETA_ONE**STEP) / (jnp.sqrt(second / (1.0 - BETA_TWO**STEP)) + EPSILON)
        + DECAY * weight
    )
    return (first, second, update)


def bias_ratio(weight, update, hidden):
    bounds = ((0, hidden), (hidden, 2 * hidden), (2 * hidden, weight.shape[0]))
    pieces = []
    for start_at, stop_at in bounds:
        weight_norm = jnp.sqrt(jnp.sum(weight[start_at:stop_at] ** 2))
        update_norm = jnp.sqrt(jnp.sum(update[start_at:stop_at] ** 2))
        pieces.append(jnp.zeros((stop_at - start_at,), jnp.float32) + weight_norm / update_norm)
    return jnp.concatenate(pieces)


def gathered_rows(node_table, owner_ids, row_ids):
    peer_count = lax.axis_size("dp")
    parts = lax.axis_size("section")
    table_rows = node_table.shape[0]
    if peer_count * node_table.size * 2 <= WHOLE_TABLE_LIMIT and table_rows % parts == 0:
        part_rows = table_rows // parts
        quarter = lax.dynamic_slice_in_dim(
            node_table, lax.axis_index("section") * part_rows, part_rows, 0
        )
        source = lax.all_gather(quarter, ("section", "dp"), axis=0, tiled=True)
        place = (row_ids // part_rows * peer_count + owner_ids) * part_rows + row_ids % part_rows
        return source, place
    frontier_rows = owner_ids.shape[0]
    slot_count = max(2, 2 * frontier_rows // peer_count)
    owner_hot = (owner_ids[:, None] == jnp.arange(peer_count)[None, :]).astype(jnp.int32)
    ranking = jnp.sum((jnp.cumsum(owner_hot, axis=0) - 1) * owner_hot, axis=1)
    placed = owner_ids * slot_count + ranking
    request = (
        jnp.zeros((peer_count * slot_count,), jnp.int32)
        .at[placed]
        .set(row_ids)
        .reshape(peer_count, slot_count)
    )
    returned = lax.all_to_all(
        node_table[lax.all_to_all(request, "dp", split_axis=0, concat_axis=0, tiled=True)],
        "dp",
        split_axis=0,
        concat_axis=0,
        tiled=True,
    )
    return returned.reshape(peer_count * slot_count, -1), placed


def on_device(
    node_table,
    owners,
    local_rows,
    inner_neighbours,
    inner_counts,
    outer_neighbours,
    outer_counts,
    labels,
    label_mask,
    weight_inner,
    weight_outer,
    weight_head,
    biases,
    first_inner,
    first_outer,
    first_head,
    first_biases,
    second_inner,
    second_outer,
    second_head,
    second_biases,
    smooth_inner,
    smooth_outer,
    smooth_head,
    smooth_biases,
):
    at = lax.axis_index("section")
    every = ("section", "dp")
    hidden = weight_inner.shape[1]
    dest_count, fan_inner = inner_neighbours.shape[1:]
    seed_count, fan_outer = outer_neighbours.shape[1:]
    classes = weight_head.shape[1]
    whole_mask, whole_labels = label_mask, labels
    whole_outer, whole_outer_counts = outer_neighbours, outer_counts
    mask_sizes = label_mask.shape

    def mine(array):
        return lax.dynamic_index_in_dim(array, at, 0, keepdims=False)

    inner_neighbours, inner_counts = mine(inner_neighbours), mine(inner_counts)
    outer_neighbours, outer_counts = mine(outer_neighbours), mine(outer_counts)
    labels, label_mask = mine(labels), mine(label_mask)
    bias_inner = biases[:hidden]
    bias_outer = biases[hidden : 2 * hidden]
    bias_head = biases[2 * hidden :]

    owner_ids, row_ids = owners.reshape(-1), local_rows.reshape(-1)
    weights = (weight_inner, weight_outer, weight_head)
    keep = jnp.arange(fan_inner)[None, :] < inner_counts[:, None]
    if on_slice_kernels(
        node_table,
        owner_ids,
        dest_count,
        fan_inner,
        hidden,
        classes,
        seed_count,
        fan_outer,
        mask_sizes,
        [weight.shape[0] for weight in weights],
    ):
        own = jnp.arange(dest_count, dtype=jnp.int32)[:, None]
        near = jnp.concatenate([jnp.where(keep, inner_neighbours, -1), own], axis=1)
        near = near.reshape(-1, BLOCK * SLOT)
        firsts = (first_inner, first_outer, first_head)
        seconds = (second_inner, second_outer, second_head)
        smooths = (smooth_inner, smooth_outer, smooth_head)
        rows = [weight.shape[0] for weight in weights]
        sums = summed_step(
            node_table,
            weights,
            firsts,
            seconds,
            biases,
            whole_mask,
            owner_ids,
            row_ids,
            near,
            whole_outer,
            whole_outer_counts,
            whole_labels,
        )
        loss, count, clip, norms, news, moment, square, average, bias_outs = finished(
            (classes, *rows),
            sums,
            weights,
            firsts,
            seconds,
            smooths,
            (biases, first_biases, second_biases, smooth_biases),
        )
        return (
            loss.reshape(()),
            count.reshape(()),
            clip.reshape(()),
            norms.T,
            *news,
            bias_outs[0],
            *moment,
            bias_outs[1],
            *square,
            bias_outs[2],
            *average,
            bias_outs[3],
        )

    label_part = jnp.sum(whole_mask.astype(jnp.float32))
    label_count = jnp.maximum(lax.psum(label_part, "dp"), 1.0)
    full_inner, full_outer, full_head = (
        lax.all_gather(weight.astype(jnp.bfloat16), every, axis=0, tiled=True)
        for weight in weights
    )
    source, place = gathered_rows(node_table, owner_ids, row_ids)
    rows = source[place[inner_neighbours]]
    summed = jnp.sum(
        jnp.where(keep[:, :, None], rows, jnp.zeros((), rows.dtype)), axis=1, dtype=jnp.float32
    )
    self_rows = source[place[:dest_count]]
    mean_one = (summed / inner_counts[:, None].astype(jnp.float32)).astype(jnp.bfloat16)
    joined_one = jnp.concatenate([self_rows, mean_one], axis=1)
    pre_one = jnp.dot(joined_one, full_inner, preferred_element_type=jnp.float32) + bias_inner
    hidden_one = jax.nn.silu(pre_one).astype(jnp.bfloat16)

    keep_outer = jnp.arange(fan_outer)[None, :] < outer_counts[:, None]
    pick = jnp.sum(
        (
            jnp.where(keep_outer, outer_neighbours, -1)[:, :, None]
            == jnp.arange(dest_count)[None, None, :]
        ).astype(jnp.float32),
        axis=1,
    ).astype(jnp.bfloat16)
    count_two = outer_counts[:, None].astype(jnp.float32)
    mean_two = (jnp.dot(pick, hidden_one, preferred_element_type=jnp.float32) / count_two).astype(
        jnp.bfloat16
    )
    joined_two = jnp.concatenate([hidden_one[:seed_count], mean_two], axis=1)
    pre_two = jnp.dot(joined_two, full_outer, preferred_element_type=jnp.float32) + bias_outer
    hidden_two = jax.nn.silu(pre_two).astype(jnp.bfloat16)

    logits = jnp.dot(hidden_two, full_head, preferred_element_type=jnp.float32) + bias_head
    shifted = logits - jnp.max(logits, axis=1, keepdims=True)
    log_total = jnp.log(jnp.sum(jnp.exp(shifted), axis=1, keepdims=True))
    chosen = (jnp.arange(classes)[None, :] == labels[:, None]).astype(jnp.float32)
    row_weight = label_mask.astype(jnp.float32)
    loss_part = jnp.sum((log_total[:, 0] - jnp.sum(shifted * chosen, axis=1)) * row_weight)
    grad_logits = (
        (jnp.exp(shifted - log_total) - chosen) * (row_weight / label_count)[:, None]
    ).astype(jnp.bfloat16)
    grad_head = outer_product(hidden_two, grad_logits)
    grad_two = against(grad_logits, full_head).astype(jnp.bfloat16).astype(jnp.float32)
    grad_pre_two = silu_slope(pre_two, grad_two)
    grad_outer = outer_product(joined_two, grad_pre_two)
    grad_joined = against(grad_pre_two, full_outer)
    share = grad_joined[:, hidden:] / count_two
    share_high = share.astype(jnp.bfloat16)
    share_low = (share - share_high.astype(jnp.float32)).astype(jnp.bfloat16)
    grad_one = outer_product(pick, share_high) + outer_product(pick, share_low)
    grad_one = jnp.concatenate(
        [grad_one[:seed_count] + grad_joined[:, :hidden], grad_one[seed_count:]], axis=0
    )
    grad_one = grad_one.astype(jnp.bfloat16).astype(jnp.float32)
    grad_pre_one = silu_slope(pre_one, grad_one)
    grad_inner = outer_product(joined_one, grad_pre_one)
    bias_part = jnp.concatenate(
        [
            jnp.sum(part.astype(jnp.float32), axis=0)
            for part in (grad_pre_one, grad_pre_two, grad_logits)
        ]
    )

    devices = lax.axis_size(every)
    grads = jnp.concatenate(
        [grad.reshape(devices, -1) for grad in (grad_inner, grad_outer, grad_head)], axis=1
    )
    shard = lax.psum_scatter(grads, every, scatter_dimension=0, tiled=True).reshape(-1)
    shards = []
    for weight in weights:
        shards.append(shard[: weight.size].reshape(weight.shape))
        shard = shard[weight.size :]
    packed = lax.psum(jnp.concatenate([bias_part, loss_part[None]]), every)
    bias_grad, loss_sum = packed[:-1], packed[-1]
    grad_partial = sum((jnp.sum(part * part) for part in shards))
    weight_partial = [jnp.sum(weight * weight) for weight in weights]
    squares = lax.psum(jnp.stack([grad_partial] + weight_partial), every)
    clip_norm = jnp.sqrt(squares[0] + jnp.sum(bias_grad * bias_grad))
    factor = jnp.minimum(1.0, CLIP / clip_norm)
    firsts = (first_inner, first_outer, first_head)
    seconds = (second_inner, second_outer, second_head)
    smooths = (smooth_inner, smooth_outer, smooth_head)
    states = [
        moments(weights[slot_at], shards[slot_at] * factor, firsts[slot_at], seconds[slot_at])
        for slot_at in range(3)
    ]
    update_square = lax.psum(jnp.stack([jnp.sum(state[2] * state[2]) for state in states]), every)
    weight_norms = jnp.sqrt(squares[1:])
    update_norms = jnp.sqrt(update_square)
    news = [
        weights[slot_at]
        - RATE * (weight_norms[slot_at] / update_norms[slot_at]) * states[slot_at][2]
        for slot_at in range(3)
    ]
    averages = [
        AVERAGE * smooths[slot_at] + (1.0 - AVERAGE) * news[slot_at] for slot_at in range(3)
    ]
    bias_first, bias_second, bias_update = moments(
        biases, bias_grad * factor, first_biases, second_biases
    )
    bias_new = biases - RATE * bias_ratio(biases, bias_update, hidden) * bias_update
    bias_average = AVERAGE * smooth_biases + (1.0 - AVERAGE) * bias_new
    return (
        loss_sum,
        label_count,
        clip_norm,
        jnp.stack([weight_norms, update_norms], axis=1),
        news[0],
        news[1],
        news[2],
        bias_new,
        states[0][0],
        states[1][0],
        states[2][0],
        bias_first,
        states[0][1],
        states[1][1],
        states[2][1],
        bias_second,
        averages[0],
        averages[1],
        averages[2],
        bias_average,
    )


def solution(mesh):
    in_specs = (
        P("dp", None),
        P("section", "dp", None),
        P("section", "dp"),
        P(None, "dp", None),
        P(None, "dp"),
        P(None, "dp", None),
        P(None, "dp"),
        P(None, "dp"),
        P(None, "dp"),
        P(("section", "dp"), None),
        P(("section", "dp"), None),
        P(("section", "dp"), None),
        P(),
        P(("section", "dp"), None),
        P(("section", "dp"), None),
        P(("section", "dp"), None),
        P(),
        P(("section", "dp"), None),
        P(("section", "dp"), None),
        P(("section", "dp"), None),
        P(),
        P(("section", "dp"), None),
        P(("section", "dp"), None),
        P(("section", "dp"), None),
        P(),
    )
    out_specs = (
        P(),
        P(),
        P(),
        P(),
        P(("section", "dp"), None),
        P(("section", "dp"), None),
        P(("section", "dp"), None),
        P(),
        P(("section", "dp"), None),
        P(("section", "dp"), None),
        P(("section", "dp"), None),
        P(),
        P(("section", "dp"), None),
        P(("section", "dp"), None),
        P(("section", "dp"), None),
        P(),
        P(("section", "dp"), None),
        P(("section", "dp"), None),
        P(("section", "dp"), None),
        P(),
    )
    return jax.shard_map(
        on_device, mesh=mesh, in_specs=in_specs, out_specs=out_specs, check_vma=False
    )
```

```python
import functools

import jax
import jax.numpy as jnp
from jax import lax
from jax.experimental import pallas as pl
from jax.experimental.pallas import tpu as pltpu
from jax.sharding import PartitionSpec as P

STEP = 5


BETA_ONE = 0.9
BETA_TWO = 0.999
EPSILON = 1e-06
DECAY = 0.01
RATE = 0.25
CLIP = 0.05
AVERAGE = 0.9


VMEM_TABLE_LIMIT = 36 * 2**20
WHOLE_TABLE_LIMIT = 64 * 2**20
MESH = pl.DeviceIdType.MESH
SLOT = 16
BLOCK = 16
SHARES = (1, 3, 3, 3, 1)
SPARE_SHARES = (1, 2, 2, 2, 2)
CHUNKS = len(SHARES)
GROUP = 4
SETS = 4
SPARE = 9
SETTLE = 3
AHEAD = 1
AHEAD_ACROSS = 1
LAG = 2
FAR_LAG = 6
SPARE_AFTER = 2
SPARE_LAG = 4
TILE = 256
PAUSE = 6
FORWARD_SLOT = 1
MEAN_SLOT = 3


class Parts:
    def __init__(self, refs, base):
        self.grads, self.half_in, self.half, self.plane_in, self.fourth, self.line_in = refs
        self.base = base


def step_kernel(
    fan_outer,
    table_ref,
    weight_refs,
    first_refs,
    second_refs,
    bias_ref,
    mask_ref,
    owner_ref,
    local_ref,
    near_ref,
    seed_near_ref,
    seed_count_ref,
    label_ref,
    out_ref,
    joined_ref,
    weights_ref,
    hits_ref,
    hits_back_ref,
    full_ref,
    packed,
    parts,
    idx_ref,
    mix_ref,
    wide,
    seed_ref,
    seed_across_ref,
    stages,
    lists,
    full_inner_ref,
    full_outer_ref,
    full_head_ref,
    count_ref,
    first_pre,
    first_hidden,
    mean_ref,
    own_part,
    inner_sum,
    early_refs,
    late_refs,
    extra_ref,
    extra_plane,
    extra_line,
    sums,
    own_sem,
    z_sem,
    spare_sem,
    x_sem,
    y_sem,
    far_sem,
    twin_sem,
    twin_own_sem,
    double_sem,
    send_sem,
    double_send_sem,
    list_sem,
    sum_sem,
    sum_send_sem,
    norm_sem,
    norm_send_sem,
    late_sem,
    late_send_sem,
):
    section, at = lax.axis_index("section"), lax.axis_index("dp")
    z, core = at // 2, at % 2
    flipped = z // 2
    height = z + flipped * (3 - 2 * z)
    pairs = table_ref.shape[0]
    spare = pairs * SPARE // 64
    quarter = (pairs - spare) // 4
    part_sizes = [quarter // sum(SHARES) * share for share in SHARES]
    spare_sizes = [spare // sum(SPARE_SHARES) * share for share in SPARE_SHARES]

    def level(value):
        return value + flipped * (3 - 2 * value)

    twin = (section, z * 2 + 1 - core)
    beside_x = (section + 1 - 2 * (section % 2), at)
    beside_y = (section + 2 - 4 * (section // 2), at)
    inner_z = (section, level(1 - height) * 2 + core)
    across_z = (section, level(2) * 2 + core)
    outer_z = (section, level(0) * 2 + core)
    skip_z = (section, ((z + 2) % 4) * 2 + core)
    sources = [level(1 - height), level(2), level(3)]
    crosses = height == 1
    plane = [((section + k) % 4, at) for k in range(1, 4)]
    beyond = [((section + k) % 4, z * 2 + 1 - core) for k in range(1, 4)]
    line = [(section, ((z + k) % 4) * 2 + core) for k in range(1, 4)]
    neighbours = [twin] + plane + beyond

    barrier = pltpu.get_barrier_semaphore()
    others = [((section + k // 8) % 4, (at + k % 8) % 8) for k in range(1, 32)]
    for partner in others:
        pl.semaphore_signal(barrier, inc=1, device_id=partner, device_id_type=MESH)
    pl.semaphore_wait(barrier, 31)

    sent, now, count = [], [0], [0]

    def region(shard, part, piece):
        start_at = shard * pairs + part * quarter + sum(part_sizes[:piece])
        return full_ref.at[pl.ds(start_at, part_sizes[piece])]

    def spare_region(shard, piece):
        start_at = shard * pairs + 4 * quarter + sum(spare_sizes[:piece])
        return full_ref.at[pl.ds(start_at, spare_sizes[piece])]

    def send(source, target, recv, device, when=None):
        number = count[0]
        count[0] += 1
        copy = pltpu.make_async_remote_copy(
            src_ref=source,
            dst_ref=target,
            send_sem=send_sem.at[number],
            recv_sem=recv,
            device_id=device,
            device_id_type=MESH,
        )
        sent.append((copy, when, now[0]))
        if when is None:
            copy.start()
        else:
            pl.when(when)(copy.start)
        return copy

    def arrived(target, recv):
        pltpu.make_async_copy(target, target, recv).wait()

    def own_piece(piece, device, number, when=None):
        start_at = section * quarter + sum(part_sizes[:piece])
        block = table_ref.at[pl.ds(start_at, part_sizes[piece])]
        send(block, region(at, section, piece), z_sem.at[number], device, when)

    for piece in range(min(AHEAD, CHUNKS)):
        own_piece(piece, inner_z, piece)
    for piece in range(min(AHEAD_ACROSS, CHUNKS)):
        own_piece(piece, across_z, CHUNKS + piece, crosses)
    whole = full_ref.at[pl.ds(at * pairs, pairs)]
    own = pltpu.make_async_copy(table_ref, whole, own_sem)
    own.start()
    send(table_ref, whole, twin_own_sem, twin)

    inner_ref, outer_ref, head_ref = weight_refs
    row_inner, row_outer, row_head = (ref.shape[0] for ref in weight_refs)
    hidden, classes = inner_ref.shape[1], head_ref.shape[1]
    head_at = row_inner + row_outer
    packed[0:row_inner, :] = inner_ref[...]
    packed[row_inner:head_at, :] = outer_ref[...]
    packed[head_at:, :] = jnp.zeros((row_head, hidden), jnp.float32)
    packed[head_at:, 0:classes] = head_ref[...]
    labelled = jnp.sum(mask_ref[...].astype(jnp.float32)).astype(jnp.int32)
    lane = lax.broadcasted_iota(jnp.int32, (1, hidden), 1)
    high_part = (labelled // 256).astype(jnp.float32)
    low_part = (labelled % 256).astype(jnp.float32)
    tail = jnp.where(lane == classes, high_part, jnp.where(lane == classes + 1, low_part, 0.0))
    packed[head_at : head_at + 1, :] += tail
    mine = (core * 4 + section) * 4 + z
    weights_ref[mine] = packed[...].astype(jnp.bfloat16)
    doubling = [(inner_z, 1), (skip_z, 2), (beside_x, 4), (beside_y, 8), (twin, 16)]
    doubled = []

    def double_start(number):
        device, size = doubling[number]
        block = weights_ref.at[pl.ds((mine // size) * size, size)]
        copy = pltpu.make_async_remote_copy(
            src_ref=block,
            dst_ref=block,
            send_sem=double_send_sem.at[number],
            recv_sem=double_sem.at[number],
            device_id=device,
            device_id_type=MESH,
        )
        copy.start()
        doubled.append(copy)

    double_start(0)

    def eye(size):
        same_place = lax.broadcasted_iota(jnp.int32, (size, size), 0) == lax.broadcasted_iota(
            jnp.int32, (size, size), 1
        )
        return same_place.astype(jnp.float32).astype(jnp.bfloat16)

    def as_low(values):
        return values.astype(jnp.float32).astype(jnp.bfloat16)

    placed = owner_ref[...] * (2 * pairs) + local_ref[...]
    pair_at = placed // 2
    high = owner_ref.shape[0]
    for k, values in enumerate((pair_at % 256, pair_at // 256, placed % 2)):
        parts[128 * k : 128 * (k + 1), :] = against(eye(128), as_low(values)).astype(jnp.bfloat16)
    looked_rows = near_ref.shape[0]
    seeds = seed_ref.shape[0]
    tiles = hits_ref.shape[1] // TILE
    seed_row = pl.ds(section, 1)
    live_seeds = seed_count_ref[seed_row, :]
    for j in range(fan_outer):
        near_seeds = seed_near_ref[j, seed_row, :]
        seed_across_ref[j : j + 1, :] = jnp.where(live_seeds > j, near_seeds, -1)
    seed_across_ref[fan_outer : fan_outer + 1, :] = label_ref[seed_row, :]
    seed_across_ref[fan_outer + 1 : fan_outer + 2, :] = mask_ref[seed_row, :]
    seed_across_ref[fan_outer + 2 :, :] = jnp.zeros((SLOT - fan_outer - 2, seeds), jnp.int32)
    shifted_up = seed_across_ref[...] + 1
    seed_ref[...] = (
        64.0 * against(eye(seeds), as_low(shifted_up // 64))
        + against(eye(seeds), as_low(shifted_up % 64))
    ).astype(jnp.int32) - 1
    total = 3 * CHUNKS
    steps = total + max(FAR_LAG, SPARE_LAG)
    per_step = -(-looked_rows // (8 * steps)) * 8
    for j in range(fan_outer):
        wide[j] = jnp.broadcast_to(seed_ref[:, j : j + 1], (seeds, TILE))

    def look_up(first, last):
        def rows_of(block, carry):
            start_at = pl.multiple_of(block * 8, 8)
            sub = lax.broadcasted_iota(jnp.int32, (high, 256), 0)
            low_at = lax.broadcasted_iota(jnp.int32, (128, 256), 0)
            row = lax.broadcasted_iota(jnp.int32, (256, 512), 0)
            column = lax.broadcasted_iota(jnp.int32, (256, 512), 1)
            for k in range(8):
                node = near_ref[pl.ds(start_at + k, 1), :]
                hot = (sub == node // 128).astype(jnp.float32).astype(jnp.bfloat16)
                got = jnp.dot(parts[...], hot, preferred_element_type=jnp.float32)
                chosen = low_at == node % 128
                found = jnp.where(chosen, got[0:128] + 256.0 * got[128:256], 0.0)
                odd = jnp.where(chosen, got[256:384], 0.0)
                entry_at = jnp.sum(found, axis=0, keepdims=True).astype(jnp.int32)
                idx_ref[block * 2 + k // 4, k % 4 : k % 4 + 1, :] = jnp.clip(
                    entry_at, 0, full_ref.shape[0] - 1
                )
                mix_ref[pl.ds(start_at + k, 1), 0:256] = jnp.sum(odd, axis=0, keepdims=True)
            odd = mix_ref[pl.ds(start_at, 8), 0:256]
            live = (near_ref[pl.ds(start_at, 8), :] >= 0).astype(jnp.float32)
            mix_ref[pl.ds(start_at, 8), :] = jnp.dot(
                (live * (1.0 - odd)).astype(jnp.bfloat16),
                (column == 2 * row).astype(jnp.float32).astype(jnp.bfloat16),
                preferred_element_type=jnp.float32,
            ) + jnp.dot(
                (live * odd).astype(jnp.bfloat16),
                (column == 2 * row + 1).astype(jnp.float32).astype(jnp.bfloat16),
                preferred_element_type=jnp.float32,
            )
            return carry

        lax.fori_loop(first // 8, last // 8, rows_of, 0)

    def mark(tile):
        start_at = tile * TILE
        dest = lax.broadcasted_iota(jnp.int32, (seeds, TILE), 1) + start_at
        hits = jnp.zeros((seeds, TILE), jnp.float32)
        for j in range(fan_outer):
            hits = hits + (wide[j] == dest).astype(jnp.float32)
        hits_ref[:, start_at : start_at + TILE] = hits.astype(jnp.bfloat16)
        dest = lax.broadcasted_iota(jnp.int32, (TILE, seeds), 0) + start_at
        hits = jnp.zeros((TILE, seeds), jnp.float32)
        for j in range(fan_outer):
            hits = hits + (seed_across_ref[j : j + 1, :] == dest).astype(jnp.float32)
        hits_back_ref[start_at : start_at + TILE, :] = hits.astype(jnp.bfloat16)

    def sort_weights():
        everyone = weights_ref[...].astype(jnp.float32)
        order = block_order()
        inner, outer, head = (
            jnp.concatenate([everyone[spot, lower:upper] for spot in order], axis=0)
            for lower, upper in ((0, row_inner), (row_inner, head_at), (head_at, head_at + row_head))
        )
        full_inner_ref[...] = inner.astype(jnp.bfloat16)
        full_outer_ref[...] = outer.astype(jnp.bfloat16)
        full_head_ref[...] = jnp.where(lane < classes, head, 0.0).astype(jnp.bfloat16)
        tails = everyone[0:4, head_at : head_at + 1] + everyone[16:20, head_at : head_at + 1]
        tails = jnp.sum(tails.reshape(4, hidden), axis=0, keepdims=True)
        scale = jnp.where(lane == classes, 256.0, jnp.where(lane == classes + 1, 1.0, 0.0))
        labels_in_all = jnp.sum(tails * scale, axis=1, keepdims=True)
        count_ref[...] = jnp.broadcast_to(jnp.maximum(labels_in_all, 1.0), count_ref.shape)

    twins = []

    def to_twin(block, number):
        send(block, block, twin_sem.at[number], twin)
        twins.append((number, now[0]))

    def from_twin(number):
        kind, step = divmod(number, total)
        turn, piece = divmod(step, CHUNKS)
        shard = sources[turn] * 2 + 1 - core
        if kind == 4:
            block = spare_region(shard, piece)
        else:
            block = region(shard, (section, beside_x[0], beside_y[0], 3 - section)[kind], piece)
        arrived(block, twin_sem.at[number])

    def settle(until):
        while twins and twins[0][1] <= until:
            from_twin(twins.pop(0)[0])
        while sent and sent[0][2] <= until - SETTLE:
            copy, when, _ = sent.pop(0)
            if when is None:
                copy.wait_send()
            else:
                pl.when(when)(copy.wait_send)

    for step in range(steps):
        now[0] = step
        if step < total:
            turn, piece = divmod(step, CHUNKS)
            shard = sources[turn] * 2 + core
            goes, number = (across_z, 2 * CHUNKS + piece) if turn == 0 else (outer_z, step)
            block = region(shard, section, piece)
            arrived(block, z_sem.at[step])
            send(block, block, z_sem.at[number], goes, crosses)
            send(block, block, x_sem.at[step], beside_x)
            send(block, block, y_sem.at[step], beside_y)
            to_twin(block, step)
            if step + AHEAD < CHUNKS:
                own_piece(step + AHEAD, inner_z, step + AHEAD)
            if step + AHEAD_ACROSS < CHUNKS:
                piece = step + AHEAD_ACROSS
                own_piece(piece, across_z, CHUNKS + piece, crosses)
            piece = step - SPARE_AFTER
            if 0 <= piece < CHUNKS:
                start_at = 4 * quarter + sum(spare_sizes[:piece])
                block = table_ref.at[pl.ds(start_at, spare_sizes[piece])]
                goal = spare_region(at, piece)
                send(block, goal, spare_sem.at[piece], inner_z)
                send(block, goal, spare_sem.at[CHUNKS + piece], across_z, crosses)
        late = step - SPARE_LAG
        if 0 <= late < total:
            turn, piece = divmod(late, CHUNKS)
            shard = sources[turn] * 2 + core
            goes, number = (across_z, 2 * CHUNKS + piece) if turn == 0 else (outer_z, late)
            block = spare_region(shard, piece)
            arrived(block, spare_sem.at[late])
            send(block, block, spare_sem.at[number], goes, crosses)
            to_twin(block, 4 * total + late)
        late = step - LAG
        if 0 <= late < total:
            turn, piece = divmod(late, CHUNKS)
            shard = sources[turn] * 2 + core
            block = region(shard, beside_x[0], piece)
            arrived(block, x_sem.at[late])
            send(block, block, far_sem.at[late], beside_y, core == piece % 2)
            to_twin(block, total + late)
            block = region(shard, beside_y[0], piece)
            arrived(block, y_sem.at[late])
            send(block, block, far_sem.at[late], beside_x, core != piece % 2)
            to_twin(block, 2 * total + late)
        later = step - FAR_LAG
        if 0 <= later < total:
            turn, piece = divmod(later, CHUNKS)
            shard = sources[turn] * 2 + core
            block = region(shard, 3 - section, piece)
            arrived(block, far_sem.at[later])
            to_twin(block, 3 * total + later)
        if step % 2 == 0 and step // 2 < len(doubling):
            doubled[step // 2].wait()
            if step // 2 + 1 < len(doubling):
                double_start(step // 2 + 1)
        first = min(step * per_step, looked_rows)
        last = min(first + per_step, looked_rows)
        if last > first:
            look_up(first, last)
        for tile in range(step * tiles // steps, (step + 1) * tiles // steps):
            mark(tile)
        settle(step - 3)

    sort_weights()
    settle(steps)
    arrived(full_ref.at[pl.ds((z * 2 + 1 - core) * pairs, pairs)], twin_own_sem)
    own.wait()

    blocks = looked_rows
    unit_at = lax.broadcasted_iota(jnp.int32, (BLOCK, 2 * BLOCK * SLOT), 1)
    same = unit_at // (2 * SLOT) == lax.broadcasted_iota(jnp.int32, unit_at.shape, 0)
    near_part = jnp.logical_and(same, unit_at % (2 * SLOT) < 2 * SLOT - 2).astype(jnp.float32)
    self_part = jnp.logical_and(same, unit_at % (2 * SLOT) >= 2 * SLOT - 2).astype(jnp.float32)
    turns = blocks // GROUP

    def fetch(turn, slot):
        return pltpu.make_async_copy(
            idx_ref.at[jnp.minimum(turn, turns - 1)], lists[slot], list_sem.at[slot]
        )

    def pick(member, slot, stage):
        def unit(number, carry):
            entry = full_ref[lists[slot][member, number]]
            stage[pl.ds(2 * number, 2), :] = entry.astype(jnp.float32)
            return carry

        lax.fori_loop(0, BLOCK * SLOT, unit, 0, unroll=BLOCK * SLOT)

    def reduce(block, stage):
        mix = mix_ref[pl.ds(block, 1), :]
        near = mix * near_part
        left = jnp.concatenate([near, mix * self_part], axis=0).astype(jnp.bfloat16)
        out = jnp.dot(left, stage[...].astype(jnp.bfloat16), preferred_element_type=jnp.float32)
        count = jnp.maximum(jnp.sum(near, axis=1, keepdims=True), 1.0)
        both = jnp.concatenate([out[BLOCK:], out[:BLOCK] / count], axis=1)
        start_at = pl.multiple_of(block * BLOCK, BLOCK)
        joined_ref[pl.ds(start_at, BLOCK), :] = both.astype(jnp.bfloat16)

    bias_inner, bias_outer, bias_head = bias_rows_of(bias_ref, hidden)

    def forward(tile):
        tile_rows = pl.ds(pl.multiple_of(tile * TILE, TILE), TILE)
        before = (
            jnp.dot(
                joined_ref[tile_rows, :], full_inner_ref[...], preferred_element_type=jnp.float32
            )
            + bias_inner
        )
        first_pre[tile_rows, :] = before
        first_hidden[tile_rows, :] = (before * lax.logistic(before)).astype(jnp.bfloat16)

    def add_mean(tile, carried):
        tile_rows = pl.ds(pl.multiple_of(tile * TILE, TILE), TILE)
        found = jnp.dot(
            hits_ref[:, tile_rows], first_hidden[tile_rows, :], preferred_element_type=jnp.float32
        )
        mean_ref[...] = mean_ref[...] * carried + found

    near_stages, far_stages = stages
    mean_ref[...] = jnp.zeros(mean_ref.shape, jnp.float32)
    joined_ref[0:TILE, :] = jnp.zeros((TILE, joined_ref.shape[1]), jnp.bfloat16)
    for slot in range(SETS):
        fetch(slot, slot).start()
    for member in range(GROUP):
        far_stages[member][...] = jnp.zeros(far_stages[member].shape, jnp.float32)

    def round_of(number, carry):
        for slot in range(SETS):
            turn = number * SETS + slot
            fetch(turn, slot).wait()
            for member in range(GROUP):
                pick(member, slot, stages[slot % 2][member])
                reduce(
                    jnp.maximum((turn - 1) * GROUP + member, 0), stages[1 - slot % 2][member]
                )
            if slot == FORWARD_SLOT:
                forward(jnp.maximum(number - 1, 0))
            if slot == MEAN_SLOT:
                add_mean(jnp.maximum(number - 1, 0), (number > 1).astype(jnp.float32))
            fetch(turn + SETS, slot).start()
        return carry

    lax.fori_loop(0, blocks // (GROUP * SETS), round_of, 0)
    for slot in range(SETS):
        fetch(0, slot).wait()
    for member in range(GROUP):
        reduce(blocks - GROUP + member, stages[(SETS - 1) % 2][member])
    forward(tiles - 1)
    add_mean(tiles - 1, 1.0)
    summing = []

    def pass_on(source, target, number, device):
        copy = pltpu.make_async_remote_copy(
            src_ref=source,
            dst_ref=target,
            send_sem=sum_send_sem.at[len(summing)],
            recv_sem=sum_sem.at[number],
            device_id=device,
            device_id_type=MESH,
        )
        summing.append(copy)
        copy.start()

    def passed(target, number):
        arrived(target, sum_sem.at[number])

    def to_other_core(part):
        pass_on(part.grads.at[pl.ds((1 - core) * 16, 16)], part.half_in, part.base, twin)

    def to_plane(part):
        passed(part.half_in, part.base)
        part.half[...] = part.grads[pl.ds(core * 16, 16)] + part.half_in[...]
        for partner in plane:
            block = part.half.at[pl.ds(partner[0] * 4, 4)]
            pass_on(block, part.plane_in.at[section], part.base + 1 + section, partner)
        part.plane_in[section] = part.half[pl.ds(section * 4, 4)]

    def to_line(part):
        for k in range(1, 4):
            other = (section + k) % 4
            passed(part.plane_in.at[other], part.base + 1 + other)
        part.fourth[...] = (part.plane_in[0] + part.plane_in[1]) + (
            part.plane_in[2] + part.plane_in[3]
        )
        for k, partner in enumerate(line):
            block = part.fourth.at[pl.ds((z + k + 1) % 4, 1)]
            pass_on(block, part.line_in.at[pl.ds(z, 1)], part.base + 5 + z, partner)
        part.line_in[z] = part.fourth[z]

    def whole_sum(part):
        for k in range(1, 4):
            other = (z + k) % 4
            passed(part.line_in.at[pl.ds(other, 1)], part.base + 5 + other)
        return (part.line_in[0] + part.line_in[1]) + (part.line_in[2] + part.line_in[3])

    def share(value, slots, base, me, partners):
        slots[me] = value
        for partner in partners:
            pass_on(slots.at[me], slots.at[me], base + me, partner)

    def collect(slots, base, me):
        count = slots.shape[0]
        for k in range(1, count):
            other = (me + k) % count
            passed(slots.at[other], base + other)
        values = [slots[k] for k in range(count)]
        while len(values) > 1:
            values = [values[k] + values[k + 1] for k in range(0, len(values), 2)]
        return values[0]

    early = Parts(early_refs, 0)
    late_grads, late_half_in, late_half, late_in = late_refs
    order = block_order()
    full_outer, full_head = full_outer_ref[...], full_head_ref[...]
    label_count = count_ref[:, 0:1]
    kept = seed_ref[:, 0:fan_outer]
    count_two = jnp.sum((kept >= 0).astype(jnp.float32), axis=1, keepdims=True)
    mean_two = (mean_ref[...] / count_two).astype(jnp.bfloat16)
    joined_two = jnp.concatenate([first_hidden[0:seeds, :], mean_two], axis=1)
    pre_two = jnp.dot(joined_two, full_outer, preferred_element_type=jnp.float32) + bias_outer
    gate_two = lax.logistic(pre_two)
    hidden_two = (pre_two * gate_two).astype(jnp.bfloat16)
    logits = jnp.dot(hidden_two, full_head, preferred_element_type=jnp.float32) + bias_head
    inside = lane < classes
    highest = jnp.max(jnp.where(inside, logits, -jnp.inf), axis=1, keepdims=True)
    shifted = jnp.where(inside, logits - highest, 0.0)
    total_exp = jnp.sum(jnp.where(inside, jnp.exp(shifted), 0.0), axis=1, keepdims=True)
    log_total = jnp.log(total_exp)
    chosen = (lane == seed_ref[:, fan_outer : fan_outer + 1]).astype(jnp.float32)
    row_weight = seed_ref[:, fan_outer + 1 : fan_outer + 2].astype(jnp.float32)
    loss = jnp.sum((log_total - jnp.sum(shifted * chosen, axis=1, keepdims=True)) * row_weight)
    grad_logits = (jnp.exp(shifted - log_total) - chosen) * (row_weight / label_count)
    grad_logits = jnp.where(inside, grad_logits, 0.0).astype(jnp.bfloat16)
    grad_head = outer_product(hidden_two, grad_logits)
    grad_two = against(grad_logits, full_head).astype(jnp.bfloat16).astype(jnp.float32)
    grad_pre_two = (grad_two * gate_two * (1.0 + pre_two * (1.0 - gate_two))).astype(jnp.bfloat16)
    grad_outer = outer_product(joined_two, grad_pre_two)
    for number, spot in enumerate(order):
        early.grads[spot, 0:row_outer, :] = grad_outer[
            number * row_outer : (number + 1) * row_outer
        ]
        early.grads[spot, row_outer : row_outer + row_head, :] = grad_head[
            number * row_head : (number + 1) * row_head
        ]
    to_other_core(early)
    extra_ref[1:2, :] = jnp.sum(grad_pre_two.astype(jnp.float32), axis=0, keepdims=True)
    extra_ref[2:3, :] = jnp.sum(grad_logits.astype(jnp.float32), axis=0, keepdims=True)
    extra_ref[3:4, :] = jnp.where(lane == 0, loss, jnp.where(lane == 1, label_count, 0.0))
    extra_ref[4:8, :] = jnp.zeros((4, hidden), jnp.float32)
    grad_joined = against(grad_pre_two, full_outer)
    share_part = grad_joined[:, hidden:] / count_two
    share_high = share_part.astype(jnp.bfloat16)
    share_low = (share_part - share_high.astype(jnp.float32)).astype(jnp.bfloat16)
    inner_sum[...] = jnp.zeros(inner_sum.shape, jnp.float32)
    share_both = jnp.concatenate([share_high, share_low], axis=0)
    own_part[...] = jnp.zeros(own_part.shape, jnp.float32)
    own_part[0:seeds, :] = grad_joined[:, 0:hidden]

    def backward(tile, bias_sum, own=None):
        tile_rows = pl.ds(pl.multiple_of(jnp.int32(tile) * TILE, TILE), TILE)
        hits = hits_back_ref[tile_rows, :]
        both_hits = jnp.concatenate([hits, hits], axis=1)
        grad_one = jnp.dot(both_hits, share_both, preferred_element_type=jnp.float32)
        if own is not None:
            grad_one = grad_one + own
        grad_one = grad_one.astype(jnp.bfloat16).astype(jnp.float32)
        before = first_pre[tile_rows, :]
        gate = lax.logistic(before)
        grad_pre = (grad_one * gate * (1.0 + before * (1.0 - gate))).astype(jnp.bfloat16)
        inner_sum[...] += outer_product(joined_ref[tile_rows, :], grad_pre)
        return bias_sum + jnp.sum(grad_pre.astype(jnp.float32), axis=0, keepdims=True)

    bias_sum = backward(0, jnp.zeros((1, hidden), jnp.float32), own_part[...])
    bias_sum = lax.fori_loop(1, PAUSE, backward, bias_sum, unroll=PAUSE - 1)
    to_plane(early)
    bias_sum = lax.fori_loop(PAUSE, tiles, backward, bias_sum, unroll=tiles - PAUSE)
    extra_ref[0:1, :] = bias_sum
    grad_inner = inner_sum[...]
    for number, spot in enumerate(order):
        late_grads[spot] = grad_inner[number * row_inner : (number + 1) * row_inner]
    pass_on(late_grads.at[pl.ds((1 - core) * 16, 16)], late_half_in, 9, twin)
    share(extra_ref[...], extra_plane, 18, section * 2 + core, neighbours)
    passed(late_half_in, 9)
    late_half[...] = late_grads[pl.ds(core * 16, 16)] + late_half_in[...]
    same_core = [((section + k // 4) % 4, (z + k % 4) % 4) for k in range(1, 16)]
    my_place = section * 4 + z
    for to_section, to_z in same_core:
        pltpu.make_async_remote_copy(
            src_ref=late_half.at[to_section * 4 + to_z],
            dst_ref=late_in.at[my_place],
            send_sem=late_send_sem,
            recv_sem=late_sem,
            device_id=(to_section, to_z * 2 + core),
            device_id_type=MESH,
        ).start()
    late_in[my_place] = late_half[my_place]
    to_line(early)
    share(collect(extra_plane, 18, section * 2 + core), extra_line, 26, z, line)

    short_lane = lax.broadcasted_iota(jnp.int32, (1, 128), 1)
    my_number = section * 8 + at

    def square_sum(value):
        return jnp.sum(jnp.sum(value * value, axis=0, keepdims=True), axis=1, keepdims=True)

    def everywhere(values, number):
        found = jnp.zeros((1, 128), jnp.float32)
        for k, value in enumerate(values):
            found = jnp.where(short_lane == k, value, found)
        sums[number, my_number] = found
        mine_there = sums.at[number, my_number]
        for partner in others:
            pltpu.make_async_remote_copy(
                src_ref=mine_there,
                dst_ref=mine_there,
                send_sem=norm_send_sem.at[number],
                recv_sem=norm_sem.at[number],
                device_id=partner,
                device_id_type=MESH,
            ).start()
        if number == 1:
            for copy in summing:
                copy.wait_send()
        all_others = sums.at[number, pl.ds(0, 31)]
        arrived(all_others, norm_sem.at[number])
        return jnp.sum(sums[number], axis=0)

    held = [ref[...] for ref in weight_refs]
    weight_squares = [square_sum(weight) for weight in held]
    rest = whole_sum(early)
    rest_square = square_sum(rest)
    extra = collect(extra_line, 26, z)
    bias_square = square_sum(extra[0:3])
    settle(steps + SETTLE)
    arrived(late_in.at[pl.ds(0, 15)], late_sem)
    shard = jnp.sum(late_in[...], axis=0)
    pieces = [shard, rest[0:row_outer], rest[row_outer:, 0:classes]]
    values = everywhere([square_sum(shard) + rest_square] + weight_squares, 0)
    grad_square = jnp.sum(jnp.where(short_lane == 0, values, 0.0), axis=1, keepdims=True)
    clip_norm = jnp.sqrt(grad_square + bias_square)
    factor = jnp.minimum(1.0, CLIP / clip_norm)
    update_squares = []
    for k in range(3):
        update = moments(held[k], pieces[k] * factor, first_refs[k][...], second_refs[k][...])[2]
        update_squares.append(square_sum(update))
    updates = everywhere(update_squares, 1)
    rows = row_inner + row_outer + row_head
    out_ref[0:row_inner, :] = shard
    out_ref[row_inner:rows, :] = rest
    out_ref[rows : rows + 8, :] = extra
    out_ref[rows + 8 : rows + 9, 0:128] = values
    out_ref[rows + 8 : rows + 9, 128:256] = updates
    out_ref[rows + 9 :, :] = jnp.zeros((7, hidden), jnp.float32)
    for number in range(2):
        arrived(sums.at[number, pl.ds(0, 31)], norm_send_sem.at[number])
    arrived(late_in.at[pl.ds(0, 15)], late_send_sem)


def block_order():
    return [(e % 2) * 16 + (e // 8) * 4 + (e % 8) // 2 for e in range(32)]


def bias_rows_of(ref, hidden):
    width = ref.shape[0] - 2 * hidden
    last = ref[pl.ds(2 * hidden, width)].reshape(1, width)
    return (
        ref[pl.ds(0, hidden)].reshape(1, hidden),
        ref[pl.ds(hidden, hidden)].reshape(1, hidden),
        jnp.concatenate([last, jnp.zeros((1, hidden - width), jnp.float32)], axis=1),
    )


def summed_step(
    node_table,
    weights,
    firsts,
    seconds,
    biases,
    label_mask,
    owner_ids,
    row_ids,
    near,
    outer_neighbours,
    outer_counts,
    labels,
):
    devices = lax.axis_size(("section", "dp"))
    table_rows, width = node_table.shape
    frontier_high = owner_ids.size // 128
    fan_outer = outer_neighbours.shape[2]
    looked = near.shape[0]
    dest_count = looked * BLOCK
    seeds = outer_neighbours.shape[1]
    hidden = weights[0].shape[1]
    row_inner = weights[0].shape[0]
    rows = sum(weight.shape[0] for weight in weights)
    total = 3 * CHUNKS
    sends = 4 * CHUNKS + 1 + 3 * total + total + 2 * total + 5 * total
    vmem = pl.BlockSpec(memory_space=pltpu.VMEM)
    stage = (pltpu.VMEM((2 * BLOCK * SLOT, width), jnp.float32),) * GROUP

    def on_the_way(depth):
        return (
            pltpu.VMEM((devices, depth, hidden), jnp.float32),
            pltpu.VMEM((16, depth, hidden), jnp.float32),
            pltpu.VMEM((16, depth, hidden), jnp.float32),
            pltpu.VMEM((4, 4, depth, hidden), jnp.float32),
            pltpu.VMEM((4, depth, hidden), jnp.float32),
            pltpu.VMEM((4, depth, hidden), jnp.float32),
        )

    return pl.pallas_call(
        functools.partial(step_kernel, fan_outer),
        out_shape=jax.ShapeDtypeStruct((rows + 16, hidden), jnp.float32),
        in_specs=[pl.BlockSpec(memory_space=pl.ANY)] + [(vmem,) * 3] * 3 + [vmem] * 8,
        out_specs=vmem,
        scratch_shapes=[
            pltpu.VMEM((dest_count, 2 * width), jnp.bfloat16),
            pltpu.VMEM((devices, rows, hidden), jnp.bfloat16),
            pltpu.VMEM((seeds, dest_count), jnp.bfloat16),
            pltpu.VMEM((dest_count, seeds), jnp.bfloat16),
            pltpu.VMEM((lax.axis_size("dp") * table_rows // 2, 2, width), jnp.bfloat16),
            pltpu.VMEM((rows, hidden), jnp.float32),
            pltpu.VMEM((384, frontier_high), jnp.bfloat16),
            pltpu.VMEM((looked // GROUP, GROUP, 256), jnp.int32),
            pltpu.VMEM((looked, 512), jnp.float32),
            pltpu.VMEM((fan_outer, seeds, TILE), jnp.int32),
            pltpu.VMEM((seeds, SLOT), jnp.int32),
            pltpu.VMEM((SLOT, seeds), jnp.int32),
            (stage, stage),
            (pltpu.SMEM((GROUP, BLOCK * SLOT), jnp.int32),) * SETS,
            pltpu.VMEM((hidden, hidden), jnp.bfloat16),
            pltpu.VMEM((2 * hidden, hidden), jnp.bfloat16),
            pltpu.VMEM((hidden, hidden), jnp.bfloat16),
            pltpu.VMEM((1, hidden), jnp.float32),
            pltpu.VMEM((dest_count, hidden), jnp.float32),
            pltpu.VMEM((dest_count, hidden), jnp.bfloat16),
            pltpu.VMEM((seeds, hidden), jnp.float32),
            pltpu.VMEM((TILE, hidden), jnp.float32),
            pltpu.VMEM((hidden, hidden), jnp.float32),
            on_the_way(rows - row_inner),
            (
                pltpu.VMEM((devices, row_inner, hidden), jnp.float32),
                pltpu.VMEM((16, row_inner, hidden), jnp.float32),
                pltpu.VMEM((16, row_inner, hidden), jnp.float32),
                pltpu.VMEM((16, row_inner, hidden), jnp.float32),
            ),
            pltpu.VMEM((8, hidden), jnp.float32),
            pltpu.VMEM((8, 8, hidden), jnp.float32),
            pltpu.VMEM((4, 8, hidden), jnp.float32),
            pltpu.VMEM((2, devices, 1, 128), jnp.float32),
            pltpu.SemaphoreType.DMA(()),
            pltpu.SemaphoreType.DMA((total,)),
            pltpu.SemaphoreType.DMA((total,)),
            pltpu.SemaphoreType.DMA((total,)),
            pltpu.SemaphoreType.DMA((total,)),
            pltpu.SemaphoreType.DMA((total,)),
            pltpu.SemaphoreType.DMA((5 * total,)),
            pltpu.SemaphoreType.DMA(()),
            pltpu.SemaphoreType.DMA((5,)),
            pltpu.SemaphoreType.DMA((sends,)),
            pltpu.SemaphoreType.DMA((5,)),
            pltpu.SemaphoreType.DMA((SETS,)),
            pltpu.SemaphoreType.DMA((30,)),
            pltpu.SemaphoreType.DMA((24,)),
            pltpu.SemaphoreType.DMA((2,)),
            pltpu.SemaphoreType.DMA((2,)),
            pltpu.SemaphoreType.DMA(()),
            pltpu.SemaphoreType.DMA(()),
        ],
        compiler_params=pltpu.CompilerParams(
            collective_id=0, has_side_effects=True, vmem_limit_bytes=56 * 2**20
        ),
    )(
        pltpu.with_memory_space_constraint(
            node_table.reshape(table_rows // 2, 2, width), pltpu.HBM
        ),
        weights,
        firsts,
        seconds,
        biases,
        label_mask,
        owner_ids.reshape(-1, 128),
        row_ids.reshape(-1, 128),
        near,
        outer_neighbours.transpose(2, 0, 1),
        outer_counts,
        labels,
    )


def final_kernel(
    sizes,
    devices,
    sums_ref,
    weight_refs,
    first_refs,
    second_refs,
    smooth_refs,
    bias_refs,
    loss_ref,
    count_ref,
    clip_ref,
    norms_ref,
    new_refs,
    moment_refs,
    square_refs,
    average_refs,
    bias_out_refs,
):
    classes, row_inner, row_outer, row_head = sizes
    hidden = sums_ref.shape[1]
    rows = row_inner + row_outer + row_head
    split = (0, row_inner, row_inner + row_outer, rows)
    widths = (hidden, hidden, classes)
    lane = lax.broadcasted_iota(jnp.int32, (1, 128), 1)

    def number(k, start_at):
        found = sums_ref[rows + 8 : rows + 9, start_at : start_at + 128]
        return jnp.sum(jnp.where(lane == k, found, 0.0), axis=1, keepdims=True)

    bias_grad = sums_ref[rows : rows + 3, :]
    bias_square = jnp.sum(jnp.sum(bias_grad * bias_grad, axis=0, keepdims=True), axis=1, keepdims=True)
    clip_norm = jnp.sqrt(number(0, 0) + bias_square)
    factor = jnp.minimum(1.0, CLIP / clip_norm)
    wide = lax.broadcasted_iota(jnp.int32, (8, 128), 1)
    deep = lax.broadcasted_iota(jnp.int32, (8, 128), 0)
    norms = jnp.zeros((8, 128), jnp.float32)
    for k in range(3):
        weight = weight_refs[k][...]
        gradient = sums_ref[split[k] : split[k + 1], 0 : widths[k]] * factor
        first, second, update = moments(weight, gradient, first_refs[k][...], second_refs[k][...])
        weight_norm, update_norm = jnp.sqrt(number(1 + k, 0)), jnp.sqrt(number(k, 128))
        fresh = weight - RATE * (weight_norm / update_norm) * update
        new_refs[k][...] = fresh
        moment_refs[k][...] = first
        square_refs[k][...] = second
        average_refs[k][...] = AVERAGE * smooth_refs[k][...] + (1.0 - AVERAGE) * fresh
        norms = jnp.where(jnp.logical_and(deep == 0, wide == k), weight_norm, norms)
        norms = jnp.where(jnp.logical_and(deep == 1, wide == k), update_norm, norms)
    norms_ref[...] = norms[0:2, 0:3]
    weight, first, second, smooth = (
        jnp.concatenate(bias_rows_of(ref, hidden), axis=0) for ref in bias_refs
    )
    first, second, update = moments(weight, bias_grad * factor, first, second)
    column = lax.broadcasted_iota(jnp.int32, weight.shape, 1)
    row = lax.broadcasted_iota(jnp.int32, weight.shape, 0)
    update = jnp.where(jnp.logical_or(row < 2, column < classes), update, 0.0)
    ratio = jnp.sqrt(jnp.sum(weight * weight, axis=1, keepdims=True)) / jnp.sqrt(
        jnp.sum(update * update, axis=1, keepdims=True)
    )
    fresh = weight - RATE * ratio * update
    average = AVERAGE * smooth + (1.0 - AVERAGE) * fresh
    for ref, value in zip(bias_out_refs, (fresh, first, second, average)):
        ref[pl.ds(0, hidden)] = value[0:1].reshape(hidden)
        ref[pl.ds(hidden, hidden)] = value[1:2].reshape(hidden)
        ref[pl.ds(2 * hidden, classes)] = value[2:3, 0:classes].reshape(classes)
    tail = sums_ref[rows + 3 : rows + 4, 0:128]
    loss_ref[...] = jnp.sum(jnp.where(lane == 0, tail, 0.0), axis=1, keepdims=True)
    count = jnp.sum(jnp.where(lane == 1, tail, 0.0), axis=1, keepdims=True)
    count_ref[...] = count / devices
    clip_ref[...] = clip_norm


def finished(sizes, sums, weights, firsts, seconds, smooths, biases):
    vmem = pl.BlockSpec(memory_space=pltpu.VMEM)
    like = [jax.ShapeDtypeStruct(weight.shape, jnp.float32) for weight in weights]
    scalar = jax.ShapeDtypeStruct((1, 1), jnp.float32)
    return pl.pallas_call(
        functools.partial(final_kernel, sizes, float(lax.axis_size(("section", "dp")))),
        out_shape=(
            scalar,
            scalar,
            scalar,
            jax.ShapeDtypeStruct((2, 3), jnp.float32),
            like,
            like,
            like,
            like,
            [jax.ShapeDtypeStruct(biases[0].shape, jnp.float32)] * 4,
        ),
        in_specs=[vmem] + [(vmem,) * 3] * 4 + [(vmem,) * 4],
        out_specs=(vmem,) * 4 + ([vmem] * 3,) * 4 + ([vmem] * 4,),
    )(sums, weights, firsts, seconds, smooths, biases)


def on_slice_kernels(
    node_table, owner_ids, dest_count, fan_inner, hidden, classes, seed_count, fan_outer, mask_sizes, weight_rows
):
    parts, peers = lax.axis_size("section"), lax.axis_size("dp")
    return (
        parts == 4
        and peers == 8
        and peers * node_table.size * 2 <= VMEM_TABLE_LIMIT
        and node_table.shape[1] == 128
        and node_table.shape[0] % 512 == 0
        and peers * node_table.shape[0] <= 131072
        and owner_ids.shape[0] % 1024 == 0
        and owner_ids.shape[0] <= 32768
        and fan_inner == SLOT - 1
        and dest_count % (BLOCK * GROUP * SETS) == 0
        and dest_count % TILE == 0
        and hidden == 256
        and classes + 2 <= hidden
        and seed_count <= TILE
        and seed_count % 128 == 0
        and dest_count < 16384
        and BLOCK * GROUP * SETS == TILE
        and fan_outer + 2 <= SLOT
        and len(mask_sizes) == 2
        and mask_sizes[0] * mask_sizes[1] <= 65536
        and all(rows % 8 == 0 for rows in weight_rows)
        and sum(weight_rows) % 16 == 0
        and dest_count // TILE > PAUSE
    )


def outer_product(left, right):
    return lax.dot_general(
        left, right, (((0,), (0,)), ((), ())), preferred_element_type=jnp.float32
    )


def against(left, right):
    return lax.dot_general(
        left, right, (((1,), (1,)), ((), ())), preferred_element_type=jnp.float32
    )


def silu_slope(before, grad_out):
    sigmoid = jax.nn.sigmoid(before)
    return (grad_out * sigmoid * (1.0 + before * (1.0 - sigmoid))).astype(jnp.bfloat16)


def moments(weight, gradient, first, second):
    first = BETA_ONE * first + (1.0 - BETA_ONE) * gradient
    second = BETA_TWO * second + (1.0 - BETA_TWO) * gradient * gradient
    update = (
        first / (1.0 - BETA_ONE**STEP) / (jnp.sqrt(second / (1.0 - BETA_TWO**STEP)) + EPSILON)
        + DECAY * weight
    )
    return (first, second, update)


def bias_ratio(weight, update, hidden):
    bounds = ((0, hidden), (hidden, 2 * hidden), (2 * hidden, weight.shape[0]))
    pieces = []
    for start_at, stop_at in bounds:
        weight_norm = jnp.sqrt(jnp.sum(weight[start_at:stop_at] ** 2))
        update_norm = jnp.sqrt(jnp.sum(update[start_at:stop_at] ** 2))
        pieces.append(jnp.zeros((stop_at - start_at,), jnp.float32) + weight_norm / update_norm)
    return jnp.concatenate(pieces)


def gathered_rows(node_table, owner_ids, row_ids):
    peer_count = lax.axis_size("dp")
    parts = lax.axis_size("section")
    table_rows = node_table.shape[0]
    if peer_count * node_table.size * 2 <= WHOLE_TABLE_LIMIT and table_rows % parts == 0:
        part_rows = table_rows // parts
        quarter = lax.dynamic_slice_in_dim(
            node_table, lax.axis_index("section") * part_rows, part_rows, 0
        )
        source = lax.all_gather(quarter, ("section", "dp"), axis=0, tiled=True)
        place = (row_ids // part_rows * peer_count + owner_ids) * part_rows + row_ids % part_rows
        return source, place
    frontier_rows = owner_ids.shape[0]
    slot_count = max(2, 2 * frontier_rows // peer_count)
    owner_hot = (owner_ids[:, None] == jnp.arange(peer_count)[None, :]).astype(jnp.int32)
    ranking = jnp.sum((jnp.cumsum(owner_hot, axis=0) - 1) * owner_hot, axis=1)
    placed = owner_ids * slot_count + ranking
    request = (
        jnp.zeros((peer_count * slot_count,), jnp.int32)
        .at[placed]
        .set(row_ids)
        .reshape(peer_count, slot_count)
    )
    returned = lax.all_to_all(
        node_table[lax.all_to_all(request, "dp", split_axis=0, concat_axis=0, tiled=True)],
        "dp",
        split_axis=0,
        concat_axis=0,
        tiled=True,
    )
    return returned.reshape(peer_count * slot_count, -1), placed


def on_device(
    node_table,
    owners,
    local_rows,
    inner_neighbours,
    inner_counts,
    outer_neighbours,
    outer_counts,
    labels,
    label_mask,
    weight_inner,
    weight_outer,
    weight_head,
    biases,
    first_inner,
    first_outer,
    first_head,
    first_biases,
    second_inner,
    second_outer,
    second_head,
    second_biases,
    smooth_inner,
    smooth_outer,
    smooth_head,
    smooth_biases,
):
    at = lax.axis_index("section")
    every = ("section", "dp")
    hidden = weight_inner.shape[1]
    dest_count, fan_inner = inner_neighbours.shape[1:]
    seed_count, fan_outer = outer_neighbours.shape[1:]
    classes = weight_head.shape[1]
    whole_mask, whole_labels = label_mask, labels
    whole_outer, whole_outer_counts = outer_neighbours, outer_counts
    mask_sizes = label_mask.shape

    def mine(array):
        return lax.dynamic_index_in_dim(array, at, 0, keepdims=False)

    inner_neighbours, inner_counts = mine(inner_neighbours), mine(inner_counts)
    outer_neighbours, outer_counts = mine(outer_neighbours), mine(outer_counts)
    labels, label_mask = mine(labels), mine(label_mask)
    bias_inner = biases[:hidden]
    bias_outer = biases[hidden : 2 * hidden]
    bias_head = biases[2 * hidden :]

    owner_ids, row_ids = owners.reshape(-1), local_rows.reshape(-1)
    weights = (weight_inner, weight_outer, weight_head)
    keep = jnp.arange(fan_inner)[None, :] < inner_counts[:, None]
    if on_slice_kernels(
        node_table,
        owner_ids,
        dest_count,
        fan_inner,
        hidden,
        classes,
        seed_count,
        fan_outer,
        mask_sizes,
        [weight.shape[0] for weight in weights],
    ):
        own = jnp.arange(dest_count, dtype=jnp.int32)[:, None]
        near = jnp.concatenate([jnp.where(keep, inner_neighbours, -1), own], axis=1)
        near = near.reshape(-1, BLOCK * SLOT)
        firsts = (first_inner, first_outer, first_head)
        seconds = (second_inner, second_outer, second_head)
        smooths = (smooth_inner, smooth_outer, smooth_head)
        rows = [weight.shape[0] for weight in weights]
        sums = summed_step(
            node_table,
            weights,
            firsts,
            seconds,
            biases,
            whole_mask,
            owner_ids,
            row_ids,
            near,
            whole_outer,
            whole_outer_counts,
            whole_labels,
        )
        loss, count, clip, norms, news, moment, square, average, bias_outs = finished(
            (classes, *rows),
            sums,
            weights,
            firsts,
            seconds,
            smooths,
            (biases, first_biases, second_biases, smooth_biases),
        )
        return (
            loss.reshape(()),
            count.reshape(()),
            clip.reshape(()),
            norms.T,
            *news,
            bias_outs[0],
            *moment,
            bias_outs[1],
            *square,
            bias_outs[2],
            *average,
            bias_outs[3],
        )

    label_part = jnp.sum(whole_mask.astype(jnp.float32))
    label_count = jnp.maximum(lax.psum(label_part, "dp"), 1.0)
    full_inner, full_outer, full_head = (
        lax.all_gather(weight.astype(jnp.bfloat16), every, axis=0, tiled=True)
        for weight in weights
    )
    source, place = gathered_rows(node_table, owner_ids, row_ids)
    rows = source[place[inner_neighbours]]
    summed = jnp.sum(
        jnp.where(keep[:, :, None], rows, jnp.zeros((), rows.dtype)), axis=1, dtype=jnp.float32
    )
    self_rows = source[place[:dest_count]]
    mean_one = (summed / inner_counts[:, None].astype(jnp.float32)).astype(jnp.bfloat16)
    joined_one = jnp.concatenate([self_rows, mean_one], axis=1)
    pre_one = jnp.dot(joined_one, full_inner, preferred_element_type=jnp.float32) + bias_inner
    hidden_one = jax.nn.silu(pre_one).astype(jnp.bfloat16)

    keep_outer = jnp.arange(fan_outer)[None, :] < outer_counts[:, None]
    pick = jnp.sum(
        (
            jnp.where(keep_outer, outer_neighbours, -1)[:, :, None]
            == jnp.arange(dest_count)[None, None, :]
        ).astype(jnp.float32),
        axis=1,
    ).astype(jnp.bfloat16)
    count_two = outer_counts[:, None].astype(jnp.float32)
    mean_two = (jnp.dot(pick, hidden_one, preferred_element_type=jnp.float32) / count_two).astype(
        jnp.bfloat16
    )
    joined_two = jnp.concatenate([hidden_one[:seed_count], mean_two], axis=1)
    pre_two = jnp.dot(joined_two, full_outer, preferred_element_type=jnp.float32) + bias_outer
    hidden_two = jax.nn.silu(pre_two).astype(jnp.bfloat16)

    logits = jnp.dot(hidden_two, full_head, preferred_element_type=jnp.float32) + bias_head
    shifted = logits - jnp.max(logits, axis=1, keepdims=True)
    log_total = jnp.log(jnp.sum(jnp.exp(shifted), axis=1, keepdims=True))
    chosen = (jnp.arange(classes)[None, :] == labels[:, None]).astype(jnp.float32)
    row_weight = label_mask.astype(jnp.float32)
    loss_part = jnp.sum((log_total[:, 0] - jnp.sum(shifted * chosen, axis=1)) * row_weight)
    grad_logits = (
        (jnp.exp(shifted - log_total) - chosen) * (row_weight / label_count)[:, None]
    ).astype(jnp.bfloat16)
    grad_head = outer_product(hidden_two, grad_logits)
    grad_two = against(grad_logits, full_head).astype(jnp.bfloat16).astype(jnp.float32)
    grad_pre_two = silu_slope(pre_two, grad_two)
    grad_outer = outer_product(joined_two, grad_pre_two)
    grad_joined = against(grad_pre_two, full_outer)
    share = grad_joined[:, hidden:] / count_two
    share_high = share.astype(jnp.bfloat16)
    share_low = (share - share_high.astype(jnp.float32)).astype(jnp.bfloat16)
    grad_one = outer_product(pick, share_high) + outer_product(pick, share_low)
    grad_one = jnp.concatenate(
        [grad_one[:seed_count] + grad_joined[:, :hidden], grad_one[seed_count:]], axis=0
    )
    grad_one = grad_one.astype(jnp.bfloat16).astype(jnp.float32)
    grad_pre_one = silu_slope(pre_one, grad_one)
    grad_inner = outer_product(joined_one, grad_pre_one)
    bias_part = jnp.concatenate(
        [
            jnp.sum(part.astype(jnp.float32), axis=0)
            for part in (grad_pre_one, grad_pre_two, grad_logits)
        ]
    )

    devices = lax.axis_size(every)
    grads = jnp.concatenate(
        [grad.reshape(devices, -1) for grad in (grad_inner, grad_outer, grad_head)], axis=1
    )
    shard = lax.psum_scatter(grads, every, scatter_dimension=0, tiled=True).reshape(-1)
    shards = []
    for weight in weights:
        shards.append(shard[: weight.size].reshape(weight.shape))
        shard = shard[weight.size :]
    packed = lax.psum(jnp.concatenate([bias_part, loss_part[None]]), every)
    bias_grad, loss_sum = packed[:-1], packed[-1]
    grad_partial = sum((jnp.sum(part * part) for part in shards))
    weight_partial = [jnp.sum(weight * weight) for weight in weights]
    squares = lax.psum(jnp.stack([grad_partial] + weight_partial), every)
    clip_norm = jnp.sqrt(squares[0] + jnp.sum(bias_grad * bias_grad))
    factor = jnp.minimum(1.0, CLIP / clip_norm)
    firsts = (first_inner, first_outer, first_head)
    seconds = (second_inner, second_outer, second_head)
    smooths = (smooth_inner, smooth_outer, smooth_head)
    states = [
        moments(weights[slot_at], shards[slot_at] * factor, firsts[slot_at], seconds[slot_at])
        for slot_at in range(3)
    ]
    update_square = lax.psum(jnp.stack([jnp.sum(state[2] * state[2]) for state in states]), every)
    weight_norms = jnp.sqrt(squares[1:])
    update_norms = jnp.sqrt(update_square)
    news = [
        weights[slot_at]
        - RATE * (weight_norms[slot_at] / update_norms[slot_at]) * states[slot_at][2]
        for slot_at in range(3)
    ]
    averages = [
        AVERAGE * smooths[slot_at] + (1.0 - AVERAGE) * news[slot_at] for slot_at in range(3)
    ]
    bias_first, bias_second, bias_update = moments(
        biases, bias_grad * factor, first_biases, second_biases
    )
    bias_new = biases - RATE * bias_ratio(biases, bias_update, hidden) * bias_update
    bias_average = AVERAGE * smooth_biases + (1.0 - AVERAGE) * bias_new
    return (
        loss_sum,
        label_count,
        clip_norm,
        jnp.stack([weight_norms, update_norms], axis=1),
        news[0],
        news[1],
        news[2],
        bias_new,
        states[0][0],
        states[1][0],
        states[2][0],
        bias_first,
        states[0][1],
        states[1][1],
        states[2][1],
        bias_second,
        averages[0],
        averages[1],
        averages[2],
        bias_average,
    )


def solution(mesh):
    in_specs = (
        P("dp", None),
        P("section", "dp", None),
        P("section", "dp"),
        P(None, "dp", None),
        P(None, "dp"),
        P(None, "dp", None),
        P(None, "dp"),
        P(None, "dp"),
        P(None, "dp"),
        P(("section", "dp"), None),
        P(("section", "dp"), None),
        P(("section", "dp"), None),
        P(),
        P(("section", "dp"), None),
        P(("section", "dp"), None),
        P(("section", "dp"), None),
        P(),
        P(("section", "dp"), None),
        P(("section", "dp"), None),
        P(("section", "dp"), None),
        P(),
        P(("section", "dp"), None),
        P(("section", "dp"), None),
        P(("section", "dp"), None),
        P(),
    )
    out_specs = (
        P(),
        P(),
        P(),
        P(),
        P(("section", "dp"), None),
        P(("section", "dp"), None),
        P(("section", "dp"), None),
        P(),
        P(("section", "dp"), None),
        P(("section", "dp"), None),
        P(("section", "dp"), None),
        P(),
        P(("section", "dp"), None),
        P(("section", "dp"), None),
        P(("section", "dp"), None),
        P(),
        P(("section", "dp"), None),
        P(("section", "dp"), None),
        P(("section", "dp"), None),
        P(),
    )
    return jax.shard_map(
        on_device, mesh=mesh, in_specs=in_specs, out_specs=out_specs, check_vma=False
    )
```
